32 devices in a mesh: tp: 4 (over x, core), dp: 8 (over z, y).
Axes of the slice: x: 2, y: 2, z: 4, core: 2. Of those that a mesh axis runs over, the one named last changes fastest.
Arguments:
- tokens: bfloat16 [16384, 768], P('dp'), may hold values from -6 to 6
- memory: bfloat16 [16384, 768], P('dp'), may hold values from -6 to 6
- cotangent: bfloat16 [16384, 768], P('dp'), may hold values from -6 to 6
- tgt_len: int32 [16], P('dp'), may hold values from 1 to 1024, 10240 in all
- src_len: int32 [16], P('dp'), may hold values from 1 to 1024, 12288 in all
- self_query: bfloat16 [768, 768], P(None, 'tp'), may hold values from -0.21875 to 0.21875
- self_key: bfloat16 [768, 768], P(None, 'tp'), may hold values from -0.21875 to 0.21875
- self_value: bfloat16 [768, 768], P(None, 'tp'), may hold values from -0.21875 to 0.21875
- self_out: bfloat16 [768, 768], P('tp'), may hold values from -1.25 to 1.25
- cross_query: bfloat16 [768, 768], P(None, 'tp'), may hold values from -0.21875 to 0.21875
- cross_key: bfloat16 [768, 768], P(None, 'tp'), may hold values from -0.21875 to 0.21875
- cross_value: bfloat16 [768, 768], P(None, 'tp'), may hold values from -0.21875 to 0.21875
- cross_out: bfloat16 [768, 768], P('tp'), may hold values from -1.25 to 1.25
- ffn_up: bfloat16 [768, 3072], P(None, 'tp'), may hold values from -0.21875 to 0.21875
- ffn_down: bfloat16 [3072, 768], P('tp'), may hold values from -0.109375 to 0.109375
- gain_one: float32 [768], replicated, may hold values from 0.5 to 1.5
- shift_one: float32 [768], replicated, may hold values from -1.8 to 1.8
- gain_two: float32 [768], replicated, may hold values from 0.5 to 1.5
- shift_two: float32 [768], replicated, may hold values from -1.8 to 1.8
- gain_three: float32 [768], replicated, may hold values from 0.5 to 1.5
- shift_three: float32 [768], replicated, may hold values from -1.8 to 1.8
Outputs:
- layer_out: bfloat16 [16384, 768], P('dp')
- tokens_grad: bfloat16 [16384, 768], P('dp')
- memory_grad: bfloat16 [16384, 768], P('dp')
- self_query_grad: float32 [768, 768], P(None, 'tp')
- self_key_grad: float32 [768, 768], P(None, 'tp')
- self_value_grad: float32 [768, 768], P(None, 'tp')
- self_out_grad: float32 [768, 768], P('tp')
- cross_query_grad: float32 [768, 768], P(None, 'tp')
- cross_key_grad: float32 [768, 768], P(None, 'tp')
- cross_value_grad: float32 [768, 768], P(None, 'tp')
- cross_out_grad: float32 [768, 768], P('tp')
- ffn_up_grad: float32 [768, 3072], P(None, 'tp')
- ffn_down_grad: float32 [3072, 768], P('tp')
- gain_one_grad: float32 [768], replicated
- shift_one_grad: float32 [768], replicated
- gain_two_grad: float32 [768], replicated
- shift_two_grad: float32 [768], replicated
- gain_three_grad: float32 [768], replicated
- shift_three_grad: float32 [768], replicated
The draws below stay inside these ranges and needn't reach their ends.
Inputs may be any that keep to these rules, and one draw needn't show every extreme that they name: `tgt_len`: one row has all 1024 slots live. `src_len`: one row has all 1024 memory slots live.
All inputs are finite; a program needn't handle non-finite values. No bound on the sum of `tgt_len` or of `src_len` on one device may be relied on, other than what follows from the above.
Results may differ from the reference program's by a relative error of at most 0.04.
Values may be sent and summed in bfloat16 or wider, within the bound.
No kernel may reach another device: no remote copies, remote signals or barrier semaphores. Data moves between devices by JAX's collectives and lax.ppermute only.
A program may use at most 192 MiB of HBM per device.

```python
import math
import jax
import jax.numpy as jnp
import numpy as np
from jax import lax

D = 768
HEADS = 12
HEAD_DIM = 64
FF = 3072
SEQ = 1024
SRC = 1024
ROWS = 16
N_TP = 4


def block_levels(stream_key, extent, pieces, smallest, high):
    def one(axis_at, blocks):
        heights = jax.random.uniform(jax.random.fold_in(jax.random.fold_in(stream_key, 6), axis_at), (blocks,), jnp.float32, smallest / len(pieces), high / len(pieces))
        return jnp.repeat(jnp.exp(heights), extent[axis_at] // blocks).reshape((-1,) + (1,) * (len(extent) - axis_at - 1))

    level = one(*pieces[0])
    for cut in pieces[1:]:
        level = level * one(*cut)
    return level


def profile(amount, total, reach, skew):
    portions = [(1 << 20) // math.isqrt(grade ** skew) + 1 for grade in range(2, amount + 1)]
    spare, holding = total - reach - (amount - 1), [1] * (amount - 1)
    while spare > 0:
        free = [i for i in range(amount - 1) if holding[i] < reach]
        whole, budget = sum([portions[i] for i in free]), spare
        for i in free:
            addition = min(reach - holding[i], max(1, budget * portions[i] // whole), spare)
            holding[i] = holding[i] + addition
            spare = spare - addition
    return np.array([reach] + holding)


def ragged(own_key, amount, total, most, lean):
    if amount == 2:
        one = jax.random.randint(own_key, (), max(1, total - most), min(most, total - 1) + 1)
        return jnp.stack([one, total - one])
    tallies = jnp.asarray(profile(amount, total, most, lean), jnp.int32)
    pairs = (amount - 1) // 2
    donor, taker = tallies[1:1 + 2 * pairs:2], tallies[2:2 + 2 * pairs:2]
    slack = jnp.minimum(donor - 1, most - taker)
    moved = jax.random.randint(jax.random.fold_in(own_key, 1), (pairs,), 0, 1 << 20) % (slack + 1)
    tallies = tallies.at[1:1 + 2 * pairs:2].set(donor - moved).at[2:2 + 2 * pairs:2].set(taker + moved)
    return tallies[jax.random.permutation(jax.random.fold_in(own_key, 2), amount)]


def centred(stream_key, shape, scale, bound, pieces=(), held_as=jnp.bfloat16):
    entries = scale * jax.random.normal(stream_key, shape, jnp.float32)
    if pieces:
        entries = entries * block_levels(stream_key, shape, pieces, -0.22, 0.18)
    return jnp.clip(entries, -bound, bound).astype(held_as)


def setup_inputs(seed: int = 0) -> dict:
    splits = jax.random.split(jax.random.key(seed), 22)
    return {
        "tokens": centred(splits[0], (ROWS * SEQ, D), 1.0, 6.0, ((0, 8),)),
        "memory": centred(splits[1], (ROWS * SRC, D), 1.0, 6.0, ((0, 8),)),
        "cotangent": centred(splits[2], (ROWS * SEQ, D), 1.0, 6.0, ((0, 8),)),
        "tgt_len": ragged(splits[3], ROWS, ROWS * SEQ * 5 // 8, SEQ, 1).astype(jnp.int32),
        "src_len": ragged(splits[4], ROWS, ROWS * SRC * 3 // 4, SRC, 1).astype(jnp.int32),
        "self_query": centred(splits[5], (D, D), D ** -0.5, 0.21875, ((1, 4),)),
        "self_key": centred(splits[6], (D, D), D ** -0.5, 0.21875, ((1, 4),)),
        "self_value": centred(splits[7], (D, D), D ** -0.5, 0.21875, ((1, 4),)),
        "self_out": centred(splits[8], (D, D), (D // 32) ** -0.5, 1.25, ((0, 4),)),
        "cross_query": centred(splits[9], (D, D), D ** -0.5, 0.21875, ((1, 4),)),
        "cross_key": centred(splits[10], (D, D), D ** -0.5, 0.21875, ((1, 4),)),
        "cross_value": centred(splits[11], (D, D), D ** -0.5, 0.21875, ((1, 4),)),
        "cross_out": centred(splits[12], (D, D), (D // 32) ** -0.5, 1.25, ((0, 4),)),
        "ffn_up": centred(splits[13], (D, FF), D ** -0.5, 0.21875, ((1, 4),)),
        "ffn_down": centred(splits[14], (FF, D), FF ** -0.5, 0.109375, ((0, 4),)),
        "gain_one": jnp.clip(1.0 + 0.1 * jax.random.normal(splits[15], (D,), jnp.float32), 0.5, 1.5),
        "shift_one": centred(splits[16], (D,), 0.3, 1.8, (), jnp.float32),
        "gain_two": jnp.clip(1.0 + 0.1 * jax.random.normal(splits[17], (D,), jnp.float32), 0.5, 1.5),
        "shift_two": centred(splits[18], (D,), 0.3, 1.8, (), jnp.float32),
        "gain_three": jnp.clip(1.0 + 0.1 * jax.random.normal(splits[19], (D,), jnp.float32), 0.5, 1.5),
        "shift_three": centred(splits[20], (D,), 0.3, 1.8, (), jnp.float32),
    }


@jax.custom_vjp
def low(v):
    return lax.optimization_barrier(v.astype(jnp.bfloat16)).astype(jnp.float32)

@jax.custom_vjp
def low_back(v):
    return v

def low_keep(v):
    return (low(v), None)

def low_pass(kept, grad):
    return (grad,)

def back_keep(v):
    return (v, None)

def back_low(kept, grad):
    return (low(grad),)
low.defvjp(low_keep, low_pass)
low_back.defvjp(back_keep, back_low)

def matmul(left, right):
    return jnp.dot(left, right, precision=lax.Precision.HIGHEST, preferred_element_type=jnp.float32)

def round_both(value):
    return low_back(low(value))

def layer_norm(resid, gain, shift):
    center = resid - lax.optimization_barrier(jnp.mean(resid, -1, keepdims=True))
    spread = lax.optimization_barrier(jnp.mean(center * center, -1, keepdims=True))
    return center * lax.rsqrt(spread + 1e-05) * gain + shift

def attend(queries, keys, values, allowed):
    length = queries.shape[0]
    query_heads = queries.reshape(length, HEADS, HEAD_DIM)
    key_heads = keys.reshape(keys.shape[0], HEADS, HEAD_DIM)
    value_heads = values.reshape(values.shape[0], HEADS, HEAD_DIM)
    scores = low_back(jnp.einsum('qhd,khd->hqk', query_heads, key_heads, precision=lax.Precision.HIGHEST))
    scores = jnp.where(allowed[None], scores, -1e+30)
    row_peak = lax.optimization_barrier(jnp.max(scores, -1, keepdims=True))
    lifted = jnp.exp(scores - row_peak)
    attn_weights = lifted / lax.optimization_barrier(jnp.sum(lifted, -1, keepdims=True))
    mixed = jnp.einsum('hqk,khd->qhd', low(attn_weights), value_heads, precision=lax.Precision.HIGHEST)
    return round_both(mixed.reshape(length, HEADS * HEAD_DIM))

def mix_groups(attended, weight, each):
    running = jnp.zeros((attended.shape[0], weight.shape[1]), jnp.float32)
    for member in range(N_TP):
        columns = slice(member * each, (member + 1) * each)
        running = running + low(matmul(attended[:, columns], weight[columns, :]))
    return low_back(running)

def row_forward(weights, token_row, memory_row, tgt_limit, src_limit):
    self_query, self_key, self_value, self_out, cross_query, cross_key, cross_value, cross_out, ffn_up, ffn_down, gain_one, shift_one, gain_two, shift_two, gain_three, shift_three = weights
    each = D // N_TP
    hidden_each = FF // N_TP
    scaling = HEAD_DIM ** (-0.5)
    positions = jnp.arange(SEQ)
    causal = (positions[None, :] <= positions[:, None]) & (positions[None, :] < tgt_limit)
    cross_mask = jnp.broadcast_to((jnp.arange(SRC) < src_limit)[None, :], (SEQ, SRC))
    query_list, key_list, value_list = ([], [], [])
    for member in range(N_TP):
        columns = slice(member * each, (member + 1) * each)
        own_copy = low_back(token_row)
        query_list.append(round_both(matmul(own_copy, self_query[:, columns]) * scaling))
        key_list.append(round_both(matmul(own_copy, self_key[:, columns])))
        value_list.append(round_both(matmul(own_copy, self_value[:, columns])))
    attended = attend(jnp.concatenate(query_list, 1), jnp.concatenate(key_list, 1), jnp.concatenate(value_list, 1), causal)
    h_one = layer_norm(token_row + mix_groups(attended, self_out, each), gain_one, shift_one)
    h_one_low = low(h_one)
    query_list, key_list, value_list = ([], [], [])
    for member in range(N_TP):
        columns = slice(member * each, (member + 1) * each)
        own_copy = low_back(h_one_low)
        own_memory = low_back(memory_row)
        query_list.append(round_both(matmul(own_copy, cross_query[:, columns]) * scaling))
        key_list.append(round_both(matmul(own_memory, cross_key[:, columns])))
        value_list.append(round_both(matmul(own_memory, cross_value[:, columns])))
    attended = attend(jnp.concatenate(query_list, 1), jnp.concatenate(key_list, 1), jnp.concatenate(value_list, 1), cross_mask)
    h_two = layer_norm(h_one + mix_groups(attended, cross_out, each), gain_two, shift_two)
    h_two_low = low(h_two)
    running = jnp.zeros((SEQ, D), jnp.float32)
    for member in range(N_TP):
        columns = slice(member * hidden_each, (member + 1) * hidden_each)
        pre_act = low_back(matmul(low_back(h_two_low), ffn_up[:, columns]))
        activated = low(jax.nn.gelu(pre_act, approximate=False))
        running = running + low(matmul(activated, ffn_down[columns, :]))
    return layer_norm(h_two + low_back(running), gain_three, shift_three)

def reference(tokens, memory, cotangent, tgt_len, src_len, self_query, self_key, self_value, self_out, cross_query, cross_key, cross_value, cross_out, ffn_up, ffn_down, gain_one, shift_one, gain_two, shift_two, gain_three, shift_three):
    weights = tuple((weight.astype(jnp.float32) for weight in (self_query, self_key, self_value, self_out, cross_query, cross_key, cross_value, cross_out, ffn_up, ffn_down, gain_one, shift_one, gain_two, shift_two, gain_three, shift_three)))
    token_rows = tokens.astype(jnp.float32).reshape(ROWS, SEQ, D)
    memory_rows = memory.astype(jnp.float32).reshape(ROWS, SRC, D)

    def forward(weight_set, token_set, memory_set):

        def step(running, element):
            return (running, row_forward(weight_set, element[0], element[1], element[2], element[3]))
        _, outputs = lax.scan(jax.checkpoint(step), jnp.zeros((), jnp.float32), (token_set, memory_set, tgt_len, src_len))
        return outputs
    outputs, pullback = jax.vjp(forward, weights, token_rows, memory_rows)
    live_mask = (jnp.arange(SEQ)[None, :] < tgt_len[:, None]).astype(jnp.float32)[..., None]
    grad_weights, grad_tokens, grad_memory = pullback(cotangent.astype(jnp.float32).reshape(ROWS, SEQ, D) * live_mask)
    return (outputs.reshape(ROWS * SEQ, D).astype(jnp.bfloat16), grad_tokens.reshape(ROWS * SEQ, D).astype(jnp.bfloat16), grad_memory.reshape(ROWS * SRC, D).astype(jnp.bfloat16), grad_weights[0], grad_weights[1], grad_weights[2], grad_weights[3], grad_weights[4], grad_weights[5], grad_weights[6], grad_weights[7], grad_weights[8], grad_weights[9], grad_weights[10], grad_weights[11], grad_weights[12], grad_weights[13], grad_weights[14], grad_weights[15])
```

```python
import functools

import jax
import jax.numpy as jnp
from jax import lax
from jax.experimental import pallas as pl
from jax.experimental.pallas import tpu as pltpu
from jax.sharding import PartitionSpec as P

HEAD_DIM = 64
WIDE = 2 * HEAD_DIM
EPS = 1e-05
MASKED = -1e30
LOG2E = 1.4426950408889634
LN2 = 0.6931471805599453
f32 = jnp.float32
bf16 = jnp.bfloat16

CORE = [(0, 1), (1, 0), (2, 3), (3, 2)]
ACROSS = [(0, 2), (2, 0), (1, 3), (3, 1)]
MIB = 1 << 20


def nn(left, right):
    return lax.dot_general(left, right, (((1,), (0,)), ((), ())), preferred_element_type=f32)


def nt(left, right):
    return lax.dot_general(left, right, (((1,), (1,)), ((), ())), preferred_element_type=f32)


def tn(left, right):
    return lax.dot_general(left, right, (((0,), (0,)), ((), ())), preferred_element_type=f32)


def lanes(rows):
    return lax.broadcasted_iota(jnp.int32, (rows, HEAD_DIM), 1)


def three_parts(value):
    high = value.astype(bf16).astype(f32)
    rest = value - high
    middle = rest.astype(bf16).astype(f32)
    return high, middle, rest - middle


def fill_queries(q_ref, rows, count, acc, heads):
    tail = jnp.where(lanes(count) == 0, 1.0, 0.0)
    for h in range(heads):
        part = acc[:, h * HEAD_DIM : (h + 1) * HEAD_DIM]
        q_ref[h, rows, :] = jnp.concatenate([part, tail], 1).astype(bf16)


def fill_keys(k_ref, v_ref, rows, start, count, acc, heads, limit):
    lane = lanes(count)
    index = start + lax.broadcasted_iota(jnp.int32, (count, HEAD_DIM), 0)
    tail = jnp.where(lane == 0, jnp.where(index < limit, 0.0, MASKED), jnp.where(lane < 4, 1.0, 0.0))
    ones = jnp.ones((count, HEAD_DIM), f32)
    for h in range(heads):
        k = acc[:, h * HEAD_DIM : (h + 1) * HEAD_DIM]
        v = acc[:, (heads + h) * HEAD_DIM : (heads + h + 1) * HEAD_DIM]
        k_ref[h, rows, :] = jnp.concatenate([k, tail], 1).astype(bf16)
        v_ref[h, rows, :] = jnp.concatenate([v, ones], 1).astype(bf16)


def attend_block(q_ref, k_ref, v_ref, att_ref, h, column, rows, count, key_end, causal):
    s = nt(q_ref[h, rows, :], k_ref[h, :key_end, :])
    if causal:
        r = lax.broadcasted_iota(jnp.int32, (count, count), 0)
        c = lax.broadcasted_iota(jnp.int32, (count, count), 1)
        diagonal = jnp.where(c <= r, s[:, key_end - count :], MASKED)
        s = diagonal if key_end == count else jnp.concatenate([s[:, : key_end - count], diagonal], 1)
    peak = jnp.max(s, 1, keepdims=True)
    p = jnp.exp2(s - peak).astype(bf16)
    o = nn(p, v_ref[h, :key_end, :])
    total = o[:, HEAD_DIM : HEAD_DIM + 1]
    att_ref[rows, column : column + HEAD_DIM] = (o[:, :HEAD_DIM] / total).astype(bf16)
    high, middle, low = three_parts(-(peak + jnp.log2(total)))
    lane = lanes(count)
    tail = jnp.where(
        lane == 0, 1.0, jnp.where(lane == 1, high, jnp.where(lane == 2, middle, jnp.where(lane == 3, low, 0.0)))
    )
    q_ref[h, rows, HEAD_DIM:] = tail.astype(bf16)


def fill_grads(do_ref, rows, count, grad, att, heads):
    lane = lanes(count)
    for h in range(heads):
        part = grad[:, h * HEAD_DIM : (h + 1) * HEAD_DIM].astype(bf16)
        mixed = att[:, h * HEAD_DIM : (h + 1) * HEAD_DIM].astype(f32)
        inner = jnp.sum(part.astype(f32) * mixed, 1, keepdims=True)
        high, middle, low = three_parts(-inner)
        tail = jnp.where(lane == 0, high, jnp.where(lane == 1, middle, jnp.where(lane == 2, low, 0.0)))
        do_ref[h, rows, :] = jnp.concatenate([part, tail.astype(bf16)], 1)


def back_block(q_ref, k_ref, v_ref, do_ref, dq_ref, dk_ref, dv_ref, h, rows, count, key_end, causal, first):
    q = q_ref[h, rows, :]
    d = do_ref[h, rows, :]
    k = k_ref[h, :key_end, :]
    v = v_ref[h, :key_end, :]
    p = jnp.exp2(nt(k, q))
    if causal:
        r = lax.broadcasted_iota(jnp.int32, (count, count), 0)
        c = lax.broadcasted_iota(jnp.int32, (count, count), 1)
        diagonal = jnp.where(r <= c, p[key_end - count :], 0.0)
        p = diagonal if key_end == count else jnp.concatenate([p[: key_end - count], diagonal], 0)
    ds = (p * nt(v, d)).astype(bf16)
    dv = nn(p.astype(bf16), d)
    dk = nn(ds, q)
    if first:
        dv_ref[h, :key_end, :] = dv
        dk_ref[h, :key_end, :] = dk
    else:
        dv_ref[h, :key_end, :] += dv
        dk_ref[h, :key_end, :] += dk
    dq_ref[h, rows, :] = tn(k, ds).T


def pack_heads(source, rows, heads, factor):
    return jnp.concatenate([source[h, rows, :HEAD_DIM] * factor for h in range(heads)], 1).astype(bf16)


def norm(resid):
    center = resid - jnp.mean(resid, -1, keepdims=True)
    scale = lax.rsqrt(jnp.mean(center * center, -1, keepdims=True) + EPS)
    return center * scale, scale


def norm_back(grad, gain, unit, scale):
    lifted = grad * gain
    first = jnp.mean(lifted, -1, keepdims=True)
    second = jnp.mean(lifted * unit, -1, keepdims=True)
    return scale * (lifted - first - unit * second)


def gelu_pair(value):
    scaled = value * 0.7071067811865476
    density = jnp.exp(-scaled * scaled) * 0.3989422804014327
    below = 0.5 * (1.0 + lax.erf(scaled))
    return value * below, below + value * density


BLOCK = 512


def self_forward_kernel(s_ref, x_ref, w_ref, *rest, heads, second):
    if second:
        att_own_ref, out_own_ref, out_ref, part_ref, q_ref, k_ref, v_ref, att_ref = rest
    else:
        m_ref, ckv_ref, ck_ref, cv_ref, q_ref, k_ref, v_ref, att_ref = rest
    row = s_ref[0]
    limit = s_ref[1 + row]
    length = x_ref.shape[0]
    each = heads * HEAD_DIM

    @pl.loop(0, length, step=BLOCK)
    def _(start):
        rows = pl.ds(pl.multiple_of(start, BLOCK), BLOCK)
        acc = nn(x_ref[rows, :], w_ref[...])
        fill_queries(q_ref, rows, BLOCK, acc[:, :each] * (HEAD_DIM ** (-0.5) * LOG2E), heads)
        fill_keys(k_ref, v_ref, rows, start, BLOCK, acc[:, each:], heads, limit)

    for block in range(length // BLOCK):
        for h in range(heads):
            attend_block(
                q_ref, k_ref, v_ref, att_ref, h, h * HEAD_DIM, pl.ds(block * BLOCK, BLOCK), BLOCK, (block + 1) * BLOCK, True
            )
    if second:

        @pl.loop(0, length, step=BLOCK)
        def _(start):
            rows = pl.ds(pl.multiple_of(start, BLOCK), BLOCK)
            part = nn(att_own_ref[rows, :], out_own_ref[...]) + nn(att_ref[rows, :], out_ref[...])
            part_ref[rows, :] = part.astype(bf16)
    else:
        source = m_ref.shape[0]

        @pl.loop(0, source, step=BLOCK)
        def _(start):
            rows = pl.ds(pl.multiple_of(start, BLOCK), BLOCK)
            acc = nn(m_ref[rows, :], ckv_ref[...])
            fill_keys(ck_ref, cv_ref, rows, start, BLOCK, acc, heads, s_ref[3 + row])


def memory_keys_kernel(s_ref, m_ref, w_ref, k_ref, v_ref, *, heads):
    row = s_ref[0]

    @pl.loop(0, m_ref.shape[0], step=BLOCK)
    def _(start):
        rows = pl.ds(pl.multiple_of(start, BLOCK), BLOCK)
        fill_keys(k_ref, v_ref, rows, start, BLOCK, nn(m_ref[rows, :], w_ref[...]), heads, s_ref[3 + row])


def cross_forward_kernel(
    s_ref, x_ref, pa_ref, pb_ref, gain_ref, shift_ref, wqa_ref, wqb_ref, ka_ref, va_ref, kb_ref, vb_ref, oa_ref, ob_ref,
    part_ref, h_ref, hl_ref, unit_ref, scale_ref, qa_ref, qb_ref, atta_ref, attb_ref, *, heads,
):
    row = s_ref[0]
    limit = s_ref[3 + row]
    length = x_ref.shape[0]
    source = ka_ref.shape[1]

    @pl.loop(0, length, step=BLOCK)
    def _(start):
        rows = pl.ds(pl.multiple_of(start, BLOCK), BLOCK)
        resid = x_ref[rows, :].astype(f32) + (pa_ref[rows, :].astype(f32) + pb_ref[rows, :].astype(f32))
        unit, scale = norm(resid)
        h = unit * gain_ref[...] + shift_ref[...]
        h_ref[rows, :] = h
        unit_ref[rows, :] = unit.astype(bf16)
        scale_ref[rows, :] = scale
        low = h.astype(bf16)
        hl_ref[rows, :] = low
        factor = HEAD_DIM ** (-0.5) * LOG2E
        fill_queries(qa_ref, rows, BLOCK, nn(low, wqa_ref[...]) * factor, heads)
        fill_queries(qb_ref, rows, BLOCK, nn(low, wqb_ref[...]) * factor, heads)

    step = 256
    live = (limit + step - 1) // step
    for count in range(1, source // step + 1):

        @pl.when(live == count)
        def _():
            for q_ref, k_ref, v_ref, att_ref in ((qa_ref, ka_ref, va_ref, atta_ref), (qb_ref, kb_ref, vb_ref, attb_ref)):

                @pl.loop(0, length, step=BLOCK)
                def _(start):
                    rows = pl.ds(pl.multiple_of(start, BLOCK), BLOCK)
                    for h in range(heads):
                        attend_block(q_ref, k_ref, v_ref, att_ref, h, h * HEAD_DIM, rows, BLOCK, count * step, False)

    @pl.loop(0, length, step=BLOCK)
    def _(start):
        rows = pl.ds(pl.multiple_of(start, BLOCK), BLOCK)
        part_ref[rows, :] = (nn(atta_ref[rows, :], oa_ref[...]) + nn(attb_ref[rows, :], ob_ref[...])).astype(bf16)


def ffn_forward_kernel(
    h_in_ref, pa_ref, pb_ref, gain_ref, shift_ref, upa_ref, upb_ref, downa_ref, downb_ref,
    part_ref, h_ref, hl_ref, unit_ref, scale_ref, acta_ref, actb_ref, slopea_ref, slopeb_ref,
):
    length = h_in_ref.shape[0]
    span = 256

    @pl.loop(0, length, step=span)
    def _(start):
        rows = pl.ds(pl.multiple_of(start, span), span)
        resid = h_in_ref[rows, :] + (pa_ref[rows, :].astype(f32) + pb_ref[rows, :].astype(f32))
        unit, scale = norm(resid)
        h = unit * gain_ref[...] + shift_ref[...]
        h_ref[rows, :] = h
        unit_ref[rows, :] = unit.astype(bf16)
        scale_ref[rows, :] = scale
        low = h.astype(bf16)
        hl_ref[rows, :] = low
        part = None
        for up_ref, down_ref, act_ref, slope_ref in (
            (upa_ref, downa_ref, acta_ref, slopea_ref),
            (upb_ref, downb_ref, actb_ref, slopeb_ref),
        ):
            act, slope = gelu_pair(nn(low, up_ref[...]))
            act = act.astype(bf16)
            act_ref[rows, :] = act
            slope_ref[rows, :] = slope.astype(bf16)
            term = nn(act, down_ref[...])
            part = term if part is None else part + term
        part_ref[rows, :] = part.astype(bf16)


def ffn_back_kernel(
    s_ref, h_ref, pa_ref, pb_ref, cot_ref, gain_ref, shift_ref, upa_ref, upb_ref, downa_ref, downb_ref, slopea_ref, slopeb_ref,
    part_ref, out_ref, d_ref, e_ref, prea_ref, preb_ref, sums_ref,
):
    row = s_ref[0]
    limit = s_ref[1 + row]
    length = h_ref.shape[0]
    span = 256
    sums_ref[...] = jnp.zeros_like(sums_ref)

    @pl.loop(0, length, step=span)
    def _(start):
        rows = pl.ds(pl.multiple_of(start, span), span)
        resid = h_ref[rows, :] + (pa_ref[rows, :].astype(f32) + pb_ref[rows, :].astype(f32))
        unit, scale = norm(resid)
        out_ref[rows, :] = (unit * gain_ref[...] + shift_ref[...]).astype(bf16)
        index = start + lax.broadcasted_iota(jnp.int32, (span, 1), 0)
        grad = jnp.where(index < limit, cot_ref[rows, :].astype(f32), 0.0)
        sums_ref[0:1, :] += jnp.sum(grad * unit, 0, keepdims=True)
        sums_ref[1:2, :] += jnp.sum(grad, 0, keepdims=True)
        d = norm_back(grad, gain_ref[...], unit, scale)
        d_ref[rows, :] = d
        e = d.astype(bf16)
        e_ref[rows, :] = e
        part = None
        for up_ref, down_ref, slope_ref, pre_ref in (
            (upa_ref, downa_ref, slopea_ref, prea_ref),
            (upb_ref, downb_ref, slopeb_ref, preb_ref),
        ):
            pre = (nt(e, down_ref[...]) * slope_ref[rows, :].astype(f32)).astype(bf16)
            pre_ref[rows, :] = pre
            term = nt(pre, up_ref[...])
            part = term if part is None else part + term
        part_ref[rows, :] = part.astype(bf16)


def ffn_grad_kernel(h_ref, act_ref, e_ref, pre_ref, grad_ref):
    step = 256
    for start in range(0, grad_ref.shape[1], step):
        columns = slice(start, start + step)
        grad_ref[0, columns, :] = tn(h_ref[:, columns], pre_ref[...]).astype(bf16)
        grad_ref[1, columns, :] = tn(act_ref[:, columns], e_ref[...]).astype(bf16)


def norm_attention_back(
    d_in_ref, pa_ref, pb_ref, gain_ref, unit_ref, scale_ref, groups, d_ref, e_ref, sums_ref, do_ref, heads
):
    length = d_in_ref.shape[0]
    sums_ref[...] = jnp.zeros_like(sums_ref)

    @pl.loop(0, length, step=BLOCK)
    def _(start):
        rows = pl.ds(pl.multiple_of(start, BLOCK), BLOCK)
        grad = d_in_ref[rows, :] + (pa_ref[rows, :].astype(f32) + pb_ref[rows, :].astype(f32))
        unit = unit_ref[rows, :].astype(f32)
        sums_ref[0:1, :] += jnp.sum(grad * unit, 0, keepdims=True)
        sums_ref[1:2, :] += jnp.sum(grad, 0, keepdims=True)
        d = norm_back(grad, gain_ref[...], unit, scale_ref[rows, :])
        d_ref[rows, :] = d
        e = d.astype(bf16)
        e_ref[rows, :] = e
        for g, (out_ref, att_ref) in enumerate(groups):
            fill_grads(do_ref.at[g], rows, BLOCK, nt(e, out_ref[...]), att_ref[rows, :], heads)


def cross_back_kernel(
    s_ref, d_in_ref, pa_ref, pb_ref, gain_ref, unit_ref, scale_ref, oa_ref, ob_ref, atta_ref, attb_ref,
    qa_ref, qb_ref, ka_ref, va_ref, kb_ref, vb_ref, wqa_ref, wqb_ref,
    part_ref, d_ref, e_ref, sums_ref, dqa_ref, dqb_ref, dkva_ref, dkvb_ref, do_ref, dq_ref, dk_ref, dv_ref, *, heads,
):
    row = s_ref[0]
    limit = s_ref[3 + row]
    length = d_in_ref.shape[0]
    source = ka_ref.shape[1]
    norm_attention_back(
        d_in_ref, pa_ref, pb_ref, gain_ref, unit_ref, scale_ref, ((oa_ref, atta_ref), (ob_ref, attb_ref)),
        d_ref, e_ref, sums_ref, do_ref, heads,
    )
    step = 256
    live = (limit + step - 1) // step
    for g, (q_ref, k_ref, v_ref, dqo_ref, dkv_ref) in enumerate(
        ((qa_ref, ka_ref, va_ref, dqa_ref, dkva_ref), (qb_ref, kb_ref, vb_ref, dqb_ref, dkvb_ref))
    ):
        for count in range(1, source // step + 1):

            @pl.when(live == count)
            def _():
                key_end = count * step

                @pl.loop(0, heads)
                def _(h):
                    for block in range(length // BLOCK):
                        back_block(
                            q_ref, k_ref, v_ref, do_ref.at[g], dq_ref, dk_ref, dv_ref, h,
                            pl.ds(block * BLOCK, BLOCK), BLOCK, key_end, False, block == 0,
                        )
                    if key_end < source:
                        dk_ref[h, key_end:, :] = jnp.zeros((source - key_end, WIDE), f32)
                        dv_ref[h, key_end:, :] = jnp.zeros((source - key_end, WIDE), f32)

        @pl.loop(0, length, step=BLOCK)
        def _(start):
            rows = pl.ds(pl.multiple_of(start, BLOCK), BLOCK)
            dqo_ref[rows, :] = pack_heads(dq_ref, rows, heads, HEAD_DIM ** (-0.5))

        @pl.loop(0, source, step=BLOCK)
        def _(start):
            rows = pl.ds(pl.multiple_of(start, BLOCK), BLOCK)
            dkv_ref[rows, :] = jnp.concatenate([pack_heads(dk_ref, rows, heads, LN2), pack_heads(dv_ref, rows, heads, 1.0)], 1)

    @pl.loop(0, length, step=BLOCK)
    def _(start):
        rows = pl.ds(pl.multiple_of(start, BLOCK), BLOCK)
        part_ref[rows, :] = (nt(dqa_ref[rows, :], wqa_ref[...]) + nt(dqb_ref[rows, :], wqb_ref[...])).astype(bf16)


def cross_grad_kernel(s_ref, h_ref, m_ref, att_ref, e_ref, dq_ref, dkv_ref, gq_ref, gkv_ref, go_ref):
    gq_ref[...] = tn(h_ref[...], dq_ref[...]).astype(bf16)
    gkv_ref[...] = tn(m_ref[...], dkv_ref[...]).astype(bf16)
    go_ref[...] = tn(att_ref[...], e_ref[...]).astype(bf16)


def pair_kernel(a_ref, b_ref, wa_ref, wb_ref, part_ref):
    @pl.loop(0, a_ref.shape[0], step=BLOCK)
    def _(start):
        rows = pl.ds(pl.multiple_of(start, BLOCK), BLOCK)
        part_ref[rows, :] = (nt(a_ref[rows, :], wa_ref[...]) + nt(b_ref[rows, :], wb_ref[...])).astype(bf16)


def self_back_heads(q_ref, k_ref, v_ref, do_ref, dq_ref, dk_ref, dv_ref, dqkv_ref, length, heads):
    block = 256

    @pl.loop(0, heads)
    def _(h):
        for at in reversed(range(length // block)):
            back_block(
                q_ref, k_ref, v_ref, do_ref, dq_ref, dk_ref, dv_ref, h,
                pl.ds(at * block, block), block, (at + 1) * block, True, at == length // block - 1,
            )

    @pl.loop(0, length, step=BLOCK)
    def _(start):
        rows = pl.ds(pl.multiple_of(start, BLOCK), BLOCK)
        dqkv_ref[rows, :] = jnp.concatenate(
            [
                pack_heads(dq_ref, rows, heads, HEAD_DIM ** (-0.5)),
                pack_heads(dk_ref, rows, heads, LN2),
                pack_heads(dv_ref, rows, heads, 1.0),
            ],
            1,
        )


def self_back_first_kernel(
    s_ref, x_ref, d_in_ref, pa_ref, pb_ref, gain_ref, unit_ref, scale_ref, oa_ref, ob_ref, atta_ref, attb_ref,
    q_ref, k_ref, v_ref,
    d_ref, e_ref, sums_ref, do_out_ref, dqkv_ref, gw_ref, go_ref, do_ref, dq_ref, dk_ref, dv_ref, *, heads,
):
    length = d_in_ref.shape[0]
    norm_attention_back(
        d_in_ref, pa_ref, pb_ref, gain_ref, unit_ref, scale_ref, ((oa_ref, atta_ref), (ob_ref, attb_ref)),
        d_ref, e_ref, sums_ref, do_ref, heads,
    )
    do_out_ref[...] = do_ref[0]
    self_back_heads(q_ref, k_ref, v_ref, do_ref.at[1], dq_ref, dk_ref, dv_ref, dqkv_ref, length, heads)
    gw_ref[...] = tn(x_ref[...], dqkv_ref[...]).astype(bf16)
    go_ref[...] = tn(attb_ref[...], e_ref[...]).astype(bf16)


def self_back_second_kernel(
    s_ref, x_ref, e_ref, att_ref, q_ref, k_ref, v_ref, do_ref, dqkv_ref, gw_ref, go_ref, dq_ref, dk_ref, dv_ref, *, heads
):
    self_back_heads(q_ref, k_ref, v_ref, do_ref, dq_ref, dk_ref, dv_ref, dqkv_ref, x_ref.shape[0], heads)
    gw_ref[...] = tn(x_ref[...], dqkv_ref[...]).astype(bf16)
    go_ref[...] = tn(att_ref[...], e_ref[...]).astype(bf16)


class Row:
    def __init__(self, array, length):
        self.array = array
        self.length = length


def call(kernel, name, inputs, outputs, scalars=None, scratch=(), micros=5.0, limit=48):
    specs, arrays = [], []
    for item in inputs:
        if isinstance(item, Row):
            specs.append(pl.BlockSpec((item.length, item.array.shape[1]), lambda i, s: (s[0], 0)))
            arrays.append(item.array)
        else:
            rank = item.ndim
            specs.append(pl.BlockSpec(item.shape, functools.partial(lambda rank, *a: (0,) * rank, rank)))
            arrays.append(item)
    shapes = [jax.ShapeDtypeStruct(shape, dtype) for shape, dtype in outputs]
    out_specs = [
        pl.BlockSpec(shape, functools.partial(lambda rank, *a: (0,) * rank, len(shape))) for shape, _ in outputs
    ]
    moved = sum(a.size * a.dtype.itemsize for a in arrays) + sum(s.size * s.dtype.itemsize for s in shapes)
    settings = dict(
        out_shape=shapes,
        compiler_params=pltpu.CompilerParams(vmem_limit_bytes=limit * MIB, dimension_semantics=("arbitrary",)),
        cost_estimate=pl.CostEstimate(flops=int(micros * 1.0e9), bytes_accessed=int(moved), transcendentals=0),
        name=name,
    )
    if scalars is None:
        return pl.pallas_call(
            kernel, grid=(1,), in_specs=specs, out_specs=out_specs, scratch_shapes=list(scratch), **settings
        )(*arrays)
    grid_spec = pltpu.PrefetchScalarGridSpec(
        num_scalar_prefetch=1, grid=(1,), in_specs=specs, out_specs=out_specs, scratch_shapes=list(scratch)
    )
    return pl.pallas_call(kernel, grid_spec=grid_spec, **settings)(scalars, *arrays)


def sum_over_dp(buffer, order, size):
    index = lax.axis_index("dp")
    pieces = buffer
    for bit in order:
        take = (index // (1 << bit)) % 2 == 1
        half = pieces.shape[0] // 2
        low, high = pieces[:half], pieces[half:]
        partner = [(i, i ^ (1 << bit)) for i in range(size)]
        got = lax.ppermute(jnp.where(take, low, high), "dp", partner)
        pieces = (jnp.where(take, high, low).astype(f32) + got.astype(f32)).astype(bf16)
    for bit in reversed(order):
        take = (index // (1 << bit)) % 2 == 1
        partner = [(i, i ^ (1 << bit)) for i in range(size)]
        got = lax.ppermute(pieces, "dp", partner)
        pieces = jnp.concatenate([jnp.where(take, got, pieces), jnp.where(take, pieces, got)], 0)
    return pieces


def local(
    size, tokens, memory, cotangent, tgt_len, src_len, self_query, self_key, self_value, self_out,
    cross_query, cross_key, cross_value, cross_out, ffn_up, ffn_down,
    gain_one, shift_one, gain_two, shift_two, gain_three, shift_three,
):
    width = tokens.shape[1]
    length = tokens.shape[0] // 2
    source = memory.shape[0] // 2
    each = self_query.shape[1]
    heads = each // HEAD_DIM
    hidden = ffn_up.shape[1]
    place = lax.axis_index("tp")
    row = place // 2
    core = place % 2
    scalars = jnp.concatenate([row.astype(jnp.int32).reshape(1), tgt_len, src_len])
    gain_one, shift_one, gain_two, shift_two, gain_three, shift_three = (
        v.reshape(1, width) for v in (gain_one, shift_one, gain_two, shift_two, gain_three, shift_three)
    )
    x = Row(tokens, length)
    mem = Row(memory, source)

    def across(value):
        return lax.ppermute(value, "tp", ACROSS)

    def sibling(value):
        return lax.ppermute(value, "tp", CORE)

    w_a = jnp.concatenate([self_query, self_key, self_value], 1)
    w_b = across(w_a)
    ckv_a = jnp.concatenate([cross_key, cross_value], 1)
    so_a, cq_a, co_a, up_a, down_a = self_out, cross_query, cross_out, ffn_up, ffn_down
    so_b = across(so_a)
    ckv_b = across(ckv_a)
    cq_b = across(cq_a)
    co_b = across(co_a)
    up_b = across(up_a)
    down_b = across(down_a)

    head_shape = ((heads, length, WIDE), bf16)
    key_shape = ((heads, source, WIDE), bf16)
    low = ((length, width), bf16)
    full = ((length, width), f32)
    column = ((length, 1), f32)
    att_shape = ((length, each), bf16)
    sums = ((8, width), f32)

    ck_a, cv_a, q_a, k_a, v_a, att_a = call(
        functools.partial(self_forward_kernel, heads=heads, second=False), "self_forward_own",
        [x, w_a, mem, ckv_a], [key_shape, key_shape, head_shape, head_shape, head_shape, att_shape], scalars, micros=10,
    )
    part, q_b, k_b, v_b, att_b = call(
        functools.partial(self_forward_kernel, heads=heads, second=True), "self_forward_other",
        [x, w_b, att_a, so_a, so_b], [low, head_shape, head_shape, head_shape, att_shape], scalars, micros=9,
    )
    part_other = sibling(part)
    ck_b, cv_b = call(
        functools.partial(memory_keys_kernel, heads=heads), "memory_keys_other", [mem, ckv_b], [key_shape, key_shape], scalars,
        micros=3,
    )
    part, h_one, h_one_low, unit_one, scale_one, cq_rows_a, cq_rows_b, catt_a, catt_b = call(
        functools.partial(cross_forward_kernel, heads=heads), "cross_forward",
        [x, part, part_other, gain_one, shift_one, cq_a, cq_b, ck_a, cv_a, ck_b, cv_b, co_a, co_b],
        [low, full, low, low, column, head_shape, head_shape, att_shape, att_shape], scalars, micros=18,
    )
    part_other = sibling(part)
    hid = ((length, hidden), bf16)
    part, h_two, h_two_low, unit_two, scale_two, act_a, act_b, slope_a, slope_b = call(
        ffn_forward_kernel, "ffn_forward",
        [h_one, part, part_other, gain_two, shift_two, up_a, up_b, down_a, down_b],
        [low, full, low, low, column, hid, hid, hid, hid], micros=12,
    )
    part_other = sibling(part)
    part, out_row, d_three, e_three, pre_a, pre_b, sums_three = call(
        ffn_back_kernel, "ffn_back",
        [h_two, part, part_other, Row(cotangent, length), gain_three, shift_three, up_a, up_b, down_a, down_b, slope_a, slope_b],
        [low, low, full, low, hid, hid, sums], scalars, micros=12,
    )
    part_other = sibling(part)
    ffn_shape = ((2, width, hidden), bf16)
    (gf_b,) = call(ffn_grad_kernel, "ffn_grad_other", [h_two_low, act_b, e_three, pre_b], [ffn_shape], micros=4)
    gf_b_got = across(gf_b)
    (gf_a,) = call(ffn_grad_kernel, "ffn_grad_own", [h_two_low, act_a, e_three, pre_a], [ffn_shape], micros=4)

    back_scratch = [
        pltpu.VMEM((2, heads, length, WIDE), bf16),
        pltpu.VMEM((heads, length, WIDE), f32),
        pltpu.VMEM((heads, source, WIDE), f32),
        pltpu.VMEM((heads, source, WIDE), f32),
    ]
    dkv_shape = ((source, 2 * each), bf16)
    part, d_two, e_two, sums_two, dcq_a, dcq_b, dckv_a, dckv_b = call(
        functools.partial(cross_back_kernel, heads=heads), "cross_back",
        [
            d_three, part, part_other, gain_two, unit_two, scale_two, co_a, co_b, catt_a, catt_b,
            cq_rows_a, cq_rows_b, ck_a, cv_a, ck_b, cv_b, cq_a, cq_b,
        ],
        [low, full, low, sums, att_shape, att_shape, dkv_shape, dkv_shape], scalars, scratch=back_scratch, micros=25,
    )
    part_other = sibling(part)
    cross_shapes = [((width, each), bf16), ((width, 2 * each), bf16), ((each, width), bf16)]
    grads_cross_b = call(
        cross_grad_kernel, "cross_grad_other", [h_one_low, mem, catt_b, e_two, dcq_b, dckv_b], cross_shapes, scalars, micros=3
    )
    grads_cross_got = [across(g) for g in grads_cross_b]
    grads_cross_a = call(
        cross_grad_kernel, "cross_grad_own", [h_one_low, mem, catt_a, e_two, dcq_a, dckv_a], cross_shapes, scalars, micros=3
    )
    (part_memory,) = call(pair_kernel, "memory_grad", [dckv_a, dckv_b, ckv_a, ckv_b], [((source, width), bf16)], micros=3)

    w_shape = ((width, 3 * each), bf16)
    o_shape = ((each, width), bf16)
    qkv_shape = ((length, 3 * each), bf16)
    d_one, e_one, sums_one, do_a, dqkv_b, gw_b, go_b = call(
        functools.partial(self_back_first_kernel, heads=heads), "self_back_other",
        [
            x, d_two, part, part_other, gain_one, unit_one, scale_one, so_a, so_b, att_a, att_b, q_b, k_b, v_b,
        ],
        [full, low, sums, head_shape, qkv_shape, w_shape, o_shape], scalars, scratch=back_scratch, micros=16,
    )
    gw_got = across(gw_b)
    go_got = across(go_b)
    dqkv_a, gw_a, go_a = call(
        functools.partial(self_back_second_kernel, heads=heads), "self_back_own",
        [x, e_one, att_a, q_a, k_a, v_a, do_a], [qkv_shape, w_shape, o_shape], scalars, scratch=back_scratch[1:], micros=11,
    )
    (part_tokens,) = call(pair_kernel, "tokens_grad", [dqkv_a, dqkv_b, w_a, w_b], [low], micros=4)

    def own_half(value, which):
        half = value.shape[0] // 2
        return jnp.where(which == 0, value[:half], value[half:])

    def whole(half):
        far = across(half)
        pair = jnp.stack([half, far])
        other = sibling(pair)
        first = jnp.where(core == 0, pair, other)
        second = jnp.where(core == 0, other, pair)
        mine = [first[0], second[0]]
        theirs = [first[1], second[1]]
        top = [jnp.where(row == 0, m, t) for m, t in zip(mine, theirs)]
        bottom = [jnp.where(row == 0, t, m) for m, t in zip(mine, theirs)]
        return jnp.concatenate(top + bottom, 0)

    layer_out = whole(own_half(out_row, core))
    memory_half = own_half(part_memory, core).astype(f32) + sibling(own_half(part_memory, 1 - core)).astype(f32)
    memory_grad = whole(memory_half.astype(bf16))
    tokens_half = own_half(d_one, core) + (
        own_half(part_tokens, core).astype(f32) + sibling(own_half(part_tokens, 1 - core)).astype(f32)
    )
    tokens_grad = whole(tokens_half.astype(bf16))

    bits = [b for b in range(size.bit_length() - 1)]
    turned = bits[1:] + bits[:1]

    def total(mine, got, order):
        return sum_over_dp((mine.astype(f32) + got.astype(f32)).astype(bf16), order, size)

    gf_sum = [total(gf_a[i], gf_b_got[i], order) for i, order in ((0, bits), (1, turned))]
    cross_sum = [total(a, b, order) for a, b, order in zip(grads_cross_a, grads_cross_got, (turned, bits, turned))]
    go_sum = total(go_a, go_got, turned)
    half = width // 2
    gw_sum = jnp.concatenate(
        [total(gw_a[:half], gw_got[:half], bits), total(gw_a[half:], gw_got[half:], turned)], 0
    )

    small = jnp.concatenate([sums_one[:2], sums_two[:2], sums_three[:2], sums_three[2:4]], 0)
    small = small + across(small)
    for bit in bits:
        small = small + lax.ppermute(small, "dp", [(i, i ^ (1 << bit)) for i in range(size)])

    gw_sum = gw_sum.astype(f32)
    ckv_sum = cross_sum[1].astype(f32)
    return (
        layer_out, tokens_grad, memory_grad,
        gw_sum[:, :each], gw_sum[:, each : 2 * each], gw_sum[:, 2 * each :], go_sum.astype(f32),
        cross_sum[0].astype(f32), ckv_sum[:, :each], ckv_sum[:, each:], cross_sum[2].astype(f32),
        gf_sum[0].astype(f32), gf_sum[1].astype(f32),
        small[0], small[1], small[2], small[3], small[4], small[5],
    )


def solution(mesh):
    rows, columns, down = P("dp", None), P(None, "tp"), P("tp", None)
    return jax.shard_map(
        functools.partial(local, mesh.shape["dp"]),
        mesh=mesh,
        in_specs=(rows, rows, rows, P("dp"), P("dp"))
        + (columns, columns, columns, down) * 2
        + (columns, down)
        + (P(),) * 6,
        out_specs=(rows, rows, rows) + (columns, columns, columns, down) * 2 + (columns, down) + (P(),) * 6,
        check_vma=False,
    )
```

```python
import functools

import jax
import jax.numpy as jnp
from jax import lax
from jax.experimental import pallas as pl
from jax.experimental.pallas import tpu as pltpu
from jax.sharding import PartitionSpec as P

HEAD_DIM = 64
WIDE = 2 * HEAD_DIM
EPS = 1e-05
MASKED = -1e30
LOG2E = 1.4426950408889634
LN2 = 0.6931471805599453
f32 = jnp.float32
bf16 = jnp.bfloat16

CORE = [(0, 1), (1, 0), (2, 3), (3, 2)]
ACROSS = [(0, 2), (2, 0), (1, 3), (3, 1)]
MIB = 1 << 20
LIMIT = 56


def nn(left, right):
    return lax.dot_general(left, right, (((1,), (0,)), ((), ())), preferred_element_type=f32)


def nt(left, right):
    return lax.dot_general(left, right, (((1,), (1,)), ((), ())), preferred_element_type=f32)


def tn(left, right):
    return lax.dot_general(left, right, (((0,), (0,)), ((), ())), preferred_element_type=f32)


def lanes(rows):
    return lax.broadcasted_iota(jnp.int32, (rows, HEAD_DIM), 1)


def three_parts(value):
    high = value.astype(bf16).astype(f32)
    rest = value - high
    middle = rest.astype(bf16).astype(f32)
    return high, middle, rest - middle


def fill_queries(q_ref, rows, count, acc, heads):
    tail = jnp.where(lanes(count) == 0, 1.0, 0.0)
    for h in range(heads):
        part = acc[:, h * HEAD_DIM : (h + 1) * HEAD_DIM]
        q_ref[h, rows, :] = jnp.concatenate([part, tail], 1).astype(bf16)


def fill_keys(k_ref, v_ref, rows, start, count, acc, heads, limit):
    lane = lanes(count)
    index = start + lax.broadcasted_iota(jnp.int32, (count, HEAD_DIM), 0)
    tail = jnp.where(lane == 0, jnp.where(index < limit, 0.0, MASKED), jnp.where(lane < 4, 1.0, 0.0))
    ones = jnp.ones((count, HEAD_DIM), f32)
    for h in range(heads):
        k = acc[:, h * HEAD_DIM : (h + 1) * HEAD_DIM]
        v = acc[:, (heads + h) * HEAD_DIM : (heads + h + 1) * HEAD_DIM]
        k_ref[h, rows, :] = jnp.concatenate([k, tail], 1).astype(bf16)
        v_ref[h, rows, :] = jnp.concatenate([v, ones], 1).astype(bf16)


def attend_block(q_ref, k_ref, v_ref, att_ref, h, column, rows, count, key_end, causal):
    s = nt(q_ref[h, rows, :], k_ref[h, :key_end, :])
    if causal:
        r = lax.broadcasted_iota(jnp.int32, (count, count), 0)
        c = lax.broadcasted_iota(jnp.int32, (count, count), 1)
        diagonal = jnp.where(c <= r, s[:, key_end - count :], MASKED)
        s = diagonal if key_end == count else jnp.concatenate([s[:, : key_end - count], diagonal], 1)
    peak = jnp.max(s, 1, keepdims=True)
    p = jnp.exp2(s - peak).astype(bf16)
    o = nn(p, v_ref[h, :key_end, :])
    total = o[:, HEAD_DIM : HEAD_DIM + 1]
    att_ref[rows, column : column + HEAD_DIM] = (o[:, :HEAD_DIM] / total).astype(bf16)
    high, middle, low = three_parts(-(peak + jnp.log2(total)))
    lane = lanes(count)
    tail = jnp.where(
        lane == 0, 1.0, jnp.where(lane == 1, high, jnp.where(lane == 2, middle, jnp.where(lane == 3, low, 0.0)))
    )
    q_ref[h, rows, HEAD_DIM:] = tail.astype(bf16)


def fill_grads(do_ref, rows, count, grad, att, heads):
    lane = lanes(count)
    for h in range(heads):
        part = grad[:, h * HEAD_DIM : (h + 1) * HEAD_DIM].astype(bf16)
        mixed = att[:, h * HEAD_DIM : (h + 1) * HEAD_DIM].astype(f32)
        inner = jnp.sum(part.astype(f32) * mixed, 1, keepdims=True)
        high, middle, low = three_parts(-inner)
        tail = jnp.where(lane == 0, high, jnp.where(lane == 1, middle, jnp.where(lane == 2, low, 0.0)))
        do_ref[h, rows, :] = jnp.concatenate([part, tail.astype(bf16)], 1)


def back_block(q_ref, k_ref, v_ref, do_ref, dq_ref, dk_ref, dv_ref, h, rows, count, key_end, causal, first):
    q = q_ref[h, rows, :]
    d = do_ref[h, rows, :]
    k = k_ref[h, :key_end, :]
    v = v_ref[h, :key_end, :]
    p = jnp.exp2(nt(k, q))
    if causal:
        r = lax.broadcasted_iota(jnp.int32, (count, count), 0)
        c = lax.broadcasted_iota(jnp.int32, (count, count), 1)
        diagonal = jnp.where(r <= c, p[key_end - count :], 0.0)
        p = diagonal if key_end == count else jnp.concatenate([p[: key_end - count], diagonal], 0)
    ds = (p * nt(v, d)).astype(bf16)
    dv = nn(p.astype(bf16), d)
    dk = nn(ds, q)
    if first:
        dv_ref[h, :key_end, :] = dv
        dk_ref[h, :key_end, :] = dk
    else:
        dv_ref[h, :key_end, :] += dv
        dk_ref[h, :key_end, :] += dk
    dq_ref[h, rows, :] = tn(k, ds).T


def pack_heads(source, rows, heads, factor):
    return jnp.concatenate([source[h, rows, :HEAD_DIM] * factor for h in range(heads)], 1).astype(bf16)


def norm(resid):
    center = resid - jnp.mean(resid, -1, keepdims=True)
    scale = lax.rsqrt(jnp.mean(center * center, -1, keepdims=True) + EPS)
    return center * scale, scale


def norm_back(grad, gain, unit, scale):
    lifted = grad * gain
    first = jnp.mean(lifted, -1, keepdims=True)
    second = jnp.mean(lifted * unit, -1, keepdims=True)
    return scale * (lifted - first - unit * second)


def gelu_pair(value):
    scaled = value * 0.7071067811865476
    density = jnp.exp(-scaled * scaled) * 0.3989422804014327
    below = 0.5 * (1.0 + lax.erf(scaled))
    return value * below, below + value * density


BLOCK = 512
SPAN = 256


def both_halves(first_ref, second_ref, blocks):
    return jnp.where(pl.program_id(0) < blocks // 2, first_ref[...], second_ref[...]).astype(f32)


def self_forward_kernel(s_ref, x_ref, w_ref, *rest, heads, second):
    if second:
        att_own_ref, out_own_ref, out_ref, part_ref, q_ref, k_ref, v_ref, att_ref = rest
    else:
        m_ref, wq_ref, wk_ref, wv_ref, so_ref, co_ref, cw_ref, o_ref, ck_ref, cv_ref, q_ref, k_ref, v_ref, att_ref = rest

        @pl.when(pl.program_id(0) == 0)
        def _():
            for at, ref in enumerate((wq_ref, wk_ref, wv_ref)):
                cw_ref[at * ref.shape[0] : (at + 1) * ref.shape[0], :] = ref[...]
            for at, ref in enumerate((so_ref, co_ref)):
                o_ref[at * ref.shape[0] : (at + 1) * ref.shape[0], :] = ref[...]

    row = s_ref[0]
    limit = s_ref[1 + row]
    each = heads * HEAD_DIM
    at = pl.program_id(0)
    start = pl.multiple_of(at * BLOCK, BLOCK)
    acc = nt(x_ref[...], w_ref[...])
    everything = pl.ds(0, BLOCK)
    fill_queries(q_ref, everything, BLOCK, acc[:, :each] * (HEAD_DIM ** (-0.5) * LOG2E), heads)
    fill_keys(k_ref, v_ref, pl.ds(start, BLOCK), start, BLOCK, acc[:, each:], heads, limit)
    for block in range(k_ref.shape[1] // BLOCK):

        @pl.when(at == block)
        def _():
            for h in range(heads):
                attend_block(
                    q_ref, k_ref, v_ref, att_ref, h, h * HEAD_DIM, everything, BLOCK, (block + 1) * BLOCK, True
                )

    if second:
        part = nn(att_own_ref[...], out_own_ref[:each, :]) + nn(att_ref[...], out_ref[:each, :])
        part_ref[...] = part.astype(bf16)
    else:
        acc = nt(m_ref[...], cw_ref[each:, :])
        fill_keys(ck_ref, cv_ref, everything, start, BLOCK, acc, heads, s_ref[3 + row])


def memory_keys_kernel(s_ref, m_ref, w_ref, k_ref, v_ref, *, heads):
    row = s_ref[0]
    acc = nt(m_ref[...], w_ref[heads * HEAD_DIM :, :])
    fill_keys(k_ref, v_ref, pl.ds(0, BLOCK), pl.program_id(0) * BLOCK, BLOCK, acc, heads, s_ref[3 + row])


def cross_forward_kernel(
    s_ref, x_ref, pa_ref, pb_first_ref, pb_second_ref, gain_ref, shift_ref, cwa_ref, cwb_ref,
    ka_ref, va_ref, kb_ref, vb_ref, oa_ref, ob_ref,
    part_ref, h_ref, hl_ref, unit_ref, scale_ref, qa_ref, qb_ref, atta_ref, attb_ref, *, heads, blocks,
):
    row = s_ref[0]
    limit = s_ref[3 + row]
    source = ka_ref.shape[1]
    each = heads * HEAD_DIM
    everything = pl.ds(0, BLOCK)
    other = both_halves(pb_first_ref, pb_second_ref, blocks)
    unit, scale = norm(x_ref[...].astype(f32) + (pa_ref[...].astype(f32) + other))
    h = unit * gain_ref[...] + shift_ref[...]
    h_ref[...] = h
    unit_ref[...] = unit.astype(bf16)
    scale_ref[...] = scale
    low = h.astype(bf16)
    hl_ref[...] = low
    factor = HEAD_DIM ** (-0.5) * LOG2E
    fill_queries(qa_ref, everything, BLOCK, nt(low, cwa_ref[:each, :]) * factor, heads)
    fill_queries(qb_ref, everything, BLOCK, nt(low, cwb_ref[:each, :]) * factor, heads)

    step = 256
    live = (limit + step - 1) // step
    for count in range(1, source // step + 1):

        @pl.when(live == count)
        def _():
            for q_ref, k_ref, v_ref, att_ref in ((qa_ref, ka_ref, va_ref, atta_ref), (qb_ref, kb_ref, vb_ref, attb_ref)):
                for h in range(heads):
                    attend_block(q_ref, k_ref, v_ref, att_ref, h, h * HEAD_DIM, everything, BLOCK, count * step, False)

    part_ref[...] = (nn(atta_ref[...], oa_ref[each:, :]) + nn(attb_ref[...], ob_ref[each:, :])).astype(bf16)


def ffn_forward_kernel(
    h_in_ref, pa_ref, pb_first_ref, pb_second_ref, gain_ref, shift_ref, upa_ref, upb_ref, downa_ref, downb_ref,
    part_ref, h_ref, hl_ref, unit_ref, scale_ref, acta_ref, actb_ref, slopea_ref, slopeb_ref, *, blocks,
):
    other = both_halves(pb_first_ref, pb_second_ref, blocks)
    unit, scale = norm(h_in_ref[...] + (pa_ref[...].astype(f32) + other))
    h = unit * gain_ref[...] + shift_ref[...]
    h_ref[...] = h
    unit_ref[...] = unit.astype(bf16)
    scale_ref[...] = scale
    low = h.astype(bf16)
    hl_ref[...] = low
    part = None
    for up_ref, down_ref, act_ref, slope_ref in (
        (upa_ref, downa_ref, acta_ref, slopea_ref),
        (upb_ref, downb_ref, actb_ref, slopeb_ref),
    ):
        act, slope = gelu_pair(nn(low, up_ref[...]))
        act = act.astype(bf16)
        act_ref[...] = act
        slope_ref[...] = slope.astype(bf16)
        term = nn(act, down_ref[...])
        part = term if part is None else part + term
    part_ref[...] = part.astype(bf16)


def ffn_back_kernel(
    s_ref, h_ref, pa_ref, pb_first_ref, pb_second_ref, cot_ref, gain_ref, shift_ref, upa_ref, upb_ref, downa_ref, downb_ref,
    slopea_ref, slopeb_ref,
    part_ref, out_ref, half_ref, d_ref, e_ref, prea_ref, preb_ref, sums_ref, *, blocks,
):
    row = s_ref[0]
    limit = s_ref[1 + row]
    at = pl.program_id(0)

    @pl.when(at == 0)
    def _():
        sums_ref[...] = jnp.zeros_like(sums_ref)

    other = both_halves(pb_first_ref, pb_second_ref, blocks)
    unit, scale = norm(h_ref[...] + (pa_ref[...].astype(f32) + other))
    out = (unit * gain_ref[...] + shift_ref[...]).astype(bf16)
    out_ref[...] = out

    @pl.when(at // (blocks // 2) == s_ref[5])
    def _():
        half_ref[...] = out

    index = at * SPAN + lax.broadcasted_iota(jnp.int32, (SPAN, 1), 0)
    grad = jnp.where(index < limit, cot_ref[...].astype(f32), 0.0)
    sums_ref[0:1, :] += jnp.sum(grad * unit, 0, keepdims=True)
    sums_ref[1:2, :] += jnp.sum(grad, 0, keepdims=True)
    d = norm_back(grad, gain_ref[...], unit, scale)
    d_ref[...] = d
    e = d.astype(bf16)
    e_ref[...] = e
    part = None
    for up_ref, down_ref, slope_ref, pre_ref in (
        (upa_ref, downa_ref, slopea_ref, prea_ref),
        (upb_ref, downb_ref, slopeb_ref, preb_ref),
    ):
        pre = (nt(e, down_ref[...]) * slope_ref[...].astype(f32)).astype(bf16)
        pre_ref[...] = pre
        term = nt(pre, up_ref[...])
        part = term if part is None else part + term
    part_ref[...] = part.astype(bf16)


def ffn_grad_kernel(h_ref, act_ref, e_ref, pre_ref, up_ref, down_ref):
    up_ref[...] = tn(h_ref[...], pre_ref[...]).astype(bf16)
    down_ref[...] = tn(act_ref[...], e_ref[...]).astype(bf16)


def norm_attention_back(
    d_in_ref, pa_ref, pb_first_ref, pb_second_ref, gain_ref, unit_ref, scale_ref, groups, d_ref, e_ref, sums_ref, do_ref,
    heads, count, blocks,
):
    @pl.when(pl.program_id(0) == 0)
    def _():
        sums_ref[...] = jnp.zeros_like(sums_ref)

    other = both_halves(pb_first_ref, pb_second_ref, blocks)
    grad = d_in_ref[...] + (pa_ref[...].astype(f32) + other)
    unit = unit_ref[...].astype(f32)
    sums_ref[0:1, :] += jnp.sum(grad * unit, 0, keepdims=True)
    sums_ref[1:2, :] += jnp.sum(grad, 0, keepdims=True)
    d = norm_back(grad, gain_ref[...], unit, scale_ref[...])
    d_ref[...] = d
    e = d.astype(bf16)
    e_ref[...] = e
    for g, (out, att_ref) in enumerate(groups):
        fill_grads(do_ref.at[g], pl.ds(0, count), count, nt(e, out), att_ref[...], heads)


def cross_back_kernel(
    s_ref, d_in_ref, pa_ref, pb_first_ref, pb_second_ref, gain_ref, unit_ref, scale_ref, oa_ref, ob_ref, atta_ref, attb_ref,
    qa_ref, qb_ref, ka_ref, va_ref, kb_ref, vb_ref, cwa_ref, cwb_ref,
    part_ref, d_ref, e_ref, sums_ref, dqa_ref, dqb_ref, dkva_ref, dkvb_ref, do_ref, dq_ref, dk_ref, dv_ref, *, heads, blocks,
):
    row = s_ref[0]
    limit = s_ref[3 + row]
    source = ka_ref.shape[1]
    each = heads * HEAD_DIM
    at = pl.program_id(0)
    norm_attention_back(
        d_in_ref, pa_ref, pb_first_ref, pb_second_ref, gain_ref, unit_ref, scale_ref,
        ((oa_ref[each:, :], atta_ref), (ob_ref[each:, :], attb_ref)),
        d_ref, e_ref, sums_ref, do_ref, heads, BLOCK, blocks,
    )

    @pl.when(at == 0)
    def _():
        dk_ref[...] = jnp.zeros_like(dk_ref)
        dv_ref[...] = jnp.zeros_like(dv_ref)

    step = 256
    live = (limit + step - 1) // step
    everything = pl.ds(0, BLOCK)
    for count in range(1, source // step + 1):

        @pl.when(live == count)
        def _():
            for g, (q_ref, k_ref, v_ref) in enumerate(((qa_ref, ka_ref, va_ref), (qb_ref, kb_ref, vb_ref))):

                @pl.loop(0, heads)
                def _(h):
                    back_block(
                        q_ref, k_ref, v_ref, do_ref.at[g], dq_ref.at[g], dk_ref.at[g], dv_ref.at[g], h,
                        everything, BLOCK, count * step, False, False,
                    )

    for g, dqo_ref in enumerate((dqa_ref, dqb_ref)):
        dqo_ref[...] = pack_heads(dq_ref.at[g], everything, heads, HEAD_DIM ** (-0.5))
    part_ref[...] = (nn(dqa_ref[...], cwa_ref[:each, :]) + nn(dqb_ref[...], cwb_ref[:each, :])).astype(bf16)

    @pl.when(at == blocks - 1)
    def _():
        for g, dkv_ref in enumerate((dkva_ref, dkvb_ref)):

            @pl.loop(0, source, step=BLOCK)
            def _(start):
                rows = pl.ds(pl.multiple_of(start, BLOCK), BLOCK)
                dkv_ref[rows, :] = jnp.concatenate(
                    [pack_heads(dk_ref.at[g], rows, heads, LN2), pack_heads(dv_ref.at[g], rows, heads, 1.0)], 1
                )


def cross_grad_kernel(s_ref, h_ref, m_ref, att_ref, e_ref, dq_ref, dkv_ref, g_ref):
    each = dq_ref.shape[1]
    g_ref[:each, :] = tn(dq_ref[...], h_ref[...]).astype(bf16)
    g_ref[each : 3 * each, :] = tn(dkv_ref[...], m_ref[...]).astype(bf16)
    g_ref[3 * each :, :] = tn(att_ref[...], e_ref[...]).astype(bf16)


def memory_grad_kernel(s_ref, a_ref, b_ref, wa_ref, wb_ref, send_ref, keep_ref, *, skip):
    part = (nn(a_ref[...], wa_ref[skip:, :]) + nn(b_ref[...], wb_ref[skip:, :])).astype(bf16)
    mine = pl.program_id(0) == s_ref[5]

    @pl.when(mine)
    def _():
        keep_ref[...] = part

    @pl.when(jnp.logical_not(mine))
    def _():
        send_ref[...] = part


def tokens_grad_kernel(s_ref, d_ref, a_ref, b_ref, wa_ref, wb_ref, send_ref, keep_ref):
    part = nn(a_ref[...], wa_ref[...]) + nn(b_ref[...], wb_ref[...])
    mine = pl.program_id(0) == s_ref[5]

    @pl.when(mine)
    def _():
        keep_ref[...] = d_ref[...] + part

    @pl.when(jnp.logical_not(mine))
    def _():
        send_ref[...] = part.astype(bf16)


def finish_kernel(keep_ref, got_ref, out_ref):
    out_ref[...] = (keep_ref[...].astype(f32) + got_ref[...].astype(f32)).astype(bf16)


def place_kernel(s_ref, *refs, shift):
    out_ref = refs[-1]
    pieces = refs[:-1]
    half = out_ref.shape[0]
    row, core, at = s_ref[0], s_ref[5], pl.program_id(0)
    if shift:
        sources = [
            (pieces[0].at[:half, :], 2 * row), (pieces[0].at[half:, :], 2 * row + 1),
            (pieces[1], 2 * (1 - row) + core), (pieces[2], 2 * (1 - row) + 1 - core),
        ]
    else:
        sources = [
            (pieces[0], 2 * row + core), (pieces[1], 2 * row + 1 - core),
            (pieces[2], 2 * (1 - row) + core), (pieces[3], 2 * (1 - row) + 1 - core),
        ]
    for ref, place in sources:

        @pl.when(at == place)
        def _():
            out_ref[...] = ref[...]


def hop_kernel(s_ref, *refs, plans, slots):
    at = 0
    scratch = refs[-1]
    inputs = sum(own + got for own, got, _ in plans)
    outs = list(refs[inputs:-1])
    for own, got, chains in plans:
        mine, theirs = refs[at : at + own], refs[at + own : at + own + got]
        at += own + got
        row = 0
        for a_ref, b_ref in zip(mine, theirs):
            count = a_ref.shape[0]
            scratch[row : row + count, :] = (a_ref[...].astype(f32) + b_ref[...].astype(f32)).astype(bf16)
            row += count
        end = max(first + rows for first, rows, _ in chains)
        if row < end:
            scratch[row:end, :] = jnp.zeros((end - row, scratch.shape[1]), bf16)
        for first, rows, bit in chains:
            if bit is None:
                outs.pop(0)[...] = scratch[first : first + rows, :]
            else:
                half = rows // 2
                high = s_ref[6 + bit]
                outs.pop(0)[...] = scratch[pl.ds(pl.multiple_of(first + (1 - high) * half, 16), half), :]
                outs.pop(0)[...] = scratch[pl.ds(pl.multiple_of(first + high * half, 16), half), :]


def gather_kernel(s_ref, *refs, chains, cuts):
    scratch = refs[-1]
    at = 0
    for first, rows, order in chains:
        piece = rows // 8
        for turn in range(8):
            place = first
            for level, bit in enumerate(order):
                flip = (turn >> (2 - level)) & 1
                value = s_ref[6 + bit] if flip == 0 else 1 - s_ref[6 + bit]
                place = place + value * (rows >> (level + 1))
            scratch[pl.ds(pl.multiple_of(place, 16), piece), :] = refs[at][...]
            at += 1
    for out_ref, (first, count) in zip(refs[at:-1], cuts):
        out_ref[...] = scratch[first : first + count, :].astype(f32)


def add_kernel(*refs):
    count = len(refs) // 3
    for a_ref, b_ref, out_ref in zip(refs[:count], refs[count : 2 * count], refs[2 * count :]):
        out_ref[...] = (a_ref[...].astype(f32) + b_ref[...].astype(f32)).astype(bf16)


def self_back_heads(q_ref, k_ref, v_ref, do_ref, dq_ref, dk_ref, dv_ref, dqkv_ref, length, heads, at):
    each = heads * HEAD_DIM

    @pl.when(at == 0)
    def _():
        dk_ref[...] = jnp.zeros_like(dk_ref)
        dv_ref[...] = jnp.zeros_like(dv_ref)

    everything = pl.ds(0, SPAN)
    for block in range(length // SPAN):

        @pl.when(at == block)
        def _():
            @pl.loop(0, heads)
            def _(h):
                back_block(
                    q_ref, k_ref, v_ref, do_ref, dq_ref, dk_ref, dv_ref, h,
                    everything, SPAN, (block + 1) * SPAN, True, False,
                )

    dqkv_ref[pl.ds(pl.multiple_of(at * SPAN, SPAN), SPAN), :each] = pack_heads(dq_ref, everything, heads, HEAD_DIM ** (-0.5))

    @pl.when(at == length // SPAN - 1)
    def _():
        @pl.loop(0, length, step=BLOCK)
        def _(start):
            rows = pl.ds(pl.multiple_of(start, BLOCK), BLOCK)
            dqkv_ref[rows, each:] = jnp.concatenate(
                [pack_heads(dk_ref, rows, heads, LN2), pack_heads(dv_ref, rows, heads, 1.0)], 1
            )


def self_back_first_kernel(
    s_ref, x_ref, d_in_ref, pa_ref, pb_first_ref, pb_second_ref, gain_ref, unit_ref, scale_ref, oa_ref, ob_ref,
    atta_ref, attb_ref, q_ref, k_ref, v_ref, sums_two_ref, sums_three_ref,
    d_ref, do_out_ref, dqkv_ref, gw_ref, ra_ref, rb_ref, e_ref, sums_ref, do_ref, dq_ref, dk_ref, dv_ref, *, heads, blocks,
):
    at = pl.program_id(0)
    each = heads * HEAD_DIM
    rows = pl.ds(pl.multiple_of(at * SPAN, SPAN), SPAN)
    norm_attention_back(
        d_in_ref, pa_ref, pb_first_ref, pb_second_ref, gain_ref, unit_ref, scale_ref,
        ((oa_ref[:each, :], atta_ref.at[rows, :]), (ob_ref[:each, :], attb_ref.at[rows, :])),
        d_ref, e_ref.at[rows, :], sums_ref, do_ref, heads, SPAN, blocks,
    )
    do_out_ref[...] = do_ref[0]
    self_back_heads(q_ref, k_ref, v_ref, do_ref.at[1], dq_ref, dk_ref, dv_ref, dqkv_ref, k_ref.shape[1], heads, at)

    @pl.when(at == blocks - 1)
    def _():
        gw_ref[...] = tn(dqkv_ref[...], x_ref[...]).astype(bf16)
        norms = jnp.concatenate(
            [sums_ref[:2, :], sums_two_ref[:2, :], sums_three_ref[:2, :], jnp.zeros((10, x_ref.shape[1]), f32)], 0
        ).astype(bf16)
        for att_ref, r_ref in ((atta_ref, ra_ref), (attb_ref, rb_ref)):
            r_ref[:each, :] = tn(att_ref[...], e_ref[...]).astype(bf16)
            r_ref[each:, :] = norms


def self_back_second_kernel(s_ref, x_ref, q_ref, k_ref, v_ref, do_ref, dqkv_ref, gw_ref, dq_ref, dk_ref, dv_ref, *, heads, blocks):
    at = pl.program_id(0)
    self_back_heads(q_ref, k_ref, v_ref, do_ref, dq_ref, dk_ref, dv_ref, dqkv_ref, k_ref.shape[1], heads, at)

    @pl.when(at == blocks - 1)
    def _():
        gw_ref[...] = tn(dqkv_ref[...], x_ref[...]).astype(bf16)


class Row:
    def __init__(self, array, length, how="whole"):
        self.array, self.length, self.how = array, length, how


class Part:
    def __init__(self, array, how="rows", pick=None):
        self.array, self.how, self.pick = array, how, pick


def block_of(shape, how, blocks, pick=None):
    rank = len(shape)
    if how == "whole":
        return pl.BlockSpec(shape, lambda *a: (0,) * rank)
    if how == "own half":
        return pl.BlockSpec(
            (2 * shape[0] // blocks,) + shape[1:], lambda i, s: (jnp.clip(i - s[5] * (blocks // 2), 0, blocks // 2 - 1), 0)
        )
    dim = rank - 2 if how == "rows" else rank - 1
    pick = pick or (lambda i: i)
    parts = blocks if how != "half" else blocks // 2
    if how == "half":
        dim = rank - 2
    block = tuple(n // parts if d == dim else n for d, n in enumerate(shape))
    return pl.BlockSpec(block, lambda i, *a: tuple(pick(i) if d == dim else 0 for d in range(rank)))


def row_of(item, blocks):
    width = item.array.shape[1]
    if item.how == "whole":
        return pl.BlockSpec((item.length, width), lambda i, s: (s[0], 0))
    if item.how == "rows":
        return pl.BlockSpec((item.length // blocks, width), lambda i, s: (s[0] * blocks + i, 0))
    return pl.BlockSpec((item.length, width // blocks), lambda i, s: (s[0], i))


def call(kernel, name, blocks, inputs, outputs, scalars=None, scratch=(), micros=5.0, limit=LIMIT, after=()):
    specs, arrays = [], []
    for item in inputs:
        if isinstance(item, Row):
            specs.append(row_of(item, blocks))
            arrays.append(item.array)
        elif isinstance(item, Part):
            specs.append(block_of(item.array.shape, item.how, blocks, item.pick))
            arrays.append(item.array)
        else:
            specs.append(block_of(item.shape, "whole", blocks))
            arrays.append(item)
    count = len(arrays)
    for item in after:
        specs.append(pl.BlockSpec(memory_space=pl.ANY))
        arrays.append(item)
    shapes = [jax.ShapeDtypeStruct(shape, dtype) for shape, dtype, _ in outputs]
    out_specs = [block_of(shape, how, blocks) for shape, _, how in outputs]
    lead = 0 if scalars is None else 1
    if after:
        inner = kernel

        def kernel(*refs):
            return inner(*refs[: lead + count], *refs[lead + count + len(after) :])

    settings = dict(
        out_shape=shapes,
        compiler_params=pltpu.CompilerParams(vmem_limit_bytes=limit * MIB, dimension_semantics=("arbitrary",)),
        cost_estimate=pl.CostEstimate(flops=int(micros * 1.0e9), bytes_accessed=0, transcendentals=0),
        name=name,
    )
    if scalars is None:
        return pl.pallas_call(
            kernel, grid=(blocks,), in_specs=specs, out_specs=out_specs, scratch_shapes=list(scratch), **settings
        )(*arrays)
    grid_spec = pltpu.PrefetchScalarGridSpec(
        num_scalar_prefetch=1, grid=(blocks,), in_specs=specs, out_specs=out_specs, scratch_shapes=list(scratch)
    )
    return pl.pallas_call(kernel, grid_spec=grid_spec, **settings)(scalars, *arrays)


def local(
    size, tokens, memory, cotangent, tgt_len, src_len, self_query, self_key, self_value, self_out,
    cross_query, cross_key, cross_value, cross_out, ffn_up, ffn_down,
    gain_one, shift_one, gain_two, shift_two, gain_three, shift_three,
):
    width = tokens.shape[1]
    length = tokens.shape[0] // 2
    source = memory.shape[0] // 2
    each = self_query.shape[1]
    heads = each // HEAD_DIM
    hidden = ffn_up.shape[1]
    place = lax.axis_index("tp").astype(jnp.int32)
    group = lax.axis_index("dp").astype(jnp.int32)
    scalars = jnp.concatenate(
        [jnp.stack([place // 2]), tgt_len, src_len, jnp.stack([place % 2] + [(group >> b) & 1 for b in range(3)])]
    )
    gain_one, shift_one, gain_two, shift_two, gain_three, shift_three = (
        v.reshape(1, width) for v in (gain_one, shift_one, gain_two, shift_two, gain_three, shift_three)
    )
    big, small = length // BLOCK, length // SPAN

    def across(value):
        return lax.ppermute(value, "tp", ACROSS)

    def sibling(value):
        return lax.ppermute(value, "tp", CORE)

    def exchange(part):
        half = length // 2
        return sibling(part[:half]), sibling(part[half:])

    def shares(part, halves, blocks):
        per = blocks // 2
        first = Part(halves[0], "half", lambda i: jnp.minimum(i, per - 1))
        second = Part(halves[1], "half", lambda i: jnp.maximum(i - per, 0))
        return [Part(part), first, second]

    w_a = jnp.concatenate([self_query.T, self_key.T, self_value.T], 0)
    w_b = across(w_a)
    up_a, down_a = ffn_up, ffn_down
    up_b = across(up_a)
    down_b = across(down_a)

    head_shape = ((heads, length, WIDE), bf16, "rows")
    key_shape = ((heads, source, WIDE), bf16, "rows")
    kept_shape = ((heads, length, WIDE), bf16, "whole")
    low = ((length, width), bf16, "rows")
    full = ((length, width), f32, "rows")
    column = ((length, 1), f32, "rows")
    att_shape = ((length, each), bf16, "rows")
    sums = ((8, width), f32, "whole")

    cw_a, o_a, ck_a, cv_a, q_a, k_a, v_a, att_a = call(
        functools.partial(self_forward_kernel, heads=heads, second=False), "self_forward_own", big,
        [
            Row(tokens, length, "rows"), w_a, Row(memory, source, "rows"), cross_query.T, cross_key.T, cross_value.T,
            self_out, cross_out,
        ],
        [
            ((3 * each, width), bf16, "whole"), ((2 * each, width), bf16, "whole"),
            key_shape, key_shape, head_shape, kept_shape, kept_shape, att_shape,
        ],
        scalars, micros=13,
    )
    o_b = across(o_a)
    cw_b = across(cw_a)
    part, q_b, k_b, v_b, att_b = call(
        functools.partial(self_forward_kernel, heads=heads, second=True), "self_forward_other", big,
        [Row(tokens, length, "rows"), w_b, Part(att_a), o_a, o_b],
        [low, head_shape, kept_shape, kept_shape, att_shape], scalars, micros=13,
    )
    halves = exchange(part)
    ck_b, cv_b = call(
        functools.partial(memory_keys_kernel, heads=heads), "memory_keys_other", big, [Row(memory, source, "rows"), cw_b],
        [key_shape, key_shape], scalars, micros=4,
    )
    part, h_one, h_one_low, unit_one, scale_one, cq_rows_a, cq_rows_b, catt_a, catt_b = call(
        functools.partial(cross_forward_kernel, heads=heads, blocks=big), "cross_forward", big,
        [Row(tokens, length, "rows"), *shares(part, halves, big), gain_one, shift_one, cw_a, cw_b, ck_a, cv_a, ck_b, cv_b, o_a, o_b],
        [low, full, low, low, column, head_shape, head_shape, att_shape, att_shape], scalars, micros=20,
    )
    halves = exchange(part)
    hid = ((length, hidden), bf16, "rows")
    part, h_two, h_two_low, unit_two, scale_two, act_a, act_b, slope_a, slope_b = call(
        functools.partial(ffn_forward_kernel, blocks=small), "ffn_forward", small,
        [Part(h_one), *shares(part, halves, small), gain_two, shift_two, up_a, up_b, down_a, down_b],
        [low, full, low, low, column, hid, hid, hid, hid], micros=13,
    )
    halves = exchange(part)
    part, out_row, out_half, d_three, e_three, pre_a, pre_b, sums_three = call(
        functools.partial(ffn_back_kernel, blocks=small), "ffn_back", small,
        [
            Part(h_two), *shares(part, halves, small), Row(cotangent, length, "rows"), gain_three, shift_three,
            up_a, up_b, down_a, down_b, Part(slope_a), Part(slope_b),
        ],
        [low, low, ((length // 2, width), bf16, "own half"), full, low, hid, hid, sums], scalars, micros=15,
    )
    halves = exchange(part)
    third = width // SPAN
    square = ((width, hidden), bf16, "rows")
    gu_b, gd_b = call(
        ffn_grad_kernel, "ffn_grad_other", third, [Part(h_two_low, "columns"), Part(act_b, "columns"), e_three, pre_b],
        [square, square], micros=6,
    )
    gu_got, gd_got = across(gu_b), across(gd_b)
    gu_a, gd_a = call(
        ffn_grad_kernel, "ffn_grad_own", third, [Part(h_two_low, "columns"), Part(act_a, "columns"), e_three, pre_a],
        [square, square], micros=6,
    )

    dkv_shape = ((source, 2 * each), bf16, "whole")
    part, d_two, e_two, sums_two, dcq_a, dcq_b, dckv_a, dckv_b = call(
        functools.partial(cross_back_kernel, heads=heads, blocks=big), "cross_back", big,
        [
            Part(d_three), *shares(part, halves, big), gain_two, Part(unit_two), Part(scale_two), o_a, o_b,
            Part(catt_a), Part(catt_b), Part(cq_rows_a), Part(cq_rows_b), ck_a, cv_a, ck_b, cv_b, cw_a, cw_b,
        ],
        [low, full, low, sums, att_shape, att_shape, dkv_shape, dkv_shape], scalars,
        scratch=[
            pltpu.VMEM((2, heads, BLOCK, WIDE), bf16),
            pltpu.VMEM((2, heads, BLOCK, WIDE), f32),
            pltpu.VMEM((2, heads, source, WIDE), f32),
            pltpu.VMEM((2, heads, source, WIDE), f32),
        ],
        micros=36,
    )
    halves = exchange(part)

    def cross_grads(name, att, dq, dkv, after=()):
        return call(
            cross_grad_kernel, name, third,
            [Part(h_one_low, "columns"), Row(memory, source, "columns"), att, Part(e_two, "columns"), dq, dkv],
            [((4 * each, width), bf16, "columns")], scalars, micros=6, after=after,
        )[0]

    gc_b = cross_grads("cross_grad_other", catt_b, dcq_b, dckv_b)
    gc_got = across(gc_b)
    gc_a = cross_grads("cross_grad_own", catt_a, dcq_a, dckv_a)
    whole_square = ((width, hidden), bf16, "rows")
    gu_one, gd_one = call(
        add_kernel, "ffn_grad_join", third, [Part(gu_a), Part(gd_a), Part(gu_got), Part(gd_got)], [whole_square] * 2, micros=3,
        after=[gc_a],
    )
    gu_sum, gd_sum = lax.psum((gu_one, gd_one), "dp")
    half_low = ((length // 2, width), bf16, "whole")
    memory_send, memory_keep = call(
        functools.partial(memory_grad_kernel, skip=each), "memory_grad", 2, [Part(dckv_a), Part(dckv_b), cw_a, cw_b],
        [half_low, half_low], scalars, micros=4, after=[gu_one],
    )

    kept_w = ((3 * each, width), bf16, "whole")
    rest_shape = ((each + 16, width), bf16, "whole")
    qkv_shape = ((length, 3 * each), bf16, "whole")
    back_scratch = [
        pltpu.VMEM((heads, SPAN, WIDE), f32),
        pltpu.VMEM((heads, length, WIDE), f32),
        pltpu.VMEM((heads, length, WIDE), f32),
    ]
    d_one, do_a, dqkv_b, gw_b, rest_a, rest_b = call(
        functools.partial(self_back_first_kernel, heads=heads, blocks=small), "self_back_other", small,
        [
            Row(tokens, length), Part(d_two), *shares(part, halves, small), gain_one, Part(unit_one), Part(scale_one), o_a, o_b,
            att_a, att_b, Part(q_b), k_b, v_b, sums_two, sums_three,
        ],
        [full, head_shape, qkv_shape, kept_w, rest_shape, rest_shape], scalars,
        scratch=[pltpu.VMEM((length, width), bf16), pltpu.VMEM((8, width), f32), pltpu.VMEM((2, heads, SPAN, WIDE), bf16)]
        + back_scratch,
        micros=25,
    )
    rest_got = across(rest_b)
    gw_got = across(gw_b)

    early = (0, 4 * each, (0, 1, 2))
    late = ((0, 512, (0, 1, 2)), (512, 384, (1, 2, 0)))

    def hop(name, plans, after=(), micros=2):
        inputs, outputs, kernel_plans, most = [], [], [], 0
        for own, got, chains in plans:
            inputs += [*own, *got]
            kernel_plans.append((len(own), len(got), chains))
            for first, rows, bit in chains:
                most = max(most, first + rows)
                outputs += [((rows, width), bf16, "whole")] if bit is None else [((rows // 2, width), bf16, "whole")] * 2
        return call(
            functools.partial(hop_kernel, plans=kernel_plans, slots=most), name, 1, inputs, outputs, scalars,
            scratch=[pltpu.VMEM((most, width), bf16)], micros=micros, after=after,
        )

    def along(value, bit):
        return lax.ppermute(value, "dp", [(i, i ^ (1 << bit)) for i in range(size)])

    def spread(piece, order):
        pieces = [piece]
        for bit in reversed(order):
            pieces = pieces + [along(p, bit) for p in pieces]
        return pieces

    small_size = size == 8
    if small_size:
        e_order = early[2]
        send, keep_e = hop("sum_cross_a", [([gc_a], [gc_got], [(0, early[1], e_order[0])])])
        got_e = along(send, e_order[0])
    dqkv_a, gw_a = call(
        functools.partial(self_back_second_kernel, heads=heads, blocks=small), "self_back_own", small,
        [Row(tokens, length), Part(q_a), k_a, v_a, Part(do_a)],
        [qkv_shape, kept_w], scalars, scratch=back_scratch, micros=15, after=[keep_e] if small_size else (),
    )
    pinned = ()
    if small_size:
        (f0, n0, o0), (f1, n1, o1) = late
        s0, k0, s1, k1, se, keep_e = hop(
            "sum_self_a",
            [
                ([gw_a, rest_a], [gw_got, rest_got], [(f0, n0, o0[0]), (f1, n1, o1[0])]),
                ([keep_e], [got_e], [(0, early[1] // 2, e_order[1])]),
            ],
            micros=3,
        )
        g0, g1, got_e = along(s0, o0[0]), along(s1, o1[0]), along(se, e_order[1])
        pinned = [k0]
    tokens_send, tokens_keep = call(
        tokens_grad_kernel, "tokens_grad", 2, [Part(d_one), Part(dqkv_a), Part(dqkv_b), w_a, w_b],
        [half_low, ((length // 2, width), f32, "whole")], scalars, micros=5, after=pinned,
    )

    def finish(name, keep, send, after=()):
        mine = call(finish_kernel, name, 2, [Part(keep), Part(sibling(send))], [((length // 2, width), bf16, "rows")], micros=2, after=after)[0]
        return mine, across(mine)

    def placed(name, pieces, shift):
        return call(
            functools.partial(place_kernel, shift=shift), name, 4, pieces, [((2 * length, width), bf16, "rows")], scalars, micros=3
        )[0]

    out_far = across(out_half)
    layer_out = placed("place_layer_out", [out_row, out_far, sibling(out_far)], True)
    mine, far = finish("memory_finish", memory_keep, memory_send)
    memory_grad = placed("place_memory_grad", [mine, sibling(mine), far, sibling(far)], False)
    mine, far = finish("tokens_finish", tokens_keep, tokens_send)
    tokens_grad = placed("place_tokens_grad", [mine, sibling(mine), far, sibling(far)], False)

    shapes = [((each, width), f32, "whole")] * 4
    if small_size:
        s0, k0, s1, k1, se, keep_e = hop(
            "sum_self_b",
            [([k0], [g0], [(0, n0 // 2, o0[1])]), ([k1], [g1], [(0, n1 // 2, o1[1])]), ([keep_e], [got_e], [(0, early[1] // 4, e_order[2])])],
        )
        g0, g1, got_e = along(s0, o0[1]), along(s1, o1[1]), along(se, e_order[2])
        s0, k0, s1, k1, piece_e = hop(
            "sum_self_c",
            [([k0], [g0], [(0, n0 // 4, o0[2])]), ([k1], [g1], [(0, n1 // 4, o1[2])]), ([keep_e], [got_e], [(0, early[1] // 8, None)])],
        )
        g0, g1 = along(s0, o0[2]), along(s1, o1[2])
        pieces_e = spread(piece_e, e_order)
        piece0, piece1 = hop("sum_self_d", [([k0], [g0], [(0, n0 // 8, None)]), ([k1], [g1], [(0, n1 // 8, None)])])
        pieces = spread(piece0, o0) + spread(piece1, o1)
        cross = call(
            functools.partial(gather_kernel, chains=[early], cuts=[(i * each, each) for i in range(4)]), "gather_cross", 1,
            pieces_e, shapes, scalars, scratch=[pltpu.VMEM((early[1], width), bf16)], micros=3,
        )
        self_grads = call(
            functools.partial(gather_kernel, chains=late, cuts=[(i * each, each) for i in range(4)] + [(4 * each, 16)]),
            "gather_self", 1, pieces, shapes + [((16, width), f32, "whole")], scalars,
            scratch=[pltpu.VMEM((896, width), bf16)], micros=3,
        )
        norms = self_grads[4]
    else:
        def add(mine, got):
            return (mine.astype(f32) + got.astype(f32)).astype(bf16)

        cross = jnp.split(lax.psum(add(gc_a, gc_got), "dp").astype(f32), 4)
        self_grads = jnp.split(lax.psum(add(gw_a, gw_got), "dp").astype(f32), 3)
        rest = lax.psum(add(rest_a, rest_got), "dp").astype(f32)
        self_grads = [*self_grads, rest[:each]]
        norms = rest[each:]
    return (
        layer_out, tokens_grad, memory_grad,
        self_grads[0].T, self_grads[1].T, self_grads[2].T, self_grads[3],
        cross[0].T, cross[1].T, cross[2].T, cross[3],
        gu_sum.astype(f32), gd_sum.astype(f32),
        *(norms[i] for i in range(6)),
    )


def solution(mesh):
    rows, columns, down = P("dp", None), P(None, "tp"), P("tp", None)
    return jax.shard_map(
        functools.partial(local, mesh.shape["dp"]),
        mesh=mesh,
        in_specs=(rows, rows, rows, P("dp"), P("dp"))
        + (columns, columns, columns, down) * 2
        + (columns, down)
        + (P(),) * 6,
        out_specs=(rows, rows, rows) + (columns, columns, columns, down) * 2 + (columns, down) + (P(),) * 6,
        check_vma=False,
    )
```

```python
import functools

import jax
import jax.numpy as jnp
from jax import lax
from jax.experimental import pallas as pl
from jax.experimental.pallas import tpu as pltpu
from jax.sharding import PartitionSpec as P

HEAD_DIM = 64
WIDE = 2 * HEAD_DIM
EPS = 1e-05
MASKED = -1e30
LOG2E = 1.4426950408889634
LN2 = 0.6931471805599453
f32 = jnp.float32
bf16 = jnp.bfloat16

CORE = [(0, 1), (1, 0), (2, 3), (3, 2)]
ACROSS = [(0, 2), (2, 0), (1, 3), (3, 1)]
MIB = 1 << 20
LIMIT = 18


def nn(left, right):
    return lax.dot_general(left, right, (((1,), (0,)), ((), ())), preferred_element_type=f32)


def nt(left, right):
    return lax.dot_general(left, right, (((1,), (1,)), ((), ())), preferred_element_type=f32)


def tn(left, right):
    return lax.dot_general(left, right, (((0,), (0,)), ((), ())), preferred_element_type=f32)


def lanes(rows):
    return lax.broadcasted_iota(jnp.int32, (rows, HEAD_DIM), 1)


def three_parts(value):
    high = value.astype(bf16).astype(f32)
    rest = value - high
    middle = rest.astype(bf16).astype(f32)
    return high, middle, rest - middle


def fill_queries(q_ref, rows, count, acc, heads):
    tail = jnp.where(lanes(count) == 0, 1.0, 0.0)
    for h in range(heads):
        part = acc[:, h * HEAD_DIM : (h + 1) * HEAD_DIM]
        q_ref[h, rows, :] = jnp.concatenate([part, tail], 1).astype(bf16)


def fill_keys(k_ref, v_ref, rows, start, count, acc, heads, limit):
    lane = lanes(count)
    index = start + lax.broadcasted_iota(jnp.int32, (count, HEAD_DIM), 0)
    tail = jnp.where(lane == 0, jnp.where(index < limit, 0.0, MASKED), jnp.where(lane < 4, 1.0, 0.0))
    ones = jnp.ones((count, HEAD_DIM), f32)
    for h in range(heads):
        k = acc[:, h * HEAD_DIM : (h + 1) * HEAD_DIM]
        v = acc[:, (heads + h) * HEAD_DIM : (heads + h + 1) * HEAD_DIM]
        k_ref[h, rows, :] = jnp.concatenate([k, tail], 1).astype(bf16)
        v_ref[h, rows, :] = jnp.concatenate([v, ones], 1).astype(bf16)


def attend_block(q_ref, k_ref, v_ref, att_ref, h, column, rows, count, key_end, causal):
    s = nt(q_ref[h, rows, :], k_ref[h, :key_end, :])
    if causal:
        r = lax.broadcasted_iota(jnp.int32, (count, count), 0)
        c = lax.broadcasted_iota(jnp.int32, (count, count), 1)
        diagonal = jnp.where(c <= r, s[:, key_end - count :], MASKED)
        s = diagonal if key_end == count else jnp.concatenate([s[:, : key_end - count], diagonal], 1)
    peak = jnp.max(s, 1, keepdims=True)
    p = jnp.exp2(s - peak).astype(bf16)
    o = nn(p, v_ref[h, :key_end, :])
    total = o[:, HEAD_DIM : HEAD_DIM + 1]
    att_ref[rows, column : column + HEAD_DIM] = (o[:, :HEAD_DIM] / total).astype(bf16)
    high, middle, low = three_parts(-(peak + jnp.log2(total)))
    lane = lanes(count)
    tail = jnp.where(
        lane == 0, 1.0, jnp.where(lane == 1, high, jnp.where(lane == 2, middle, jnp.where(lane == 3, low, 0.0)))
    )
    q_ref[h, rows, HEAD_DIM:] = tail.astype(bf16)


def fill_grads(do_ref, rows, count, grad, att, heads):
    lane = lanes(count)
    for h in range(heads):
        part = grad[:, h * HEAD_DIM : (h + 1) * HEAD_DIM].astype(bf16)
        mixed = att[:, h * HEAD_DIM : (h + 1) * HEAD_DIM].astype(f32)
        inner = jnp.sum(part.astype(f32) * mixed, 1, keepdims=True)
        high, middle, low = three_parts(-inner)
        tail = jnp.where(lane == 0, high, jnp.where(lane == 1, middle, jnp.where(lane == 2, low, 0.0)))
        do_ref[h, rows, :] = jnp.concatenate([part, tail.astype(bf16)], 1)


def back_block(q_ref, k_ref, v_ref, do_ref, dq_ref, dk_ref, dv_ref, h, rows, count, key_end, causal, first):
    q = q_ref[h, rows, :]
    d = do_ref[h, rows, :]
    k = k_ref[h, :key_end, :]
    v = v_ref[h, :key_end, :]
    p = jnp.exp2(nt(k, q))
    if causal:
        r = lax.broadcasted_iota(jnp.int32, (count, count), 0)
        c = lax.broadcasted_iota(jnp.int32, (count, count), 1)
        diagonal = jnp.where(r <= c, p[key_end - count :], 0.0)
        p = diagonal if key_end == count else jnp.concatenate([p[: key_end - count], diagonal], 0)
    ds = (p * nt(v, d)).astype(bf16)
    dv = nn(p.astype(bf16), d)
    dk = nn(ds, q)
    if first:
        dv_ref[h, :key_end, :] = dv
        dk_ref[h, :key_end, :] = dk
    else:
        dv_ref[h, :key_end, :] += dv
        dk_ref[h, :key_end, :] += dk
    dq_ref[h, rows, :] = tn(k, ds).T


def pack_heads(source, rows, heads, factor):
    return jnp.concatenate([source[h, rows, :HEAD_DIM] * factor for h in range(heads)], 1).astype(bf16)


def norm(resid):
    center = resid - jnp.mean(resid, -1, keepdims=True)
    scale = lax.rsqrt(jnp.mean(center * center, -1, keepdims=True) + EPS)
    return center * scale, scale


def norm_back(grad, gain, unit, scale):
    lifted = grad * gain
    first = jnp.mean(lifted, -1, keepdims=True)
    second = jnp.mean(lifted * unit, -1, keepdims=True)
    return scale * (lifted - first - unit * second)


def gelu_pair(value):
    scaled = value * 0.7071067811865476
    density = jnp.exp(-scaled * scaled) * 0.3989422804014327
    below = 0.5 * (1.0 + lax.erf(scaled))
    return value * below, below + value * density


BLOCK = 512
SPAN = 256
ROW, TGT, SRC, CORE_AT, BIT = 0, 1, 3, 5, 6
FACTOR = HEAD_DIM ** (-0.5) * LOG2E


def vector(ref):
    return ref[...].reshape(1, ref.shape[0])


def branch_of(shares, blocks):
    own0, own1, got0, got1 = shares
    first = pl.program_id(0) < blocks // 2
    own = jnp.where(first, own0[...], own1[...]).astype(f32)
    return own + jnp.where(first, got0[...], got1[...]).astype(f32)


def put_part(first_ref, second_ref, value, blocks):
    at = pl.program_id(0)

    @pl.when(at < blocks // 2)
    def _():
        first_ref[...] = value

    @pl.when(at >= blocks // 2)
    def _():
        second_ref[...] = value


def rows_at(size):
    return pl.ds(pl.multiple_of(pl.program_id(0) * size, size), size)


def project_own_kernel(
    s_ref, x_ref, m_ref, sq_ref, sk_ref, sv_ref, cq_ref, ck_ref, cv_ref, so_ref, co_ref, down_ref,
    q_ref, k_ref, v_ref, mk_ref, mv_ref, wa_ref, cwa_ref, half_out_ref, half_down_ref, *, heads,
):
    each = heads * HEAD_DIM
    at = pl.program_id(0)

    @pl.when(at == 0)
    def _():
        for n, ref in enumerate((sq_ref, sk_ref, sv_ref)):
            wa_ref[n * each : (n + 1) * each, :] = ref[...]
        for n, ref in enumerate((cq_ref, ck_ref, cv_ref)):
            cwa_ref[n * each : (n + 1) * each, :] = ref[...]
        half_out_ref[...] = jnp.where(s_ref[BIT] == 0, so_ref[...], co_ref[...])
        half_down_ref[...] = down_ref[...]

    limit = s_ref[TGT + s_ref[ROW]]
    memory_limit = s_ref[SRC + s_ref[ROW]]
    rows = pl.ds(0, BLOCK)
    acc = nt(x_ref[...], wa_ref[...])
    fill_queries(q_ref, rows, BLOCK, acc[:, :each] * FACTOR, heads)
    fill_keys(k_ref, v_ref, rows, at * BLOCK, BLOCK, acc[:, each:], heads, limit)
    acc = nt(m_ref[...], cwa_ref[each:, :])
    fill_keys(mk_ref, mv_ref, rows, at * BLOCK, BLOCK, acc, heads, memory_limit)


def causal_blocks(q_ref, k_ref, v_ref, att_ref, heads):
    at = pl.program_id(0)
    for block in range(k_ref.shape[1] // BLOCK):

        @pl.when(at == block)
        def _():
            for h in range(heads):
                attend_block(q_ref, k_ref, v_ref, att_ref, h, h * HEAD_DIM, pl.ds(0, BLOCK), BLOCK, (block + 1) * BLOCK, True)


def self_own_kernel(q_in_ref, k_ref, v_ref, q_ref, k_out_ref, v_out_ref, att_ref, *, heads):
    q_ref[...] = q_in_ref[...]
    k_out_ref[...] = k_ref[:, rows_at(BLOCK), :]
    v_out_ref[...] = v_ref[:, rows_at(BLOCK), :]
    causal_blocks(q_ref, k_ref, v_ref, att_ref, heads)


def self_other_kernel(s_ref, x_ref, near_ref, far_ref, w_ref, q_ref, k_out_ref, v_out_ref, att_ref, k_ref, v_ref, *, heads):
    each = heads * HEAD_DIM
    at = pl.program_id(0)
    half = near_ref.shape[0]
    high = s_ref[BIT]

    @pl.when(at == 0)
    def _():
        w_ref[pl.ds(pl.multiple_of(high * half, 16), half), :] = near_ref[...]
        w_ref[pl.ds(pl.multiple_of((1 - high) * half, 16), half), :] = far_ref[...]

    acc = nt(x_ref[...], w_ref[...])
    fill_queries(q_ref, pl.ds(0, BLOCK), BLOCK, acc[:, :each] * FACTOR, heads)
    fill_keys(k_ref, v_ref, rows_at(BLOCK), at * BLOCK, BLOCK, acc[:, each:], heads, s_ref[TGT + s_ref[ROW]])
    k_out_ref[...] = k_ref[:, rows_at(BLOCK), :]
    v_out_ref[...] = v_ref[:, rows_at(BLOCK), :]
    causal_blocks(q_ref, k_ref, v_ref, att_ref, heads)


def self_out_kernel(s_ref, atta_ref, attb_ref, soa_ref, near_ref, far_ref, part0_ref, part1_ref, sob_ref, cob_ref, *, blocks):
    @pl.when(pl.program_id(0) == 0)
    def _():
        low = s_ref[BIT] == 0
        sob_ref[...] = jnp.where(low, near_ref[...], far_ref[...])
        cob_ref[...] = jnp.where(low, far_ref[...], near_ref[...])

    part = nn(atta_ref[...], soa_ref[...]) + nn(attb_ref[...], sob_ref[...])
    put_part(part0_ref, part1_ref, part.astype(bf16), blocks)


def cross_blocks(q_ref, k_ref, v_ref, att_ref, heads, limit):
    step = 256
    live = (limit + step - 1) // step
    for count in range(1, k_ref.shape[1] // step + 1):

        @pl.when(live == count)
        def _():
            for h in range(heads):
                attend_block(q_ref, k_ref, v_ref, att_ref, h, h * HEAD_DIM, pl.ds(0, BLOCK), BLOCK, count * step, False)


def cross_own_kernel(
    s_ref, x_ref, own0, own1, got0, got1, gain_ref, shift_ref, cq_ref, k_ref, v_ref,
    h_ref, hl_ref, unit_ref, scale_ref, q_ref, att_ref, *, heads, blocks,
):
    unit, scale = norm(x_ref[...].astype(f32) + branch_of((own0, own1, got0, got1), blocks))
    h = unit * vector(gain_ref) + vector(shift_ref)
    h_ref[...] = h
    unit_ref[...] = unit.astype(bf16)
    scale_ref[...] = scale
    low = h.astype(bf16)
    hl_ref[...] = low
    fill_queries(q_ref, pl.ds(0, BLOCK), BLOCK, nt(low, cq_ref[...]) * FACTOR, heads)
    cross_blocks(q_ref, k_ref, v_ref, att_ref, heads, s_ref[SRC + s_ref[ROW]])


def cross_other_kernel(
    s_ref, m_ref, hl_ref, cwb_ref, atta_ref, coa_ref, cob_ref, part0_ref, part1_ref, k_ref, v_ref, q_ref, att_ref, *, heads, blocks,
):
    each = heads * HEAD_DIM
    limit = s_ref[SRC + s_ref[ROW]]

    @pl.when(pl.program_id(0) == 0)
    def _():
        @pl.loop(0, m_ref.shape[0], step=BLOCK)
        def _(start):
            rows = pl.ds(pl.multiple_of(start, BLOCK), BLOCK)
            fill_keys(k_ref, v_ref, rows, start, BLOCK, nt(m_ref[rows, :], cwb_ref[each:, :]), heads, limit)

    fill_queries(q_ref, pl.ds(0, BLOCK), BLOCK, nt(hl_ref[...], cwb_ref[:each, :]) * FACTOR, heads)
    cross_blocks(q_ref, k_ref, v_ref, att_ref, heads, limit)
    part = nn(atta_ref[...], coa_ref[...]) + nn(att_ref[...], cob_ref[...])
    put_part(part0_ref, part1_ref, part.astype(bf16), blocks)


def ffn_own_kernel(
    h_in_ref, own0, own1, got0, got1, gain_ref, shift_ref, up_ref, down_ref,
    h_ref, hl_ref, unit_ref, scale_ref, act_ref, slope_ref, term_ref, *, blocks,
):
    unit, scale = norm(h_in_ref[...] + branch_of((own0, own1, got0, got1), blocks))
    h = unit * vector(gain_ref) + vector(shift_ref)
    h_ref[...] = h
    unit_ref[...] = unit.astype(bf16)
    scale_ref[...] = scale
    low = h.astype(bf16)
    hl_ref[...] = low
    act, slope = gelu_pair(nn(low, up_ref[...]))
    act = act.astype(bf16)
    act_ref[...] = act
    slope_ref[...] = slope.astype(bf16)
    term_ref[...] = nn(act, down_ref[...])


def ffn_other_kernel(
    s_ref, hl_ref, term_ref, up_ref, near_ref, far_ref, part0_ref, part1_ref, act_ref, slope_ref, down_ref, *, blocks
):
    half = near_ref.shape[0]
    high = s_ref[BIT + 1]

    @pl.when(pl.program_id(0) == 0)
    def _():
        down_ref[pl.ds(pl.multiple_of(high * half, 16), half), :] = near_ref[...]
        down_ref[pl.ds(pl.multiple_of((1 - high) * half, 16), half), :] = far_ref[...]

    act, slope = gelu_pair(nn(hl_ref[...], up_ref[...]))
    act = act.astype(bf16)
    act_ref[...] = act
    slope_ref[...] = slope.astype(bf16)
    put_part(part0_ref, part1_ref, (term_ref[...] + nn(act, down_ref[...])).astype(bf16), blocks)


def ffn_back_kernel(
    s_ref, h_ref, own0, own1, got0, got1, cot_ref, gain_ref, shift_ref, upa_ref, upb_ref, downa_ref, downb_ref, slopea_ref, slopeb_ref,
    part0_ref, part1_ref, out_ref, d_ref, e_ref, prea_ref, preb_ref, sums_ref, *, blocks,
):
    limit = s_ref[TGT + s_ref[ROW]]
    at = pl.program_id(0)

    @pl.when(at == 0)
    def _():
        sums_ref[...] = jnp.zeros_like(sums_ref)

    gain = vector(gain_ref)
    unit, scale = norm(h_ref[...] + branch_of((own0, own1, got0, got1), blocks))
    out_ref[...] = (unit * gain + vector(shift_ref)).astype(bf16)
    index = at * SPAN + lax.broadcasted_iota(jnp.int32, (SPAN, 1), 0)
    grad = jnp.where(index < limit, cot_ref[...].astype(f32), 0.0)
    sums_ref[0:1, :] += jnp.sum(grad * unit, 0, keepdims=True)
    sums_ref[1:2, :] += jnp.sum(grad, 0, keepdims=True)
    d = norm_back(grad, gain, unit, scale)
    d_ref[...] = d
    e = d.astype(bf16)
    e_ref[...] = e
    part = None
    for up_ref, down_ref, slope_ref, pre_ref in (
        (upa_ref, downa_ref, slopea_ref, prea_ref),
        (upb_ref, downb_ref, slopeb_ref, preb_ref),
    ):
        pre = (nt(e, down_ref[...]) * slope_ref[...].astype(f32)).astype(bf16)
        pre_ref[...] = pre
        term = nt(pre, up_ref[...])
        part = term if part is None else part + term
    put_part(part0_ref, part1_ref, part.astype(bf16), blocks)


def ffn_grad_kernel(h_ref, act_ref, e_ref, pre_ref, up_ref, down_ref):
    up_ref[...] = tn(h_ref[...], pre_ref[...]).astype(bf16)
    down_ref[...] = tn(act_ref[...], e_ref[...]).astype(bf16)


def norm_step(d_in_ref, shares, gain, unit_ref, scale_ref, d_ref, e_ref, sums_ref, blocks):
    @pl.when(pl.program_id(0) == 0)
    def _():
        sums_ref[...] = jnp.zeros_like(sums_ref)

    grad = d_in_ref[...] + branch_of(shares, blocks)
    unit = unit_ref[...].astype(f32)
    sums_ref[0:1, :] += jnp.sum(grad * unit, 0, keepdims=True)
    sums_ref[1:2, :] += jnp.sum(grad, 0, keepdims=True)
    d = norm_back(grad, gain, unit, scale_ref[...])
    d_ref[...] = d
    e = d.astype(bf16)
    e_ref[...] = e
    return e


def cross_back_heads(s_ref, q_ref, k_ref, v_ref, do_ref, dqo_ref, dkv_ref, dq_ref, dk_ref, dv_ref, heads, blocks):
    at = pl.program_id(0)
    source = k_ref.shape[1]

    @pl.when(at == 0)
    def _():
        dk_ref[...] = jnp.zeros_like(dk_ref)
        dv_ref[...] = jnp.zeros_like(dv_ref)

    step = 256
    live = (s_ref[SRC + s_ref[ROW]] + step - 1) // step
    rows = pl.ds(0, BLOCK)
    for count in range(1, source // step + 1):

        @pl.when(live == count)
        def _():
            @pl.loop(0, heads)
            def _(h):
                back_block(q_ref, k_ref, v_ref, do_ref, dq_ref, dk_ref, dv_ref, h, rows, BLOCK, count * step, False, False)

    dqo_ref[...] = pack_heads(dq_ref, rows, heads, HEAD_DIM ** (-0.5))

    @pl.when(at == blocks - 1)
    def _():
        @pl.loop(0, source, step=BLOCK)
        def _(start):
            some = pl.ds(pl.multiple_of(start, BLOCK), BLOCK)
            dkv_ref[some, :] = jnp.concatenate(
                [pack_heads(dk_ref, some, heads, LN2), pack_heads(dv_ref, some, heads, 1.0)], 1
            )


def cross_back_other_kernel(
    s_ref, d_in_ref, own0, own1, got0, got1, gain_ref, unit_ref, scale_ref, coa_ref, cob_ref, atta_ref, attb_ref,
    q_ref, k_ref, v_ref,
    d_ref, e_ref, sums_ref, doa_ref, dqo_ref, dkv_ref, do_ref, dq_ref, dk_ref, dv_ref, *, heads, blocks,
):
    e = norm_step(
        d_in_ref, (own0, own1, got0, got1), vector(gain_ref), unit_ref, scale_ref, d_ref, e_ref, sums_ref, blocks
    )
    fill_grads(doa_ref, pl.ds(0, BLOCK), BLOCK, nt(e, coa_ref[...]), atta_ref[...], heads)
    fill_grads(do_ref, pl.ds(0, BLOCK), BLOCK, nt(e, cob_ref[...]), attb_ref[...], heads)
    cross_back_heads(s_ref, q_ref, k_ref, v_ref, do_ref, dqo_ref, dkv_ref, dq_ref, dk_ref, dv_ref, heads, blocks)


def cross_back_own_kernel(
    s_ref, q_ref, k_ref, v_ref, do_ref, dqb_ref, cqa_ref, cwb_ref,
    part0_ref, part1_ref, dqo_ref, dkv_ref, dq_ref, dk_ref, dv_ref, *, heads, blocks,
):
    cross_back_heads(s_ref, q_ref, k_ref, v_ref, do_ref, dqo_ref, dkv_ref, dq_ref, dk_ref, dv_ref, heads, blocks)
    part = nn(dqo_ref[...], cqa_ref[...]) + nn(dqb_ref[...], cwb_ref[: heads * HEAD_DIM, :])
    put_part(part0_ref, part1_ref, part.astype(bf16), blocks)


def cross_grad_kernel(s_ref, h_ref, m_ref, att_ref, e_ref, dq_ref, dkv_ref, g_ref):
    each = dq_ref.shape[1]
    g_ref[:each, :] = tn(dq_ref[...], h_ref[...]).astype(bf16)
    g_ref[each : 3 * each, :] = tn(dkv_ref[...], m_ref[...]).astype(bf16)
    g_ref[3 * each :, :] = tn(att_ref[...], e_ref[...]).astype(bf16)


def memory_grad_kernel(s_ref, a_ref, b_ref, wa_ref, wb_ref, out_ref, send_ref, keep_ref, half_ref):
    half_ref[...] = out_ref[...]
    each = a_ref.shape[1] // 2
    part = (nn(a_ref[...], wa_ref[each:, :]) + nn(b_ref[...], wb_ref[each:, :])).astype(bf16)
    mine = pl.program_id(0) == s_ref[CORE_AT]

    @pl.when(mine)
    def _():
        keep_ref[...] = part

    @pl.when(jnp.logical_not(mine))
    def _():
        send_ref[...] = part


def norm_one_back_kernel(
    s_ref, d_in_ref, own0, own1, got0, got1, gain_ref, unit_ref, scale_ref, soa_ref, sob_ref, atta_ref, attb_ref,
    sums_two_ref, sums_three_ref, d_ref, doa_ref, dob_ref, ra_ref, rb_ref, e_ref, sums_ref, *, heads, blocks,
):
    each = heads * HEAD_DIM
    rows = rows_at(SPAN)
    e = norm_step(
        d_in_ref, (own0, own1, got0, got1), vector(gain_ref), unit_ref, scale_ref, d_ref, e_ref.at[rows, :], sums_ref, blocks
    )
    fill_grads(doa_ref, pl.ds(0, SPAN), SPAN, nt(e, soa_ref[...]), atta_ref[rows, :], heads)
    fill_grads(dob_ref, pl.ds(0, SPAN), SPAN, nt(e, sob_ref[...]), attb_ref[rows, :], heads)

    @pl.when(pl.program_id(0) == blocks - 1)
    def _():
        norms = jnp.concatenate(
            [sums_ref[:2, :], sums_two_ref[:2, :], sums_three_ref[:2, :], jnp.zeros((10, d_in_ref.shape[1]), f32)], 0
        ).astype(bf16)
        for att_ref, r_ref in ((atta_ref, ra_ref), (attb_ref, rb_ref)):
            r_ref[:each, :] = tn(att_ref[...], e_ref[...]).astype(bf16)
            r_ref[each:, :] = norms


def self_back_kernel(s_ref, x_ref, q_ref, k_ref, v_ref, do_ref, dqkv_ref, gw_ref, dq_ref, dk_ref, dv_ref, *, heads, blocks):
    at = pl.program_id(0)
    each = heads * HEAD_DIM
    length = k_ref.shape[1]

    @pl.when(at == 0)
    def _():
        dk_ref[...] = jnp.zeros_like(dk_ref)
        dv_ref[...] = jnp.zeros_like(dv_ref)

    rows = pl.ds(0, SPAN)
    for block in range(blocks):

        @pl.when(at == block)
        def _():
            @pl.loop(0, heads)
            def _(h):
                back_block(q_ref, k_ref, v_ref, do_ref, dq_ref, dk_ref, dv_ref, h, rows, SPAN, (block + 1) * SPAN, True, False)

    dqkv_ref[rows_at(SPAN), :each] = pack_heads(dq_ref, rows, heads, HEAD_DIM ** (-0.5))

    @pl.when(at == blocks - 1)
    def _():
        @pl.loop(0, length, step=BLOCK)
        def _(start):
            some = pl.ds(pl.multiple_of(start, BLOCK), BLOCK)
            dqkv_ref[some, each:] = jnp.concatenate(
                [pack_heads(dk_ref, some, heads, LN2), pack_heads(dv_ref, some, heads, 1.0)], 1
            )
        gw_ref[...] = tn(dqkv_ref[...], x_ref[...]).astype(bf16)


def tokens_grad_kernel(s_ref, d_ref, a_ref, b_ref, wa_ref, wb_ref, send_ref, keep_ref):
    part = nn(a_ref[...], wa_ref[...]) + nn(b_ref[...], wb_ref[...])
    mine = pl.program_id(0) == s_ref[CORE_AT]

    @pl.when(mine)
    def _():
        keep_ref[...] = d_ref[...] + part

    @pl.when(jnp.logical_not(mine))
    def _():
        send_ref[...] = part.astype(bf16)


def place_kernel(s_ref, *refs, shift):
    out_ref = refs[-1]
    pieces = refs[:-1]
    half = out_ref.shape[0]
    row, core, at = s_ref[ROW], s_ref[CORE_AT], pl.program_id(0)
    if shift:
        sources = [
            (pieces[0].at[:half, :], 2 * row), (pieces[0].at[half:, :], 2 * row + 1),
            (pieces[1], 2 * (1 - row) + core), (pieces[2], 2 * (1 - row) + 1 - core),
        ]
    else:
        sources = [
            (pieces[0], 2 * row + core), (pieces[1], 2 * row + 1 - core),
            (pieces[2], 2 * (1 - row) + core), (pieces[3], 2 * (1 - row) + 1 - core),
        ]
    for ref, place in sources:

        @pl.when(at == place)
        def _():
            out_ref[...] = ref[...]


def step_kernel(s_ref, *refs, plans):
    scratch = refs[-1]
    inputs = sum(plan[1] for plan in plans)
    ins, outs = list(refs[:inputs]), list(refs[inputs:-1])
    for kind, count, rows, bit, cuts in plans:
        mine, ins = ins[:count], ins[count:]
        if kind == "sum":
            at = 0
            for a_ref, b_ref in zip(mine[: count // 2], mine[count // 2 :]):
                size = a_ref.shape[0]
                scratch[at : at + size, :] = (a_ref[...].astype(f32) + b_ref[...].astype(f32)).astype(bf16)
                at += size
            if at < rows:
                scratch[at:rows, :] = jnp.zeros((rows - at, scratch.shape[1]), bf16)
            if bit is None:
                outs.pop(0)[...] = scratch[:rows, :]
            else:
                half, high = rows // 2, s_ref[BIT + bit]
                outs.pop(0)[...] = scratch[pl.ds(pl.multiple_of((1 - high) * half, 16), half), :]
                outs.pop(0)[...] = scratch[pl.ds(pl.multiple_of(high * half, 16), half), :]
        else:
            high, size = s_ref[BIT + bit], mine[0].shape[0]
            target = outs.pop(0) if kind == "pack" else scratch
            target[pl.ds(pl.multiple_of(high * size, 16), size), :] = mine[0][...]
            target[pl.ds(pl.multiple_of((1 - high) * size, 16), size), :] = mine[1][...]
            for first, size in cuts:
                outs.pop(0)[...] = scratch[first : first + size, :].astype(f32)


class Row:
    def __init__(self, array, length, how="whole"):
        self.array, self.length, self.how = array, length, how


class Part:
    def __init__(self, array, how="rows", pick=None):
        self.array, self.how, self.pick = array, how, pick


class Pick:
    def __init__(self, array, scalar, parts):
        self.array, self.scalar, self.parts = array, scalar, parts


class Far:
    def __init__(self, array):
        self.array = array


def block_of(shape, how, blocks, pick=None, once=False):
    rank = len(shape)
    if rank == 1:
        return pl.BlockSpec(shape, lambda *a: (0,))
    if isinstance(how, tuple):
        how, pick = how
    if how == "whole":
        return pl.BlockSpec(shape, lambda *a: (0,) * rank, pipeline_mode=pl.Buffered(1) if once else None)
    pick = pick or (lambda i: i)
    dim = rank - 1 if how == "columns" else rank - 2
    parts = blocks // 2 if how == "half" else blocks
    block = tuple(n // parts if d == dim else n for d, n in enumerate(shape))
    return pl.BlockSpec(block, lambda i, *a: tuple(pick(i) if d == dim else 0 for d in range(rank)))


def row_of(item, blocks):
    width = item.array.shape[1]
    if item.how == "whole":
        return pl.BlockSpec((item.length, width), lambda i, s: (s[0], 0))
    if item.how == "rows":
        return pl.BlockSpec((item.length // blocks, width), lambda i, s: (s[0] * blocks + i, 0))
    if item.how[0] == "part":
        return pl.BlockSpec((item.length // blocks, width), lambda i, s: (s[item.how[1]] * blocks + i, 0))
    return pl.BlockSpec((item.length, width // blocks), lambda i, s: (s[0], i))


class Held:
    def __init__(self, array, how="rows"):
        self.array, self.how = array, how


def view_of(shape, how, blocks):
    rank = len(shape)
    if how == "whole":
        return None
    if how == "rows":
        size = shape[-2] // blocks

        def rows(ref):
            place = pl.ds(pl.multiple_of(pl.program_id(0) * size, size), size)
            return ref.at[place, :] if rank == 2 else ref.at[:, place, :]

        return rows
    size = shape[-1] // blocks
    return lambda ref: ref.at[:, pl.ds(pl.multiple_of(pl.program_id(0) * size, size), size)]


def call(kernel, name, blocks, inputs, outputs, scalars=None, scratch=(), micros=5.0, limit=LIMIT, after=(), scale=1.0):
    specs, arrays, views = [], [], []
    here = pl.BlockSpec(memory_space=pltpu.VMEM)
    for item in inputs:
        view = None
        if isinstance(item, Row):
            specs.append(row_of(item, blocks))
            arrays.append(pltpu.with_memory_space_constraint(item.array, pltpu.HBM))
        elif isinstance(item, Part):
            specs.append(block_of(item.array.shape, item.how, blocks, item.pick))
            arrays.append(item.array)
        elif isinstance(item, Pick):
            rows, width = item.array.shape
            specs.append(pl.BlockSpec((rows // item.parts, width), functools.partial(lambda at, i, s: (s[at], 0), item.scalar)))
            arrays.append(pltpu.with_memory_space_constraint(item.array, pltpu.HBM))
        elif isinstance(item, Far):
            specs.append(block_of(item.array.shape, "whole", blocks, once=True))
            arrays.append(pltpu.with_memory_space_constraint(item.array, pltpu.HBM))
        elif isinstance(item, Held):
            specs.append(here)
            arrays.append(pltpu.with_memory_space_constraint(item.array, pltpu.VMEM))
            view = view_of(item.array.shape, item.how, blocks)
        else:
            specs.append(block_of(item.shape, "whole", blocks, once=True))
            arrays.append(item)
        views.append(view)
    for item in after:
        specs.append(pl.BlockSpec(memory_space=pl.ANY))
        arrays.append(item)
        views.append("skip")
    shapes, out_specs = [], []
    for shape, dtype, how in outputs:
        if how[:4] == "held":
            shapes.append(pltpu.VMEM(shape, dtype))
            out_specs.append(here)
            views.append(view_of(shape, how[5:], blocks))
        else:
            far = how[:3] == "hbm"
            shapes.append(pltpu.HBM(shape, dtype) if far else jax.ShapeDtypeStruct(shape, dtype))
            out_specs.append(block_of(shape, how[4:] if far else how, blocks))
            views.append(None)
    lead = 0 if scalars is None else 1

    def viewed(*refs):
        passed = list(refs[:lead])
        for ref, view in zip(refs[lead : lead + len(views)], views):
            if view == "skip":
                continue
            passed.append(ref if view is None else view(ref))
        return kernel(*passed, *refs[lead + len(views) :])

    settings = dict(
        out_shape=shapes,
        compiler_params=pltpu.CompilerParams(vmem_limit_bytes=limit * MIB, dimension_semantics=("arbitrary",)),
        cost_estimate=pl.CostEstimate(flops=int(micros * scale * 1.0e9), bytes_accessed=0, transcendentals=0),
        name=name,
    )
    if scalars is None:
        return pl.pallas_call(
            viewed, grid=(blocks,), in_specs=specs, out_specs=out_specs, scratch_shapes=list(scratch), **settings
        )(*arrays)
    grid_spec = pltpu.PrefetchScalarGridSpec(
        num_scalar_prefetch=1, grid=(blocks,), in_specs=specs, out_specs=out_specs, scratch_shapes=list(scratch)
    )
    return pl.pallas_call(viewed, grid_spec=grid_spec, **settings)(scalars, *arrays)


def local(
    size, tokens, memory, cotangent, tgt_len, src_len, self_query, self_key, self_value, self_out,
    cross_query, cross_key, cross_value, cross_out, ffn_up, ffn_down,
    gain_one, shift_one, gain_two, shift_two, gain_three, shift_three,
):
    width = tokens.shape[1]
    length = tokens.shape[0] // 2
    source = memory.shape[0] // 2
    each = self_query.shape[1]
    heads = each // HEAD_DIM
    hidden = ffn_up.shape[1]
    place = lax.axis_index("tp").astype(jnp.int32)
    group = lax.axis_index("dp").astype(jnp.int32)
    scalars = jnp.concatenate(
        [jnp.stack([place // 2]), tgt_len, src_len, jnp.stack([place % 2] + [(group >> b) & 1 for b in range(3)])]
    )
    big, small, third = length // BLOCK, length // SPAN, width // SPAN
    short = size == 8

    def across(value):
        return lax.ppermute(value, "tp", ACROSS)

    def sibling(value):
        return lax.ppermute(value, "tp", CORE)

    def along(value, bit):
        return lax.ppermute(value, "dp", [(i, i ^ (1 << bit)) for i in range(size)])

    def shares(part, blocks):
        per = blocks // 2
        first, second = (lambda i: jnp.minimum(i, per - 1)), (lambda i: jnp.maximum(i - per, 0))
        got = [sibling(p) for p in part]
        return [Part(v, "half", pick) for v, pick in zip((*part, *got), (first, second) * 2)]

    def part_shapes(blocks):
        per = blocks // 2
        first, second = (lambda i: jnp.minimum(i, per - 1)), (lambda i: jnp.maximum(i - per, 0))
        return [((length // 2, width), bf16, ("half", pick)) for pick in (first, second)]

    head_rows = ((heads, length, WIDE), bf16, "hbm rows")
    head_held = ((heads, length, WIDE), bf16, "held rows")
    key_held = ((heads, source, WIDE), bf16, "held rows")
    held = ((length, width), f32, "held rows")
    held_low = ((length, width), bf16, "held rows")
    column = ((length, 1), f32, "held rows")
    att_held = ((length, each), bf16, "held rows")
    hid = ((length, hidden), bf16, "held rows")
    sums = ((8, width), f32, "whole")
    low = ((length, width), bf16, "rows")
    square = ((width, hidden), bf16, "rows")
    half_low = ((length // 2, width), bf16, "whole")
    out_shape = ((each, width), bf16, "whole")
    qkv = functools.partial(pltpu.VMEM, (heads, length, WIDE))

    w_parts = (self_query.T, self_key.T, self_value.T)
    c_parts = (cross_query.T, cross_key.T, cross_value.T)
    bit = scalars[BIT]
    w_half = lax.dynamic_slice_in_dim(jnp.concatenate(w_parts, 0), bit * (3 * each // 2), 3 * each // 2, 0)
    w_near = across(w_half)
    q_new, k_new, v_new, ck_a, cv_a, w_a, cw_a, o_half, down_half = call(
        functools.partial(project_own_kernel, heads=heads), "project_own", big,
        [
            Row(tokens, length, "rows"), Row(memory, source, "rows"), *(Far(v) for v in (*w_parts, *c_parts, self_out, cross_out)),
            Pick(ffn_down, BIT + 1, 2),
        ],
        [
            head_held, head_held, head_held, key_held, key_held, ((3 * each, width), bf16, "whole"),
            ((3 * each, width), bf16, "whole"), out_shape, ((hidden // 2, width), bf16, "whole"),
        ],
        scalars, micros=7, scale=0.05,
    )
    o_near = across(o_half)
    cw_b = across(cw_a)
    up_b = across(ffn_up)
    down_near = across(down_half)
    down_far = along(down_near, 1)
    w_far = along(w_near, 0)
    q_a, k_a, v_a, att_a = call(
        functools.partial(self_own_kernel, heads=heads), "self_own", big, [Held(q_new), Held(k_new, "whole"), Held(v_new, "whole")],
        [head_rows, head_rows, head_rows, att_held], micros=6, scale=0.05, after=[w_near],
    )
    o_far = along(o_near, 0)
    w_b, q_b, k_b, v_b, att_b = call(
        functools.partial(self_other_kernel, heads=heads), "self_other", big, [Row(tokens, length, "rows"), w_near, w_far],
        [((3 * each, width), bf16, "whole"), head_rows, head_rows, head_rows, att_held], scalars, scratch=[qkv(bf16), qkv(bf16)],
        micros=9, scale=0.05, after=[o_near],
    )
    part0, part1, so_b, co_b = call(
        functools.partial(self_out_kernel, blocks=big), "self_out", big, [Held(att_a), Held(att_b), self_out, o_near, o_far],
        [*part_shapes(big), out_shape, out_shape], scalars, micros=3, scale=0.05,
    )
    h_one, h_one_low, unit_one, scale_one, cq_a, catt_a = call(
        functools.partial(cross_own_kernel, heads=heads, blocks=big), "cross_own", big,
        [Row(tokens, length, "rows"), *shares((part0, part1), big), gain_one, shift_one, c_parts[0], Held(ck_a, "whole"), Held(cv_a, "whole")],
        [held, held_low, held_low, column, head_held, att_held], scalars, micros=10, scale=0.05,
    )
    part0, part1, ck_b, cv_b, cq_b, catt_b = call(
        functools.partial(cross_other_kernel, heads=heads, blocks=big), "cross_other", big,
        [Row(memory, source), Held(h_one_low), cw_b, Held(catt_a), cross_out, co_b],
        [
            *part_shapes(big), ((heads, source, WIDE), bf16, "held whole"), ((heads, source, WIDE), bf16, "held whole"),
            head_held, att_held,
        ],
        scalars, micros=11, scale=0.05, after=[down_near],
    )
    h_two, h_two_low, unit_two, scale_two, act_a, slope_a, term = call(
        functools.partial(ffn_own_kernel, blocks=small), "ffn_own", small,
        [Held(h_one), *shares((part0, part1), small), gain_two, shift_two, Held(ffn_up, "whole"), Held(ffn_down, "whole")],
        [held, held_low, held_low, column, hid, hid, held], micros=7, scale=0.05,
    )
    part0, part1, act_b, slope_b, down_b = call(
        functools.partial(ffn_other_kernel, blocks=small), "ffn_other", small,
        [Held(h_two_low), Held(term), up_b, down_near, down_far],
        [*part_shapes(small), hid, hid, ((hidden, width), bf16, "held whole")], scalars, micros=5, scale=0.05,
    )

    part0, part1, out_row, d_three, e_three, pre_a, pre_b, sums_three = call(
        functools.partial(ffn_back_kernel, blocks=small), "ffn_back", small,
        [
            Held(h_two), *shares((part0, part1), small), Row(cotangent, length, "rows"), gain_three, shift_three,
            Held(ffn_up, "whole"), up_b, Held(ffn_down, "whole"), Held(down_b, "whole"), Held(slope_a), Held(slope_b),
        ],
        [*part_shapes(small), low, held, held_low, hid, hid, sums], scalars, micros=11,
    )
    part = (part0, part1)
    gu_b, gd_b = call(
        ffn_grad_kernel, "ffn_grad_other", third,
        [Held(h_two_low, "columns"), Held(act_b, "columns"), Held(e_three, "whole"), Held(pre_b, "whole")], [square, square], micros=4,
    )
    gu_got, gd_got = across(gu_b), across(gd_b)
    gu_a, gd_a = call(
        ffn_grad_kernel, "ffn_grad_own", third,
        [Held(h_two_low, "columns"), Held(act_a, "columns"), Held(e_three, "whole"), Held(pre_a, "whole")], [square, square], micros=4,
    )
    back_scratch = [
        pltpu.VMEM((heads, BLOCK, WIDE), f32), pltpu.VMEM((heads, source, WIDE), f32), pltpu.VMEM((heads, source, WIDE), f32),
    ]
    dkv_held = ((source, 2 * each), bf16, "held whole")
    d_two, e_two, sums_two, do_a, dcq_b, dckv_b = call(
        functools.partial(cross_back_other_kernel, heads=heads, blocks=big), "cross_back_other", big,
        [
            Held(d_three), *shares(part, big), gain_two, Held(unit_two), Held(scale_two), cross_out, co_b, Held(catt_a), Held(catt_b),
            Held(cq_b), Held(ck_b, "whole"), Held(cv_b, "whole"),
        ],
        [held, held_low, sums, head_held, att_held, dkv_held], scalars,
        scratch=[pltpu.VMEM((heads, BLOCK, WIDE), bf16)] + back_scratch, micros=18,
    )

    def step(name, plans, after=(), micros=2):
        inputs, outputs, kernel_plans, counts, most = [], [], [], [], 16
        for kind, arrays, rows, bit, cuts in plans:
            inputs += arrays
            if kind == "sum":
                made = [((rows, width), bf16, "whole")] if bit is None else [((rows // 2, width), bf16, "whole")] * 2
            elif kind == "pack":
                made = [((rows, width), bf16, "whole")]
            else:
                made = [((size, width), f32, "hbm whole") for _, size in cuts]
            if kind != "pack":
                most = max(most, rows)
            outputs += made
            counts.append(len(made))
            kernel_plans.append((kind, len(arrays), rows, bit, cuts))
        made = list(
            call(
                functools.partial(step_kernel, plans=kernel_plans), name, 1, inputs, outputs, scalars,
                scratch=[pltpu.VMEM((most, width), bf16)], micros=micros, after=after,
            )
        )
        return [made[sum(counts[:n]) : sum(counts[: n + 1])] for n in range(len(counts))]

    class Chain:
        def __init__(self, mine, got, rows, cuts):
            self.arrays, self.rows, self.cuts, self.stage = [*mine, *got], rows, cuts, 0

        def plan(self):
            stage = self.stage
            if stage <= 3:
                return ("sum", self.arrays, self.rows >> stage, stage if stage < 3 else None, ())
            bit = 6 - stage
            return ("wide" if stage == 6 else "pack", self.arrays, self.rows >> bit, bit, self.cuts if stage == 6 else ())

        def take(self, made):
            stage, self.stage = self.stage, self.stage + 1
            if stage < 3:
                self.arrays = [made[1], along(made[0], stage)]
            elif stage < 6:
                self.arrays = [made[0], along(made[0], 5 - stage)]
            else:
                self.done = made

    def advance(name, chains, plans=(), after=(), micros=2):
        made = step(name, [c.plan() for c in chains] + list(plans), after, micros)
        for chain, one in zip(chains, made):
            chain.take(one)
        return [made[0][-1]], [m[0] for m in made[len(chains) :]]

    everything = [(0, width)]
    thirds = [(n * each, each) for n in range(3)]
    pin = []
    if short:
        up = Chain([gu_a], [gu_got], width, everything)
        pin, _ = advance("step_0", [up], after=[dcq_b])
    part0, part1, dcq_a, dckv_a = call(
        functools.partial(cross_back_own_kernel, heads=heads, blocks=big), "cross_back_own", big,
        [Held(cq_a), Held(ck_a, "whole"), Held(cv_a, "whole"), Held(do_a), Held(dcq_b), c_parts[0], cw_b],
        [*part_shapes(big), att_held, dkv_held], scalars, scratch=back_scratch, micros=16, after=pin,
    )
    part = (part0, part1)

    def cross_grads(name, att, dq, dkv, after=()):
        return call(
            cross_grad_kernel, name, third,
            [
                Held(h_one_low, "columns"), Row(memory, source, "columns"), Held(att, "whole"), Held(e_two, "columns"),
                Held(dq, "whole"), Held(dkv, "whole"),
            ],
            [((4 * each, width), bf16, "columns")], scalars, micros=5, after=after,
        )[0]

    gc_b = cross_grads("cross_grad_other", catt_b, dcq_b, dckv_b, [dcq_a])
    gc_got = across(gc_b)
    if short:
        down = Chain([gd_a], [gd_got], width, everything)
        pin, _ = advance("step_1", [up, down], after=[gc_b])
    gc_a = cross_grads("cross_grad_own", catt_a, dcq_a, dckv_a, pin)
    memory_send, memory_keep, out_half = call(
        memory_grad_kernel, "memory_grad", 2,
        [Held(dckv_a), Held(dckv_b), cw_a, cw_b, Row(out_row, length // 2, ("part", CORE_AT))],
        [half_low, half_low, ((length // 2, width), bf16, "rows")], scalars, micros=5, after=[gc_a],
    )
    out_far = across(out_half)
    memory_got = sibling(memory_send)
    pin = [memory_send]
    if short:
        cross = Chain([gc_a], [gc_got], 4 * each, [(n * each, each) for n in range(4)])
        pin, _ = advance("step_2", [up, down, cross], after=[memory_send])
    rest_shape = ((each + 16, width), bf16, "whole")
    d_one, do_a, do_b, rest_a, rest_b = call(
        functools.partial(norm_one_back_kernel, heads=heads, blocks=small), "norm_one_back", small,
        [
            Held(d_two), *shares(part, small), gain_one, Held(unit_one), Held(scale_one), self_out, so_b,
            Held(att_a, "whole"), Held(att_b, "whole"), sums_two, sums_three,
        ],
        [held, head_held, head_held, rest_shape, rest_shape], scalars,
        scratch=[pltpu.VMEM((length, width), bf16), pltpu.VMEM((8, width), f32)], micros=6, after=pin,
    )
    rest_got = across(rest_b)
    kept_w = ((3 * each, width), bf16, "whole")
    qkv_held = ((length, 3 * each), bf16, "held whole")
    self_scratch = [
        pltpu.VMEM((heads, SPAN, WIDE), f32), pltpu.VMEM((heads, length, WIDE), f32), pltpu.VMEM((heads, length, WIDE), f32),
    ]

    def self_back(name, q, k, v, do, after=()):
        return call(
            functools.partial(self_back_kernel, heads=heads, blocks=small), name, small,
            [Row(tokens, length), Part(q), k, v, Held(do)], [qkv_held, kept_w], scalars, scratch=self_scratch, micros=14, after=after,
        )

    pin = []
    if short:
        pin, _ = advance("step_3", [up, down, cross], after=[do_b])
    dqkv_b, gw_b = self_back("self_back_other", q_b, k_b, v_b, do_b, pin)
    gw_got = across(gw_b)

    pin = []
    if short:
        rest = Chain([rest_a], [rest_got], 256, [(0, each), (each, 16)])
        pin, _ = advance("step_4", [up, down, cross, rest], (), [dqkv_b], 3)
    dqkv_a, gw_a = self_back("self_back_own", q_a, k_a, v_a, do_a, pin)
    memory_plan = ("sum", [memory_keep, memory_got], length // 2, None, ())
    if short:
        own = Chain([gw_a], [gw_got], 640, thirds)
        pin, (mine,) = advance("step_5", [own, up, down, cross, rest], [memory_plan], (), 4)
    else:
        ((mine,),) = step("memory_finish", [memory_plan], [gw_a])
        pin = []
    far = across(mine)
    memory_pieces = [mine, sibling(mine), far, sibling(far)]
    tokens_send, tokens_keep = call(
        tokens_grad_kernel, "tokens_grad", 2, [Held(d_one), Held(dqkv_a), Held(dqkv_b), w_a, w_b],
        [half_low, ((length // 2, width), f32, "whole")], scalars, micros=6, after=pin,
    )
    tokens_plan = ("sum", [tokens_keep, sibling(tokens_send)], length // 2, None, ())

    def placed(name, pieces, shift, after=()):
        return call(
            functools.partial(place_kernel, shift=shift), name, 4, pieces, [((2 * length, width), bf16, "hbm rows")], scalars,
            micros=4, after=after,
        )[0]

    if short:
        pin, (mine,) = advance("step_6", [own, up, down, cross, rest], [tokens_plan], [tokens_send], 3)
    else:
        ((mine,),) = step("tokens_finish", [tokens_plan])
        pin = []
    far = across(mine)
    tokens_pieces = [mine, sibling(mine), far, sibling(far)]
    layer_out = placed("place_layer_out", [out_row, out_far, sibling(out_far)], True, pin)
    if short:
        pin, _ = advance("step_7", [own, down, cross, rest], (), [layer_out])
        memory_grad = placed("place_memory_grad", memory_pieces, False, pin)
        pin, _ = advance("step_8", [own, cross, rest], (), [memory_grad])
        pin, _ = advance("step_9", [own, rest], (), pin)
        tokens_grad = placed("place_tokens_grad", tokens_pieces, False, pin)
        pin, _ = advance("step_10", [own, rest], (), [tokens_grad])
        advance("step_11", [own], (), pin)
        (gu_wide,), (gd_wide,), cross, own = up.done, down.done, cross.done, own.done
        rest, norms = rest.done
    else:
        memory_grad = placed("place_memory_grad", memory_pieces, False)
        tokens_grad = placed("place_tokens_grad", tokens_pieces, False)

        def total(mine, got):
            return lax.psum((mine.astype(f32) + got.astype(f32)).astype(bf16), "dp").astype(f32)

        gu_wide, gd_wide = total(gu_a, gu_got), total(gd_a, gd_got)
        cross = jnp.split(total(gc_a, gc_got), 4)
        own = jnp.split(total(gw_a, gw_got), 3)
        rest = total(rest_a, rest_got)
        rest, norms = rest[:each], rest[each:]
    return (
        layer_out, tokens_grad, memory_grad,
        own[0].T, own[1].T, own[2].T, rest,
        cross[0].T, cross[1].T, cross[2].T, cross[3],
        gu_wide, gd_wide, *(norms[i] for i in range(6)),
    )


def solution(mesh):
    rows, columns, down = P("dp", None), P(None, "tp"), P("tp", None)
    return jax.shard_map(
        functools.partial(local, mesh.shape["dp"]),
        mesh=mesh,
        in_specs=(rows, rows, rows, P("dp"), P("dp"))
        + (columns, columns, columns, down) * 2
        + (columns, down)
        + (P(),) * 6,
        out_specs=(rows, rows, rows) + (columns, columns, columns, down) * 2 + (columns, down) + (P(),) * 6,
        check_vma=False,
    )
```

```python
import functools

import jax
import jax.numpy as jnp
from jax import lax
from jax.experimental import pallas as pl
from jax.experimental.pallas import tpu as pltpu
from jax.sharding import PartitionSpec as P

HEAD_DIM = 64
WIDE = 2 * HEAD_DIM
EPS = 1e-05
MASKED = -1e30
LOG2E = 1.4426950408889634
LN2 = 0.6931471805599453
f32 = jnp.float32
bf16 = jnp.bfloat16

CORE = [(0, 1), (1, 0), (2, 3), (3, 2)]
ACROSS = [(0, 2), (2, 0), (1, 3), (3, 1)]
MIB = 1 << 20
LIMIT = 16

ROWS, WHOLE, COLUMNS, HALF, PART, SKIP, ARBITRARY = "rows", "whole", "columns", "half", "part", "skip", "arbitrary"
HELD_ROWS, HELD_WHOLE, FAR_ROWS, FAR_WHOLE = "held rows", "held whole", "hbm rows", "hbm whole"
SUM, PACK, WIDEN, STACK, LAST = "sum", "pack", "wide", "stack", "last"


def nn(left, right):
    return lax.dot_general(left, right, (((1,), (0,)), ((), ())), preferred_element_type=f32)


def nt(left, right):
    return lax.dot_general(left, right, (((1,), (1,)), ((), ())), preferred_element_type=f32)


def tn(left, right):
    return lax.dot_general(left, right, (((0,), (0,)), ((), ())), preferred_element_type=f32)


def lanes(rows):
    return lax.broadcasted_iota(jnp.int32, (rows, HEAD_DIM), 1)


def three_parts(value):
    high = value.astype(bf16).astype(f32)
    rest = value - high
    middle = rest.astype(bf16).astype(f32)
    return high, middle, rest - middle


def fill_queries(q_ref, rows, count, acc, heads):
    tail = jnp.where(lanes(count) == 0, 1.0, 0.0)
    for h in range(heads):
        part = acc[:, h * HEAD_DIM : (h + 1) * HEAD_DIM]
        q_ref[h, rows, :] = jnp.concatenate([part, tail], 1).astype(bf16)


def fill_keys(k_ref, v_ref, rows, start, count, acc, heads, limit):
    lane = lanes(count)
    index = start + lax.broadcasted_iota(jnp.int32, (count, HEAD_DIM), 0)
    tail = jnp.where(lane == 0, jnp.where(index < limit, 0.0, MASKED), jnp.where(lane < 4, 1.0, 0.0))
    ones = jnp.ones((count, HEAD_DIM), f32)
    for h in range(heads):
        k = acc[:, h * HEAD_DIM : (h + 1) * HEAD_DIM]
        v = acc[:, (heads + h) * HEAD_DIM : (heads + h + 1) * HEAD_DIM]
        k_ref[h, rows, :] = jnp.concatenate([k, tail], 1).astype(bf16)
        v_ref[h, rows, :] = jnp.concatenate([v, ones], 1).astype(bf16)


def attend_block(q_ref, k_ref, v_ref, att_ref, h, column, rows, count, key_end, causal):
    s = nt(q_ref[h, rows, :], k_ref[h, :key_end, :])
    if causal:
        r = lax.broadcasted_iota(jnp.int32, (count, count), 0)
        c = lax.broadcasted_iota(jnp.int32, (count, count), 1)
        diagonal = jnp.where(c <= r, s[:, key_end - count :], MASKED)
        s = diagonal if key_end == count else jnp.concatenate([s[:, : key_end - count], diagonal], 1)
    peak = jnp.max(s, 1, keepdims=True)
    p = jnp.exp2(s - peak).astype(bf16)
    o = nn(p, v_ref[h, :key_end, :])
    total = o[:, HEAD_DIM : HEAD_DIM + 1]
    att_ref[rows, column : column + HEAD_DIM] = (o[:, :HEAD_DIM] / total).astype(bf16)
    high, middle, low = three_parts(-(peak + jnp.log2(total)))
    lane = lanes(count)
    tail = jnp.where(
        lane == 0, 1.0, jnp.where(lane == 1, high, jnp.where(lane == 2, middle, jnp.where(lane == 3, low, 0.0)))
    )
    q_ref[h, rows, HEAD_DIM:] = tail.astype(bf16)


def fill_grads(do_ref, rows, count, grad, att, heads):
    lane = lanes(count)
    for h in range(heads):
        part = grad[:, h * HEAD_DIM : (h + 1) * HEAD_DIM].astype(bf16)
        mixed = att[:, h * HEAD_DIM : (h + 1) * HEAD_DIM].astype(f32)
        inner = jnp.sum(part.astype(f32) * mixed, 1, keepdims=True)
        high, middle, low = three_parts(-inner)
        tail = jnp.where(lane == 0, high, jnp.where(lane == 1, middle, jnp.where(lane == 2, low, 0.0)))
        do_ref[h, rows, :] = jnp.concatenate([part, tail.astype(bf16)], 1)


def back_block(q_ref, k_ref, v_ref, do_ref, dq_ref, dk_ref, dv_ref, h, rows, count, key_end, causal, first):
    q = q_ref[h, rows, :]
    d = do_ref[h, rows, :]
    k = k_ref[h, :key_end, :]
    v = v_ref[h, :key_end, :]
    p = jnp.exp2(nt(k, q))
    if causal:
        r = lax.broadcasted_iota(jnp.int32, (count, count), 0)
        c = lax.broadcasted_iota(jnp.int32, (count, count), 1)
        diagonal = jnp.where(r <= c, p[key_end - count :], 0.0)
        p = diagonal if key_end == count else jnp.concatenate([p[: key_end - count], diagonal], 0)
    ds = (p * nt(v, d)).astype(bf16)
    dv = nn(p.astype(bf16), d)
    dk = nn(ds, q)
    if first:
        dv_ref[h, :key_end, :] = dv
        dk_ref[h, :key_end, :] = dk
    else:
        dv_ref[h, :key_end, :] += dv
        dk_ref[h, :key_end, :] += dk
    dq_ref[h, rows, :] = tn(k, ds).T


def pack_heads(source, rows, heads, factor):
    return jnp.concatenate([source[h, rows, :HEAD_DIM] * factor for h in range(heads)], 1).astype(bf16)


def norm(resid):
    center = resid - jnp.mean(resid, -1, keepdims=True)
    scale = lax.rsqrt(jnp.mean(center * center, -1, keepdims=True) + EPS)
    return center * scale, scale


def norm_back(grad, gain, unit, scale):
    lifted = grad * gain
    first = jnp.mean(lifted, -1, keepdims=True)
    second = jnp.mean(lifted * unit, -1, keepdims=True)
    return scale * (lifted - first - unit * second)


def gelu_pair(value):
    scaled = value * 0.7071067811865476
    density = jnp.exp(-scaled * scaled) * 0.3989422804014327
    below = 0.5 * (1.0 + lax.erf(scaled))
    return value * below, below + value * density


BLOCK = 512
SPAN = 256
ROW, TGT, SRC, CORE_AT, BIT = 0, 1, 3, 5, 6
FACTOR = HEAD_DIM ** (-0.5) * LOG2E


def vector(ref):
    return ref[...].reshape(1, ref.shape[0])


def branch_of(shares, blocks):
    own0, own1, got0, got1 = shares
    first = pl.program_id(0) < blocks // 2
    own = jnp.where(first, own0[...], own1[...]).astype(f32)
    return own + jnp.where(first, got0[...], got1[...]).astype(f32)


def put_part(first_ref, second_ref, value, blocks):
    at = pl.program_id(0)

    @pl.when(at < blocks // 2)
    def _():
        first_ref[...] = value

    @pl.when(at >= blocks // 2)
    def _():
        second_ref[...] = value


def rows_at(size):
    return pl.ds(pl.multiple_of(pl.program_id(0) * size, size), size)


def project_own_kernel(
    s_ref, x_ref, m_ref, sq_ref, sk_ref, sv_ref, cq_ref, ck_ref, cv_ref, so_ref, co_ref,
    q_ref, k_ref, v_ref, mk_ref, mv_ref, wa_ref, cwa_ref, half_out_ref, half_cw_ref, *, heads,
):
    each = heads * HEAD_DIM
    at = pl.program_id(0)

    @pl.when(at == 0)
    def _():
        for n, ref in enumerate((sq_ref, sk_ref, sv_ref)):
            wa_ref[n * each : (n + 1) * each, :] = ref[...]
        for n, ref in enumerate((cq_ref, ck_ref, cv_ref)):
            cwa_ref[n * each : (n + 1) * each, :] = ref[...]
        half_out_ref[...] = jnp.where(s_ref[BIT] == 0, so_ref[...], co_ref[...])
        half = half_cw_ref.shape[0]
        half_cw_ref[...] = cwa_ref[pl.ds(pl.multiple_of(s_ref[BIT + 1] * half, 16), half), :]

    limit = s_ref[TGT + s_ref[ROW]]
    memory_limit = s_ref[SRC + s_ref[ROW]]
    rows = pl.ds(0, BLOCK)
    acc = nt(x_ref[...], wa_ref[...])
    fill_queries(q_ref, rows, BLOCK, acc[:, :each] * FACTOR, heads)
    fill_keys(k_ref, v_ref, rows, at * BLOCK, BLOCK, acc[:, each:], heads, limit)
    acc = nt(m_ref[...], cwa_ref[each:, :])
    fill_keys(mk_ref, mv_ref, rows, at * BLOCK, BLOCK, acc, heads, memory_limit)


def causal_blocks(q_ref, k_ref, v_ref, att_ref, heads):
    at = pl.program_id(0)
    for block in range(k_ref.shape[1] // BLOCK):

        @pl.when(at == block)
        def _():
            for h in range(heads):
                attend_block(q_ref, k_ref, v_ref, att_ref, h, h * HEAD_DIM, pl.ds(0, BLOCK), BLOCK, (block + 1) * BLOCK, True)


def self_own_kernel(
    s_ref, q_in_ref, k_ref, v_ref, up_ref, down_ref, q_ref, k_out_ref, v_out_ref, att_ref, halves_ref, *, heads
):
    half = up_ref.shape[0]
    halves_ref[:half, :] = up_ref[...]
    halves_ref[half:, :] = down_ref[...]
    q_ref[...] = q_in_ref[...]
    k_out_ref[...] = k_ref[:, rows_at(BLOCK), :]
    v_out_ref[...] = v_ref[:, rows_at(BLOCK), :]
    causal_blocks(q_ref, k_ref, v_ref, att_ref, heads)


def self_other_kernel(s_ref, x_ref, near_ref, far_ref, w_ref, q_ref, k_out_ref, v_out_ref, att_ref, k_ref, v_ref, *, heads):
    each = heads * HEAD_DIM
    at = pl.program_id(0)

    @pl.when(at == 0)
    def _():
        put_halves(w_ref, near_ref, far_ref, s_ref[BIT])

    acc = nt(x_ref[...], w_ref[...])
    fill_queries(q_ref, pl.ds(0, BLOCK), BLOCK, acc[:, :each] * FACTOR, heads)
    fill_keys(k_ref, v_ref, rows_at(BLOCK), at * BLOCK, BLOCK, acc[:, each:], heads, s_ref[TGT + s_ref[ROW]])
    k_out_ref[...] = k_ref[:, rows_at(BLOCK), :]
    v_out_ref[...] = v_ref[:, rows_at(BLOCK), :]
    causal_blocks(q_ref, k_ref, v_ref, att_ref, heads)


def self_out_kernel(s_ref, atta_ref, attb_ref, soa_ref, near_ref, far_ref, part0_ref, part1_ref, sob_ref, cob_ref, *, blocks):
    @pl.when(pl.program_id(0) == 0)
    def _():
        low = s_ref[BIT] == 0
        sob_ref[...] = jnp.where(low, near_ref[...], far_ref[...])
        cob_ref[...] = jnp.where(low, far_ref[...], near_ref[...])

    part = nn(atta_ref[...], soa_ref[...]) + nn(attb_ref[...], sob_ref[...])
    put_part(part0_ref, part1_ref, part.astype(bf16), blocks)


def cross_blocks(q_ref, k_ref, v_ref, att_ref, heads, limit):
    step = 256
    live = (limit + step - 1) // step
    for count in range(1, k_ref.shape[1] // step + 1):

        @pl.when(live == count)
        def _():
            for h in range(heads):
                attend_block(q_ref, k_ref, v_ref, att_ref, h, h * HEAD_DIM, pl.ds(0, BLOCK), BLOCK, count * step, False)


def cross_own_kernel(
    s_ref, x_ref, own0, own1, got0, got1, gain_ref, shift_ref, cq_ref, k_ref, v_ref,
    h_ref, hl_ref, unit_ref, scale_ref, q_ref, att_ref, *, heads, blocks,
):
    unit, scale = norm(x_ref[...].astype(f32) + branch_of((own0, own1, got0, got1), blocks))
    h = unit * vector(gain_ref) + vector(shift_ref)
    h_ref[...] = h
    unit_ref[...] = unit.astype(bf16)
    scale_ref[...] = scale
    low = h.astype(bf16)
    hl_ref[...] = low
    fill_queries(q_ref, pl.ds(0, BLOCK), BLOCK, nt(low, cq_ref[...]) * FACTOR, heads)
    cross_blocks(q_ref, k_ref, v_ref, att_ref, heads, s_ref[SRC + s_ref[ROW]])


def put_halves(target_ref, near_ref, far_ref, high):
    half = near_ref.shape[0]
    target_ref[pl.ds(pl.multiple_of(high * half, 16), half), :] = near_ref[...]
    target_ref[pl.ds(pl.multiple_of((1 - high) * half, 16), half), :] = far_ref[...]


def cross_other_kernel(s_ref, m_ref, hl_ref, near_ref, far_ref, cwb_ref, k_ref, v_ref, q_ref, att_ref, *, heads):
    each = heads * HEAD_DIM
    limit = s_ref[SRC + s_ref[ROW]]

    @pl.when(pl.program_id(0) == 0)
    def _():
        put_halves(cwb_ref, near_ref, far_ref, s_ref[BIT + 1])

        @pl.loop(0, m_ref.shape[0], step=BLOCK)
        def _(start):
            rows = pl.ds(pl.multiple_of(start, BLOCK), BLOCK)
            fill_keys(k_ref, v_ref, rows, start, BLOCK, nt(m_ref[rows, :], cwb_ref[each:, :]), heads, limit)

    fill_queries(q_ref, pl.ds(0, BLOCK), BLOCK, nt(hl_ref[...], cwb_ref[:each, :]) * FACTOR, heads)
    cross_blocks(q_ref, k_ref, v_ref, att_ref, heads, limit)


def cross_out_kernel(atta_ref, attb_ref, coa_ref, cob_ref, part0_ref, part1_ref, *, blocks):
    part = nn(atta_ref[...], coa_ref[...]) + nn(attb_ref[...], cob_ref[...])
    put_part(part0_ref, part1_ref, part.astype(bf16), blocks)


def ffn_own_kernel(
    h_in_ref, own0, own1, got0, got1, gain_ref, shift_ref, up_ref, down_ref,
    h_ref, hl_ref, unit_ref, scale_ref, act_ref, slope_ref, term_ref, *, blocks,
):
    unit, scale = norm(h_in_ref[...] + branch_of((own0, own1, got0, got1), blocks))
    h = unit * vector(gain_ref) + vector(shift_ref)
    h_ref[...] = h
    unit_ref[...] = unit.astype(bf16)
    scale_ref[...] = scale
    low = h.astype(bf16)
    hl_ref[...] = low
    act, slope = gelu_pair(nn(low, up_ref[...]))
    act = act.astype(bf16)
    act_ref[...] = act
    slope_ref[...] = slope.astype(bf16)
    term_ref[...] = nn(act, down_ref[...])


def ffn_other_kernel(
    s_ref, hl_ref, term_ref, up_near_ref, up_far_ref, down_near_ref, down_far_ref,
    part0_ref, part1_ref, act_ref, slope_ref, up_ref, down_ref, *, blocks,
):
    @pl.when(pl.program_id(0) == 0)
    def _():
        put_halves(up_ref, up_near_ref, up_far_ref, s_ref[BIT])
        put_halves(down_ref, down_near_ref, down_far_ref, s_ref[BIT + 1])

    act, slope = gelu_pair(nn(hl_ref[...], up_ref[...]))
    act = act.astype(bf16)
    act_ref[...] = act
    slope_ref[...] = slope.astype(bf16)
    put_part(part0_ref, part1_ref, (term_ref[...] + nn(act, down_ref[...])).astype(bf16), blocks)


def ffn_back_kernel(
    s_ref, h_ref, own0, own1, got0, got1, cot_ref, gain_ref, shift_ref, upa_ref, upb_ref, downa_ref, downb_ref, slopea_ref, slopeb_ref,
    part0_ref, part1_ref, out_ref, d_ref, e_ref, prea_ref, preb_ref, sums_ref, *, blocks,
):
    limit = s_ref[TGT + s_ref[ROW]]
    at = pl.program_id(0)

    @pl.when(at == 0)
    def _():
        sums_ref[...] = jnp.zeros_like(sums_ref)

    gain = vector(gain_ref)
    unit, scale = norm(h_ref[...] + branch_of((own0, own1, got0, got1), blocks))
    out_ref[...] = (unit * gain + vector(shift_ref)).astype(bf16)
    index = at * SPAN + lax.broadcasted_iota(jnp.int32, (SPAN, 1), 0)
    grad = jnp.where(index < limit, cot_ref[...].astype(f32), 0.0)
    sums_ref[0:1, :] += jnp.sum(grad * unit, 0, keepdims=True)
    sums_ref[1:2, :] += jnp.sum(grad, 0, keepdims=True)
    d = norm_back(grad, gain, unit, scale)
    d_ref[...] = d
    e = d.astype(bf16)
    e_ref[...] = e
    part = None
    for up_ref, down_ref, slope_ref, pre_ref in (
        (upa_ref, downa_ref, slopea_ref, prea_ref),
        (upb_ref, downb_ref, slopeb_ref, preb_ref),
    ):
        pre = (nt(e, down_ref[...]) * slope_ref[...].astype(f32)).astype(bf16)
        pre_ref[...] = pre
        term = nt(pre, up_ref[...])
        part = term if part is None else part + term
    put_part(part0_ref, part1_ref, part.astype(bf16), blocks)


def ffn_grad_kernel(s_ref, h_ref, act_ref, e_ref, pre_ref, up_ref, send_ref, keep_ref):
    up_ref[...] = tn(h_ref[...], pre_ref[...]).astype(bf16)
    down = tn(act_ref[...], e_ref[...]).astype(bf16)
    mine = pl.program_id(0) == s_ref[BIT]

    @pl.when(mine)
    def _():
        keep_ref[...] = down

    @pl.when(jnp.logical_not(mine))
    def _():
        send_ref[...] = down


def norm_step(d_in_ref, shares, gain, unit_ref, scale_ref, d_ref, e_ref, sums_ref, blocks):
    @pl.when(pl.program_id(0) == 0)
    def _():
        sums_ref[...] = jnp.zeros_like(sums_ref)

    grad = d_in_ref[...] + branch_of(shares, blocks)
    unit = unit_ref[...].astype(f32)
    sums_ref[0:1, :] += jnp.sum(grad * unit, 0, keepdims=True)
    sums_ref[1:2, :] += jnp.sum(grad, 0, keepdims=True)
    d = norm_back(grad, gain, unit, scale_ref[...])
    d_ref[...] = d
    e = d.astype(bf16)
    e_ref[...] = e
    return e


def cross_back_heads(s_ref, q_ref, k_ref, v_ref, do_ref, dqo_ref, dkv_ref, dq_ref, dk_ref, dv_ref, heads, blocks):
    at = pl.program_id(0)
    source = k_ref.shape[1]

    @pl.when(at == 0)
    def _():
        dk_ref[...] = jnp.zeros_like(dk_ref)
        dv_ref[...] = jnp.zeros_like(dv_ref)

    step = 256
    live = (s_ref[SRC + s_ref[ROW]] + step - 1) // step
    rows = pl.ds(0, BLOCK)
    for count in range(1, source // step + 1):

        @pl.when(live == count)
        def _():
            @pl.loop(0, heads)
            def _(h):
                back_block(q_ref, k_ref, v_ref, do_ref, dq_ref, dk_ref, dv_ref, h, rows, BLOCK, count * step, False, False)

    dqo_ref[...] = pack_heads(dq_ref, rows, heads, HEAD_DIM ** (-0.5))

    @pl.when(at == blocks - 1)
    def _():
        @pl.loop(0, source, step=BLOCK)
        def _(start):
            some = pl.ds(pl.multiple_of(start, BLOCK), BLOCK)
            dkv_ref[some, :] = jnp.concatenate(
                [pack_heads(dk_ref, some, heads, LN2), pack_heads(dv_ref, some, heads, 1.0)], 1
            )


def cross_back_other_kernel(
    s_ref, d_in_ref, own0, own1, got0, got1, gain_ref, unit_ref, scale_ref, coa_ref, cob_ref, atta_ref, attb_ref,
    q_ref, k_ref, v_ref,
    d_ref, e_ref, sums_ref, doa_ref, dqo_ref, dkv_ref, do_ref, dq_ref, dk_ref, dv_ref, *, heads, blocks,
):
    e = norm_step(
        d_in_ref, (own0, own1, got0, got1), vector(gain_ref), unit_ref, scale_ref, d_ref, e_ref, sums_ref, blocks
    )
    fill_grads(doa_ref, pl.ds(0, BLOCK), BLOCK, nt(e, coa_ref[...]), atta_ref[...], heads)
    fill_grads(do_ref, pl.ds(0, BLOCK), BLOCK, nt(e, cob_ref[...]), attb_ref[...], heads)
    cross_back_heads(s_ref, q_ref, k_ref, v_ref, do_ref, dqo_ref, dkv_ref, dq_ref, dk_ref, dv_ref, heads, blocks)


def cross_back_own_kernel(
    s_ref, q_ref, k_ref, v_ref, do_ref, dqb_ref, cqa_ref, cwb_ref,
    part0_ref, part1_ref, dqo_ref, dkv_ref, dq_ref, dk_ref, dv_ref, *, heads, blocks,
):
    cross_back_heads(s_ref, q_ref, k_ref, v_ref, do_ref, dqo_ref, dkv_ref, dq_ref, dk_ref, dv_ref, heads, blocks)
    part = nn(dqo_ref[...], cqa_ref[...]) + nn(dqb_ref[...], cwb_ref[: heads * HEAD_DIM, :])
    put_part(part0_ref, part1_ref, part.astype(bf16), blocks)


def cross_grad_kernel(s_ref, h_ref, m_ref, att_ref, e_ref, dq_ref, dkv_ref, g_ref):
    each = dq_ref.shape[1]
    g_ref[:each, :] = tn(dq_ref[...], h_ref[...]).astype(bf16)
    g_ref[each : 3 * each, :] = tn(dkv_ref[...], m_ref[...]).astype(bf16)
    g_ref[3 * each :, :] = tn(att_ref[...], e_ref[...]).astype(bf16)


def relay_kernel(s_ref, in_ref, first_ref, second_ref):
    half = first_ref.shape[0]
    first_ref[...] = in_ref[:half, :]
    second_ref[...] = in_ref[half:, :]


def memory_grad_kernel(s_ref, a_ref, b_ref, wa_ref, wb_ref, out_ref, send_ref, keep_ref, half_ref):
    half_ref[...] = out_ref[...]
    each = a_ref.shape[1] // 2
    part = (nn(a_ref[...], wa_ref[each:, :]) + nn(b_ref[...], wb_ref[each:, :])).astype(bf16)
    mine = pl.program_id(0) == s_ref[CORE_AT]

    @pl.when(mine)
    def _():
        keep_ref[...] = part

    @pl.when(jnp.logical_not(mine))
    def _():
        send_ref[...] = part


def norm_one_back_kernel(
    s_ref, d_in_ref, own0, own1, got0, got1, gain_ref, unit_ref, scale_ref, soa_ref, sob_ref, atta_ref, attb_ref,
    sums_two_ref, sums_three_ref, d_ref, doa_ref, dob_ref, ra_ref, rb_ref, e_ref, sums_ref, *, heads, blocks,
):
    each = heads * HEAD_DIM
    rows = rows_at(SPAN)
    e = norm_step(
        d_in_ref, (own0, own1, got0, got1), vector(gain_ref), unit_ref, scale_ref, d_ref, e_ref.at[rows, :], sums_ref, blocks
    )
    fill_grads(doa_ref, pl.ds(0, SPAN), SPAN, nt(e, soa_ref[...]), atta_ref[rows, :], heads)
    fill_grads(dob_ref, pl.ds(0, SPAN), SPAN, nt(e, sob_ref[...]), attb_ref[rows, :], heads)

    @pl.when(pl.program_id(0) == blocks - 1)
    def _():
        norms = jnp.concatenate(
            [sums_ref[:2, :], sums_two_ref[:2, :], sums_three_ref[:2, :], jnp.zeros((10, d_in_ref.shape[1]), f32)], 0
        ).astype(bf16)
        for att_ref, r_ref in ((atta_ref, ra_ref), (attb_ref, rb_ref)):
            r_ref[:each, :] = tn(att_ref[...], e_ref[...]).astype(bf16)
            r_ref[each:, :] = norms


def self_back_kernel(s_ref, x_ref, q_ref, k_ref, v_ref, do_ref, dqkv_ref, gw_ref, dq_ref, dk_ref, dv_ref, *, heads, blocks):
    at = pl.program_id(0)
    each = heads * HEAD_DIM
    length = k_ref.shape[1]

    @pl.when(at == 0)
    def _():
        dk_ref[...] = jnp.zeros_like(dk_ref)
        dv_ref[...] = jnp.zeros_like(dv_ref)

    rows = pl.ds(0, SPAN)
    for block in range(blocks):

        @pl.when(at == block)
        def _():
            @pl.loop(0, heads)
            def _(h):
                back_block(q_ref, k_ref, v_ref, do_ref, dq_ref, dk_ref, dv_ref, h, rows, SPAN, (block + 1) * SPAN, True, False)

    dqkv_ref[rows_at(SPAN), :each] = pack_heads(dq_ref, rows, heads, HEAD_DIM ** (-0.5))

    @pl.when(at == blocks - 1)
    def _():
        @pl.loop(0, length, step=BLOCK)
        def _(start):
            some = pl.ds(pl.multiple_of(start, BLOCK), BLOCK)
            dqkv_ref[some, each:] = jnp.concatenate(
                [pack_heads(dk_ref, some, heads, LN2), pack_heads(dv_ref, some, heads, 1.0)], 1
            )
        gw_ref[...] = tn(dqkv_ref[...], x_ref[...]).astype(bf16)


def tokens_grad_kernel(s_ref, d_ref, a_ref, b_ref, wa_ref, wb_ref, send_ref, keep_ref):
    part = nn(a_ref[...], wa_ref[...]) + nn(b_ref[...], wb_ref[...])
    mine = pl.program_id(0) == s_ref[CORE_AT]

    @pl.when(mine)
    def _():
        keep_ref[...] = d_ref[...] + part

    @pl.when(jnp.logical_not(mine))
    def _():
        send_ref[...] = part.astype(bf16)


def place_kernel(s_ref, *refs, shift):
    pieces, out_ref, mark_ref = refs[:-2], refs[-2], refs[-1]
    half = out_ref.shape[0]
    row, core, at = s_ref[ROW], s_ref[CORE_AT], pl.program_id(0)
    mark_ref[...] = jnp.zeros_like(mark_ref)
    if shift:
        sources = [
            (pieces[0].at[:half, :], 2 * row), (pieces[0].at[half:, :], 2 * row + 1),
            (pieces[1], 2 * (1 - row) + core), (pieces[2], 2 * (1 - row) + 1 - core),
        ]
    else:
        sources = [
            (pieces[0].at[:half, :], 2 * row + core), (pieces[1].at[:half, :], 2 * row + 1 - core),
            (pieces[0].at[half:, :], 2 * (1 - row) + core), (pieces[1].at[half:, :], 2 * (1 - row) + 1 - core),
        ]
    for ref, place in sources:

        @pl.when(at == place)
        def _():
            out_ref[...] = ref[...]


def step_kernel(s_ref, *refs, plans):
    scratch = refs[-1]
    inputs = sum(plan[1] for plan in plans)
    ins, outs = list(refs[:inputs]), list(refs[inputs:-1])
    for kind, count, rows, bit, cuts, parts in plans:
        mine, ins = ins[:count], ins[count:]
        if kind == SUM:
            at = 0
            for a_ref, b_ref in zip(mine[: count // 2], mine[count // 2 :]):
                size = min(a_ref.shape[0], rows - at)
                scratch[at : at + size, :] = (a_ref[:size, :].astype(f32) + b_ref[:size, :].astype(f32)).astype(bf16)
                at += size
            if at < rows:
                scratch[at:rows, :] = jnp.zeros((rows - at, scratch.shape[1]), bf16)
            if bit is None:
                outs.pop(0)[...] = scratch[:rows, :]
            else:
                half, high = rows // 2, s_ref[BIT + bit]
                outs.pop(0)[...] = scratch[pl.ds(pl.multiple_of((1 - high) * half, 16), half), :]
                outs.pop(0)[...] = scratch[pl.ds(pl.multiple_of(high * half, 16), half), :]
        elif kind == LAST:
            outs.pop(0)[...] = mine[0][-rows:, :].astype(f32) + mine[1][-rows:, :].astype(f32)
        elif kind == STACK:
            size, target = mine[0].shape[0], outs.pop(0)
            target[:size, :] = mine[0][...]
            target[size:, :] = mine[1][...]
        else:
            high, size = s_ref[BIT + bit], mine[0].shape[0] // parts
            target = outs.pop(0) if kind == PACK else scratch
            for part in range(parts):
                some, first = slice(part * size, (part + 1) * size), 2 * part * size
                target[pl.ds(pl.multiple_of(first + high * size, 16), size), :] = mine[0][some, :]
                target[pl.ds(pl.multiple_of(first + (1 - high) * size, 16), size), :] = mine[1][some, :]
            for first, size in cuts:
                outs.pop(0)[...] = scratch[first : first + size, :].astype(f32)


class Row:
    def __init__(self, array, length, how=WHOLE):
        self.array, self.length, self.how = array, length, how


class Part:
    def __init__(self, array, how=ROWS, pick=None):
        self.array, self.how, self.pick = array, how, pick


class Pick:
    def __init__(self, array, scalar, parts):
        self.array, self.scalar, self.parts = array, scalar, parts


class Far:
    def __init__(self, array):
        self.array = array


def block_of(shape, how, blocks, pick=None, once=False):
    rank = len(shape)
    if rank == 1:
        return pl.BlockSpec(shape, lambda *a: (0,))
    if isinstance(how, tuple):
        how, pick = how
    if how == WHOLE:
        return pl.BlockSpec(shape, lambda *a: (0,) * rank, pipeline_mode=pl.Buffered(1) if once else None)
    pick = pick or (lambda i: i)
    dim = rank - 1 if how == COLUMNS else rank - 2
    parts = blocks // 2 if how == HALF else blocks
    block = tuple(n // parts if d == dim else n for d, n in enumerate(shape))
    return pl.BlockSpec(block, lambda i, *a: tuple(pick(i) if d == dim else 0 for d in range(rank)))


def row_of(item, blocks):
    width = item.array.shape[1]
    if item.how == WHOLE:
        return pl.BlockSpec((item.length, width), lambda i, s: (s[0], 0))
    if item.how == ROWS:
        return pl.BlockSpec((item.length // blocks, width), lambda i, s: (s[0] * blocks + i, 0))
    if item.how[0] == PART:
        return pl.BlockSpec((item.length // blocks, width), lambda i, s: (s[item.how[1]] * blocks + i, 0))
    return pl.BlockSpec((item.length, width // blocks), lambda i, s: (s[0], i))


class Held:
    def __init__(self, array, how=ROWS):
        self.array, self.how = array, how


def view_of(shape, how, blocks):
    rank = len(shape)
    if how == WHOLE:
        return None
    if how == ROWS:
        size = shape[-2] // blocks

        def rows(ref):
            place = pl.ds(pl.multiple_of(pl.program_id(0) * size, size), size)
            return ref.at[place, :] if rank == 2 else ref.at[:, place, :]

        return rows
    size = shape[-1] // blocks
    return lambda ref: ref.at[:, pl.ds(pl.multiple_of(pl.program_id(0) * size, size), size)]


def call(kernel, blocks, inputs, outputs, scalars=None, scratch=(), micros=5.0, limit=LIMIT, after=(), scale=0.4):
    specs, arrays, views = [], [], []
    here = pl.BlockSpec(memory_space=pltpu.VMEM)
    for item in inputs:
        view = None
        if isinstance(item, Row):
            specs.append(row_of(item, blocks))
            arrays.append(pltpu.with_memory_space_constraint(item.array, pltpu.HBM))
        elif isinstance(item, Part):
            specs.append(block_of(item.array.shape, item.how, blocks, item.pick))
            arrays.append(item.array)
        elif isinstance(item, Pick):
            rows, width = item.array.shape
            specs.append(pl.BlockSpec((rows // item.parts, width), functools.partial(lambda at, i, s: (s[at], 0), item.scalar)))
            arrays.append(pltpu.with_memory_space_constraint(item.array, pltpu.HBM))
        elif isinstance(item, Far):
            specs.append(block_of(item.array.shape, WHOLE, blocks, once=True))
            arrays.append(pltpu.with_memory_space_constraint(item.array, pltpu.HBM))
        elif isinstance(item, Held):
            specs.append(here)
            arrays.append(pltpu.with_memory_space_constraint(item.array, pltpu.VMEM))
            view = view_of(item.array.shape, item.how, blocks)
        else:
            specs.append(block_of(item.shape, WHOLE, blocks, once=True))
            arrays.append(item)
        views.append(view)
    for item in after:
        specs.append(pl.BlockSpec(memory_space=pl.ANY))
        arrays.append(item)
        views.append(SKIP)
    shapes, out_specs = [], []
    for shape, dtype, how in outputs:
        if how[:4] == "held":
            shapes.append(pltpu.VMEM(shape, dtype))
            out_specs.append(here)
            views.append(view_of(shape, how[5:], blocks))
        else:
            far = how[:3] == "hbm"
            shapes.append(pltpu.HBM(shape, dtype) if far else jax.ShapeDtypeStruct(shape, dtype))
            out_specs.append(block_of(shape, how[4:] if far else how, blocks))
            views.append(None)
    lead = 0 if scalars is None else 1

    def viewed(*refs):
        passed = list(refs[:lead])
        for ref, view in zip(refs[lead : lead + len(views)], views):
            if view == SKIP:
                continue
            passed.append(ref if view is None else view(ref))
        return kernel(*passed, *refs[lead + len(views) :])

    settings = dict(
        out_shape=shapes,
        compiler_params=pltpu.CompilerParams(vmem_limit_bytes=limit * MIB, dimension_semantics=(ARBITRARY,)),
        cost_estimate=pl.CostEstimate(flops=int(micros * scale * 1.0e9), bytes_accessed=0, transcendentals=0),
        name=getattr(kernel, "func", kernel).__name__,
    )
    if scalars is None:
        return pl.pallas_call(
            viewed, grid=(blocks,), in_specs=specs, out_specs=out_specs, scratch_shapes=list(scratch), **settings
        )(*arrays)
    grid_spec = pltpu.PrefetchScalarGridSpec(
        num_scalar_prefetch=1, grid=(blocks,), in_specs=specs, out_specs=out_specs, scratch_shapes=list(scratch)
    )
    return pl.pallas_call(viewed, grid_spec=grid_spec, **settings)(scalars, *arrays)


def local(
    size, tokens, memory, cotangent, tgt_len, src_len, self_query, self_key, self_value, self_out,
    cross_query, cross_key, cross_value, cross_out, ffn_up, ffn_down,
    gain_one, shift_one, gain_two, shift_two, gain_three, shift_three,
):
    width = tokens.shape[1]
    length = tokens.shape[0] // 2
    source = memory.shape[0] // 2
    each = self_query.shape[1]
    heads = each // HEAD_DIM
    hidden = ffn_up.shape[1]
    place = lax.axis_index("tp").astype(jnp.int32)
    group = lax.axis_index("dp").astype(jnp.int32)
    scalars = jnp.concatenate(
        [jnp.stack([place // 2]), tgt_len, src_len, jnp.stack([place % 2] + [(group >> b) & 1 for b in range(3)])]
    )
    big, small, third = length // BLOCK, length // SPAN, width // SPAN
    short = size == 8

    def across(value):
        return lax.ppermute(value, "tp", ACROSS)

    def sibling(value):
        return lax.ppermute(value, "tp", CORE)

    def along(value, bit):
        return lax.ppermute(value, "dp", [(i, i ^ (1 << bit)) for i in range(size)])

    def shares(part, blocks):
        per = blocks // 2
        first, second = (lambda i: jnp.minimum(i, per - 1)), (lambda i: jnp.maximum(i - per, 0))
        got = [sibling(p) for p in part]
        return [Part(v, HALF, pick) for v, pick in zip((*part, *got), (first, second) * 2)]

    def part_shapes(blocks):
        per = blocks // 2
        first, second = (lambda i: jnp.minimum(i, per - 1)), (lambda i: jnp.maximum(i - per, 0))
        return [((length // 2, width), bf16, (HALF, pick)) for pick in (first, second)]

    head_rows = ((heads, length, WIDE), bf16, FAR_ROWS)
    head_held = ((heads, length, WIDE), bf16, HELD_ROWS)
    key_held = ((heads, source, WIDE), bf16, HELD_ROWS)
    held = ((length, width), f32, HELD_ROWS)
    held_low = ((length, width), bf16, HELD_ROWS)
    column = ((length, 1), f32, HELD_ROWS)
    att_held = ((length, each), bf16, HELD_ROWS)
    hid = ((length, hidden), bf16, HELD_ROWS)
    sums = ((8, width), f32, WHOLE)
    low = ((length, width), bf16, ROWS)
    square = ((width, hidden), bf16, ROWS)
    half_low = ((length // 2, width), bf16, WHOLE)
    out_shape = ((each, width), bf16, WHOLE)
    qkv = functools.partial(pltpu.VMEM, (heads, length, WIDE))

    w_parts = (self_query.T, self_key.T, self_value.T)
    c_parts = (cross_query.T, cross_key.T, cross_value.T)
    bit = scalars[BIT]
    w_half = lax.dynamic_slice_in_dim(jnp.concatenate(w_parts, 0), bit * (3 * each // 2), 3 * each // 2, 0)
    w_near = across(w_half)
    q_new, k_new, v_new, ck_a, cv_a, w_a, cw_a, o_half, cw_half = call(
        functools.partial(project_own_kernel, heads=heads), big,
        [
            Row(tokens, length, ROWS), Row(memory, source, ROWS), *(Far(v) for v in (*w_parts, *c_parts, self_out, cross_out)),
        ],
        [
            head_held, head_held, head_held, key_held, key_held, ((3 * each, width), bf16, WHOLE),
            ((3 * each, width), bf16, WHOLE), out_shape, ((3 * each // 2, width), bf16, WHOLE),
        ],
        scalars, micros=7, scale=0.4,
    )
    o_near = across(o_half)
    cw_near = across(cw_half)
    w_far = along(w_near, 0)
    quarter = ((hidden // 2, width), bf16, WHOLE)
    q_a, k_a, v_a, att_a, ffn_half = call(
        functools.partial(self_own_kernel, heads=heads), big,
        [Held(q_new), Held(k_new, WHOLE), Held(v_new, WHOLE), Pick(ffn_up, BIT, 2), Pick(ffn_down, BIT + 1, 2)],
        [head_rows, head_rows, head_rows, att_held, ((width, width), bf16, WHOLE)], scalars, micros=6, scale=0.4, after=[w_near],
    )
    ffn_near = across(ffn_half)
    cw_far = along(cw_near, 1)
    o_far = along(o_near, 0)
    w_b, q_b, k_b, v_b, att_b = call(
        functools.partial(self_other_kernel, heads=heads), big, [Row(tokens, length, ROWS), w_near, w_far],
        [((3 * each, width), bf16, WHOLE), head_rows, head_rows, head_rows, att_held], scalars, scratch=[qkv(bf16), qkv(bf16)],
        micros=9, scale=0.4, after=[o_near],
    )
    part0, part1, so_b, co_b = call(
        functools.partial(self_out_kernel, blocks=big), big, [Held(att_a), Held(att_b), self_out, o_near, o_far],
        [*part_shapes(big), out_shape, out_shape], scalars, micros=3, scale=0.4, after=[cw_near],
    )
    h_one, h_one_low, unit_one, scale_one, cq_a, catt_a = call(
        functools.partial(cross_own_kernel, heads=heads, blocks=big), big,
        [Row(tokens, length, ROWS), *shares((part0, part1), big), gain_one, shift_one, c_parts[0], Held(ck_a, WHOLE), Held(cv_a, WHOLE)],
        [held, held_low, held_low, column, head_held, att_held], scalars, micros=10, scale=0.4,
    )
    up_near, down_near = call(
        relay_kernel, 1, [ffn_near], [quarter, quarter], scalars, micros=1, after=[scale_one]
    )
    up_far, down_far = along(up_near, 0), along(down_near, 1)
    cw_b, ck_b, cv_b, cq_b, catt_b = call(
        functools.partial(cross_other_kernel, heads=heads), big,
        [Row(memory, source), Held(h_one_low), cw_near, cw_far],
        [((3 * each, width), bf16, WHOLE), ((heads, source, WIDE), bf16, HELD_WHOLE), ((heads, source, WIDE), bf16, HELD_WHOLE), head_held, att_held],
        scalars, micros=100, scale=1.0, after=[up_near, down_near],
    )
    part0, part1 = call(
        functools.partial(cross_out_kernel, blocks=big), big, [Held(catt_a), Held(catt_b), cross_out, co_b],
        part_shapes(big), micros=2, scale=0.4, after=[up_far, down_far],
    )
    h_two, h_two_low, unit_two, scale_two, act_a, slope_a, term = call(
        functools.partial(ffn_own_kernel, blocks=small), small,
        [Held(h_one), *shares((part0, part1), small), gain_two, shift_two, Held(ffn_up, WHOLE), Held(ffn_down, WHOLE)],
        [held, held_low, held_low, column, hid, hid, held], micros=7, scale=0.4,
    )
    part0, part1, act_b, slope_b, up_b, down_b = call(
        functools.partial(ffn_other_kernel, blocks=small), small,
        [Held(h_two_low), Held(term), up_near, up_far, down_near, down_far],
        [*part_shapes(small), hid, hid, ((width, hidden), bf16, HELD_WHOLE), ((hidden, width), bf16, HELD_WHOLE)], scalars, micros=5, scale=0.4,
    )

    part0, part1, out_row, d_three, e_three, pre_a, pre_b, sums_three = call(
        functools.partial(ffn_back_kernel, blocks=small), small,
        [
            Held(h_two), *shares((part0, part1), small), Row(cotangent, length, ROWS), gain_three, shift_three,
            Held(ffn_up, WHOLE), Held(up_b, WHOLE), Held(ffn_down, WHOLE), Held(down_b, WHOLE), Held(slope_a), Held(slope_b),
        ],
        [*part_shapes(small), ((length, width), bf16, FAR_ROWS), held, held_low, hid, hid, sums], scalars, micros=11,
    )
    part = (part0, part1)
    quarter = ((width // 2, hidden), bf16, WHOLE)

    def ffn_grads(act, pre, after=()):
        return call(
            ffn_grad_kernel, 2,
            [Held(h_two_low, COLUMNS), Held(act, COLUMNS), Held(e_three, WHOLE), Held(pre, WHOLE)],
            [square, quarter, quarter], scalars, micros=4, after=after,
        )

    gu_b, send_b, keep_b = ffn_grads(act_b, pre_b)
    gu_got, got_b = across(gu_b), along(send_b, 0)
    gu_a, send_a, keep_a = ffn_grads(act_a, pre_a, [send_b])
    got_a = along(send_a, 0)
    back_scratch = [
        pltpu.VMEM((heads, BLOCK, WIDE), f32), pltpu.VMEM((heads, source, WIDE), f32), pltpu.VMEM((heads, source, WIDE), f32),
    ]
    dkv_held = ((source, 2 * each), bf16, HELD_WHOLE)
    d_two, e_two, sums_two, do_a, dcq_b, dckv_b = call(
        functools.partial(cross_back_other_kernel, heads=heads, blocks=big), big,
        [
            Held(d_three), *shares(part, big), gain_two, Held(unit_two), Held(scale_two), cross_out, co_b, Held(catt_a), Held(catt_b),
            Held(cq_b), Held(ck_b, WHOLE), Held(cv_b, WHOLE),
        ],
        [held, held_low, sums, head_held, att_held, dkv_held], scalars,
        scratch=[pltpu.VMEM((heads, BLOCK, WIDE), bf16)] + back_scratch, micros=18,
    )

    def cross_grads(att, dq, dkv, after=()):
        return call(
            cross_grad_kernel, third,
            [
                Held(h_one_low, COLUMNS), Row(memory, source, COLUMNS), Held(att, WHOLE), Held(e_two, COLUMNS),
                Held(dq, WHOLE), Held(dkv, WHOLE),
            ],
            [((4 * each, width), bf16, COLUMNS)], scalars, micros=5, after=after,
        )[0]

    def step(plans, after=(), micros=2):
        inputs, outputs, kernel_plans, counts, most = [], [], [], [], 16
        for kind, arrays, rows, bit, cuts, parts in plans:
            inputs += arrays
            if kind == SUM:
                made = [((rows, width), bf16, WHOLE)] if bit is None else [((rows // 2, width), bf16, WHOLE)] * 2
            elif kind == LAST:
                made = [((rows, width), f32, WHOLE)]
            elif kind in (PACK, STACK):
                made = [((rows, width), bf16, WHOLE)]
            else:
                made = [((size, width), f32, FAR_WHOLE) for _, size in cuts]
            if kind not in (PACK, STACK, LAST):
                most = max(most, rows)
            outputs += made
            counts.append(len(made))
            kernel_plans.append((kind, len(arrays), rows, bit, cuts, parts))
        made = list(
            call(
                functools.partial(step_kernel, plans=kernel_plans), 1, inputs, outputs, scalars,
                scratch=[pltpu.VMEM((most, width), bf16)], micros=micros, after=after,
            )
        )
        return [made[sum(counts[:n]) : sum(counts[: n + 1])] for n in range(len(counts))]

    class Chain:
        def __init__(self, mine, got, rows, cuts, bits=(0, 1, 2), back=(2, 1, 0), parts=1):
            self.arrays, self.rows, self.cuts, self.stage = [*mine, *got], rows, cuts, 0
            self.bits, self.back, self.parts = bits, back, parts

        def plan(self):
            count = len(self.bits)
            if self.stage <= count:
                bit = self.bits[self.stage] if self.stage < count else None
                return (SUM, self.arrays, self.rows >> self.stage, bit, (), 1)
            at = self.stage - count
            rows, last = self.rows >> count << at, at == len(self.back)
            return (WIDEN if last else PACK, self.arrays, rows, self.back[at - 1], self.cuts if last else (), self.parts if last else 1)

        def take(self, made):
            stage, count, self.stage = self.stage, len(self.bits), self.stage + 1
            if stage < count:
                self.arrays = [made[1], along(made[0], self.bits[stage])]
            elif stage < count + len(self.back):
                self.arrays = [made[0], along(made[0], self.back[stage - count])]
            else:
                self.done = made

    def advance(chains, plans=(), after=(), micros=2):
        made = step([c.plan() for c in chains] + list(plans), after, micros)
        for chain, one in zip(chains, made):
            chain.take(one)
        return [made[0][-1]], [m[0] for m in made[len(chains) :]]

    def plain(arrays, rows):
        return (SUM, arrays, rows, None, (), 1)

    def last(mine, got):
        return (LAST, [mine, got], 16, None, (), 1)

    pin = []
    if short:
        (send_u, keep_u), (down_a,), (down_b,) = step(
            [
                (SUM, [gu_a, gu_got], width, 0, (), 1), plain([keep_a, got_a], width // 2), plain([keep_b, got_b], width // 2),
            ],
            [dcq_b],
        )
        got_u, got_d = along(send_u, 0), across(down_b)
        pin = [keep_u]
    gc_b = cross_grads(catt_b, dcq_b, dckv_b, pin)
    part0, part1, dcq_a, dckv_a = call(
        functools.partial(cross_back_own_kernel, heads=heads, blocks=big), big,
        [Held(cq_a), Held(ck_a, WHOLE), Held(cv_a, WHOLE), Held(do_a), Held(dcq_b), c_parts[0], cw_b],
        [*part_shapes(big), att_held, dkv_held], scalars, scratch=back_scratch, micros=16, after=[gc_b],
    )
    part = (part0, part1)

    gc_got = across(gc_b)
    if short:
        ffn = Chain([keep_u, down_a], [got_u, got_d], width, [(0, width), (width, width)], (1, 2), (2, 1, 0), 2)
        pin, _ = advance([ffn], after=[dcq_a])
    memory_send, memory_keep, out_half = call(
        memory_grad_kernel, 2,
        [Held(dckv_a), Held(dckv_b), cw_a, cw_b, Row(out_row, length // 2, (PART, CORE_AT))],
        [half_low, half_low, ((length // 2, width), bf16, ROWS)], scalars, micros=5, after=pin,
    )
    out_far = across(out_half)
    memory_got = sibling(memory_send)
    gc_a = cross_grads(catt_a, dcq_a, dckv_a, [memory_send])
    memory_plan = plain([memory_keep, memory_got], length // 2)
    pin = [gc_a]
    rest_shape = ((each + 16, width), bf16, WHOLE)
    d_one, do_a, do_b, rest_a, rest_b = call(
        functools.partial(norm_one_back_kernel, heads=heads, blocks=small), small,
        [
            Held(d_two), *shares(part, small), gain_one, Held(unit_one), Held(scale_one), self_out, so_b,
            Held(att_a, WHOLE), Held(att_b, WHOLE), sums_two, sums_three,
        ],
        [held, head_held, head_held, rest_shape, rest_shape], scalars,
        scratch=[pltpu.VMEM((length, width), bf16), pltpu.VMEM((8, width), f32)], micros=6, after=pin,
    )
    rest_got = across(rest_b)
    kept_w = ((3 * each, width), bf16, WHOLE)
    qkv_held = ((length, 3 * each), bf16, HELD_WHOLE)
    self_scratch = [
        pltpu.VMEM((heads, SPAN, WIDE), f32), pltpu.VMEM((heads, length, WIDE), f32), pltpu.VMEM((heads, length, WIDE), f32),
    ]

    def self_back(q, k, v, do, after=()):
        return call(
            functools.partial(self_back_kernel, heads=heads, blocks=small), small,
            [Row(tokens, length), Part(q), k, v, Held(do)], [qkv_held, kept_w], scalars, scratch=self_scratch, micros=14, after=after,
        )

    pin = []
    if short:
        cross = Chain([gc_a], [gc_got], 4 * each, [(n * each, each) for n in range(4)])
        pin, _ = advance([ffn, cross], after=[do_b])
    dqkv_b, gw_b = self_back(q_b, k_b, v_b, do_b, pin)
    gw_got = across(gw_b)

    pin = []
    if short:
        pin, (norms,) = advance([ffn, cross], [last(rest_a, rest_got)], [dqkv_b])
        norms = last(norms, along(norms, 0))
    dqkv_a, gw_a = self_back(q_a, k_a, v_a, do_a, pin)
    pin = []
    if short:
        own = Chain([gw_a, rest_a], [gw_got, rest_got], 4 * each, [(n * each, each) for n in range(4)])
        pin, (memory_mine, norms) = advance([own, ffn, cross], [memory_plan, norms])
        norms = last(norms, along(norms, 1))
    else:
        ((memory_mine,),) = step([memory_plan], [gw_a])
    memory_far = across(memory_mine)
    tokens_send, tokens_keep = call(
        tokens_grad_kernel, 2, [Held(d_one), Held(dqkv_a), Held(dqkv_b), w_a, w_b],
        [half_low, ((length // 2, width), f32, WHOLE)], scalars, micros=6, after=pin,
    )
    def placed(pieces, shift, after=()):
        return call(
            functools.partial(place_kernel, shift=shift), 4, pieces,
            [((2 * length, width), bf16, FAR_ROWS), ((8, WIDE), f32, WHOLE)], scalars, micros=4, after=after,
        )

    def pair(mine, far):
        return (STACK, [mine, far], length, None, (), 1)

    if short:
        out_sibling = sibling(out_far)
        pin, _ = advance([own, ffn, cross], (), [tokens_send, out_sibling])
        tokens_plan = plain([tokens_keep, sibling(tokens_send)], length // 2)
        pin, _ = advance([own, cross], (), pin)
        layer_out, mark = placed([out_row, out_far, out_sibling], True, pin)
        pin, (tokens_mine, memory_pair) = advance([own, ffn, cross], [tokens_plan, pair(memory_mine, memory_far)], [mark], 3)
        tokens_far, memory_sibling = across(tokens_mine), sibling(memory_pair)
        pin, (norms,) = advance([own], [norms], [*pin, memory_sibling])
        norms = last(norms, along(norms, 2))
        memory_grad, mark = placed([memory_pair, memory_sibling], False, pin)
        pin, (tokens_pair, norms) = advance([own, cross], [pair(tokens_mine, tokens_far), norms], [mark])
        tokens_grad, mark = placed([tokens_pair, sibling(tokens_pair)], False, pin)
        advance([own], (), [mark])
        (gu_wide, gd_wide), cross, own = ffn.done, cross.done, own.done
        rest = own[3]
    else:
        tokens_plan = plain([tokens_keep, sibling(tokens_send)], length // 2)
        (tokens_mine,), (memory_pair,) = step([tokens_plan, pair(memory_mine, memory_far)])
        ((tokens_pair,),) = step([pair(tokens_mine, across(tokens_mine))])
        layer_out, _ = placed([out_row, out_far, sibling(out_far)], True)
        memory_grad, _ = placed([memory_pair, sibling(memory_pair)], False)
        tokens_grad, _ = placed([tokens_pair, sibling(tokens_pair)], False)

        def total(mine, got):
            return lax.psum((mine.astype(f32) + got.astype(f32)).astype(bf16), "dp").astype(f32)

        high = scalars[BIT] == 1
        down_a, down_b = (
            jnp.where(high, jnp.concatenate([send, keep]), jnp.concatenate([keep, send]))
            for send, keep in ((send_a, keep_a), (send_b, keep_b))
        )
        gu_wide, gd_wide = total(gu_a, gu_got), total(down_a, across(down_b))
        cross = jnp.split(total(gc_a, gc_got), 4)
        own = jnp.split(total(gw_a, gw_got), 3)
        rest = total(rest_a, rest_got)
        rest, norms = rest[:each], rest[each:]
    return (
        layer_out, tokens_grad, memory_grad,
        own[0].T, own[1].T, own[2].T, rest,
        cross[0].T, cross[1].T, cross[2].T, cross[3],
        gu_wide, gd_wide, *(norms[i] for i in range(6)),
    )


def solution(mesh):
    rows, columns, down = P("dp", None), P(None, "tp"), P("tp", None)
    return jax.shard_map(
        functools.partial(local, mesh.shape["dp"]),
        mesh=mesh,
        in_specs=(rows, rows, rows, P("dp"), P("dp"))
        + (columns, columns, columns, down) * 2
        + (columns, down)
        + (P(),) * 6,
        out_specs=(rows, rows, rows) + (columns, columns, columns, down) * 2 + (columns, down) + (P(),) * 6,
        check_vma=False,
    )
```

```python
import functools

import jax
import jax.numpy as jnp
from jax import lax
from jax.experimental import pallas as pl
from jax.experimental.pallas import tpu as pltpu
from jax.sharding import PartitionSpec as P

HEAD_DIM = 64
WIDE = 2 * HEAD_DIM
EPS = 1e-05
MASKED = -1e30
LOG2E = 1.4426950408889634
LN2 = 0.6931471805599453
f32 = jnp.float32
bf16 = jnp.bfloat16

CORE = [(0, 1), (1, 0), (2, 3), (3, 2)]
ACROSS = [(0, 2), (2, 0), (1, 3), (3, 1)]
MIB = 1 << 20
LIMIT = 16

ROWS, WHOLE, COLUMNS, HALF, PART, SKIP, ARBITRARY = "rows", "whole", "columns", "half", "part", "skip", "arbitrary"
HELD_ROWS, HELD_WHOLE, FAR_ROWS, FAR_WHOLE = "held rows", "held whole", "hbm rows", "hbm whole"
SUM, PACK, WIDEN, STACK, LAST, PASS = "sum", "pack", "wide", "stack", "last", "pass"


def nn(left, right):
    return lax.dot_general(left, right, (((1,), (0,)), ((), ())), preferred_element_type=f32)


def nt(left, right):
    return lax.dot_general(left, right, (((1,), (1,)), ((), ())), preferred_element_type=f32)


def tn(left, right):
    return lax.dot_general(left, right, (((0,), (0,)), ((), ())), preferred_element_type=f32)


def lanes(rows):
    return lax.broadcasted_iota(jnp.int32, (rows, HEAD_DIM), 1)


def three_parts(value):
    high = value.astype(bf16).astype(f32)
    rest = value - high
    middle = rest.astype(bf16).astype(f32)
    return high, middle, rest - middle


def fill_queries(q_ref, rows, count, acc, heads):
    tail = jnp.where(lanes(count) == 0, 1.0, 0.0)
    for h in range(heads):
        part = acc[:, h * HEAD_DIM : (h + 1) * HEAD_DIM]
        q_ref[h, rows, :] = jnp.concatenate([part, tail], 1).astype(bf16)


def fill_keys(k_ref, v_ref, rows, start, count, acc, heads, limit):
    lane = lanes(count)
    index = start + lax.broadcasted_iota(jnp.int32, (count, HEAD_DIM), 0)
    tail = jnp.where(lane == 0, jnp.where(index < limit, 0.0, MASKED), jnp.where(lane < 4, 1.0, 0.0))
    ones = jnp.ones((count, HEAD_DIM), f32)
    for h in range(heads):
        k = acc[:, h * HEAD_DIM : (h + 1) * HEAD_DIM]
        v = acc[:, (heads + h) * HEAD_DIM : (heads + h + 1) * HEAD_DIM]
        k_ref[h, rows, :] = jnp.concatenate([k, tail], 1).astype(bf16)
        v_ref[h, rows, :] = jnp.concatenate([v, ones], 1).astype(bf16)


def attend_block(q_ref, k_ref, v_ref, att_ref, h, rows, count, key_end, causal):
    s = nt(q_ref[h, rows, :], k_ref[h, :key_end, :])
    if causal:
        r = lax.broadcasted_iota(jnp.int32, (count, count), 0)
        c = lax.broadcasted_iota(jnp.int32, (count, count), 1)
        diagonal = jnp.where(c <= r, s[:, key_end - count :], MASKED)
        s = diagonal if key_end == count else jnp.concatenate([s[:, : key_end - count], diagonal], 1)
    peak = jnp.max(s, 1, keepdims=True)
    p = jnp.exp2(s - peak).astype(bf16)
    o = nn(p, v_ref[h, :key_end, :])
    total = o[:, HEAD_DIM : HEAD_DIM + 1]
    mixed = (o / total).astype(bf16)
    att_ref[rows, h * WIDE : (h + 1) * WIDE] = mixed
    high, middle, low = three_parts(-(peak + jnp.log2(total)))
    lane = lanes(count)
    tail = jnp.where(
        lane == 0, 1.0, jnp.where(lane == 1, high, jnp.where(lane == 2, middle, jnp.where(lane == 3, low, 0.0)))
    )
    q_ref[h, rows, HEAD_DIM:] = tail.astype(bf16)


def widen_out(wide_ref, out_ref, heads):
    wide_ref[...] = jnp.zeros_like(wide_ref)
    for h in range(heads):
        wide_ref[h * WIDE : h * WIDE + HEAD_DIM, :] = out_ref[h * HEAD_DIM : (h + 1) * HEAD_DIM, :]


def narrow_out(out_ref, wide, first, heads):
    for h in range(heads):
        out_ref[first + h * HEAD_DIM : first + (h + 1) * HEAD_DIM, :] = wide[h * WIDE : h * WIDE + HEAD_DIM, :]


def fill_grads(do_ref, inner_ref, rows, places, e, wide_ref, att, heads):
    grad = nt(e, wide_ref[...]).astype(bf16)
    ones = jnp.ones((8, WIDE), bf16)
    for h in range(heads):
        part = grad[:, h * WIDE : (h + 1) * WIDE]
        do_ref[h, rows, :] = part
        product = part.astype(f32) * att[:, h * WIDE : (h + 1) * WIDE].astype(f32)
        high = product.astype(bf16)
        inner_ref[h, :, places] = nt(ones, high) + nt(ones, (product - high.astype(f32)).astype(bf16))


def back_block(q_ref, k_ref, v_ref, do_ref, inner_ref, dq_ref, dk_ref, dv_ref, h, rows, places, count, key_end, causal):
    q = q_ref[h, rows, :]
    d = do_ref[h, rows, :]
    k = k_ref[h, :key_end, :]
    v = v_ref[h, :key_end, :]
    p = jnp.exp2(nt(k, q))
    if causal:
        r = lax.broadcasted_iota(jnp.int32, (count, count), 0)
        c = lax.broadcasted_iota(jnp.int32, (count, count), 1)
        diagonal = jnp.where(r <= c, p[key_end - count :], 0.0)
        p = diagonal if key_end == count else jnp.concatenate([p[: key_end - count], diagonal], 0)
    ds = (p * (nt(v, d) - inner_ref[h, 0:1, places])).astype(bf16)
    dv = nn(p.astype(bf16), d)
    dk = nn(ds, q)
    dv_ref[h, :key_end, :] += dv
    dk_ref[h, :key_end, :] += dk
    dq_ref[h, rows, :] = tn(k, ds).T


def pack_heads(source, rows, heads, factor):
    return jnp.concatenate([source[h, rows, :HEAD_DIM] * factor for h in range(heads)], 1).astype(bf16)


def norm(resid):
    center = resid - jnp.mean(resid, -1, keepdims=True)
    scale = lax.rsqrt(jnp.mean(center * center, -1, keepdims=True) + EPS)
    return center * scale, scale


def norm_back(grad, gain, unit, scale):
    lifted = grad * gain
    first = jnp.mean(lifted, -1, keepdims=True)
    second = jnp.mean(lifted * unit, -1, keepdims=True)
    return scale * (lifted - first - unit * second)


def gelu_pair(value):
    scaled = value * 0.7071067811865476
    density = jnp.exp(-scaled * scaled) * 0.3989422804014327
    below = 0.5 * (1.0 + lax.erf(scaled))
    return value * below, below + value * density


BLOCK = 512
SPAN = 256
ROW, TGT, SRC, CORE_AT, BIT = 0, 1, 3, 5, 6
FACTOR = HEAD_DIM ** (-0.5) * LOG2E


def vector(ref):
    return ref[...].reshape(1, ref.shape[0])


def branch_of(shares, blocks):
    own0, own1, got0, got1 = shares
    first = pl.program_id(0) < blocks // 2
    own = jnp.where(first, own0[...], own1[...]).astype(f32)
    return own + jnp.where(first, got0[...], got1[...]).astype(f32)


def put_part(first_ref, second_ref, value, blocks):
    at = pl.program_id(0)

    @pl.when(at < blocks // 2)
    def _():
        first_ref[...] = value

    @pl.when(at >= blocks // 2)
    def _():
        second_ref[...] = value


def rows_at(size):
    return pl.ds(pl.multiple_of(pl.program_id(0) * size, size), size)


def project_own_kernel(
    s_ref, x_ref, m_ref, sq_ref, sk_ref, sv_ref, cq_ref, ck_ref, cv_ref, so_ref, co_ref,
    q_ref, k_ref, v_ref, k_out_ref, v_out_ref, mk_ref, mv_ref, wa_ref, cwa_ref, half_out_ref, half_cw_ref, *, heads,
):
    each = heads * HEAD_DIM
    at = pl.program_id(0)

    @pl.when(at == 0)
    def _():
        for n, ref in enumerate((sq_ref, sk_ref, sv_ref)):
            wa_ref[n * each : (n + 1) * each, :] = ref[...]
        for n, ref in enumerate((cq_ref, ck_ref, cv_ref)):
            cwa_ref[n * each : (n + 1) * each, :] = ref[...]
        half_out_ref[...] = jnp.where(s_ref[BIT] == 0, so_ref[...], co_ref[...])
        half = half_cw_ref.shape[0]
        half_cw_ref[...] = cwa_ref[pl.ds(pl.multiple_of(s_ref[BIT + 1] * half, 16), half), :]

    limit = s_ref[TGT + s_ref[ROW]]
    memory_limit = s_ref[SRC + s_ref[ROW]]
    rows = pl.ds(0, BLOCK)
    acc = nt(x_ref[...], wa_ref[...])
    fill_queries(q_ref, rows, BLOCK, acc[:, :each] * FACTOR, heads)
    fill_keys(k_ref, v_ref, rows, at * BLOCK, BLOCK, acc[:, each:], heads, limit)
    k_out_ref[...] = k_ref[...]
    v_out_ref[...] = v_ref[...]
    acc = nt(m_ref[...], cwa_ref[each:, :])
    fill_keys(mk_ref, mv_ref, rows, at * BLOCK, BLOCK, acc, heads, memory_limit)


def causal_blocks(q_ref, k_ref, v_ref, att_ref, heads):
    at = pl.program_id(0)
    for block in range(k_ref.shape[1] // BLOCK):

        @pl.when(at == block)
        def _():
            for h in range(heads):
                attend_block(q_ref, k_ref, v_ref, att_ref, h, pl.ds(0, BLOCK), BLOCK, (block + 1) * BLOCK, True)


def self_own_kernel(s_ref, q_in_ref, k_ref, v_ref, up_ref, down_ref, q_ref, att_ref, halves_ref, mark_ref, *, heads):
    half = up_ref.shape[0]
    halves_ref[:half, :] = up_ref[...]
    halves_ref[half:, :] = down_ref[...]
    mark_ref[...] = jnp.zeros_like(mark_ref)
    q_ref[...] = q_in_ref[...]
    causal_blocks(q_ref, k_ref, v_ref, att_ref, heads)


def self_other_kernel(s_ref, x_ref, near_ref, far_ref, w_ref, q_ref, k_out_ref, v_out_ref, att_ref, k_ref, v_ref, *, heads):
    each = heads * HEAD_DIM
    at = pl.program_id(0)

    @pl.when(at == 0)
    def _():
        put_halves(w_ref, near_ref, far_ref, s_ref[BIT])

    acc = nt(x_ref[...], w_ref[...])
    fill_queries(q_ref, pl.ds(0, BLOCK), BLOCK, acc[:, :each] * FACTOR, heads)
    fill_keys(k_ref, v_ref, rows_at(BLOCK), at * BLOCK, BLOCK, acc[:, each:], heads, s_ref[TGT + s_ref[ROW]])
    k_out_ref[...] = k_ref[:, rows_at(BLOCK), :]
    v_out_ref[...] = v_ref[:, rows_at(BLOCK), :]
    causal_blocks(q_ref, k_ref, v_ref, att_ref, heads)


def self_out_kernel(
    s_ref, atta_ref, attb_ref, soa_ref, near_ref, far_ref, part0_ref, part1_ref, sob_ref, cob_ref, wide_ref, *, heads, blocks
):
    @pl.when(pl.program_id(0) == 0)
    def _():
        low = s_ref[BIT] == 0
        sob_ref[...] = jnp.where(low, near_ref[...], far_ref[...])
        cob_ref[...] = jnp.where(low, far_ref[...], near_ref[...])
        widen_out(wide_ref.at[0], soa_ref, heads)
        widen_out(wide_ref.at[1], sob_ref, heads)

    part = nn(atta_ref[...], wide_ref[0]) + nn(attb_ref[...], wide_ref[1])
    put_part(part0_ref, part1_ref, part.astype(bf16), blocks)


def cross_blocks(q_ref, k_ref, v_ref, att_ref, heads, limit):
    step = 256
    live = (limit + step - 1) // step
    for count in range(1, k_ref.shape[1] // step + 1):

        @pl.when(live == count)
        def _():
            for h in range(heads):
                attend_block(q_ref, k_ref, v_ref, att_ref, h, pl.ds(0, BLOCK), BLOCK, count * step, False)


def cross_own_kernel(
    s_ref, x_ref, own0, own1, got0, got1, gain_ref, shift_ref, cq_ref, k_ref, v_ref,
    h_ref, hl_ref, unit_ref, scale_ref, q_ref, att_ref, *, heads, blocks,
):
    unit, scale = norm(x_ref[...].astype(f32) + branch_of((own0, own1, got0, got1), blocks))
    h = unit * vector(gain_ref) + vector(shift_ref)
    h_ref[...] = h
    unit_ref[...] = unit.astype(bf16)
    scale_ref[...] = scale
    low = h.astype(bf16)
    hl_ref[...] = low
    fill_queries(q_ref, pl.ds(0, BLOCK), BLOCK, nt(low, cq_ref[...]) * FACTOR, heads)
    cross_blocks(q_ref, k_ref, v_ref, att_ref, heads, s_ref[SRC + s_ref[ROW]])


def put_halves(target_ref, near_ref, far_ref, high):
    half = near_ref.shape[0]
    target_ref[pl.ds(pl.multiple_of(high * half, 16), half), :] = near_ref[...]
    target_ref[pl.ds(pl.multiple_of((1 - high) * half, 16), half), :] = far_ref[...]


def cross_other_kernel(s_ref, m_ref, hl_ref, near_ref, far_ref, cwb_ref, k_ref, v_ref, q_ref, att_ref, *, heads):
    each = heads * HEAD_DIM
    limit = s_ref[SRC + s_ref[ROW]]

    @pl.when(pl.program_id(0) == 0)
    def _():
        put_halves(cwb_ref, near_ref, far_ref, s_ref[BIT + 1])

        @pl.loop(0, m_ref.shape[0], step=BLOCK)
        def _(start):
            rows = pl.ds(pl.multiple_of(start, BLOCK), BLOCK)
            fill_keys(k_ref, v_ref, rows, start, BLOCK, nt(m_ref[rows, :], cwb_ref[each:, :]), heads, limit)

    fill_queries(q_ref, pl.ds(0, BLOCK), BLOCK, nt(hl_ref[...], cwb_ref[:each, :]) * FACTOR, heads)
    cross_blocks(q_ref, k_ref, v_ref, att_ref, heads, limit)


def cross_out_kernel(atta_ref, attb_ref, coa_ref, cob_ref, part0_ref, part1_ref, wide_ref, *, heads, blocks):
    @pl.when(pl.program_id(0) == 0)
    def _():
        widen_out(wide_ref.at[0], coa_ref, heads)
        widen_out(wide_ref.at[1], cob_ref, heads)

    part = nn(atta_ref[...], wide_ref[0]) + nn(attb_ref[...], wide_ref[1])
    put_part(part0_ref, part1_ref, part.astype(bf16), blocks)


def ffn_own_kernel(
    h_in_ref, own0, own1, got0, got1, gain_ref, shift_ref, up_ref, down_ref,
    h_ref, hl_ref, unit_ref, scale_ref, act_ref, slope_ref, term_ref, *, blocks,
):
    unit, scale = norm(h_in_ref[...] + branch_of((own0, own1, got0, got1), blocks))
    h = unit * vector(gain_ref) + vector(shift_ref)
    h_ref[...] = h
    unit_ref[...] = unit.astype(bf16)
    scale_ref[...] = scale
    low = h.astype(bf16)
    hl_ref[...] = low
    act, slope = gelu_pair(nn(low, up_ref[...]))
    act = act.astype(bf16)
    act_ref[...] = act
    slope_ref[...] = slope.astype(bf16)
    term_ref[...] = nn(act, down_ref[...])


def ffn_other_kernel(
    s_ref, hl_ref, term_ref, up_near_ref, up_far_ref, down_near_ref, down_far_ref,
    part0_ref, part1_ref, act_ref, slope_ref, up_ref, down_ref, *, blocks,
):
    @pl.when(pl.program_id(0) == 0)
    def _():
        put_halves(up_ref, up_near_ref, up_far_ref, s_ref[BIT])
        put_halves(down_ref, down_near_ref, down_far_ref, s_ref[BIT + 1])

    act, slope = gelu_pair(nn(hl_ref[...], up_ref[...]))
    act = act.astype(bf16)
    act_ref[...] = act
    slope_ref[...] = slope.astype(bf16)
    put_part(part0_ref, part1_ref, (term_ref[...] + nn(act, down_ref[...])).astype(bf16), blocks)


def ffn_back_kernel(
    s_ref, h_ref, own0, own1, got0, got1, cot_ref, gain_ref, shift_ref, upa_ref, upb_ref, downa_ref, downb_ref, slopea_ref, slopeb_ref,
    part0_ref, part1_ref, out_ref, d_ref, e_ref, prea_ref, preb_ref, sums_ref, *, blocks,
):
    limit = s_ref[TGT + s_ref[ROW]]
    at = pl.program_id(0)

    @pl.when(at == 0)
    def _():
        sums_ref[...] = jnp.zeros_like(sums_ref)

    gain = vector(gain_ref)
    unit, scale = norm(h_ref[...] + branch_of((own0, own1, got0, got1), blocks))
    out_ref[...] = (unit * gain + vector(shift_ref)).astype(bf16)
    index = at * SPAN + lax.broadcasted_iota(jnp.int32, (SPAN, 1), 0)
    grad = jnp.where(index < limit, cot_ref[...].astype(f32), 0.0)
    sums_ref[0:1, :] += jnp.sum(grad * unit, 0, keepdims=True)
    sums_ref[1:2, :] += jnp.sum(grad, 0, keepdims=True)
    d = norm_back(grad, gain, unit, scale)
    d_ref[...] = d
    e = d.astype(bf16)
    e_ref[...] = e
    part = None
    for up_ref, down_ref, slope_ref, pre_ref in (
        (upa_ref, downa_ref, slopea_ref, prea_ref),
        (upb_ref, downb_ref, slopeb_ref, preb_ref),
    ):
        pre = (nt(e, down_ref[...]) * slope_ref[...].astype(f32)).astype(bf16)
        pre_ref[...] = pre
        term = nt(pre, up_ref[...])
        part = term if part is None else part + term
    put_part(part0_ref, part1_ref, part.astype(bf16), blocks)


def ffn_grad_kernel(s_ref, h_ref, act_ref, e_ref, pre_ref, up_ref, send_ref, keep_ref):
    up_ref[...] = tn(h_ref[...], pre_ref[...]).astype(bf16)
    down = tn(act_ref[...], e_ref[...]).astype(bf16)
    mine = pl.program_id(0) == s_ref[BIT]

    @pl.when(mine)
    def _():
        keep_ref[...] = down

    @pl.when(jnp.logical_not(mine))
    def _():
        send_ref[...] = down


def norm_step(d_in_ref, shares, gain, unit_ref, scale_ref, d_ref, e_ref, sums_ref, blocks):
    @pl.when(pl.program_id(0) == 0)
    def _():
        sums_ref[...] = jnp.zeros_like(sums_ref)

    grad = d_in_ref[...] + branch_of(shares, blocks)
    unit = unit_ref[...].astype(f32)
    sums_ref[0:1, :] += jnp.sum(grad * unit, 0, keepdims=True)
    sums_ref[1:2, :] += jnp.sum(grad, 0, keepdims=True)
    d = norm_back(grad, gain, unit, scale_ref[...])
    d_ref[...] = d
    e = d.astype(bf16)
    e_ref[...] = e
    return e


def cross_back_heads(s_ref, q_ref, k_ref, v_ref, do_ref, inner_ref, dqo_ref, dkv_ref, dq_ref, dk_ref, dv_ref, heads, blocks):
    at = pl.program_id(0)
    source = k_ref.shape[1]

    @pl.when(at == 0)
    def _():
        dk_ref[...] = jnp.zeros_like(dk_ref)
        dv_ref[...] = jnp.zeros_like(dv_ref)

    step = 256
    live = (s_ref[SRC + s_ref[ROW]] + step - 1) // step
    rows = pl.ds(0, BLOCK)
    for count in range(1, source // step + 1):

        @pl.when(live == count)
        def _():
            @pl.loop(0, heads)
            def _(h):
                back_block(
                    q_ref, k_ref, v_ref, do_ref, inner_ref, dq_ref, dk_ref, dv_ref, h, rows, rows_at(BLOCK), BLOCK, count * step, False
                )

    dqo_ref[...] = pack_heads(dq_ref, rows, heads, HEAD_DIM ** (-0.5))

    @pl.when(at == blocks - 1)
    def _():
        @pl.loop(0, source, step=BLOCK)
        def _(start):
            some = pl.ds(pl.multiple_of(start, BLOCK), BLOCK)
            dkv_ref[some, :] = jnp.concatenate(
                [pack_heads(dk_ref, some, heads, LN2), pack_heads(dv_ref, some, heads, 1.0)], 1
            )


def cross_back_other_kernel(
    s_ref, d_in_ref, own0, own1, got0, got1, gain_ref, unit_ref, scale_ref, coa_ref, cob_ref, atta_ref, attb_ref,
    q_ref, k_ref, v_ref,
    d_ref, e_ref, sums_ref, doa_ref, innera_ref, dqo_ref, dkv_ref, wide_ref, do_ref, inner_ref, dq_ref, dk_ref, dv_ref, *, heads, blocks,
):
    @pl.when(pl.program_id(0) == 0)
    def _():
        widen_out(wide_ref.at[0], coa_ref, heads)
        widen_out(wide_ref.at[1], cob_ref, heads)

    e = norm_step(
        d_in_ref, (own0, own1, got0, got1), vector(gain_ref), unit_ref, scale_ref, d_ref, e_ref, sums_ref, blocks
    )
    rows, places = pl.ds(0, BLOCK), rows_at(BLOCK)
    fill_grads(doa_ref, innera_ref, rows, places, e, wide_ref.at[0], atta_ref[...], heads)
    fill_grads(do_ref, inner_ref, rows, places, e, wide_ref.at[1], attb_ref[...], heads)
    cross_back_heads(s_ref, q_ref, k_ref, v_ref, do_ref, inner_ref, dqo_ref, dkv_ref, dq_ref, dk_ref, dv_ref, heads, blocks)


def cross_back_own_kernel(
    s_ref, q_ref, k_ref, v_ref, do_ref, inner_ref, dqb_ref, cqa_ref, cwb_ref,
    part0_ref, part1_ref, dqo_ref, dkv_ref, dq_ref, dk_ref, dv_ref, *, heads, blocks,
):
    cross_back_heads(s_ref, q_ref, k_ref, v_ref, do_ref, inner_ref, dqo_ref, dkv_ref, dq_ref, dk_ref, dv_ref, heads, blocks)
    part = nn(dqo_ref[...], cqa_ref[...]) + nn(dqb_ref[...], cwb_ref[: heads * HEAD_DIM, :])
    put_part(part0_ref, part1_ref, part.astype(bf16), blocks)


def cross_grad_kernel(s_ref, h_ref, m_ref, att_ref, e_ref, dq_ref, dkv_ref, g_ref):
    each = dq_ref.shape[1]
    g_ref[:each, :] = tn(dq_ref[...], h_ref[...]).astype(bf16)
    g_ref[each : 3 * each, :] = tn(dkv_ref[...], m_ref[...]).astype(bf16)
    narrow_out(g_ref, tn(att_ref[...], e_ref[...]).astype(bf16), 3 * each, each // HEAD_DIM)


def pass_kernel(s_ref, in_ref, out_ref):
    out_ref[...] = in_ref[...]


def relay_kernel(s_ref, in_ref, first_ref, second_ref):
    half = first_ref.shape[0]
    first_ref[...] = in_ref[:half, :]
    second_ref[...] = in_ref[half:, :]


def memory_grad_kernel(s_ref, a_ref, b_ref, wa_ref, wb_ref, send_ref, keep_ref):
    each = a_ref.shape[1] // 2
    part = (nn(a_ref[...], wa_ref[each:, :]) + nn(b_ref[...], wb_ref[each:, :])).astype(bf16)
    mine = pl.program_id(0) == s_ref[CORE_AT]

    @pl.when(mine)
    def _():
        keep_ref[...] = part

    @pl.when(jnp.logical_not(mine))
    def _():
        send_ref[...] = part


def norm_one_back_kernel(
    s_ref, d_in_ref, own0, own1, got0, got1, gain_ref, unit_ref, scale_ref, soa_ref, sob_ref, atta_ref, attb_ref,
    sums_two_ref, sums_three_ref, d_ref, doa_ref, dob_ref, innera_ref, innerb_ref, ra_ref, rb_ref, e_ref, sums_ref, wide_ref, *, heads, blocks,
):
    @pl.when(pl.program_id(0) == 0)
    def _():
        widen_out(wide_ref.at[0], soa_ref, heads)
        widen_out(wide_ref.at[1], sob_ref, heads)

    each = heads * HEAD_DIM
    rows = rows_at(SPAN)
    e = norm_step(
        d_in_ref, (own0, own1, got0, got1), vector(gain_ref), unit_ref, scale_ref, d_ref, e_ref.at[rows, :], sums_ref, blocks
    )
    fill_grads(doa_ref, innera_ref, pl.ds(0, SPAN), rows, e, wide_ref.at[0], atta_ref[rows, :], heads)
    fill_grads(dob_ref, innerb_ref, pl.ds(0, SPAN), rows, e, wide_ref.at[1], attb_ref[rows, :], heads)

    @pl.when(pl.program_id(0) == blocks - 1)
    def _():
        norms = jnp.concatenate(
            [sums_ref[:2, :], sums_two_ref[:2, :], sums_three_ref[:2, :], jnp.zeros((10, d_in_ref.shape[1]), f32)], 0
        ).astype(bf16)
        for att_ref, r_ref in ((atta_ref, ra_ref), (attb_ref, rb_ref)):
            narrow_out(r_ref, tn(att_ref[...], e_ref[...]).astype(bf16), 0, heads)
            r_ref[each:, :] = norms


def self_back_kernel(s_ref, x_ref, q_ref, k_ref, v_ref, do_ref, inner_ref, dqkv_ref, gw_ref, dq_ref, dk_ref, dv_ref, *, heads, blocks):
    at = pl.program_id(0)
    each = heads * HEAD_DIM
    length = k_ref.shape[1]

    @pl.when(at == 0)
    def _():
        dk_ref[...] = jnp.zeros_like(dk_ref)
        dv_ref[...] = jnp.zeros_like(dv_ref)

    rows = pl.ds(0, SPAN)
    for block in range(blocks):

        @pl.when(at == block)
        def _():
            @pl.loop(0, heads)
            def _(h):
                back_block(
                    q_ref, k_ref, v_ref, do_ref, inner_ref, dq_ref, dk_ref, dv_ref, h, rows, pl.ds(block * SPAN, SPAN), SPAN,
                    (block + 1) * SPAN, True,
                )

    dqkv_ref[rows_at(SPAN), :each] = pack_heads(dq_ref, rows, heads, HEAD_DIM ** (-0.5))

    @pl.when(at == blocks - 1)
    def _():
        @pl.loop(0, length, step=BLOCK)
        def _(start):
            some = pl.ds(pl.multiple_of(start, BLOCK), BLOCK)
            dqkv_ref[some, each:] = jnp.concatenate(
                [pack_heads(dk_ref, some, heads, LN2), pack_heads(dv_ref, some, heads, 1.0)], 1
            )
        gw_ref[...] = tn(dqkv_ref[...], x_ref[...]).astype(bf16)


def tokens_grad_kernel(s_ref, d_ref, a_ref, b_ref, wa_ref, wb_ref, send_ref, keep_ref):
    part = nn(a_ref[...], wa_ref[...]) + nn(b_ref[...], wb_ref[...])
    mine = pl.program_id(0) == s_ref[CORE_AT]

    @pl.when(mine)
    def _():
        keep_ref[...] = d_ref[...] + part

    @pl.when(jnp.logical_not(mine))
    def _():
        send_ref[...] = part.astype(bf16)


def place_kernel(s_ref, *refs, shift):
    pieces, out_ref, mark_ref = refs[:-2], refs[-2], refs[-1]
    half = out_ref.shape[0]
    row, core, at = s_ref[ROW], s_ref[CORE_AT], pl.program_id(0)
    mark_ref[...] = jnp.zeros_like(mark_ref)
    if shift:
        sources = [
            (pieces[0].at[:half, :], 2 * row), (pieces[0].at[half:, :], 2 * row + 1),
            (pieces[1], 2 * (1 - row) + core), (pieces[2], 2 * (1 - row) + 1 - core),
        ]
    else:
        sources = [
            (pieces[0].at[:half, :], 2 * row + core), (pieces[1].at[:half, :], 2 * row + 1 - core),
            (pieces[0].at[half:, :], 2 * (1 - row) + core), (pieces[1].at[half:, :], 2 * (1 - row) + 1 - core),
        ]
    for ref, place in sources:

        @pl.when(at == place)
        def _():
            out_ref[...] = ref[...]


def step_kernel(s_ref, *refs, plans):
    scratch = refs[-1]
    inputs = sum(plan[1] for plan in plans)
    ins, outs = list(refs[:inputs]), list(refs[inputs:-1])
    for kind, count, rows, bit, cuts, parts in plans:
        mine, ins = ins[:count], ins[count:]
        if kind == SUM:
            at = 0
            for a_ref, b_ref in zip(mine[: count // 2], mine[count // 2 :]):
                size = min(a_ref.shape[0], rows - at)
                scratch[at : at + size, :] = (a_ref[:size, :].astype(f32) + b_ref[:size, :].astype(f32)).astype(bf16)
                at += size
            if at < rows:
                scratch[at:rows, :] = jnp.zeros((rows - at, scratch.shape[1]), bf16)
            if bit is None:
                outs.pop(0)[...] = scratch[:rows, :]
            else:
                half, high = rows // 2, s_ref[BIT + bit]
                outs.pop(0)[...] = scratch[pl.ds(pl.multiple_of((1 - high) * half, 16), half), :]
                outs.pop(0)[...] = scratch[pl.ds(pl.multiple_of(high * half, 16), half), :]
        elif kind == LAST:
            outs.pop(0)[...] = mine[0][-rows:, :].astype(f32) + mine[1][-rows:, :].astype(f32)
        elif kind == PASS:
            outs.pop(0)[...] = mine[0][...]
        elif kind == STACK:
            size, target = mine[0].shape[0], outs.pop(0)
            target[:size, :] = mine[0][...]
            target[size:, :] = mine[1][...]
        else:
            high, size = s_ref[BIT + bit], mine[0].shape[0] // parts
            target = outs.pop(0) if kind == PACK else scratch
            for part in range(parts):
                some, first = slice(part * size, (part + 1) * size), 2 * part * size
                target[pl.ds(pl.multiple_of(first + high * size, 16), size), :] = mine[0][some, :]
                target[pl.ds(pl.multiple_of(first + (1 - high) * size, 16), size), :] = mine[1][some, :]
            for first, size in cuts:
                outs.pop(0)[...] = scratch[first : first + size, :].astype(f32)


class Row:
    def __init__(self, array, length, how=WHOLE):
        self.array, self.length, self.how = array, length, how


class Part:
    def __init__(self, array, how=ROWS, pick=None):
        self.array, self.how, self.pick = array, how, pick


class Pick:
    def __init__(self, array, scalar, parts):
        self.array, self.scalar, self.parts = array, scalar, parts


class Far:
    def __init__(self, array):
        self.array = array


def block_of(shape, how, blocks, pick=None, once=False):
    rank = len(shape)
    if rank == 1:
        return pl.BlockSpec(shape, lambda *a: (0,))
    if isinstance(how, tuple):
        how, pick = how
    if how == WHOLE:
        return pl.BlockSpec(shape, lambda *a: (0,) * rank, pipeline_mode=pl.Buffered(1) if once else None)
    pick = pick or (lambda i: i)
    dim = rank - 1 if how == COLUMNS else rank - 2
    parts = blocks // 2 if how == HALF else blocks
    block = tuple(n // parts if d == dim else n for d, n in enumerate(shape))
    return pl.BlockSpec(block, lambda i, *a: tuple(pick(i) if d == dim else 0 for d in range(rank)))


def row_of(item, blocks):
    width = item.array.shape[1]
    if item.how == WHOLE:
        return pl.BlockSpec((item.length, width), lambda i, s: (s[0], 0))
    if item.how == ROWS:
        return pl.BlockSpec((item.length // blocks, width), lambda i, s: (s[0] * blocks + i, 0))
    if item.how[0] == PART:
        return pl.BlockSpec((item.length // blocks, width), lambda i, s: (s[item.how[1]] * blocks + i, 0))
    return pl.BlockSpec((item.length, width // blocks), lambda i, s: (s[0], i))


class Held:
    def __init__(self, array, how=ROWS):
        self.array, self.how = array, how


def view_of(shape, how, blocks):
    rank = len(shape)
    if how == WHOLE:
        return None
    if how == ROWS:
        size = shape[-2] // blocks

        def rows(ref):
            place = pl.ds(pl.multiple_of(pl.program_id(0) * size, size), size)
            return ref.at[place, :] if rank == 2 else ref.at[:, place, :]

        return rows
    size = shape[-1] // blocks
    return lambda ref: ref.at[:, pl.ds(pl.multiple_of(pl.program_id(0) * size, size), size)]


def call(kernel, blocks, inputs, outputs, scalars=None, scratch=(), micros=5.0, limit=LIMIT, after=(), scale=0.4):
    specs, arrays, views = [], [], []
    here = pl.BlockSpec(memory_space=pltpu.VMEM)
    for item in inputs:
        view = None
        if isinstance(item, Row):
            specs.append(row_of(item, blocks))
            arrays.append(pltpu.with_memory_space_constraint(item.array, pltpu.HBM))
        elif isinstance(item, Part):
            specs.append(block_of(item.array.shape, item.how, blocks, item.pick))
            arrays.append(item.array)
        elif isinstance(item, Pick):
            rows, width = item.array.shape
            specs.append(pl.BlockSpec((rows // item.parts, width), functools.partial(lambda at, i, s: (s[at], 0), item.scalar)))
            arrays.append(pltpu.with_memory_space_constraint(item.array, pltpu.HBM))
        elif isinstance(item, Far):
            specs.append(block_of(item.array.shape, WHOLE, blocks, once=True))
            arrays.append(pltpu.with_memory_space_constraint(item.array, pltpu.HBM))
        elif isinstance(item, Held):
            specs.append(here)
            arrays.append(pltpu.with_memory_space_constraint(item.array, pltpu.VMEM))
            view = view_of(item.array.shape, item.how, blocks)
        else:
            specs.append(block_of(item.shape, WHOLE, blocks, once=True))
            arrays.append(item)
        views.append(view)
    for item in after:
        specs.append(pl.BlockSpec(memory_space=pl.ANY))
        arrays.append(pltpu.with_memory_space_constraint(item.array, pltpu.HBM) if isinstance(item, Far) else item)
        views.append(SKIP)
    shapes, out_specs = [], []
    for shape, dtype, how in outputs:
        if how[:4] == "held":
            shapes.append(pltpu.VMEM(shape, dtype))
            out_specs.append(here)
            views.append(view_of(shape, how[5:], blocks))
        else:
            far = how[:3] == "hbm"
            shapes.append(pltpu.HBM(shape, dtype) if far else jax.ShapeDtypeStruct(shape, dtype))
            out_specs.append(block_of(shape, how[4:] if far else how, blocks))
            views.append(None)
    lead = 0 if scalars is None else 1

    def viewed(*refs):
        passed = list(refs[:lead])
        for ref, view in zip(refs[lead : lead + len(views)], views):
            if view == SKIP:
                continue
            passed.append(ref if view is None else view(ref))
        return kernel(*passed, *refs[lead + len(views) :])

    settings = dict(
        out_shape=shapes,
        compiler_params=pltpu.CompilerParams(vmem_limit_bytes=limit * MIB, dimension_semantics=(ARBITRARY,)),
        cost_estimate=pl.CostEstimate(flops=int(micros * scale * 1.0e9), bytes_accessed=0, transcendentals=0),
        name=getattr(kernel, "func", kernel).__name__,
    )
    if scalars is None:
        return pl.pallas_call(
            viewed, grid=(blocks,), in_specs=specs, out_specs=out_specs, scratch_shapes=list(scratch), **settings
        )(*arrays)
    grid_spec = pltpu.PrefetchScalarGridSpec(
        num_scalar_prefetch=1, grid=(blocks,), in_specs=specs, out_specs=out_specs, scratch_shapes=list(scratch)
    )
    return pl.pallas_call(viewed, grid_spec=grid_spec, **settings)(scalars, *arrays)


def local(
    size, tokens, memory, cotangent, tgt_len, src_len, self_query, self_key, self_value, self_out,
    cross_query, cross_key, cross_value, cross_out, ffn_up, ffn_down,
    gain_one, shift_one, gain_two, shift_two, gain_three, shift_three,
):
    width = tokens.shape[1]
    length = tokens.shape[0] // 2
    source = memory.shape[0] // 2
    each = self_query.shape[1]
    heads = each // HEAD_DIM
    hidden = ffn_up.shape[1]
    place = lax.axis_index("tp").astype(jnp.int32)
    group = lax.axis_index("dp").astype(jnp.int32)
    scalars = jnp.concatenate(
        [jnp.stack([place // 2]), tgt_len, src_len, jnp.stack([place % 2] + [(group >> b) & 1 for b in range(3)])]
    )
    big, small, third = length // BLOCK, length // SPAN, width // SPAN
    short = size == 8

    def across(value):
        return lax.ppermute(value, "tp", ACROSS)

    def sibling(value):
        return lax.ppermute(value, "tp", CORE)

    def along(value, bit):
        return lax.ppermute(value, "dp", [(i, i ^ (1 << bit)) for i in range(size)])

    def shares(part, blocks):
        per = blocks // 2
        first, second = (lambda i: jnp.minimum(i, per - 1)), (lambda i: jnp.maximum(i - per, 0))
        got = [sibling(p) for p in part]
        return [Part(v, HALF, pick) for v, pick in zip((*part, *got), (first, second) * 2)]

    def part_shapes(blocks):
        per = blocks // 2
        first, second = (lambda i: jnp.minimum(i, per - 1)), (lambda i: jnp.maximum(i - per, 0))
        return [((length // 2, width), bf16, (HALF, pick)) for pick in (first, second)]

    head_rows = ((heads, length, WIDE), bf16, FAR_ROWS)
    head_held = ((heads, length, WIDE), bf16, HELD_ROWS)
    key_held = ((heads, source, WIDE), bf16, HELD_ROWS)
    held = ((length, width), f32, HELD_ROWS)
    held_low = ((length, width), bf16, HELD_ROWS)
    column = ((length, 1), f32, HELD_ROWS)
    att_held = ((length, heads * WIDE), bf16, HELD_ROWS)
    dq_held = ((length, each), bf16, HELD_ROWS)
    hid = ((length, hidden), bf16, HELD_ROWS)
    sums = ((8, width), f32, WHOLE)
    low = ((length, width), bf16, ROWS)
    square = ((width, hidden), bf16, ROWS)
    half_low = ((length // 2, width), bf16, WHOLE)
    out_shape = ((each, width), bf16, WHOLE)
    qkv = functools.partial(pltpu.VMEM, (heads, length, WIDE))
    wide_out = pltpu.VMEM((2, heads * WIDE, width), bf16)
    inner_held = ((heads, 8, length), f32, HELD_WHOLE)

    w_parts = (self_query.T, self_key.T, self_value.T)
    c_parts = (cross_query.T, cross_key.T, cross_value.T)
    bit = scalars[BIT]
    w_half = lax.dynamic_slice_in_dim(jnp.concatenate(w_parts, 0), bit * (3 * each // 2), 3 * each // 2, 0)
    w_near = across(w_half)
    q_new, k_new, v_new, k_a, v_a, ck_a, cv_a, w_a, cw_a, o_half, cw_half = call(
        functools.partial(project_own_kernel, heads=heads), big,
        [
            Row(tokens, length, ROWS), Row(memory, source, ROWS), *(Far(v) for v in (*w_parts, *c_parts, self_out, cross_out)),
        ],
        [
            head_held, head_held, head_held, head_rows, head_rows, key_held, key_held, ((3 * each, width), bf16, WHOLE),
            ((3 * each, width), bf16, WHOLE), out_shape, ((3 * each // 2, width), bf16, WHOLE),
        ],
        scalars, micros=7, scale=0.4,
    )
    o_near = across(o_half)
    cw_near = across(cw_half)
    (w_near,) = call(
        pass_kernel, 1, [w_near], [((3 * each // 2, width), bf16, WHOLE)], scalars, micros=1, scale=0.4, after=[o_half]
    )
    w_far = along(w_near, 0)
    quarter = ((hidden // 2, width), bf16, WHOLE)
    q_a, att_a, ffn_half, mark = call(
        functools.partial(self_own_kernel, heads=heads), big,
        [Held(q_new), Held(k_new, WHOLE), Held(v_new, WHOLE), Pick(ffn_up, BIT, 2), Pick(ffn_down, BIT + 1, 2)],
        [head_rows, att_held, ((width, width), bf16, WHOLE), ((8, WIDE), f32, WHOLE)], scalars, micros=6, scale=0.4, after=[w_near],
    )
    ffn_near = across(ffn_half)
    cw_far = along(cw_near, 1)
    (o_near,) = call(pass_kernel, 1, [o_near], [out_shape], scalars, micros=1, scale=0.4, after=[mark])
    o_far = along(o_near, 0)
    w_b, q_b, k_b, v_b, att_b = call(
        functools.partial(self_other_kernel, heads=heads), big, [Row(tokens, length, ROWS), w_near, w_far],
        [((3 * each, width), bf16, WHOLE), head_rows, head_rows, head_rows, att_held], scalars, scratch=[qkv(bf16), qkv(bf16)],
        micros=9, scale=0.4,
    )
    part0, part1, so_b, co_b = call(
        functools.partial(self_out_kernel, heads=heads, blocks=big), big, [Held(att_a), Held(att_b), self_out, o_near, o_far],
        [*part_shapes(big), out_shape, out_shape], scalars, scratch=[wide_out], micros=3, scale=0.4, after=[cw_near],
    )
    h_one, h_one_low, unit_one, scale_one, cq_a, catt_a = call(
        functools.partial(cross_own_kernel, heads=heads, blocks=big), big,
        [Row(tokens, length, ROWS), *shares((part0, part1), big), gain_one, shift_one, c_parts[0], Held(ck_a, WHOLE), Held(cv_a, WHOLE)],
        [held, held_low, held_low, column, head_held, att_held], scalars, micros=10, scale=0.4,
    )
    up_near, down_near = call(
        relay_kernel, 1, [ffn_near], [quarter, quarter], scalars, micros=1, after=[scale_one]
    )
    up_far, down_far = along(up_near, 0), along(down_near, 1)
    cw_b, ck_b, cv_b, cq_b, catt_b = call(
        functools.partial(cross_other_kernel, heads=heads), big,
        [Row(memory, source), Held(h_one_low), cw_near, cw_far],
        [((3 * each, width), bf16, WHOLE), ((heads, source, WIDE), bf16, HELD_WHOLE), ((heads, source, WIDE), bf16, HELD_WHOLE), head_held, att_held],
        scalars, micros=100, scale=1.0, after=[up_near, down_near],
    )
    part0, part1 = call(
        functools.partial(cross_out_kernel, heads=heads, blocks=big), big, [Held(catt_a), Held(catt_b), cross_out, co_b],
        part_shapes(big), scratch=[wide_out], micros=2, scale=0.4, after=[up_far, down_far],
    )
    h_two, h_two_low, unit_two, scale_two, act_a, slope_a, term = call(
        functools.partial(ffn_own_kernel, blocks=small), small,
        [Held(h_one), *shares((part0, part1), small), gain_two, shift_two, Held(ffn_up, WHOLE), Held(ffn_down, WHOLE)],
        [held, held_low, held_low, column, hid, hid, held], micros=7, scale=0.4,
    )
    part0, part1, act_b, slope_b, up_b, down_b = call(
        functools.partial(ffn_other_kernel, blocks=small), small,
        [Held(h_two_low), Held(term), up_near, up_far, down_near, down_far],
        [*part_shapes(small), hid, hid, ((width, hidden), bf16, HELD_WHOLE), ((hidden, width), bf16, HELD_WHOLE)], scalars, micros=5, scale=0.4,
    )

    part0, part1, out_row, d_three, e_three, pre_a, pre_b, sums_three = call(
        functools.partial(ffn_back_kernel, blocks=small), small,
        [
            Held(h_two), *shares((part0, part1), small), Row(cotangent, length, ROWS), gain_three, shift_three,
            Held(ffn_up, WHOLE), Held(up_b, WHOLE), Held(ffn_down, WHOLE), Held(down_b, WHOLE), Held(slope_a), Held(slope_b),
        ],
        [*part_shapes(small), ((length, width), bf16, FAR_ROWS), held, held_low, hid, hid, sums], scalars, micros=11,
    )
    part = (part0, part1)
    quarter = ((width // 2, hidden), bf16, WHOLE)

    def ffn_grads(act, pre, after=()):
        return call(
            ffn_grad_kernel, 2,
            [Held(h_two_low, COLUMNS), Held(act, COLUMNS), Held(e_three, WHOLE), Held(pre, WHOLE)],
            [square, quarter, quarter], scalars, micros=4, after=after,
        )

    gu_b, send_b, keep_b = ffn_grads(act_b, pre_b)
    gu_got, got_b = across(gu_b), along(send_b, 0)
    gu_a, send_a, keep_a = ffn_grads(act_a, pre_a, [send_b])
    got_a = along(send_a, 0)
    back_scratch = [
        pltpu.VMEM((heads, BLOCK, WIDE), f32), pltpu.VMEM((heads, source, WIDE), f32), pltpu.VMEM((heads, source, WIDE), f32),
    ]
    dkv_held = ((source, 2 * each), bf16, HELD_WHOLE)
    d_two, e_two, sums_two, do_a, inner_a, dcq_b, dckv_b = call(
        functools.partial(cross_back_other_kernel, heads=heads, blocks=big), big,
        [
            Held(d_three), *shares(part, big), gain_two, Held(unit_two), Held(scale_two), cross_out, co_b, Held(catt_a), Held(catt_b), Held(cq_b), Held(ck_b, WHOLE), Held(cv_b, WHOLE),
        ],
        [held, held_low, sums, head_held, inner_held, dq_held, dkv_held], scalars,
        scratch=[wide_out, pltpu.VMEM((heads, BLOCK, WIDE), bf16), pltpu.VMEM((heads, 8, length), f32)] + back_scratch, micros=18,
    )

    def cross_grads(att, dq, dkv, after=()):
        return call(
            cross_grad_kernel, third,
            [
                Held(h_one_low, COLUMNS), Row(memory, source, COLUMNS), Held(att, WHOLE), Held(e_two, COLUMNS),
                Held(dq, WHOLE), Held(dkv, WHOLE),
            ],
            [((4 * each, width), bf16, COLUMNS)], scalars, micros=5, after=after,
        )[0]

    def step(plans, after=(), micros=2):
        inputs, outputs, kernel_plans, counts, most = [], [], [], [], 16
        for kind, arrays, rows, bit, cuts, parts in plans:
            inputs += arrays
            if kind == SUM:
                made = [((rows, width), bf16, WHOLE)] if bit is None else [((rows // 2, width), bf16, WHOLE)] * 2
            elif kind == LAST:
                made = [((rows, width), f32, WHOLE)]
            elif kind in (PACK, STACK, PASS):
                made = [((rows, width), bit if kind == PASS else bf16, WHOLE)]
            else:
                made = [((size, width), f32, FAR_WHOLE) for _, size in cuts]
            if kind not in (PACK, STACK, LAST, PASS):
                most = max(most, rows)
            outputs += made
            counts.append(len(made))
            kernel_plans.append((kind, len(arrays), rows, bit, cuts, parts))
        made = list(
            call(
                functools.partial(step_kernel, plans=kernel_plans), 1, inputs, outputs, scalars,
                scratch=[pltpu.VMEM((most, width), bf16)], micros=micros, after=after,
            )
        )
        return [made[sum(counts[:n]) : sum(counts[: n + 1])] for n in range(len(counts))]

    class Chain:
        def __init__(self, mine, got, rows, cuts, bits=(0, 1, 2), back=(2, 1, 0), parts=1):
            self.arrays, self.rows, self.cuts, self.stage = [*mine, *got], rows, cuts, 0
            self.bits, self.back, self.parts = bits, back, parts

        def plan(self):
            count = len(self.bits)
            if self.stage <= count:
                bit = self.bits[self.stage] if self.stage < count else None
                return (SUM, self.arrays, self.rows >> self.stage, bit, (), 1)
            at = self.stage - count
            rows, last = self.rows >> count << at, at == len(self.back)
            return (WIDEN if last else PACK, self.arrays, rows, self.back[at - 1], self.cuts if last else (), self.parts if last else 1)

        def take(self, made):
            stage, count, self.stage = self.stage, len(self.bits), self.stage + 1
            if stage < count:
                self.arrays = [made[1], along(made[0], self.bits[stage])]
            elif stage < count + len(self.back):
                self.arrays = [made[0], along(made[0], self.back[stage - count])]
            else:
                self.done = made

    def advance(chains, plans=(), after=(), micros=2):
        made = step([c.plan() for c in chains] + list(plans), after, micros)
        for chain, one in zip(chains, made):
            chain.take(one)
        return [made[0][-1]], [m[0] for m in made[len(chains) :]]

    def plain(arrays, rows):
        return (SUM, arrays, rows, None, (), 1)

    def last(mine, got):
        return (LAST, [mine, got], 16, None, (), 1)

    gc_b = cross_grads(catt_b, dcq_b, dckv_b)
    if short:
        (send_u, keep_u), (down_a,), (down_b,), (gc_b,) = step(
            [
                (SUM, [gu_a, gu_got], width, 0, (), 1), plain([keep_a, got_a], width // 2), plain([keep_b, got_b], width // 2),
                (PASS, [gc_b], 4 * each, bf16, (), 1),
            ],
            [gc_b],
        )
        got_u, got_d = along(send_u, 0), across(down_b)
    part0, part1, dcq_a, dckv_a = call(
        functools.partial(cross_back_own_kernel, heads=heads, blocks=big), big,
        [Held(cq_a), Held(ck_a, WHOLE), Held(cv_a, WHOLE), Held(do_a), Held(inner_a, WHOLE), Held(dcq_b), c_parts[0], cw_b],
        [*part_shapes(big), dq_held, dkv_held], scalars, scratch=back_scratch, micros=16, after=[gc_b],
    )
    part = (part0, part1)

    gc_got = across(gc_b)
    pin = []
    if short:
        ffn = Chain([keep_u, down_a], [got_u, got_d], width, [(0, width), (width, width)], (1, 2), (2, 1, 0), 2)
        pin, _ = advance([ffn], after=[dcq_a])
    memory_send, memory_keep = call(
        memory_grad_kernel, 2, [Held(dckv_a), Held(dckv_b), cw_a, cw_b], [half_low, half_low], scalars, micros=5, after=pin,
    )
    memory_got = sibling(memory_send)
    gc_a = cross_grads(catt_a, dcq_a, dckv_a, [memory_send])
    memory_plan = plain([memory_keep, memory_got], length // 2)
    pin = [gc_a]
    rest_shape = ((each + 16, width), bf16, WHOLE)
    d_one, do_a, do_b, inner_a, inner_b, rest_a, rest_b = call(
        functools.partial(norm_one_back_kernel, heads=heads, blocks=small), small,
        [
            Held(d_two), *shares(part, small), gain_one, Held(unit_one), Held(scale_one), self_out, so_b,
            Held(att_a, WHOLE), Held(att_b, WHOLE), sums_two, sums_three,
        ],
        [held, head_held, head_held, inner_held, inner_held, rest_shape, rest_shape], scalars,
        scratch=[pltpu.VMEM((length, width), bf16), pltpu.VMEM((8, width), f32), wide_out], micros=6, after=pin,
    )
    rest_got = across(rest_b)
    kept_w = ((3 * each, width), bf16, WHOLE)
    qkv_held = ((length, 3 * each), bf16, HELD_WHOLE)
    self_scratch = [
        pltpu.VMEM((heads, SPAN, WIDE), f32), pltpu.VMEM((heads, length, WIDE), f32), pltpu.VMEM((heads, length, WIDE), f32),
    ]

    def self_back(q, k, v, do, inner, after=()):
        return call(
            functools.partial(self_back_kernel, heads=heads, blocks=small), small,
            [Row(tokens, length), Part(q), k, v, Held(do), Held(inner, WHOLE)], [qkv_held, kept_w], scalars, scratch=self_scratch, micros=14, after=after,
        )

    pin = []
    if short:
        cross = Chain([gc_a], [gc_got], 4 * each, [(n * each, each) for n in range(4)])
        pin, _ = advance([ffn, cross], after=[do_b])
    dqkv_b, gw_b = self_back(q_b, k_b, v_b, do_b, inner_b, pin)
    gw_got = across(gw_b)

    pin = []
    if short:
        pin, (norms,) = advance([ffn, cross], [last(rest_a, rest_got)], [dqkv_b])
        norms = last(norms, along(norms, 0))
    dqkv_a, gw_a = self_back(q_a, k_a, v_a, do_a, inner_a, pin)
    pin = []
    if short:
        own = Chain([gw_a, rest_a], [gw_got, rest_got], 4 * each, [(n * each, each) for n in range(4)])
        pin, (memory_mine, norms) = advance([own, ffn, cross], [memory_plan, norms])
    else:
        ((memory_mine,),) = step([memory_plan], [gw_a])
    tokens_send, tokens_keep = call(
        tokens_grad_kernel, 2, [Held(d_one), Held(dqkv_a), Held(dqkv_b), w_a, w_b],
        [half_low, ((length // 2, width), f32, WHOLE)], scalars, micros=6, after=pin,
    )
    (out_half,) = call(
        pass_kernel, 1, [Row(out_row, length // 2, (PART, CORE_AT))], [half_low], scalars, micros=1, after=[tokens_send]
    )
    out_far = across(out_half)

    def placed(pieces, shift, after=()):
        return call(
            functools.partial(place_kernel, shift=shift), 4, pieces,
            [((2 * length, width), bf16, FAR_ROWS), ((8, WIDE), f32, WHOLE)], scalars, micros=4, after=after,
        )

    def passed(value, rows=length // 2, dtype=bf16):
        return (PASS, [value], rows, dtype, (), 1)

    def pair(mine, far):
        return (STACK, [mine, far], length, None, (), 1)

    if short:
        pin, (memory_mine,) = advance([own, ffn, cross], [passed(memory_mine)], [out_half])
        memory_far = across(memory_mine)
        pin, (tokens_send,) = advance([own, cross], [passed(tokens_send)], [*pin, out_far])
        tokens_plan = plain([tokens_keep, sibling(tokens_send)], length // 2)
        pin, (tokens_mine, memory_pair, out_far) = advance(
            [own, cross], [tokens_plan, pair(memory_mine, memory_far), passed(out_far)], [*pin, ffn.arrays[1]]
        )
        tokens_far, memory_sibling, out_sibling = across(tokens_mine), sibling(memory_pair), sibling(out_far)
        ((gu_wide, gd_wide),) = step([ffn.plan()], pin, 4)
        pin, (norms,) = advance([own], [passed(norms, 16, f32)], [Far(gu_wide), memory_sibling, out_sibling])
        norms = last(norms, along(norms, 2))
        memory_grad, mark = placed([memory_pair, memory_sibling], False, pin)
        pin, (tokens_pair, norms) = advance([own], [pair(tokens_mine, tokens_far), norms], [mark, cross.arrays[1]])
        norms = last(norms, along(norms, 1))
        (cross,) = step([cross.plan()], pin, 3)
        layer_out, mark = placed([out_row, out_far, out_sibling], True, [Far(cross[0])])
        tokens_grad, mark = placed([tokens_pair, sibling(tokens_pair)], False, [mark])
        _, (norms,) = advance([own], [norms], [mark])
        own = own.done
        rest = own[3]
    else:
        memory_far = across(memory_mine)
        tokens_plan = plain([tokens_keep, sibling(tokens_send)], length // 2)
        (tokens_mine,), (memory_pair,) = step([tokens_plan, pair(memory_mine, memory_far)])
        ((tokens_pair,),) = step([pair(tokens_mine, across(tokens_mine))])
        layer_out, _ = placed([out_row, out_far, sibling(out_far)], True)
        memory_grad, _ = placed([memory_pair, sibling(memory_pair)], False)
        tokens_grad, _ = placed([tokens_pair, sibling(tokens_pair)], False)

        def total(mine, got):
            return lax.psum((mine.astype(f32) + got.astype(f32)).astype(bf16), "dp").astype(f32)

        high = scalars[BIT] == 1
        down_a, down_b = (
            jnp.where(high, jnp.concatenate([send, keep]), jnp.concatenate([keep, send]))
            for send, keep in ((send_a, keep_a), (send_b, keep_b))
        )
        gu_wide, gd_wide = total(gu_a, gu_got), total(down_a, across(down_b))
        cross = jnp.split(total(gc_a, gc_got), 4)
        own = jnp.split(total(gw_a, gw_got), 3)
        rest = total(rest_a, rest_got)
        rest, norms = rest[:each], rest[each:]
    return (
        layer_out, tokens_grad, memory_grad,
        own[0].T, own[1].T, own[2].T, rest,
        cross[0].T, cross[1].T, cross[2].T, cross[3],
        gu_wide, gd_wide, *(norms[i] for i in range(6)),
    )


def solution(mesh):
    rows, columns, down = P("dp", None), P(None, "tp"), P("tp", None)
    return jax.shard_map(
        functools.partial(local, mesh.shape["dp"]),
        mesh=mesh,
        in_specs=(rows, rows, rows, P("dp"), P("dp"))
        + (columns, columns, columns, down) * 2
        + (columns, down)
        + (P(),) * 6,
        out_specs=(rows, rows, rows) + (columns, columns, columns, down) * 2 + (columns, down) + (P(),) * 6,
        check_vma=False,
    )
```

```python
import functools

import jax
import jax.numpy as jnp
from jax import lax
from jax.experimental import pallas as pl
from jax.experimental.pallas import tpu as pltpu
from jax.sharding import PartitionSpec as P

HEAD_DIM = 64
WIDE = 2 * HEAD_DIM
EPS = 1e-05
MASKED = -1e30
LOG2E = 1.4426950408889634
LN2 = 0.6931471805599453
f32 = jnp.float32
bf16 = jnp.bfloat16

CORE = [(0, 1), (1, 0), (2, 3), (3, 2)]
ACROSS = [(0, 2), (2, 0), (1, 3), (3, 1)]
MIB = 1 << 20
LIMIT = 16

ROWS, WHOLE, COLUMNS, HALF, PART, SKIP, ARBITRARY = "rows", "whole", "columns", "half", "part", "skip", "arbitrary"
HELD_ROWS, HELD_WHOLE, FAR_ROWS, FAR_WHOLE = "held rows", "held whole", "hbm rows", "hbm whole"
SUM, PACK, WIDEN, STACK, LAST, PASS = "sum", "pack", "wide", "stack", "last", "pass"


def nn(left, right):
    return lax.dot_general(left, right, (((1,), (0,)), ((), ())), preferred_element_type=f32)


def nt(left, right):
    return lax.dot_general(left, right, (((1,), (1,)), ((), ())), preferred_element_type=f32)


def tn(left, right):
    return lax.dot_general(left, right, (((0,), (0,)), ((), ())), preferred_element_type=f32)


def lanes(rows):
    return lax.broadcasted_iota(jnp.int32, (rows, HEAD_DIM), 1)


def three_parts(value):
    high = value.astype(bf16).astype(f32)
    rest = value - high
    middle = rest.astype(bf16).astype(f32)
    return high, middle, rest - middle


def fill_queries(q_ref, rows, count, acc, heads):
    tail = jnp.where(lanes(count) == 0, 1.0, 0.0)
    for h in range(heads):
        part = acc[:, h * HEAD_DIM : (h + 1) * HEAD_DIM]
        q_ref[h, rows, :] = jnp.concatenate([part, tail], 1).astype(bf16)


def fill_keys(k_ref, v_ref, rows, start, count, acc, heads, limit):
    lane = lanes(count)
    index = start + lax.broadcasted_iota(jnp.int32, (count, HEAD_DIM), 0)
    tail = jnp.where(lane == 0, jnp.where(index < limit, 0.0, MASKED), jnp.where(lane < 4, 1.0, 0.0))
    ones = jnp.ones((count, HEAD_DIM), f32)
    for h in range(heads):
        k = acc[:, h * HEAD_DIM : (h + 1) * HEAD_DIM]
        v = acc[:, (heads + h) * HEAD_DIM : (heads + h + 1) * HEAD_DIM]
        k_ref[h, rows, :] = jnp.concatenate([k, tail], 1).astype(bf16)
        v_ref[h, rows, :] = jnp.concatenate([v, ones], 1).astype(bf16)


def attend_block(q_ref, k_ref, v_ref, att_ref, h, rows, count, key_end, causal):
    s = nt(q_ref[h, rows, :], k_ref[h, :key_end, :])
    if causal:
        r = lax.broadcasted_iota(jnp.int32, (count, count), 0)
        c = lax.broadcasted_iota(jnp.int32, (count, count), 1)
        diagonal = jnp.where(c <= r, s[:, key_end - count :], MASKED)
        s = diagonal if key_end == count else jnp.concatenate([s[:, : key_end - count], diagonal], 1)
    peak = jnp.max(s, 1, keepdims=True)
    p = jnp.exp2(s - peak).astype(bf16)
    o = nn(p, v_ref[h, :key_end, :])
    total = jnp.broadcast_to(o[:, HEAD_DIM : HEAD_DIM + 1], o.shape)
    att_ref[rows, h * WIDE : (h + 1) * WIDE] = (o / total).astype(bf16)
    high, middle, low = three_parts(-(peak + jnp.log2(total)))
    lane = lax.broadcasted_iota(jnp.int32, o.shape, 1)
    tail = jnp.where(lane == 65, high, jnp.where(lane == 66, middle, jnp.where(lane == 67, low, q_ref[h, rows, :].astype(f32))))
    q_ref[h, rows, :] = tail.astype(bf16)


def widen_out(wide_ref, out_ref, heads):
    wide_ref[...] = jnp.zeros_like(wide_ref)
    for h in range(heads):
        wide_ref[h * WIDE : h * WIDE + HEAD_DIM, :] = out_ref[h * HEAD_DIM : (h + 1) * HEAD_DIM, :]


def narrow_out(out_ref, wide, first, heads):
    for h in range(heads):
        out_ref[first + h * HEAD_DIM : first + (h + 1) * HEAD_DIM, :] = wide[h * WIDE : h * WIDE + HEAD_DIM, :]


def fill_grads(do_ref, inner_ref, rows, places, e, wide_ref, att, heads):
    grad = nt(e, wide_ref[...]).astype(bf16)
    ones = jnp.ones((8, WIDE), bf16)
    for h in range(heads):
        part = grad[:, h * WIDE : (h + 1) * WIDE]
        do_ref[h, rows, :] = part
        product = part.astype(f32) * att[:, h * WIDE : (h + 1) * WIDE].astype(f32)
        high = product.astype(bf16)
        inner_ref[h, :, places] = nt(ones, high) + nt(ones, (product - high.astype(f32)).astype(bf16))


def back_block(q_ref, k_ref, v_ref, do_ref, inner_ref, dq_ref, dk_ref, dv_ref, h, rows, places, count, key_end, causal):
    q = q_ref[h, rows, :]
    d = do_ref[h, rows, :]
    k = k_ref[h, :key_end, :]
    v = v_ref[h, :key_end, :]
    p = jnp.exp2(nt(k, q))
    if causal:
        r = lax.broadcasted_iota(jnp.int32, (count, count), 0)
        c = lax.broadcasted_iota(jnp.int32, (count, count), 1)
        diagonal = jnp.where(r <= c, p[key_end - count :], 0.0)
        p = diagonal if key_end == count else jnp.concatenate([p[: key_end - count], diagonal], 0)
    ds = (p * (nt(v, d) - inner_ref[h, 0:1, places])).astype(bf16)
    dv = nn(p.astype(bf16), d)
    dk = nn(ds, q)
    dv_ref[h, :key_end, :] += dv
    dk_ref[h, :key_end, :] += dk
    dq_ref[h, rows, :] = tn(k, ds).T


def pack_heads(source, rows, heads, factor):
    return jnp.concatenate([source[h, rows, :HEAD_DIM] * factor for h in range(heads)], 1).astype(bf16)


def norm(resid):
    center = resid - jnp.mean(resid, -1, keepdims=True)
    scale = lax.rsqrt(jnp.mean(center * center, -1, keepdims=True) + EPS)
    return center * scale, scale


def norm_back(grad, gain, unit, scale):
    lifted = grad * gain
    first = jnp.mean(lifted, -1, keepdims=True)
    second = jnp.mean(lifted * unit, -1, keepdims=True)
    return scale * (lifted - first - unit * second)


def gelu_pair(value):
    scaled = value * 0.7071067811865476
    density = jnp.exp(-scaled * scaled) * 0.3989422804014327
    below = 0.5 * (1.0 + lax.erf(scaled))
    return value * below, below + value * density


BLOCK = 512
SPAN = 256
ROW, TGT, SRC, CORE_AT, BIT = 0, 1, 3, 5, 6
FACTOR = HEAD_DIM ** (-0.5) * LOG2E


def vector(ref):
    return ref[...].reshape(1, ref.shape[0])


def branch_of(shares, blocks):
    own0, own1, got0, got1 = shares
    first = pl.program_id(0) < blocks // 2
    own = jnp.where(first, own0[...], own1[...]).astype(f32)
    return own + jnp.where(first, got0[...], got1[...]).astype(f32)


def put_part(first_ref, second_ref, value, blocks):
    at = pl.program_id(0)

    @pl.when(at < blocks // 2)
    def _():
        first_ref[...] = value

    @pl.when(at >= blocks // 2)
    def _():
        second_ref[...] = value


def rows_at(size):
    return pl.ds(pl.multiple_of(pl.program_id(0) * size, size), size)


def project_own_kernel(
    s_ref, x_ref, m_ref, sq_ref, sk_ref, sv_ref, cq_ref, ck_ref, cv_ref, so_ref, co_ref,
    q_ref, k_ref, v_ref, k_out_ref, v_out_ref, mk_ref, mv_ref, wa_ref, cwa_ref, half_out_ref, half_cw_ref, *, heads,
):
    each = heads * HEAD_DIM
    at = pl.program_id(0)

    @pl.when(at == 0)
    def _():
        for n, ref in enumerate((sq_ref, sk_ref, sv_ref)):
            wa_ref[n * each : (n + 1) * each, :] = ref[...]
        for n, ref in enumerate((cq_ref, ck_ref, cv_ref)):
            cwa_ref[n * each : (n + 1) * each, :] = ref[...]
        half_out_ref[...] = jnp.where(s_ref[BIT] == 0, so_ref[...], co_ref[...])
        half = half_cw_ref.shape[0]
        half_cw_ref[...] = cwa_ref[pl.ds(pl.multiple_of(s_ref[BIT + 1] * half, 16), half), :]

    limit = s_ref[TGT + s_ref[ROW]]
    memory_limit = s_ref[SRC + s_ref[ROW]]
    rows = pl.ds(0, BLOCK)
    acc = nt(x_ref[...], wa_ref[...])
    fill_queries(q_ref, rows, BLOCK, acc[:, :each] * FACTOR, heads)
    fill_keys(k_ref, v_ref, rows, at * BLOCK, BLOCK, acc[:, each:], heads, limit)
    k_out_ref[...] = k_ref[...]
    v_out_ref[...] = v_ref[...]
    acc = nt(m_ref[...], cwa_ref[each:, :])
    fill_keys(mk_ref, mv_ref, rows, at * BLOCK, BLOCK, acc, heads, memory_limit)


def causal_blocks(q_ref, k_ref, v_ref, att_ref, heads):
    at = pl.program_id(0)
    for block in range(k_ref.shape[1] // BLOCK):

        @pl.when(at == block)
        def _():
            for h in range(heads):
                attend_block(q_ref, k_ref, v_ref, att_ref, h, pl.ds(0, BLOCK), BLOCK, (block + 1) * BLOCK, True)


def self_own_kernel(s_ref, q_in_ref, k_ref, v_ref, up_ref, down_ref, q_ref, att_ref, halves_ref, mark_ref, *, heads):
    half = up_ref.shape[0]
    halves_ref[:half, :] = up_ref[...]
    halves_ref[half:, :] = down_ref[...]
    mark_ref[...] = jnp.zeros_like(mark_ref)
    q_ref[...] = q_in_ref[...]
    causal_blocks(q_ref, k_ref, v_ref, att_ref, heads)


def self_other_kernel(s_ref, x_ref, near_ref, far_ref, w_ref, q_ref, k_out_ref, v_out_ref, att_ref, k_ref, v_ref, *, heads):
    each = heads * HEAD_DIM
    at = pl.program_id(0)

    @pl.when(at == 0)
    def _():
        put_halves(w_ref, near_ref, far_ref, s_ref[BIT])

    acc = nt(x_ref[...], w_ref[...])
    fill_queries(q_ref, pl.ds(0, BLOCK), BLOCK, acc[:, :each] * FACTOR, heads)
    fill_keys(k_ref, v_ref, rows_at(BLOCK), at * BLOCK, BLOCK, acc[:, each:], heads, s_ref[TGT + s_ref[ROW]])
    k_out_ref[...] = k_ref[:, rows_at(BLOCK), :]
    v_out_ref[...] = v_ref[:, rows_at(BLOCK), :]
    causal_blocks(q_ref, k_ref, v_ref, att_ref, heads)


def self_out_kernel(
    s_ref, atta_ref, attb_ref, soa_ref, near_ref, far_ref, part0_ref, part1_ref, sob_ref, cob_ref, wide_ref, *, heads, blocks
):
    @pl.when(pl.program_id(0) == 0)
    def _():
        low = s_ref[BIT] == 0
        sob_ref[...] = jnp.where(low, near_ref[...], far_ref[...])
        cob_ref[...] = jnp.where(low, far_ref[...], near_ref[...])
        widen_out(wide_ref.at[0], soa_ref, heads)
        widen_out(wide_ref.at[1], sob_ref, heads)

    part = nn(atta_ref[...], wide_ref[0]) + nn(attb_ref[...], wide_ref[1])
    put_part(part0_ref, part1_ref, part.astype(bf16), blocks)


def cross_blocks(q_ref, k_ref, v_ref, att_ref, heads, limit):
    step = 256
    live = (limit + step - 1) // step
    for count in range(1, k_ref.shape[1] // step + 1):

        @pl.when(live == count)
        def _():
            for h in range(heads):
                attend_block(q_ref, k_ref, v_ref, att_ref, h, pl.ds(0, BLOCK), BLOCK, count * step, False)


def cross_own_kernel(
    s_ref, x_ref, own0, own1, got0, got1, gain_ref, shift_ref, cq_ref, k_ref, v_ref,
    h_ref, hl_ref, unit_ref, scale_ref, q_ref, att_ref, *, heads, blocks,
):
    unit, scale = norm(x_ref[...].astype(f32) + branch_of((own0, own1, got0, got1), blocks))
    h = unit * vector(gain_ref) + vector(shift_ref)
    h_ref[...] = h
    unit_ref[...] = unit.astype(bf16)
    scale_ref[...] = scale
    low = h.astype(bf16)
    hl_ref[...] = low
    fill_queries(q_ref, pl.ds(0, BLOCK), BLOCK, nt(low, cq_ref[...]) * FACTOR, heads)
    cross_blocks(q_ref, k_ref, v_ref, att_ref, heads, s_ref[SRC + s_ref[ROW]])


def put_halves(target_ref, near_ref, far_ref, high):
    half = near_ref.shape[0]
    target_ref[pl.ds(pl.multiple_of(high * half, 16), half), :] = near_ref[...]
    target_ref[pl.ds(pl.multiple_of((1 - high) * half, 16), half), :] = far_ref[...]


def cross_other_kernel(s_ref, m_ref, hl_ref, near_ref, far_ref, cwb_ref, k_ref, v_ref, q_ref, att_ref, *, heads):
    each = heads * HEAD_DIM
    limit = s_ref[SRC + s_ref[ROW]]

    @pl.when(pl.program_id(0) == 0)
    def _():
        put_halves(cwb_ref, near_ref, far_ref, s_ref[BIT + 1])

        @pl.loop(0, m_ref.shape[0], step=BLOCK)
        def _(start):
            rows = pl.ds(pl.multiple_of(start, BLOCK), BLOCK)
            fill_keys(k_ref, v_ref, rows, start, BLOCK, nt(m_ref[rows, :], cwb_ref[each:, :]), heads, limit)

    fill_queries(q_ref, pl.ds(0, BLOCK), BLOCK, nt(hl_ref[...], cwb_ref[:each, :]) * FACTOR, heads)
    cross_blocks(q_ref, k_ref, v_ref, att_ref, heads, limit)


def cross_out_kernel(atta_ref, attb_ref, coa_ref, cob_ref, part0_ref, part1_ref, wide_ref, *, heads, blocks):
    @pl.when(pl.program_id(0) == 0)
    def _():
        widen_out(wide_ref.at[0], coa_ref, heads)
        widen_out(wide_ref.at[1], cob_ref, heads)

    part = nn(atta_ref[...], wide_ref[0]) + nn(attb_ref[...], wide_ref[1])
    put_part(part0_ref, part1_ref, part.astype(bf16), blocks)


def ffn_own_kernel(
    h_in_ref, own0, own1, got0, got1, gain_ref, shift_ref, up_ref, down_ref,
    h_ref, hl_ref, unit_ref, scale_ref, act_ref, slope_ref, term_ref, *, blocks,
):
    unit, scale = norm(h_in_ref[...] + branch_of((own0, own1, got0, got1), blocks))
    h = unit * vector(gain_ref) + vector(shift_ref)
    h_ref[...] = h
    unit_ref[...] = unit.astype(bf16)
    scale_ref[...] = scale
    low = h.astype(bf16)
    hl_ref[...] = low
    act, slope = gelu_pair(nn(low, up_ref[...]))
    act = act.astype(bf16)
    act_ref[...] = act
    slope_ref[...] = slope.astype(bf16)
    term_ref[...] = nn(act, down_ref[...])


def ffn_other_kernel(
    s_ref, hl_ref, term_ref, up_near_ref, up_far_ref, down_near_ref, down_far_ref,
    part0_ref, part1_ref, act_ref, slope_ref, up_ref, down_ref, *, blocks,
):
    @pl.when(pl.program_id(0) == 0)
    def _():
        put_halves(up_ref, up_near_ref, up_far_ref, s_ref[BIT])
        put_halves(down_ref, down_near_ref, down_far_ref, s_ref[BIT + 1])

    act, slope = gelu_pair(nn(hl_ref[...], up_ref[...]))
    act = act.astype(bf16)
    act_ref[...] = act
    slope_ref[...] = slope.astype(bf16)
    put_part(part0_ref, part1_ref, (term_ref[...] + nn(act, down_ref[...])).astype(bf16), blocks)


def ffn_back_kernel(
    s_ref, h_ref, own0, own1, got0, got1, cot_ref, gain_ref, shift_ref, upa_ref, upb_ref, downa_ref, downb_ref, slopea_ref, slopeb_ref,
    part0_ref, part1_ref, out_ref, d_ref, e_ref, prea_ref, preb_ref, sums_ref, *, blocks,
):
    limit = s_ref[TGT + s_ref[ROW]]
    at = pl.program_id(0)

    @pl.when(at == 0)
    def _():
        sums_ref[...] = jnp.zeros_like(sums_ref)

    gain = vector(gain_ref)
    unit, scale = norm(h_ref[...] + branch_of((own0, own1, got0, got1), blocks))
    out_ref[...] = (unit * gain + vector(shift_ref)).astype(bf16)
    index = at * SPAN + lax.broadcasted_iota(jnp.int32, (SPAN, 1), 0)
    grad = jnp.where(index < limit, cot_ref[...].astype(f32), 0.0)
    sums_ref[0:1, :] += jnp.sum(grad * unit, 0, keepdims=True)
    sums_ref[1:2, :] += jnp.sum(grad, 0, keepdims=True)
    d = norm_back(grad, gain, unit, scale)
    d_ref[...] = d
    e = d.astype(bf16)
    e_ref[...] = e
    part = None
    for up_ref, down_ref, slope_ref, pre_ref in (
        (upa_ref, downa_ref, slopea_ref, prea_ref),
        (upb_ref, downb_ref, slopeb_ref, preb_ref),
    ):
        pre = (nt(e, down_ref[...]) * slope_ref[...].astype(f32)).astype(bf16)
        pre_ref[...] = pre
        term = nt(pre, up_ref[...])
        part = term if part is None else part + term
    put_part(part0_ref, part1_ref, part.astype(bf16), blocks)


def ffn_grad_kernel(s_ref, h_ref, act_ref, e_ref, pre_ref, up_ref, send_ref, keep_ref):
    up_ref[...] = tn(h_ref[...], pre_ref[...]).astype(bf16)
    down = tn(act_ref[...], e_ref[...]).astype(bf16)
    mine = pl.program_id(0) == s_ref[BIT]

    @pl.when(mine)
    def _():
        keep_ref[...] = down

    @pl.when(jnp.logical_not(mine))
    def _():
        send_ref[...] = down


def norm_step(d_in_ref, shares, gain, unit_ref, scale_ref, d_ref, e_ref, sums_ref, blocks):
    @pl.when(pl.program_id(0) == 0)
    def _():
        sums_ref[...] = jnp.zeros_like(sums_ref)

    grad = d_in_ref[...] + branch_of(shares, blocks)
    unit = unit_ref[...].astype(f32)
    sums_ref[0:1, :] += jnp.sum(grad * unit, 0, keepdims=True)
    sums_ref[1:2, :] += jnp.sum(grad, 0, keepdims=True)
    d = norm_back(grad, gain, unit, scale_ref[...])
    d_ref[...] = d
    e = d.astype(bf16)
    e_ref[...] = e
    return e


def cross_back_heads(s_ref, q_ref, k_ref, v_ref, do_ref, inner_ref, dqo_ref, dkv_ref, dq_ref, dk_ref, dv_ref, heads, blocks):
    at = pl.program_id(0)
    source = k_ref.shape[1]

    @pl.when(at == 0)
    def _():
        dk_ref[...] = jnp.zeros_like(dk_ref)
        dv_ref[...] = jnp.zeros_like(dv_ref)

    step = 256
    live = (s_ref[SRC + s_ref[ROW]] + step - 1) // step
    rows = pl.ds(0, BLOCK)
    for count in range(1, source // step + 1):

        @pl.when(live == count)
        def _():
            @pl.loop(0, heads)
            def _(h):
                back_block(
                    q_ref, k_ref, v_ref, do_ref, inner_ref, dq_ref, dk_ref, dv_ref, h, rows, rows_at(BLOCK), BLOCK, count * step, False
                )

    dqo_ref[...] = pack_heads(dq_ref, rows, heads, HEAD_DIM ** (-0.5))

    @pl.when(at == blocks - 1)
    def _():
        @pl.loop(0, source, step=BLOCK)
        def _(start):
            some = pl.ds(pl.multiple_of(start, BLOCK), BLOCK)
            dkv_ref[some, :] = jnp.concatenate(
                [pack_heads(dk_ref, some, heads, LN2), pack_heads(dv_ref, some, heads, 1.0)], 1
            )


def cross_back_other_kernel(
    s_ref, d_in_ref, own0, own1, got0, got1, gain_ref, unit_ref, scale_ref, coa_ref, cob_ref, atta_ref, attb_ref,
    q_ref, k_ref, v_ref,
    d_ref, e_ref, sums_ref, doa_ref, innera_ref, dqo_ref, dkv_ref, wide_ref, do_ref, inner_ref, dq_ref, dk_ref, dv_ref, *, heads, blocks,
):
    @pl.when(pl.program_id(0) == 0)
    def _():
        widen_out(wide_ref.at[0], coa_ref, heads)
        widen_out(wide_ref.at[1], cob_ref, heads)

    e = norm_step(
        d_in_ref, (own0, own1, got0, got1), vector(gain_ref), unit_ref, scale_ref, d_ref, e_ref, sums_ref, blocks
    )
    rows, places = pl.ds(0, BLOCK), rows_at(BLOCK)
    fill_grads(doa_ref, innera_ref, rows, places, e, wide_ref.at[0], atta_ref[...], heads)
    fill_grads(do_ref, inner_ref, rows, places, e, wide_ref.at[1], attb_ref[...], heads)
    cross_back_heads(s_ref, q_ref, k_ref, v_ref, do_ref, inner_ref, dqo_ref, dkv_ref, dq_ref, dk_ref, dv_ref, heads, blocks)


def cross_back_own_kernel(
    s_ref, q_ref, k_ref, v_ref, do_ref, inner_ref, dqb_ref, cqa_ref, cwb_ref,
    part0_ref, part1_ref, dqo_ref, dkv_ref, dq_ref, dk_ref, dv_ref, *, heads, blocks,
):
    cross_back_heads(s_ref, q_ref, k_ref, v_ref, do_ref, inner_ref, dqo_ref, dkv_ref, dq_ref, dk_ref, dv_ref, heads, blocks)
    part = nn(dqo_ref[...], cqa_ref[...]) + nn(dqb_ref[...], cwb_ref[: heads * HEAD_DIM, :])
    put_part(part0_ref, part1_ref, part.astype(bf16), blocks)


def cross_grad_kernel(s_ref, h_ref, m_ref, att_ref, e_ref, dq_ref, dkv_ref, g_ref):
    each = dq_ref.shape[1]
    g_ref[:each, :] = tn(dq_ref[...], h_ref[...]).astype(bf16)
    g_ref[each : 3 * each, :] = tn(dkv_ref[...], m_ref[...]).astype(bf16)
    narrow_out(g_ref, tn(att_ref[...], e_ref[...]).astype(bf16), 3 * each, each // HEAD_DIM)


def pass_kernel(s_ref, in_ref, out_ref):
    out_ref[...] = in_ref[...]


def relay_kernel(s_ref, in_ref, first_ref, second_ref):
    half = first_ref.shape[0]
    first_ref[...] = in_ref[:half, :]
    second_ref[...] = in_ref[half:, :]


def memory_grad_kernel(s_ref, a_ref, b_ref, wa_ref, wb_ref, send_ref, keep_ref):
    each = a_ref.shape[1] // 2
    part = (nn(a_ref[...], wa_ref[each:, :]) + nn(b_ref[...], wb_ref[each:, :])).astype(bf16)
    mine = pl.program_id(0) == s_ref[CORE_AT]

    @pl.when(mine)
    def _():
        keep_ref[...] = part

    @pl.when(jnp.logical_not(mine))
    def _():
        send_ref[...] = part


def norm_one_back_kernel(
    s_ref, d_in_ref, own0, own1, got0, got1, gain_ref, unit_ref, scale_ref, soa_ref, sob_ref, atta_ref, attb_ref,
    sums_two_ref, sums_three_ref, d_ref, doa_ref, dob_ref, innera_ref, innerb_ref, ra_ref, rb_ref, e_ref, sums_ref, wide_ref, *, heads, blocks,
):
    @pl.when(pl.program_id(0) == 0)
    def _():
        widen_out(wide_ref.at[0], soa_ref, heads)
        widen_out(wide_ref.at[1], sob_ref, heads)

    each = heads * HEAD_DIM
    rows = rows_at(SPAN)
    e = norm_step(
        d_in_ref, (own0, own1, got0, got1), vector(gain_ref), unit_ref, scale_ref, d_ref, e_ref.at[rows, :], sums_ref, blocks
    )
    fill_grads(doa_ref, innera_ref, pl.ds(0, SPAN), rows, e, wide_ref.at[0], atta_ref[rows, :], heads)
    fill_grads(dob_ref, innerb_ref, pl.ds(0, SPAN), rows, e, wide_ref.at[1], attb_ref[rows, :], heads)

    @pl.when(pl.program_id(0) == blocks - 1)
    def _():
        norms = jnp.concatenate(
            [sums_ref[:2, :], sums_two_ref[:2, :], sums_three_ref[:2, :], jnp.zeros((10, d_in_ref.shape[1]), f32)], 0
        ).astype(bf16)
        for att_ref, r_ref in ((atta_ref, ra_ref), (attb_ref, rb_ref)):
            narrow_out(r_ref, tn(att_ref[...], e_ref[...]).astype(bf16), 0, heads)
            r_ref[each:, :] = norms


def self_back_kernel(s_ref, x_ref, q_ref, k_ref, v_ref, do_ref, inner_ref, dqkv_ref, gw_ref, dq_ref, dk_ref, dv_ref, *, heads, blocks):
    at = pl.program_id(0)
    each = heads * HEAD_DIM
    length = k_ref.shape[1]

    @pl.when(at == 0)
    def _():
        dk_ref[...] = jnp.zeros_like(dk_ref)
        dv_ref[...] = jnp.zeros_like(dv_ref)

    rows = pl.ds(0, SPAN)
    for block in range(blocks):

        @pl.when(at == block)
        def _():
            @pl.loop(0, heads)
            def _(h):
                back_block(
                    q_ref, k_ref, v_ref, do_ref, inner_ref, dq_ref, dk_ref, dv_ref, h, rows, pl.ds(block * SPAN, SPAN), SPAN,
                    (block + 1) * SPAN, True,
                )

    dqkv_ref[rows_at(SPAN), :each] = pack_heads(dq_ref, rows, heads, HEAD_DIM ** (-0.5))

    @pl.when(at == blocks - 1)
    def _():
        @pl.loop(0, length, step=BLOCK)
        def _(start):
            some = pl.ds(pl.multiple_of(start, BLOCK), BLOCK)
            dqkv_ref[some, each:] = jnp.concatenate(
                [pack_heads(dk_ref, some, heads, LN2), pack_heads(dv_ref, some, heads, 1.0)], 1
            )
        gw_ref[...] = tn(dqkv_ref[...], x_ref[...]).astype(bf16)


def tokens_grad_kernel(s_ref, d_ref, a_ref, b_ref, wa_ref, wb_ref, send_ref, keep_ref):
    part = nn(a_ref[...], wa_ref[...]) + nn(b_ref[...], wb_ref[...])
    mine = pl.program_id(0) == s_ref[CORE_AT]

    @pl.when(mine)
    def _():
        keep_ref[...] = d_ref[...] + part

    @pl.when(jnp.logical_not(mine))
    def _():
        send_ref[...] = part.astype(bf16)


def place_kernel(s_ref, *refs, shift):
    pieces, out_ref, mark_ref = refs[:-2], refs[-2], refs[-1]
    half = out_ref.shape[0]
    row, core, at = s_ref[ROW], s_ref[CORE_AT], pl.program_id(0)
    mark_ref[...] = jnp.zeros_like(mark_ref)
    if shift:
        sources = [
            (pieces[0].at[:half, :], 2 * row), (pieces[0].at[half:, :], 2 * row + 1),
            (pieces[1], 2 * (1 - row) + core), (pieces[2], 2 * (1 - row) + 1 - core),
        ]
    else:
        sources = [
            (pieces[0].at[:half, :], 2 * row + core), (pieces[1].at[:half, :], 2 * row + 1 - core),
            (pieces[0].at[half:, :], 2 * (1 - row) + core), (pieces[1].at[half:, :], 2 * (1 - row) + 1 - core),
        ]
    for ref, place in sources:

        @pl.when(at == place)
        def _():
            out_ref[...] = ref[...]


def step_kernel(s_ref, *refs, plans):
    scratch = refs[-1]
    inputs = sum(plan[1] for plan in plans)
    ins, outs = list(refs[:inputs]), list(refs[inputs:-1])
    for kind, count, rows, bit, cuts, parts in plans:
        mine, ins = ins[:count], ins[count:]
        if kind == SUM:
            at = 0
            for a_ref, b_ref in zip(mine[: count // 2], mine[count // 2 :]):
                size = min(a_ref.shape[0], rows - at)
                scratch[at : at + size, :] = (a_ref[:size, :].astype(f32) + b_ref[:size, :].astype(f32)).astype(bf16)
                at += size
            if at < rows:
                scratch[at:rows, :] = jnp.zeros((rows - at, scratch.shape[1]), bf16)
            if bit is None:
                outs.pop(0)[...] = scratch[:rows, :]
            else:
                half, high = rows // 2, s_ref[BIT + bit]
                outs.pop(0)[...] = scratch[pl.ds(pl.multiple_of((1 - high) * half, 16), half), :]
                outs.pop(0)[...] = scratch[pl.ds(pl.multiple_of(high * half, 16), half), :]
        elif kind == LAST:
            outs.pop(0)[...] = mine[0][-rows:, :].astype(f32) + mine[1][-rows:, :].astype(f32)
        elif kind == PASS:
            outs.pop(0)[...] = mine[0][...]
        elif kind == STACK:
            size, target = mine[0].shape[0], outs.pop(0)
            target[:size, :] = mine[0][...]
            target[size:, :] = mine[1][...]
        else:
            high, size = s_ref[BIT + bit], mine[0].shape[0] // parts
            target = outs.pop(0) if kind == PACK else scratch
            for part in range(parts):
                some, first = slice(part * size, (part + 1) * size), 2 * part * size
                target[pl.ds(pl.multiple_of(first + high * size, 16), size), :] = mine[0][some, :]
                target[pl.ds(pl.multiple_of(first + (1 - high) * size, 16), size), :] = mine[1][some, :]
            for first, size in cuts:
                outs.pop(0)[...] = scratch[first : first + size, :].astype(f32)


class Row:
    def __init__(self, array, length, how=WHOLE):
        self.array, self.length, self.how = array, length, how


class Part:
    def __init__(self, array, how=ROWS, pick=None):
        self.array, self.how, self.pick = array, how, pick


class Pick:
    def __init__(self, array, scalar, parts):
        self.array, self.scalar, self.parts = array, scalar, parts


class Far:
    def __init__(self, array):
        self.array = array


def block_of(shape, how, blocks, pick=None, once=False):
    rank = len(shape)
    if rank == 1:
        return pl.BlockSpec(shape, lambda *a: (0,))
    if isinstance(how, tuple):
        how, pick = how
    if how == WHOLE:
        return pl.BlockSpec(shape, lambda *a: (0,) * rank, pipeline_mode=pl.Buffered(1) if once else None)
    pick = pick or (lambda i: i)
    dim = rank - 1 if how == COLUMNS else rank - 2
    parts = blocks // 2 if how == HALF else blocks
    block = tuple(n // parts if d == dim else n for d, n in enumerate(shape))
    return pl.BlockSpec(block, lambda i, *a: tuple(pick(i) if d == dim else 0 for d in range(rank)))


def row_of(item, blocks):
    width = item.array.shape[1]
    if item.how == WHOLE:
        return pl.BlockSpec((item.length, width), lambda i, s: (s[0], 0))
    if item.how == ROWS:
        return pl.BlockSpec((item.length // blocks, width), lambda i, s: (s[0] * blocks + i, 0))
    if item.how[0] == PART:
        return pl.BlockSpec((item.length // blocks, width), lambda i, s: (s[item.how[1]] * blocks + i, 0))
    return pl.BlockSpec((item.length, width // blocks), lambda i, s: (s[0], i))


class Held:
    def __init__(self, array, how=ROWS):
        self.array, self.how = array, how


def view_of(shape, how, blocks):
    rank = len(shape)
    if how == WHOLE:
        return None
    if how == ROWS:
        size = shape[-2] // blocks

        def rows(ref):
            place = pl.ds(pl.multiple_of(pl.program_id(0) * size, size), size)
            return ref.at[place, :] if rank == 2 else ref.at[:, place, :]

        return rows
    size = shape[-1] // blocks
    return lambda ref: ref.at[:, pl.ds(pl.multiple_of(pl.program_id(0) * size, size), size)]


def call(kernel, blocks, inputs, outputs, scalars=None, scratch=(), micros=5.0, limit=LIMIT, after=(), scale=0.9):
    specs, arrays, views = [], [], []
    here = pl.BlockSpec(memory_space=pltpu.VMEM)
    for item in inputs:
        view = None
        if isinstance(item, Row):
            specs.append(row_of(item, blocks))
            arrays.append(pltpu.with_memory_space_constraint(item.array, pltpu.HBM))
        elif isinstance(item, Part):
            specs.append(block_of(item.array.shape, item.how, blocks, item.pick))
            arrays.append(item.array)
        elif isinstance(item, Pick):
            rows, width = item.array.shape
            specs.append(pl.BlockSpec((rows // item.parts, width), functools.partial(lambda at, i, s: (s[at], 0), item.scalar)))
            arrays.append(pltpu.with_memory_space_constraint(item.array, pltpu.HBM))
        elif isinstance(item, Far):
            specs.append(block_of(item.array.shape, WHOLE, blocks, once=True))
            arrays.append(pltpu.with_memory_space_constraint(item.array, pltpu.HBM))
        elif isinstance(item, Held):
            specs.append(here)
            arrays.append(pltpu.with_memory_space_constraint(item.array, pltpu.VMEM))
            view = view_of(item.array.shape, item.how, blocks)
        else:
            specs.append(block_of(item.shape, WHOLE, blocks, once=True))
            arrays.append(item)
        views.append(view)
    for item in after:
        specs.append(pl.BlockSpec(memory_space=pl.ANY))
        arrays.append(pltpu.with_memory_space_constraint(item.array, pltpu.HBM) if isinstance(item, Far) else item)
        views.append(SKIP)
    shapes, out_specs = [], []
    for shape, dtype, how in outputs:
        if how[:4] == "held":
            shapes.append(pltpu.VMEM(shape, dtype))
            out_specs.append(here)
            views.append(view_of(shape, how[5:], blocks))
        else:
            far = how[:3] == "hbm"
            shapes.append(pltpu.HBM(shape, dtype) if far else jax.ShapeDtypeStruct(shape, dtype))
            out_specs.append(block_of(shape, how[4:] if far else how, blocks))
            views.append(None)
    lead = 0 if scalars is None else 1

    def viewed(*refs):
        passed = list(refs[:lead])
        for ref, view in zip(refs[lead : lead + len(views)], views):
            if view == SKIP:
                continue
            passed.append(ref if view is None else view(ref))
        return kernel(*passed, *refs[lead + len(views) :])

    settings = dict(
        out_shape=shapes,
        compiler_params=pltpu.CompilerParams(vmem_limit_bytes=limit * MIB, dimension_semantics=(ARBITRARY,)),
        cost_estimate=pl.CostEstimate(flops=int(micros * scale * 1.0e9), bytes_accessed=0, transcendentals=0),
        name=getattr(kernel, "func", kernel).__name__,
    )
    if scalars is None:
        return pl.pallas_call(
            viewed, grid=(blocks,), in_specs=specs, out_specs=out_specs, scratch_shapes=list(scratch), **settings
        )(*arrays)
    grid_spec = pltpu.PrefetchScalarGridSpec(
        num_scalar_prefetch=1, grid=(blocks,), in_specs=specs, out_specs=out_specs, scratch_shapes=list(scratch)
    )
    return pl.pallas_call(viewed, grid_spec=grid_spec, **settings)(scalars, *arrays)


def local(
    size, tokens, memory, cotangent, tgt_len, src_len, self_query, self_key, self_value, self_out,
    cross_query, cross_key, cross_value, cross_out, ffn_up, ffn_down,
    gain_one, shift_one, gain_two, shift_two, gain_three, shift_three,
):
    width = tokens.shape[1]
    length = tokens.shape[0] // 2
    source = memory.shape[0] // 2
    each = self_query.shape[1]
    heads = each // HEAD_DIM
    hidden = ffn_up.shape[1]
    place = lax.axis_index("tp").astype(jnp.int32)
    group = lax.axis_index("dp").astype(jnp.int32)
    scalars = jnp.concatenate(
        [jnp.stack([place // 2]), tgt_len, src_len, jnp.stack([place % 2] + [(group >> b) & 1 for b in range(3)])]
    )
    big, small, third = length // BLOCK, length // SPAN, width // SPAN
    short = size == 8

    def across(value):
        return lax.ppermute(value, "tp", ACROSS)

    def sibling(value):
        return lax.ppermute(value, "tp", CORE)

    def along(value, bit):
        return lax.ppermute(value, "dp", [(i, i ^ (1 << bit)) for i in range(size)])

    def shares(part, blocks):
        per = blocks // 2
        first, second = (lambda i: jnp.minimum(i, per - 1)), (lambda i: jnp.maximum(i - per, 0))
        got = [sibling(p) for p in part]
        return [Part(v, HALF, pick) for v, pick in zip((*part, *got), (first, second) * 2)]

    def part_shapes(blocks):
        per = blocks // 2
        first, second = (lambda i: jnp.minimum(i, per - 1)), (lambda i: jnp.maximum(i - per, 0))
        return [((length // 2, width), bf16, (HALF, pick)) for pick in (first, second)]

    head_rows = ((heads, length, WIDE), bf16, FAR_ROWS)
    head_held = ((heads, length, WIDE), bf16, HELD_ROWS)
    key_held = ((heads, source, WIDE), bf16, HELD_ROWS)
    held = ((length, width), f32, HELD_ROWS)
    held_low = ((length, width), bf16, HELD_ROWS)
    column = ((length, 1), f32, HELD_ROWS)
    att_held = ((length, heads * WIDE), bf16, HELD_ROWS)
    dq_held = ((length, each), bf16, HELD_ROWS)
    hid = ((length, hidden), bf16, HELD_ROWS)
    sums = ((8, width), f32, WHOLE)
    low = ((length, width), bf16, ROWS)
    square = ((width, hidden), bf16, ROWS)
    half_low = ((length // 2, width), bf16, WHOLE)
    out_shape = ((each, width), bf16, WHOLE)
    qkv = functools.partial(pltpu.VMEM, (heads, length, WIDE))
    wide_out = pltpu.VMEM((2, heads * WIDE, width), bf16)
    inner_held = ((heads, 8, length), f32, HELD_WHOLE)

    w_parts = (self_query.T, self_key.T, self_value.T)
    c_parts = (cross_query.T, cross_key.T, cross_value.T)
    bit = scalars[BIT]
    w_half = lax.dynamic_slice_in_dim(jnp.concatenate(w_parts, 0), bit * (3 * each // 2), 3 * each // 2, 0)
    w_near = across(w_half)
    q_new, k_new, v_new, k_a, v_a, ck_a, cv_a, w_a, cw_a, o_half, cw_half = call(
        functools.partial(project_own_kernel, heads=heads), big,
        [
            Row(tokens, length, ROWS), Row(memory, source, ROWS), *(Far(v) for v in (*w_parts, *c_parts, self_out, cross_out)),
        ],
        [
            head_held, head_held, head_held, head_rows, head_rows, key_held, key_held, ((3 * each, width), bf16, WHOLE),
            ((3 * each, width), bf16, WHOLE), out_shape, ((3 * each // 2, width), bf16, WHOLE),
        ],
        scalars, micros=7, scale=0.4,
    )
    o_near = across(o_half)
    cw_near = across(cw_half)
    (w_near,) = call(
        pass_kernel, 1, [w_near], [((3 * each // 2, width), bf16, WHOLE)], scalars, micros=1, scale=0.4, after=[o_half]
    )
    w_far = along(w_near, 0)
    quarter = ((hidden // 2, width), bf16, WHOLE)
    q_a, att_a, ffn_half, mark = call(
        functools.partial(self_own_kernel, heads=heads), big,
        [Held(q_new), Held(k_new, WHOLE), Held(v_new, WHOLE), Pick(ffn_up, BIT, 2), Pick(ffn_down, BIT + 1, 2)],
        [head_rows, att_held, ((width, width), bf16, WHOLE), ((8, WIDE), f32, WHOLE)], scalars, micros=6, scale=0.4, after=[w_near],
    )
    ffn_near = across(ffn_half)
    cw_far = along(cw_near, 1)
    (o_near,) = call(pass_kernel, 1, [o_near], [out_shape], scalars, micros=1, scale=0.4, after=[mark])
    o_far = along(o_near, 0)
    w_b, q_b, k_b, v_b, att_b = call(
        functools.partial(self_other_kernel, heads=heads), big, [Row(tokens, length, ROWS), w_near, w_far],
        [((3 * each, width), bf16, WHOLE), head_rows, head_rows, head_rows, att_held], scalars, scratch=[qkv(bf16), qkv(bf16)],
        micros=9, scale=0.4,
    )
    part0, part1, so_b, co_b = call(
        functools.partial(self_out_kernel, heads=heads, blocks=big), big, [Held(att_a), Held(att_b), self_out, o_near, o_far],
        [*part_shapes(big), out_shape, out_shape], scalars, scratch=[wide_out], micros=3, scale=0.4, after=[cw_near],
    )
    h_one, h_one_low, unit_one, scale_one, cq_a, catt_a = call(
        functools.partial(cross_own_kernel, heads=heads, blocks=big), big,
        [Row(tokens, length, ROWS), *shares((part0, part1), big), gain_one, shift_one, c_parts[0], Held(ck_a, WHOLE), Held(cv_a, WHOLE)],
        [held, held_low, held_low, column, head_held, att_held], scalars, micros=10, scale=0.4,
    )
    up_near, down_near = call(
        relay_kernel, 1, [ffn_near], [quarter, quarter], scalars, micros=1, after=[scale_one]
    )
    up_far, down_far = along(up_near, 0), along(down_near, 1)
    cw_b, ck_b, cv_b, cq_b, catt_b = call(
        functools.partial(cross_other_kernel, heads=heads), big,
        [Row(memory, source), Held(h_one_low), cw_near, cw_far],
        [((3 * each, width), bf16, WHOLE), ((heads, source, WIDE), bf16, HELD_WHOLE), ((heads, source, WIDE), bf16, HELD_WHOLE), head_held, att_held],
        scalars, micros=100, scale=1.0, after=[up_near, down_near],
    )
    part0, part1 = call(
        functools.partial(cross_out_kernel, heads=heads, blocks=big), big, [Held(catt_a), Held(catt_b), cross_out, co_b],
        part_shapes(big), scratch=[wide_out], micros=2, scale=0.4, after=[up_far, down_far],
    )
    h_two, h_two_low, unit_two, scale_two, act_a, slope_a, term = call(
        functools.partial(ffn_own_kernel, blocks=big), big,
        [Held(h_one), *shares((part0, part1), big), gain_two, shift_two, Held(ffn_up, WHOLE), Held(ffn_down, WHOLE)],
        [held, held_low, held_low, column, hid, hid, held], micros=7, scale=0.4, limit=24,
    )
    part0, part1, act_b, slope_b, up_b, down_b = call(
        functools.partial(ffn_other_kernel, blocks=big), big,
        [Held(h_two_low), Held(term), up_near, up_far, down_near, down_far],
        [*part_shapes(big), hid, hid, ((width, hidden), bf16, HELD_WHOLE), ((hidden, width), bf16, HELD_WHOLE)], scalars, micros=5, scale=0.4, limit=24,
    )

    part0, part1, out_row, d_three, e_three, pre_a, pre_b, sums_three = call(
        functools.partial(ffn_back_kernel, blocks=small), small,
        [
            Held(h_two), *shares((part0, part1), small), Row(cotangent, length, ROWS), gain_three, shift_three,
            Held(ffn_up, WHOLE), Held(up_b, WHOLE), Held(ffn_down, WHOLE), Held(down_b, WHOLE), Held(slope_a), Held(slope_b),
        ],
        [*part_shapes(small), ((length, width), bf16, FAR_ROWS), held, held_low, hid, hid, sums], scalars, micros=11,
    )
    part = (part0, part1)
    quarter = ((width // 2, hidden), bf16, WHOLE)

    def ffn_grads(act, pre, after=()):
        return call(
            ffn_grad_kernel, 2,
            [Held(h_two_low, COLUMNS), Held(act, COLUMNS), Held(e_three, WHOLE), Held(pre, WHOLE)],
            [square, quarter, quarter], scalars, micros=4, after=after,
        )

    gu_b, send_b, keep_b = ffn_grads(act_b, pre_b)
    gu_got, got_b = across(gu_b), along(send_b, 0)
    gu_a, send_a, keep_a = ffn_grads(act_a, pre_a, [send_b])
    got_a = along(send_a, 0)
    back_scratch = [
        pltpu.VMEM((heads, BLOCK, WIDE), f32), pltpu.VMEM((heads, source, WIDE), f32), pltpu.VMEM((heads, source, WIDE), f32),
    ]
    dkv_held = ((source, 2 * each), bf16, HELD_WHOLE)
    d_two, e_two, sums_two, do_a, inner_a, dcq_b, dckv_b = call(
        functools.partial(cross_back_other_kernel, heads=heads, blocks=big), big,
        [
            Held(d_three), *shares(part, big), gain_two, Held(unit_two), Held(scale_two), cross_out, co_b, Held(catt_a), Held(catt_b), Held(cq_b), Held(ck_b, WHOLE), Held(cv_b, WHOLE),
        ],
        [held, held_low, sums, head_held, inner_held, dq_held, dkv_held], scalars,
        scratch=[wide_out, pltpu.VMEM((heads, BLOCK, WIDE), bf16), pltpu.VMEM((heads, 8, length), f32)] + back_scratch, micros=18,
    )

    def cross_grads(att, dq, dkv, after=()):
        return call(
            cross_grad_kernel, third,
            [
                Held(h_one_low, COLUMNS), Row(memory, source, COLUMNS), Held(att, WHOLE), Held(e_two, COLUMNS),
                Held(dq, WHOLE), Held(dkv, WHOLE),
            ],
            [((4 * each, width), bf16, COLUMNS)], scalars, micros=5, after=after,
        )[0]

    def step(plans, after=(), micros=2):
        inputs, outputs, kernel_plans, counts, most = [], [], [], [], 16
        for kind, arrays, rows, bit, cuts, parts in plans:
            inputs += arrays
            if kind == SUM:
                made = [((rows, width), bf16, WHOLE)] if bit is None else [((rows // 2, width), bf16, WHOLE)] * 2
            elif kind == LAST:
                made = [((rows, width), f32, WHOLE)]
            elif kind in (PACK, STACK, PASS):
                made = [((rows, width), bit if kind == PASS else bf16, WHOLE)]
            else:
                made = [((size, width), f32, FAR_WHOLE) for _, size in cuts]
            if kind not in (PACK, STACK, LAST, PASS):
                most = max(most, rows)
            outputs += made
            counts.append(len(made))
            kernel_plans.append((kind, len(arrays), rows, bit, cuts, parts))
        made = list(
            call(
                functools.partial(step_kernel, plans=kernel_plans), 1, inputs, outputs, scalars,
                scratch=[pltpu.VMEM((most, width), bf16)], micros=micros, after=after,
            )
        )
        return [made[sum(counts[:n]) : sum(counts[: n + 1])] for n in range(len(counts))]

    class Chain:
        def __init__(self, mine, got, rows, cuts, bits=(0, 1, 2), back=(2, 1, 0), parts=1):
            self.arrays, self.rows, self.cuts, self.stage = [*mine, *got], rows, cuts, 0
            self.bits, self.back, self.parts = bits, back, parts

        def plan(self):
            count = len(self.bits)
            if self.stage <= count:
                bit = self.bits[self.stage] if self.stage < count else None
                return (SUM, self.arrays, self.rows >> self.stage, bit, (), 1)
            at = self.stage - count
            rows, last = self.rows >> count << at, at == len(self.back)
            return (WIDEN if last else PACK, self.arrays, rows, self.back[at - 1], self.cuts if last else (), self.parts if last else 1)

        def take(self, made):
            stage, count, self.stage = self.stage, len(self.bits), self.stage + 1
            if stage < count:
                self.arrays = [made[1], along(made[0], self.bits[stage])]
            elif stage < count + len(self.back):
                self.arrays = [made[0], along(made[0], self.back[stage - count])]
            else:
                self.done = made

    def advance(chains, plans=(), after=(), micros=2):
        made = step([c.plan() for c in chains] + list(plans), after, micros)
        for chain, one in zip(chains, made):
            chain.take(one)
        return [made[0][-1]], [m[0] for m in made[len(chains) :]]

    def plain(arrays, rows):
        return (SUM, arrays, rows, None, (), 1)

    def last(mine, got):
        return (LAST, [mine, got], 16, None, (), 1)

    gc_b = cross_grads(catt_b, dcq_b, dckv_b)
    if short:
        (send_u, keep_u), (down_a,), (down_b,), (gc_b,) = step(
            [
                (SUM, [gu_a, gu_got], width, 0, (), 1), plain([keep_a, got_a], width // 2), plain([keep_b, got_b], width // 2),
                (PASS, [gc_b], 4 * each, bf16, (), 1),
            ],
            [gc_b],
        )
        got_u, got_d = along(send_u, 0), across(down_b)
    part0, part1, dcq_a, dckv_a = call(
        functools.partial(cross_back_own_kernel, heads=heads, blocks=big), big,
        [Held(cq_a), Held(ck_a, WHOLE), Held(cv_a, WHOLE), Held(do_a), Held(inner_a, WHOLE), Held(dcq_b), c_parts[0], cw_b],
        [*part_shapes(big), dq_held, dkv_held], scalars, scratch=back_scratch, micros=16, after=[gc_b],
    )
    part = (part0, part1)

    gc_got = across(gc_b)
    pin = []
    if short:
        ffn = Chain([keep_u, down_a], [got_u, got_d], width, [(0, width), (width, width)], (1, 2), (2, 1, 0), 2)
        pin, _ = advance([ffn], after=[dcq_a])
    memory_send, memory_keep = call(
        memory_grad_kernel, 2, [Held(dckv_a), Held(dckv_b), cw_a, cw_b], [half_low, half_low], scalars, micros=5, after=pin,
    )
    memory_got = sibling(memory_send)
    gc_a = cross_grads(catt_a, dcq_a, dckv_a, [memory_send])
    memory_plan = plain([memory_keep, memory_got], length // 2)
    pin = [gc_a]
    rest_shape = ((each + 16, width), bf16, WHOLE)
    d_one, do_a, do_b, inner_a, inner_b, rest_a, rest_b = call(
        functools.partial(norm_one_back_kernel, heads=heads, blocks=small), small,
        [
            Held(d_two), *shares(part, small), gain_one, Held(unit_one), Held(scale_one), self_out, so_b,
            Held(att_a, WHOLE), Held(att_b, WHOLE), sums_two, sums_three,
        ],
        [held, head_held, head_held, inner_held, inner_held, rest_shape, rest_shape], scalars,
        scratch=[pltpu.VMEM((length, width), bf16), pltpu.VMEM((8, width), f32), wide_out], micros=6, after=pin,
    )
    rest_got = across(rest_b)
    kept_w = ((3 * each, width), bf16, WHOLE)
    qkv_held = ((length, 3 * each), bf16, HELD_WHOLE)
    self_scratch = [
        pltpu.VMEM((heads, SPAN, WIDE), f32), pltpu.VMEM((heads, length, WIDE), f32), pltpu.VMEM((heads, length, WIDE), f32),
    ]

    def self_back(q, k, v, do, inner, after=()):
        return call(
            functools.partial(self_back_kernel, heads=heads, blocks=small), small,
            [Row(tokens, length), Part(q), k, v, Held(do), Held(inner, WHOLE)], [qkv_held, kept_w], scalars, scratch=self_scratch, micros=14, after=after,
        )

    pin = []
    if short:
        cross = Chain([gc_a], [gc_got], 4 * each, [(n * each, each) for n in range(4)])
        pin, _ = advance([ffn, cross], after=[do_b])
    dqkv_b, gw_b = self_back(q_b, k_b, v_b, do_b, inner_b, pin)
    gw_got = across(gw_b)

    pin = []
    if short:
        pin, (norms,) = advance([ffn, cross], [last(rest_a, rest_got)], [dqkv_b])
        norms = last(norms, along(norms, 0))
    dqkv_a, gw_a = self_back(q_a, k_a, v_a, do_a, inner_a, pin)
    pin = []
    if short:
        own = Chain([gw_a, rest_a], [gw_got, rest_got], 4 * each, [(n * each, each) for n in range(4)])
        pin, (memory_mine, norms) = advance([own, ffn, cross], [memory_plan, norms])
    else:
        ((memory_mine,),) = step([memory_plan], [gw_a])
    tokens_send, tokens_keep = call(
        tokens_grad_kernel, 2, [Held(d_one), Held(dqkv_a), Held(dqkv_b), w_a, w_b],
        [half_low, ((length // 2, width), f32, WHOLE)], scalars, micros=6, after=pin,
    )
    (out_half,) = call(
        pass_kernel, 1, [Row(out_row, length // 2, (PART, CORE_AT))], [half_low], scalars, micros=1, after=[tokens_send]
    )
    out_far = across(out_half)

    def placed(pieces, shift, after=()):
        return call(
            functools.partial(place_kernel, shift=shift), 4, pieces,
            [((2 * length, width), bf16, FAR_ROWS), ((8, WIDE), f32, WHOLE)], scalars, micros=4, after=after,
        )

    def passed(value, rows=length // 2, dtype=bf16):
        return (PASS, [value], rows, dtype, (), 1)

    def pair(mine, far):
        return (STACK, [mine, far], length, None, (), 1)

    if short:
        pin, (memory_mine,) = advance([own, ffn, cross], [passed(memory_mine)], [out_half])
        memory_far = across(memory_mine)
        pin, (tokens_send,) = advance([own, cross], [passed(tokens_send)], [*pin, out_far])
        tokens_plan = plain([tokens_keep, sibling(tokens_send)], length // 2)
        pin, (tokens_mine, memory_pair, out_far) = advance(
            [own, cross], [tokens_plan, pair(memory_mine, memory_far), passed(out_far)], [*pin, ffn.arrays[1]]
        )
        tokens_far, memory_sibling, out_sibling = across(tokens_mine), sibling(memory_pair), sibling(out_far)
        ((gu_wide, gd_wide),) = step([ffn.plan()], pin, 4)
        pin, (norms,) = advance([own], [passed(norms, 16, f32)], [Far(gu_wide), memory_sibling, out_sibling])
        norms = last(norms, along(norms, 2))
        memory_grad, mark = placed([memory_pair, memory_sibling], False, pin)
        pin, (tokens_pair, norms) = advance([own], [pair(tokens_mine, tokens_far), norms], [mark, cross.arrays[1]])
        norms = last(norms, along(norms, 1))
        (cross,) = step([cross.plan()], pin, 3)
        layer_out, mark = placed([out_row, out_far, out_sibling], True, [Far(cross[0])])
        tokens_grad, mark = placed([tokens_pair, sibling(tokens_pair)], False, [mark])
        _, (norms,) = advance([own], [norms], [mark])
        own = own.done
        rest = own[3]
    else:
        memory_far = across(memory_mine)
        tokens_plan = plain([tokens_keep, sibling(tokens_send)], length // 2)
        (tokens_mine,), (memory_pair,) = step([tokens_plan, pair(memory_mine, memory_far)])
        ((tokens_pair,),) = step([pair(tokens_mine, across(tokens_mine))])
        layer_out, _ = placed([out_row, out_far, sibling(out_far)], True)
        memory_grad, _ = placed([memory_pair, sibling(memory_pair)], False)
        tokens_grad, _ = placed([tokens_pair, sibling(tokens_pair)], False)

        def total(mine, got):
            return lax.psum((mine.astype(f32) + got.astype(f32)).astype(bf16), "dp").astype(f32)

        high = scalars[BIT] == 1
        down_a, down_b = (
            jnp.where(high, jnp.concatenate([send, keep]), jnp.concatenate([keep, send]))
            for send, keep in ((send_a, keep_a), (send_b, keep_b))
        )
        gu_wide, gd_wide = total(gu_a, gu_got), total(down_a, across(down_b))
        cross = jnp.split(total(gc_a, gc_got), 4)
        own = jnp.split(total(gw_a, gw_got), 3)
        rest = total(rest_a, rest_got)
        rest, norms = rest[:each], rest[each:]
    return (
        layer_out, tokens_grad, memory_grad,
        own[0].T, own[1].T, own[2].T, rest,
        cross[0].T, cross[1].T, cross[2].T, cross[3],
        gu_wide, gd_wide, *(norms[i] for i in range(6)),
    )


def solution(mesh):
    rows, columns, down = P("dp", None), P(None, "tp"), P("tp", None)
    return jax.shard_map(
        functools.partial(local, mesh.shape["dp"]),
        mesh=mesh,
        in_specs=(rows, rows, rows, P("dp"), P("dp"))
        + (columns, columns, columns, down) * 2
        + (columns, down)
        + (P(),) * 6,
        out_specs=(rows, rows, rows) + (columns, columns, columns, down) * 2 + (columns, down) + (P(),) * 6,
        check_vma=False,
    )
```

```python
import functools

import jax
import jax.numpy as jnp
from jax import lax
from jax.experimental import pallas as pl
from jax.experimental.pallas import tpu as pltpu
from jax.sharding import PartitionSpec as P

HEAD_DIM = 64
WIDE = 2 * HEAD_DIM
EPS = 1e-05
MASKED = -1e30
LOG2E = 1.4426950408889634
LN2 = 0.6931471805599453
f32 = jnp.float32
bf16 = jnp.bfloat16

CORE = [(0, 1), (1, 0), (2, 3), (3, 2)]
ACROSS = [(0, 2), (2, 0), (1, 3), (3, 1)]
MIB = 1 << 20
LIMIT = 16

ROWS, WHOLE, COLUMNS, HALF, PART, SKIP, ARBITRARY = "rows", "whole", "columns", "half", "part", "skip", "arbitrary"
HELD_ROWS, HELD_WHOLE, FAR_ROWS, FAR_WHOLE = "held rows", "held whole", "hbm rows", "hbm whole"
SUM, PACK, WIDEN, STACK, LAST, PASS, TWIN, SPLIT = "sum", "pack", "wide", "stack", "last", "pass", "twin", "split"


def nn(left, right):
    return lax.dot_general(left, right, (((1,), (0,)), ((), ())), preferred_element_type=f32)


def nt(left, right):
    return lax.dot_general(left, right, (((1,), (1,)), ((), ())), preferred_element_type=f32)


def tn(left, right):
    return lax.dot_general(left, right, (((0,), (0,)), ((), ())), preferred_element_type=f32)


def lanes(rows):
    return lax.broadcasted_iota(jnp.int32, (rows, HEAD_DIM), 1)


def three_parts(value):
    high = value.astype(bf16).astype(f32)
    rest = value - high
    middle = rest.astype(bf16).astype(f32)
    return high, middle, rest - middle


def fill_queries(q_ref, rows, count, acc, heads):
    tail = jnp.where(lanes(count) == 0, 1.0, 0.0)
    for h in range(heads):
        part = acc[:, h * HEAD_DIM : (h + 1) * HEAD_DIM]
        q_ref[h, rows, :] = jnp.concatenate([part, tail], 1).astype(bf16)


def fill_keys(k_ref, v_ref, rows, start, count, acc, heads, limit):
    lane = lanes(count)
    index = start + lax.broadcasted_iota(jnp.int32, (count, HEAD_DIM), 0)
    tail = jnp.where(lane == 0, jnp.where(index < limit, 0.0, MASKED), jnp.where(lane < 4, 1.0, 0.0))
    ones = jnp.ones((count, HEAD_DIM), f32)
    for h in range(heads):
        k = acc[:, h * HEAD_DIM : (h + 1) * HEAD_DIM]
        v = acc[:, (heads + h) * HEAD_DIM : (heads + h + 1) * HEAD_DIM]
        k_ref[h, rows, :] = jnp.concatenate([k, tail], 1).astype(bf16)
        v_ref[h, rows, :] = jnp.concatenate([v, ones], 1).astype(bf16)


def attend_block(q_ref, k_ref, v_ref, att_ref, h, rows, count, key_end, causal):
    s = nt(q_ref[h, rows, :], k_ref[h, :key_end, :])
    if causal:
        r = lax.broadcasted_iota(jnp.int32, (count, count), 0)
        c = lax.broadcasted_iota(jnp.int32, (count, count), 1)
        diagonal = jnp.where(c <= r, s[:, key_end - count :], MASKED)
        s = diagonal if key_end == count else jnp.concatenate([s[:, : key_end - count], diagonal], 1)
    peak = jnp.max(s, 1, keepdims=True)
    p = jnp.exp2(s - peak).astype(bf16)
    o = nn(p, v_ref[h, :key_end, :])
    total = jnp.broadcast_to(o[:, HEAD_DIM : HEAD_DIM + 1], o.shape)
    att_ref[rows, h * WIDE : (h + 1) * WIDE] = (o / total).astype(bf16)
    high, middle, low = three_parts(-(peak + jnp.log2(total)))
    lane = lax.broadcasted_iota(jnp.int32, o.shape, 1)
    tail = jnp.where(lane == 65, high, jnp.where(lane == 66, middle, jnp.where(lane == 67, low, q_ref[h, rows, :].astype(f32))))
    q_ref[h, rows, :] = tail.astype(bf16)


def widen_out(wide_ref, out_ref, heads):
    wide_ref[...] = jnp.zeros_like(wide_ref)
    for h in range(heads):
        wide_ref[h * WIDE : h * WIDE + HEAD_DIM, :] = out_ref[h * HEAD_DIM : (h + 1) * HEAD_DIM, :]


def narrow_out(out_ref, wide, first, heads):
    for h in range(heads):
        out_ref[first + h * HEAD_DIM : first + (h + 1) * HEAD_DIM, :] = wide[h * WIDE : h * WIDE + HEAD_DIM, :]


def fill_grads(do_ref, inner_ref, rows, places, e, wide_ref, att, heads):
    grad = nt(e, wide_ref[...]).astype(bf16)
    ones = jnp.ones((8, WIDE), bf16)
    for h in range(heads):
        part = grad[:, h * WIDE : (h + 1) * WIDE]
        do_ref[h, rows, :] = part
        product = part.astype(f32) * att[:, h * WIDE : (h + 1) * WIDE].astype(f32)
        high = product.astype(bf16)
        inner_ref[h, :, places] = nt(ones, high) + nt(ones, (product - high.astype(f32)).astype(bf16))


def back_block(q_ref, k_ref, v_ref, do_ref, inner_ref, dq_ref, dk_ref, dv_ref, h, rows, places, count, key_end, causal):
    q = q_ref[h, rows, :]
    d = do_ref[h, rows, :]
    k = k_ref[h, :key_end, :]
    v = v_ref[h, :key_end, :]
    p = jnp.exp2(nt(k, q))
    if causal:
        r = lax.broadcasted_iota(jnp.int32, (count, count), 0)
        c = lax.broadcasted_iota(jnp.int32, (count, count), 1)
        diagonal = jnp.where(r <= c, p[key_end - count :], 0.0)
        p = diagonal if key_end == count else jnp.concatenate([p[: key_end - count], diagonal], 0)
    ds = (p * (nt(v, d) - inner_ref[h, 0:1, places])).astype(bf16)
    dv = nn(p.astype(bf16), d)
    dk = nn(ds, q)
    dv_ref[h, :key_end, :] += dv
    dk_ref[h, :key_end, :] += dk
    dq_ref[h, rows, :] = tn(k, ds).T


def pack_heads(source, rows, heads, factor):
    return jnp.concatenate([source[h, rows, :HEAD_DIM] * factor for h in range(heads)], 1).astype(bf16)


def norm(resid):
    center = resid - jnp.mean(resid, -1, keepdims=True)
    scale = lax.rsqrt(jnp.mean(center * center, -1, keepdims=True) + EPS)
    return center * scale, scale


def norm_back(grad, gain, unit, scale):
    lifted = grad * gain
    first = jnp.mean(lifted, -1, keepdims=True)
    second = jnp.mean(lifted * unit, -1, keepdims=True)
    return scale * (lifted - first - unit * second)


def gelu_pair(value):
    scaled = value * 0.7071067811865476
    density = jnp.exp(-scaled * scaled) * 0.3989422804014327
    below = 0.5 * (1.0 + lax.erf(scaled))
    return value * below, below + value * density


BLOCK = 512
SPAN = 256
ROW, TGT, SRC, CORE_AT, BIT = 0, 1, 3, 5, 6
FACTOR = HEAD_DIM ** (-0.5) * LOG2E


def vector(ref):
    return ref[...].reshape(1, ref.shape[0])


def branch_of(shares, blocks):
    own0, own1, got0, got1 = shares
    first = pl.program_id(0) < blocks // 2
    own = jnp.where(first, own0[...], own1[...]).astype(f32)
    return own + jnp.where(first, got0[...], got1[...]).astype(f32)


def put_part(first_ref, second_ref, value, blocks):
    at = pl.program_id(0)

    @pl.when(at < blocks // 2)
    def _():
        first_ref[...] = value

    @pl.when(at >= blocks // 2)
    def _():
        second_ref[...] = value


def rows_at(size):
    return pl.ds(pl.multiple_of(pl.program_id(0) * size, size), size)


def project_own_kernel(
    s_ref, x_ref, m_ref, sq_ref, sk_ref, sv_ref, cq_ref, ck_ref, cv_ref, so_ref, co_ref,
    q_ref, k_ref, v_ref, k_out_ref, v_out_ref, mk_ref, mv_ref, wa_ref, cwa_ref, half_out_ref, half_cw_ref, *, heads,
):
    each = heads * HEAD_DIM
    at = pl.program_id(0)

    @pl.when(at == 0)
    def _():
        for n, ref in enumerate((sq_ref, sk_ref, sv_ref)):
            wa_ref[n * each : (n + 1) * each, :] = ref[...]
        for n, ref in enumerate((cq_ref, ck_ref, cv_ref)):
            cwa_ref[n * each : (n + 1) * each, :] = ref[...]
        half_out_ref[...] = jnp.where(s_ref[BIT] == 0, so_ref[...], co_ref[...])
        half = half_cw_ref.shape[0]
        half_cw_ref[...] = cwa_ref[pl.ds(pl.multiple_of(s_ref[BIT + 1] * half, 16), half), :]

    limit = s_ref[TGT + s_ref[ROW]]
    memory_limit = s_ref[SRC + s_ref[ROW]]
    rows = pl.ds(0, BLOCK)
    acc = nt(x_ref[...], wa_ref[...])
    fill_queries(q_ref, rows, BLOCK, acc[:, :each] * FACTOR, heads)
    fill_keys(k_ref, v_ref, rows, at * BLOCK, BLOCK, acc[:, each:], heads, limit)
    k_out_ref[...] = k_ref[...]
    v_out_ref[...] = v_ref[...]
    acc = nt(m_ref[...], cwa_ref[each:, :])
    fill_keys(mk_ref, mv_ref, rows, at * BLOCK, BLOCK, acc, heads, memory_limit)


def causal_blocks(q_ref, k_ref, v_ref, att_ref, heads):
    at = pl.program_id(0)
    for block in range(k_ref.shape[1] // BLOCK):

        @pl.when(at == block)
        def _():
            for h in range(heads):
                attend_block(q_ref, k_ref, v_ref, att_ref, h, pl.ds(0, BLOCK), BLOCK, (block + 1) * BLOCK, True)


def self_own_kernel(s_ref, q_in_ref, k_ref, v_ref, up_ref, down_ref, q_ref, att_ref, halves_ref, mark_ref, *, heads):
    half = up_ref.shape[0]
    halves_ref[:half, :] = up_ref[...]
    halves_ref[half:, :] = down_ref[...]
    mark_ref[...] = jnp.zeros_like(mark_ref)
    q_ref[...] = q_in_ref[...]
    causal_blocks(q_ref, k_ref, v_ref, att_ref, heads)


def self_other_kernel(s_ref, x_ref, near_ref, far_ref, w_ref, q_ref, k_out_ref, v_out_ref, att_ref, k_ref, v_ref, *, heads):
    each = heads * HEAD_DIM
    at = pl.program_id(0)

    @pl.when(at == 0)
    def _():
        put_halves(w_ref, near_ref, far_ref, s_ref[BIT])

    acc = nt(x_ref[...], w_ref[...])
    fill_queries(q_ref, pl.ds(0, BLOCK), BLOCK, acc[:, :each] * FACTOR, heads)
    fill_keys(k_ref, v_ref, rows_at(BLOCK), at * BLOCK, BLOCK, acc[:, each:], heads, s_ref[TGT + s_ref[ROW]])
    k_out_ref[...] = k_ref[:, rows_at(BLOCK), :]
    v_out_ref[...] = v_ref[:, rows_at(BLOCK), :]
    causal_blocks(q_ref, k_ref, v_ref, att_ref, heads)


def self_out_kernel(
    s_ref, atta_ref, attb_ref, soa_ref, near_ref, far_ref, part0_ref, part1_ref, sob_ref, cob_ref, wide_ref, *, heads, blocks
):
    @pl.when(pl.program_id(0) == 0)
    def _():
        low = s_ref[BIT] == 0
        sob_ref[...] = jnp.where(low, near_ref[...], far_ref[...])
        cob_ref[...] = jnp.where(low, far_ref[...], near_ref[...])
        widen_out(wide_ref.at[0], soa_ref, heads)
        widen_out(wide_ref.at[1], sob_ref, heads)

    part = nn(atta_ref[...], wide_ref[0]) + nn(attb_ref[...], wide_ref[1])
    put_part(part0_ref, part1_ref, part.astype(bf16), blocks)


def cross_blocks(q_ref, k_ref, v_ref, att_ref, heads, limit):
    step = 256
    live = (limit + step - 1) // step
    for count in range(1, k_ref.shape[1] // step + 1):

        @pl.when(live == count)
        def _():
            for h in range(heads):
                attend_block(q_ref, k_ref, v_ref, att_ref, h, pl.ds(0, BLOCK), BLOCK, count * step, False)


def cross_own_kernel(
    s_ref, x_ref, own0, own1, got0, got1, gain_ref, shift_ref, cq_ref, k_ref, v_ref,
    h_ref, hl_ref, unit_ref, scale_ref, q_ref, att_ref, *, heads, blocks,
):
    unit, scale = norm(x_ref[...].astype(f32) + branch_of((own0, own1, got0, got1), blocks))
    h = unit * vector(gain_ref) + vector(shift_ref)
    h_ref[...] = h
    unit_ref[...] = unit.astype(bf16)
    scale_ref[...] = scale
    low = h.astype(bf16)
    hl_ref[...] = low
    fill_queries(q_ref, pl.ds(0, BLOCK), BLOCK, nt(low, cq_ref[...]) * FACTOR, heads)
    cross_blocks(q_ref, k_ref, v_ref, att_ref, heads, s_ref[SRC + s_ref[ROW]])


def put_halves(target_ref, near_ref, far_ref, high):
    half = near_ref.shape[0]
    target_ref[pl.ds(pl.multiple_of(high * half, 16), half), :] = near_ref[...]
    target_ref[pl.ds(pl.multiple_of((1 - high) * half, 16), half), :] = far_ref[...]


def cross_other_kernel(s_ref, m_ref, hl_ref, near_ref, far_ref, cwb_ref, k_ref, v_ref, q_ref, att_ref, *, heads):
    each = heads * HEAD_DIM
    limit = s_ref[SRC + s_ref[ROW]]

    @pl.when(pl.program_id(0) == 0)
    def _():
        put_halves(cwb_ref, near_ref, far_ref, s_ref[BIT + 1])

        @pl.loop(0, m_ref.shape[0], step=BLOCK)
        def _(start):
            rows = pl.ds(pl.multiple_of(start, BLOCK), BLOCK)
            fill_keys(k_ref, v_ref, rows, start, BLOCK, nt(m_ref[rows, :], cwb_ref[each:, :]), heads, limit)

    fill_queries(q_ref, pl.ds(0, BLOCK), BLOCK, nt(hl_ref[...], cwb_ref[:each, :]) * FACTOR, heads)
    cross_blocks(q_ref, k_ref, v_ref, att_ref, heads, limit)


def cross_out_kernel(atta_ref, attb_ref, coa_ref, cob_ref, part0_ref, part1_ref, wide_ref, *, heads, blocks):
    @pl.when(pl.program_id(0) == 0)
    def _():
        widen_out(wide_ref.at[0], coa_ref, heads)
        widen_out(wide_ref.at[1], cob_ref, heads)

    part = nn(atta_ref[...], wide_ref[0]) + nn(attb_ref[...], wide_ref[1])
    put_part(part0_ref, part1_ref, part.astype(bf16), blocks)


def ffn_own_kernel(
    h_in_ref, own0, own1, got0, got1, gain_ref, shift_ref, up_ref, down_ref,
    h_ref, hl_ref, unit_ref, scale_ref, act_ref, slope_ref, term_ref, *, blocks,
):
    unit, scale = norm(h_in_ref[...] + branch_of((own0, own1, got0, got1), blocks))
    h = unit * vector(gain_ref) + vector(shift_ref)
    h_ref[...] = h
    unit_ref[...] = unit.astype(bf16)
    scale_ref[...] = scale
    low = h.astype(bf16)
    hl_ref[...] = low
    act, slope = gelu_pair(nn(low, up_ref[...]))
    act = act.astype(bf16)
    act_ref[...] = act
    slope_ref[...] = slope.astype(bf16)
    term_ref[...] = nn(act, down_ref[...])


def ffn_other_kernel(
    s_ref, hl_ref, term_ref, up_near_ref, up_far_ref, down_near_ref, down_far_ref,
    part0_ref, part1_ref, act_ref, slope_ref, up_ref, down_ref, *, blocks,
):
    @pl.when(pl.program_id(0) == 0)
    def _():
        put_halves(up_ref, up_near_ref, up_far_ref, s_ref[BIT])
        put_halves(down_ref, down_near_ref, down_far_ref, s_ref[BIT + 1])

    act, slope = gelu_pair(nn(hl_ref[...], up_ref[...]))
    act = act.astype(bf16)
    act_ref[...] = act
    slope_ref[...] = slope.astype(bf16)
    put_part(part0_ref, part1_ref, (term_ref[...] + nn(act, down_ref[...])).astype(bf16), blocks)


def ffn_back_kernel(
    s_ref, h_ref, own0, own1, got0, got1, cot_ref, gain_ref, shift_ref, upa_ref, upb_ref, downa_ref, downb_ref, slopea_ref, slopeb_ref,
    part0_ref, part1_ref, out_ref, d_ref, e_ref, prea_ref, preb_ref, sums_ref, *, blocks,
):
    limit = s_ref[TGT + s_ref[ROW]]
    at = pl.program_id(0)

    @pl.when(at == 0)
    def _():
        sums_ref[...] = jnp.zeros_like(sums_ref)

    gain = vector(gain_ref)
    unit, scale = norm(h_ref[...] + branch_of((own0, own1, got0, got1), blocks))
    out_ref[...] = (unit * gain + vector(shift_ref)).astype(bf16)
    index = at * SPAN + lax.broadcasted_iota(jnp.int32, (SPAN, 1), 0)
    grad = jnp.where(index < limit, cot_ref[...].astype(f32), 0.0)
    sums_ref[0:1, :] += jnp.sum(grad * unit, 0, keepdims=True)
    sums_ref[1:2, :] += jnp.sum(grad, 0, keepdims=True)
    d = norm_back(grad, gain, unit, scale)
    d_ref[...] = d
    e = d.astype(bf16)
    e_ref[...] = e
    part = None
    for up_ref, down_ref, slope_ref, pre_ref in (
        (upa_ref, downa_ref, slopea_ref, prea_ref),
        (upb_ref, downb_ref, slopeb_ref, preb_ref),
    ):
        pre = (nt(e, down_ref[...]) * slope_ref[...].astype(f32)).astype(bf16)
        pre_ref[...] = pre
        term = nt(pre, up_ref[...])
        part = term if part is None else part + term
    put_part(part0_ref, part1_ref, part.astype(bf16), blocks)


def ffn_grad_kernel(s_ref, h_ref, act_ref, e_ref, pre_ref, up_ref, send_ref, keep_ref):
    up_ref[...] = tn(h_ref[...], pre_ref[...]).astype(bf16)
    down = tn(act_ref[...], e_ref[...]).astype(bf16)
    mine = pl.program_id(0) == s_ref[BIT]

    @pl.when(mine)
    def _():
        keep_ref[...] = down

    @pl.when(jnp.logical_not(mine))
    def _():
        send_ref[...] = down


def norm_step(d_in_ref, shares, gain, unit_ref, scale_ref, d_ref, e_ref, sums_ref, blocks):
    @pl.when(pl.program_id(0) == 0)
    def _():
        sums_ref[...] = jnp.zeros_like(sums_ref)

    grad = d_in_ref[...] + branch_of(shares, blocks)
    unit = unit_ref[...].astype(f32)
    sums_ref[0:1, :] += jnp.sum(grad * unit, 0, keepdims=True)
    sums_ref[1:2, :] += jnp.sum(grad, 0, keepdims=True)
    d = norm_back(grad, gain, unit, scale_ref[...])
    d_ref[...] = d
    e = d.astype(bf16)
    e_ref[...] = e
    return e


def cross_back_heads(s_ref, q_ref, k_ref, v_ref, do_ref, inner_ref, dqo_ref, dkv_ref, dq_ref, dk_ref, dv_ref, heads, blocks):
    at = pl.program_id(0)
    source = k_ref.shape[1]

    @pl.when(at == 0)
    def _():
        dk_ref[...] = jnp.zeros_like(dk_ref)
        dv_ref[...] = jnp.zeros_like(dv_ref)

    step = 256
    live = (s_ref[SRC + s_ref[ROW]] + step - 1) // step
    rows = pl.ds(0, BLOCK)
    for count in range(1, source // step + 1):

        @pl.when(live == count)
        def _():
            @pl.loop(0, heads)
            def _(h):
                back_block(
                    q_ref, k_ref, v_ref, do_ref, inner_ref, dq_ref, dk_ref, dv_ref, h, rows, rows_at(BLOCK), BLOCK, count * step, False
                )

    dqo_ref[...] = pack_heads(dq_ref, rows, heads, HEAD_DIM ** (-0.5))

    @pl.when(at == blocks - 1)
    def _():
        @pl.loop(0, source, step=BLOCK)
        def _(start):
            some = pl.ds(pl.multiple_of(start, BLOCK), BLOCK)
            dkv_ref[some, :] = jnp.concatenate(
                [pack_heads(dk_ref, some, heads, LN2), pack_heads(dv_ref, some, heads, 1.0)], 1
            )


def cross_back_other_kernel(
    s_ref, d_in_ref, own0, own1, got0, got1, gain_ref, unit_ref, scale_ref, coa_ref, cob_ref, atta_ref, attb_ref,
    q_ref, k_ref, v_ref,
    d_ref, e_ref, sums_ref, doa_ref, innera_ref, dqo_ref, dkv_ref, wide_ref, do_ref, inner_ref, dq_ref, dk_ref, dv_ref, *, heads, blocks,
):
    @pl.when(pl.program_id(0) == 0)
    def _():
        widen_out(wide_ref.at[0], coa_ref, heads)
        widen_out(wide_ref.at[1], cob_ref, heads)

    e = norm_step(
        d_in_ref, (own0, own1, got0, got1), vector(gain_ref), unit_ref, scale_ref, d_ref, e_ref, sums_ref, blocks
    )
    rows, places = pl.ds(0, BLOCK), rows_at(BLOCK)
    fill_grads(doa_ref, innera_ref, rows, places, e, wide_ref.at[0], atta_ref[...], heads)
    fill_grads(do_ref, inner_ref, rows, places, e, wide_ref.at[1], attb_ref[...], heads)
    cross_back_heads(s_ref, q_ref, k_ref, v_ref, do_ref, inner_ref, dqo_ref, dkv_ref, dq_ref, dk_ref, dv_ref, heads, blocks)


def cross_back_own_kernel(
    s_ref, q_ref, k_ref, v_ref, do_ref, inner_ref, dqb_ref, cqa_ref, cwb_ref,
    part0_ref, part1_ref, dqo_ref, dkv_ref, dq_ref, dk_ref, dv_ref, *, heads, blocks,
):
    cross_back_heads(s_ref, q_ref, k_ref, v_ref, do_ref, inner_ref, dqo_ref, dkv_ref, dq_ref, dk_ref, dv_ref, heads, blocks)
    part = nn(dqo_ref[...], cqa_ref[...]) + nn(dqb_ref[...], cwb_ref[: heads * HEAD_DIM, :])
    put_part(part0_ref, part1_ref, part.astype(bf16), blocks)


def cross_grad_kernel(s_ref, h_ref, m_ref, att_ref, e_ref, dq_ref, dkv_ref, g_ref):
    each = dq_ref.shape[1]
    g_ref[:each, :] = tn(dq_ref[...], h_ref[...]).astype(bf16)
    g_ref[each : 3 * each, :] = tn(dkv_ref[...], m_ref[...]).astype(bf16)
    narrow_out(g_ref, tn(att_ref[...], e_ref[...]).astype(bf16), 3 * each, each // HEAD_DIM)


def pass_kernel(s_ref, in_ref, out_ref):
    out_ref[...] = in_ref[...]


def relay_kernel(s_ref, in_ref, first_ref, second_ref):
    half = first_ref.shape[0]
    first_ref[...] = in_ref[:half, :]
    second_ref[...] = in_ref[half:, :]


def memory_grad_kernel(s_ref, a_ref, b_ref, wa_ref, wb_ref, send_ref, keep_ref):
    each = a_ref.shape[1] // 2
    part = (nn(a_ref[...], wa_ref[each:, :]) + nn(b_ref[...], wb_ref[each:, :])).astype(bf16)
    mine = pl.program_id(0) == s_ref[CORE_AT]

    @pl.when(mine)
    def _():
        keep_ref[...] = part

    @pl.when(jnp.logical_not(mine))
    def _():
        send_ref[...] = part


def norm_one_back_kernel(
    s_ref, d_in_ref, own0, own1, got0, got1, gain_ref, unit_ref, scale_ref, soa_ref, sob_ref, atta_ref, attb_ref,
    sums_two_ref, sums_three_ref, d_ref, doa_ref, dob_ref, innera_ref, innerb_ref, ra_ref, rb_ref, e_ref, sums_ref, wide_ref, *, heads, blocks,
):
    @pl.when(pl.program_id(0) == 0)
    def _():
        widen_out(wide_ref.at[0], soa_ref, heads)
        widen_out(wide_ref.at[1], sob_ref, heads)

    each = heads * HEAD_DIM
    rows = rows_at(SPAN)
    e = norm_step(
        d_in_ref, (own0, own1, got0, got1), vector(gain_ref), unit_ref, scale_ref, d_ref, e_ref.at[rows, :], sums_ref, blocks
    )
    fill_grads(doa_ref, innera_ref, pl.ds(0, SPAN), rows, e, wide_ref.at[0], atta_ref[rows, :], heads)
    fill_grads(dob_ref, innerb_ref, pl.ds(0, SPAN), rows, e, wide_ref.at[1], attb_ref[rows, :], heads)

    @pl.when(pl.program_id(0) == blocks - 1)
    def _():
        norms = jnp.concatenate(
            [sums_ref[:2, :], sums_two_ref[:2, :], sums_three_ref[:2, :], jnp.zeros((10, d_in_ref.shape[1]), f32)], 0
        ).astype(bf16)
        for att_ref, r_ref in ((atta_ref, ra_ref), (attb_ref, rb_ref)):
            narrow_out(r_ref, tn(att_ref[...], e_ref[...]).astype(bf16), 0, heads)
            r_ref[each:, :] = norms


def self_back_kernel(s_ref, x_ref, q_ref, k_ref, v_ref, do_ref, inner_ref, dqkv_ref, gw_ref, dq_ref, dk_ref, dv_ref, *, heads, blocks):
    at = pl.program_id(0)
    each = heads * HEAD_DIM
    length = k_ref.shape[1]

    @pl.when(at == 0)
    def _():
        dk_ref[...] = jnp.zeros_like(dk_ref)
        dv_ref[...] = jnp.zeros_like(dv_ref)

    rows = pl.ds(0, SPAN)
    for block in range(blocks):

        @pl.when(at == block)
        def _():
            @pl.loop(0, heads)
            def _(h):
                back_block(
                    q_ref, k_ref, v_ref, do_ref, inner_ref, dq_ref, dk_ref, dv_ref, h, rows, pl.ds(block * SPAN, SPAN), SPAN,
                    (block + 1) * SPAN, True,
                )

    dqkv_ref[rows_at(SPAN), :each] = pack_heads(dq_ref, rows, heads, HEAD_DIM ** (-0.5))

    @pl.when(at == blocks - 1)
    def _():
        @pl.loop(0, length, step=BLOCK)
        def _(start):
            some = pl.ds(pl.multiple_of(start, BLOCK), BLOCK)
            dqkv_ref[some, each:] = jnp.concatenate(
                [pack_heads(dk_ref, some, heads, LN2), pack_heads(dv_ref, some, heads, 1.0)], 1
            )
        gw_ref[...] = tn(dqkv_ref[...], x_ref[...]).astype(bf16)


def tokens_grad_kernel(s_ref, d_ref, a_ref, b_ref, wa_ref, wb_ref, send_ref, keep_ref):
    part = nn(a_ref[...], wa_ref[...]) + nn(b_ref[...], wb_ref[...])
    mine = pl.program_id(0) == s_ref[CORE_AT]

    @pl.when(mine)
    def _():
        keep_ref[...] = d_ref[...] + part

    @pl.when(jnp.logical_not(mine))
    def _():
        send_ref[...] = part.astype(bf16)


def place_kernel(s_ref, *refs, shift):
    pieces, out_ref, mark_ref = refs[:-2], refs[-2], refs[-1]
    half = out_ref.shape[0]
    row, core, at = s_ref[ROW], s_ref[CORE_AT], pl.program_id(0)
    mark_ref[...] = jnp.zeros_like(mark_ref)
    if shift:
        sources = [
            (pieces[0].at[:half, :], 2 * row), (pieces[0].at[half:, :], 2 * row + 1),
            (pieces[1], 2 * (1 - row) + core), (pieces[2], 2 * (1 - row) + 1 - core),
        ]
    else:
        sources = [
            (pieces[0].at[:half, :], 2 * row + core), (pieces[1].at[:half, :], 2 * row + 1 - core),
            (pieces[0].at[half:, :], 2 * (1 - row) + core), (pieces[1].at[half:, :], 2 * (1 - row) + 1 - core),
        ]
    for ref, place in sources:

        @pl.when(at == place)
        def _():
            out_ref[...] = ref[...]


def step_kernel(s_ref, *refs, plans):
    scratch = refs[-1]
    inputs = sum(plan[1] for plan in plans)
    ins, outs = list(refs[:inputs]), list(refs[inputs:-1])
    for kind, count, rows, bit, cuts, parts in plans:
        mine, ins = ins[:count], ins[count:]
        if kind == SUM:
            at = 0
            for a_ref, b_ref in zip(mine[: count // 2], mine[count // 2 :]):
                size = min(a_ref.shape[0], rows - at)
                scratch[at : at + size, :] = (a_ref[:size, :].astype(f32) + b_ref[:size, :].astype(f32)).astype(bf16)
                at += size
            if at < rows:
                scratch[at:rows, :] = jnp.zeros((rows - at, scratch.shape[1]), bf16)
            if bit is None:
                outs.pop(0)[...] = scratch[:rows, :]
            else:
                half, high = rows // 2, s_ref[BIT + bit]
                outs.pop(0)[...] = scratch[pl.ds(pl.multiple_of((1 - high) * half, 16), half), :]
                outs.pop(0)[...] = scratch[pl.ds(pl.multiple_of(high * half, 16), half), :]
        elif kind == TWIN:
            for part in range(2):
                total = (mine[part][...].astype(f32) + mine[part + 2][...].astype(f32)).astype(bf16)
                scratch[part * rows : (part + 1) * rows, :] = total
            half, high = rows // 2, s_ref[BIT + bit]
            send_ref, keep_ref = outs.pop(0), outs.pop(0)
            for part in range(2):
                place = slice(part * half, (part + 1) * half)
                send_ref[place, :] = scratch[pl.ds(pl.multiple_of(part * rows + (1 - high) * half, 16), half), :]
                keep_ref[place, :] = scratch[pl.ds(pl.multiple_of(part * rows + high * half, 16), half), :]
        elif kind == SPLIT:
            total = (mine[0][...].astype(f32) + mine[1][...].astype(f32)).astype(bf16)
            outs.pop(0)[...] = total[: rows // 2, :]
            outs.pop(0)[...] = total[rows // 2 :, :]
        elif kind == LAST:
            outs.pop(0)[...] = mine[0][-rows:, :].astype(f32) + mine[1][-rows:, :].astype(f32)
        elif kind == PASS:
            outs.pop(0)[...] = mine[0][...]
        elif kind == STACK:
            size, target = mine[0].shape[0], outs.pop(0)
            target[:size, :] = mine[0][...]
            target[size:, :] = mine[1][...]
        else:
            high, size = s_ref[BIT + bit], mine[0].shape[0] // parts
            target = outs.pop(0) if kind == PACK else scratch
            for part in range(parts):
                some, first = slice(part * size, (part + 1) * size), 2 * part * size
                target[pl.ds(pl.multiple_of(first + high * size, 16), size), :] = mine[0][some, :]
                target[pl.ds(pl.multiple_of(first + (1 - high) * size, 16), size), :] = mine[1][some, :]
            for first, size in cuts:
                outs.pop(0)[...] = scratch[first : first + size, :].astype(f32)


class Row:
    def __init__(self, array, length, how=WHOLE):
        self.array, self.length, self.how = array, length, how


class Part:
    def __init__(self, array, how=ROWS, pick=None):
        self.array, self.how, self.pick = array, how, pick


class Pick:
    def __init__(self, array, scalar, parts):
        self.array, self.scalar, self.parts = array, scalar, parts


class Far:
    def __init__(self, array):
        self.array = array


def block_of(shape, how, blocks, pick=None, once=False):
    rank = len(shape)
    if rank == 1:
        return pl.BlockSpec(shape, lambda *a: (0,))
    if isinstance(how, tuple):
        how, pick = how
    if how == WHOLE:
        return pl.BlockSpec(shape, lambda *a: (0,) * rank, pipeline_mode=pl.Buffered(1) if once else None)
    pick = pick or (lambda i: i)
    dim = rank - 1 if how == COLUMNS else rank - 2
    parts = blocks // 2 if how == HALF else blocks
    block = tuple(n // parts if d == dim else n for d, n in enumerate(shape))
    return pl.BlockSpec(block, lambda i, *a: tuple(pick(i) if d == dim else 0 for d in range(rank)))


def row_of(item, blocks):
    width = item.array.shape[1]
    if item.how == WHOLE:
        return pl.BlockSpec((item.length, width), lambda i, s: (s[0], 0))
    if item.how == ROWS:
        return pl.BlockSpec((item.length // blocks, width), lambda i, s: (s[0] * blocks + i, 0))
    if item.how[0] == PART:
        return pl.BlockSpec((item.length // blocks, width), lambda i, s: (s[item.how[1]] * blocks + i, 0))
    return pl.BlockSpec((item.length, width // blocks), lambda i, s: (s[0], i))


class Held:
    def __init__(self, array, how=ROWS):
        self.array, self.how = array, how


def view_of(shape, how, blocks):
    rank = len(shape)
    if how == WHOLE:
        return None
    if how == ROWS:
        size = shape[-2] // blocks

        def rows(ref):
            place = pl.ds(pl.multiple_of(pl.program_id(0) * size, size), size)
            return ref.at[place, :] if rank == 2 else ref.at[:, place, :]

        return rows
    size = shape[-1] // blocks
    return lambda ref: ref.at[:, pl.ds(pl.multiple_of(pl.program_id(0) * size, size), size)]


def call(kernel, blocks, inputs, outputs, scalars=None, scratch=(), micros=5.0, limit=LIMIT, after=(), scale=0.9):
    specs, arrays, views = [], [], []
    here = pl.BlockSpec(memory_space=pltpu.VMEM)
    for item in inputs:
        view = None
        if isinstance(item, Row):
            specs.append(row_of(item, blocks))
            arrays.append(pltpu.with_memory_space_constraint(item.array, pltpu.HBM))
        elif isinstance(item, Part):
            specs.append(block_of(item.array.shape, item.how, blocks, item.pick))
            arrays.append(item.array)
        elif isinstance(item, Pick):
            rows, width = item.array.shape
            specs.append(pl.BlockSpec((rows // item.parts, width), functools.partial(lambda at, i, s: (s[at], 0), item.scalar)))
            arrays.append(pltpu.with_memory_space_constraint(item.array, pltpu.HBM))
        elif isinstance(item, Far):
            specs.append(block_of(item.array.shape, WHOLE, blocks, once=True))
            arrays.append(pltpu.with_memory_space_constraint(item.array, pltpu.HBM))
        elif isinstance(item, Held):
            specs.append(here)
            arrays.append(pltpu.with_memory_space_constraint(item.array, pltpu.VMEM))
            view = view_of(item.array.shape, item.how, blocks)
        else:
            specs.append(block_of(item.shape, WHOLE, blocks, once=True))
            arrays.append(item)
        views.append(view)
    for item in after:
        specs.append(pl.BlockSpec(memory_space=pl.ANY))
        arrays.append(pltpu.with_memory_space_constraint(item.array, pltpu.HBM) if isinstance(item, Far) else item)
        views.append(SKIP)
    shapes, out_specs = [], []
    for shape, dtype, how in outputs:
        if how[:4] == "held":
            shapes.append(pltpu.VMEM(shape, dtype))
            out_specs.append(here)
            views.append(view_of(shape, how[5:], blocks))
        else:
            far = how[:3] == "hbm"
            shapes.append(pltpu.HBM(shape, dtype) if far else jax.ShapeDtypeStruct(shape, dtype))
            out_specs.append(block_of(shape, how[4:] if far else how, blocks))
            views.append(None)
    lead = 0 if scalars is None else 1

    def viewed(*refs):
        passed = list(refs[:lead])
        for ref, view in zip(refs[lead : lead + len(views)], views):
            if view == SKIP:
                continue
            passed.append(ref if view is None else view(ref))
        return kernel(*passed, *refs[lead + len(views) :])

    settings = dict(
        out_shape=shapes,
        compiler_params=pltpu.CompilerParams(vmem_limit_bytes=limit * MIB, dimension_semantics=(ARBITRARY,)),
        cost_estimate=pl.CostEstimate(flops=int(micros * scale * 1.0e9), bytes_accessed=0, transcendentals=0),
        name=getattr(kernel, "func", kernel).__name__,
    )
    if scalars is None:
        return pl.pallas_call(
            viewed, grid=(blocks,), in_specs=specs, out_specs=out_specs, scratch_shapes=list(scratch), **settings
        )(*arrays)
    grid_spec = pltpu.PrefetchScalarGridSpec(
        num_scalar_prefetch=1, grid=(blocks,), in_specs=specs, out_specs=out_specs, scratch_shapes=list(scratch)
    )
    return pl.pallas_call(viewed, grid_spec=grid_spec, **settings)(scalars, *arrays)


def local(
    size, tokens, memory, cotangent, tgt_len, src_len, self_query, self_key, self_value, self_out,
    cross_query, cross_key, cross_value, cross_out, ffn_up, ffn_down,
    gain_one, shift_one, gain_two, shift_two, gain_three, shift_three,
):
    width = tokens.shape[1]
    length = tokens.shape[0] // 2
    source = memory.shape[0] // 2
    each = self_query.shape[1]
    heads = each // HEAD_DIM
    hidden = ffn_up.shape[1]
    place = lax.axis_index("tp").astype(jnp.int32)
    group = lax.axis_index("dp").astype(jnp.int32)
    scalars = jnp.concatenate(
        [jnp.stack([place // 2]), tgt_len, src_len, jnp.stack([place % 2] + [(group >> b) & 1 for b in range(3)])]
    )
    big, small, third = length // BLOCK, length // SPAN, width // SPAN
    short = size == 8

    def across(value):
        return lax.ppermute(value, "tp", ACROSS)

    def sibling(value):
        return lax.ppermute(value, "tp", CORE)

    def along(value, bit):
        return lax.ppermute(value, "dp", [(i, i ^ (1 << bit)) for i in range(size)])

    def shares(part, blocks):
        per = blocks // 2
        first, second = (lambda i: jnp.minimum(i, per - 1)), (lambda i: jnp.maximum(i - per, 0))
        got = [sibling(p) for p in part]
        return [Part(v, HALF, pick) for v, pick in zip((*part, *got), (first, second) * 2)]

    def part_shapes(blocks):
        per = blocks // 2
        first, second = (lambda i: jnp.minimum(i, per - 1)), (lambda i: jnp.maximum(i - per, 0))
        return [((length // 2, width), bf16, (HALF, pick)) for pick in (first, second)]

    head_rows = ((heads, length, WIDE), bf16, FAR_ROWS)
    head_held = ((heads, length, WIDE), bf16, HELD_ROWS)
    key_held = ((heads, source, WIDE), bf16, HELD_ROWS)
    held = ((length, width), f32, HELD_ROWS)
    held_low = ((length, width), bf16, HELD_ROWS)
    column = ((length, 1), f32, HELD_ROWS)
    att_held = ((length, heads * WIDE), bf16, HELD_ROWS)
    dq_held = ((length, each), bf16, HELD_ROWS)
    hid = ((length, hidden), bf16, HELD_ROWS)
    sums = ((8, width), f32, WHOLE)
    low = ((length, width), bf16, ROWS)
    square = ((width, hidden), bf16, ROWS)
    half_low = ((length // 2, width), bf16, WHOLE)
    out_shape = ((each, width), bf16, WHOLE)
    qkv = functools.partial(pltpu.VMEM, (heads, length, WIDE))
    wide_out = pltpu.VMEM((2, heads * WIDE, width), bf16)
    inner_held = ((heads, 8, length), f32, HELD_WHOLE)

    w_parts = (self_query.T, self_key.T, self_value.T)
    c_parts = (cross_query.T, cross_key.T, cross_value.T)
    bit = scalars[BIT]
    w_half = lax.dynamic_slice_in_dim(jnp.concatenate(w_parts, 0), bit * (3 * each // 2), 3 * each // 2, 0)
    w_near = across(w_half)
    q_new, k_new, v_new, k_a, v_a, ck_a, cv_a, w_a, cw_a, o_half, cw_half = call(
        functools.partial(project_own_kernel, heads=heads), big,
        [
            Row(tokens, length, ROWS), Row(memory, source, ROWS), *(Far(v) for v in (*w_parts, *c_parts, self_out, cross_out)),
        ],
        [
            head_held, head_held, head_held, head_rows, head_rows, key_held, key_held, ((3 * each, width), bf16, WHOLE),
            ((3 * each, width), bf16, WHOLE), out_shape, ((3 * each // 2, width), bf16, WHOLE),
        ],
        scalars, micros=7, scale=0.4,
    )
    o_near = across(o_half)
    cw_near = across(cw_half)
    (w_near,) = call(
        pass_kernel, 1, [w_near], [((3 * each // 2, width), bf16, WHOLE)], scalars, micros=1, scale=0.4, after=[o_half]
    )
    w_far = along(w_near, 0)
    quarter = ((hidden // 2, width), bf16, WHOLE)
    q_a, att_a, ffn_half, mark = call(
        functools.partial(self_own_kernel, heads=heads), big,
        [Held(q_new), Held(k_new, WHOLE), Held(v_new, WHOLE), Pick(ffn_up, BIT, 2), Pick(ffn_down, BIT + 1, 2)],
        [head_rows, att_held, ((width, width), bf16, WHOLE), ((8, WIDE), f32, WHOLE)], scalars, micros=6, scale=0.4, after=[w_near],
    )
    ffn_near = across(ffn_half)
    cw_far = along(cw_near, 1)
    (o_near,) = call(pass_kernel, 1, [o_near], [out_shape], scalars, micros=1, scale=0.4, after=[mark])
    o_far = along(o_near, 0)
    w_b, q_b, k_b, v_b, att_b = call(
        functools.partial(self_other_kernel, heads=heads), big, [Row(tokens, length, ROWS), w_near, w_far],
        [((3 * each, width), bf16, WHOLE), head_rows, head_rows, head_rows, att_held], scalars, scratch=[qkv(bf16), qkv(bf16)],
        micros=9, scale=0.4,
    )
    part0, part1, so_b, co_b = call(
        functools.partial(self_out_kernel, heads=heads, blocks=big), big, [Held(att_a), Held(att_b), self_out, o_near, o_far],
        [*part_shapes(big), out_shape, out_shape], scalars, scratch=[wide_out], micros=3, scale=0.4, after=[cw_near],
    )
    h_one, h_one_low, unit_one, scale_one, cq_a, catt_a = call(
        functools.partial(cross_own_kernel, heads=heads, blocks=big), big,
        [Row(tokens, length, ROWS), *shares((part0, part1), big), gain_one, shift_one, c_parts[0], Held(ck_a, WHOLE), Held(cv_a, WHOLE)],
        [held, held_low, held_low, column, head_held, att_held], scalars, micros=10, scale=0.4,
    )
    up_near, down_near = call(
        relay_kernel, 1, [ffn_near], [quarter, quarter], scalars, micros=1, after=[scale_one]
    )
    up_far, down_far = along(up_near, 0), along(down_near, 1)
    cw_b, ck_b, cv_b, cq_b, catt_b = call(
        functools.partial(cross_other_kernel, heads=heads), big,
        [Row(memory, source), Held(h_one_low), cw_near, cw_far],
        [((3 * each, width), bf16, WHOLE), ((heads, source, WIDE), bf16, HELD_WHOLE), ((heads, source, WIDE), bf16, HELD_WHOLE), head_held, att_held],
        scalars, micros=100, scale=1.0, after=[up_near, down_near],
    )
    part0, part1 = call(
        functools.partial(cross_out_kernel, heads=heads, blocks=big), big, [Held(catt_a), Held(catt_b), cross_out, co_b],
        part_shapes(big), scratch=[wide_out], micros=2, scale=0.4, after=[up_far, down_far],
    )
    h_two, h_two_low, unit_two, scale_two, act_a, slope_a, term = call(
        functools.partial(ffn_own_kernel, blocks=big), big,
        [Held(h_one), *shares((part0, part1), big), gain_two, shift_two, Held(ffn_up, WHOLE), Held(ffn_down, WHOLE)],
        [held, held_low, held_low, column, hid, hid, held], micros=7, scale=0.4, limit=24,
    )
    part0, part1, act_b, slope_b, up_b, down_b = call(
        functools.partial(ffn_other_kernel, blocks=big), big,
        [Held(h_two_low), Held(term), up_near, up_far, down_near, down_far],
        [*part_shapes(big), hid, hid, ((width, hidden), bf16, HELD_WHOLE), ((hidden, width), bf16, HELD_WHOLE)], scalars, micros=5, scale=0.4, limit=24,
    )

    part0, part1, out_row, d_three, e_three, pre_a, pre_b, sums_three = call(
        functools.partial(ffn_back_kernel, blocks=small), small,
        [
            Held(h_two), *shares((part0, part1), small), Row(cotangent, length, ROWS), gain_three, shift_three,
            Held(ffn_up, WHOLE), Held(up_b, WHOLE), Held(ffn_down, WHOLE), Held(down_b, WHOLE), Held(slope_a), Held(slope_b),
        ],
        [*part_shapes(small), ((length, width), bf16, FAR_ROWS), held, held_low, hid, hid, sums], scalars, micros=11,
    )
    part = (part0, part1)
    quarter = ((width // 2, hidden), bf16, WHOLE)

    def ffn_grads(act, pre, after=()):
        return call(
            ffn_grad_kernel, 2,
            [Held(h_two_low, COLUMNS), Held(act, COLUMNS), Held(e_three, WHOLE), Held(pre, WHOLE)],
            [square, quarter, quarter], scalars, micros=4, after=after,
        )

    gu_b, send_b, keep_b = ffn_grads(act_b, pre_b)
    gu_got, got_b = across(gu_b), along(send_b, 0)
    gu_a, send_a, keep_a = ffn_grads(act_a, pre_a, [send_b])
    got_a = along(send_a, 0)
    back_scratch = [
        pltpu.VMEM((heads, BLOCK, WIDE), f32), pltpu.VMEM((heads, source, WIDE), f32), pltpu.VMEM((heads, source, WIDE), f32),
    ]
    dkv_held = ((source, 2 * each), bf16, HELD_WHOLE)
    d_two, e_two, sums_two, do_a, inner_a, dcq_b, dckv_b = call(
        functools.partial(cross_back_other_kernel, heads=heads, blocks=big), big,
        [
            Held(d_three), *shares(part, big), gain_two, Held(unit_two), Held(scale_two), cross_out, co_b, Held(catt_a), Held(catt_b), Held(cq_b), Held(ck_b, WHOLE), Held(cv_b, WHOLE),
        ],
        [held, held_low, sums, head_held, inner_held, dq_held, dkv_held], scalars,
        scratch=[wide_out, pltpu.VMEM((heads, BLOCK, WIDE), bf16), pltpu.VMEM((heads, 8, length), f32)] + back_scratch, micros=6,
    )

    def cross_grads(att, dq, dkv, after=()):
        return call(
            cross_grad_kernel, third,
            [
                Held(h_one_low, COLUMNS), Row(memory, source, COLUMNS), Held(att, WHOLE), Held(e_two, COLUMNS),
                Held(dq, WHOLE), Held(dkv, WHOLE),
            ],
            [((4 * each, width), bf16, COLUMNS)], scalars, micros=5, after=after,
        )[0]

    def step(plans, after=(), micros=2):
        inputs, outputs, kernel_plans, counts, most = [], [], [], [], 16
        for kind, arrays, rows, bit, cuts, parts in plans:
            inputs += arrays
            if kind == SUM:
                made = [((rows, width), bf16, WHOLE)] if bit is None else [((rows // 2, width), bf16, WHOLE)] * 2
            elif kind == TWIN:
                made = [((rows, width), bf16, WHOLE)] * 2
                most = max(most, 2 * rows)
            elif kind == SPLIT:
                made = [((rows // 2, width), bf16, WHOLE)] * 2
            elif kind == LAST:
                made = [((rows, width), f32, WHOLE)]
            elif kind in (PACK, STACK, PASS):
                made = [((rows, width), bit if kind == PASS else bf16, WHOLE)]
            else:
                made = [((size, width), f32, FAR_WHOLE) for _, size in cuts]
            if kind in (SUM, WIDEN):
                most = max(most, rows)
            outputs += made
            counts.append(len(made))
            kernel_plans.append((kind, len(arrays), rows, bit, cuts, parts))
        made = list(
            call(
                functools.partial(step_kernel, plans=kernel_plans), 1, inputs, outputs, scalars,
                scratch=[pltpu.VMEM((most, width), bf16)], micros=micros, after=after,
            )
        )
        return [made[sum(counts[:n]) : sum(counts[: n + 1])] for n in range(len(counts))]

    class Chain:
        def __init__(self, mine, got, rows, cuts, bits=(0, 1, 2), back=(2, 1, 0), parts=1):
            self.arrays, self.rows, self.cuts, self.stage = [*mine, *got], rows, cuts, 0
            self.bits, self.back, self.parts = bits, back, parts

        def plan(self):
            count = len(self.bits)
            if self.stage <= count:
                bit = self.bits[self.stage] if self.stage < count else None
                return (SUM, self.arrays, self.rows >> self.stage, bit, (), 1)
            at = self.stage - count
            rows, last = self.rows >> count << at, at == len(self.back)
            bit = self.back[at - 1]
            return (WIDEN if last else PACK, self.arrays, rows, bit, self.cuts if last else (), self.parts if bit < 2 else 1)

        def take(self, made):
            stage, count, self.stage = self.stage, len(self.bits), self.stage + 1
            if stage < count:
                self.arrays = [made[1], along(made[0], self.bits[stage])]
            elif stage < count + len(self.back):
                self.arrays = [made[0], along(made[0], self.back[stage - count])]
            else:
                self.done = made

    def advance(chains, plans=(), after=(), micros=2):
        made = step([c.plan() for c in chains] + list(plans), after, micros)
        for chain, one in zip(chains, made):
            chain.take(one)
        return [made[0][-1]], [m[0] for m in made[len(chains) :]]

    def plain(arrays, rows):
        return (SUM, arrays, rows, None, (), 1)

    def last(mine, got):
        return (LAST, [mine, got], 16, None, (), 1)

    gc_b = cross_grads(catt_b, dcq_b, dckv_b)
    if short:
        (send_u, keep_u), (send_d, keep_d), (gc_b,) = step(
            [
                (SUM, [gu_a, gu_got], width, 0, (), 1), (TWIN, [keep_a, keep_b, got_a, got_b], width // 2, 1, (), 1),
                (PASS, [gc_b], 4 * each, bf16, (), 1),
            ],
            [gc_b],
        )
        got_u, got_d = along(send_u, 0), along(send_d, 1)
    part0, part1, dcq_a, dckv_a = call(
        functools.partial(cross_back_own_kernel, heads=heads, blocks=big), big,
        [Held(cq_a), Held(ck_a, WHOLE), Held(cv_a, WHOLE), Held(do_a), Held(inner_a, WHOLE), Held(dcq_b), c_parts[0], cw_b],
        [*part_shapes(big), dq_held, dkv_held], scalars, scratch=back_scratch, micros=16, after=[gc_b],
    )
    part = (part0, part1)

    gc_got = across(gc_b)
    pin = []
    if short:
        (send_u, keep_u), (down_a, down_b) = step(
            [(SUM, [keep_u, got_u], width // 2, 1, (), 1), (SPLIT, [keep_d, got_d], width // 2, None, (), 1)], [dcq_a]
        )
        ffn = Chain(
            [keep_u, down_a], [along(send_u, 1), across(down_b)], width // 2, [(0, width), (width, width)], (2,), (2, 1, 0), 2
        )
        pin = [keep_u]
    memory_send, memory_keep = call(
        memory_grad_kernel, 2, [Held(dckv_a), Held(dckv_b), cw_a, cw_b], [half_low, half_low], scalars, micros=5, after=pin,
    )
    memory_got = sibling(memory_send)
    gc_a = cross_grads(catt_a, dcq_a, dckv_a, [memory_send])
    memory_plan = plain([memory_keep, memory_got], length // 2)
    pin = [gc_a]
    rest_shape = ((each + 16, width), bf16, WHOLE)
    d_one, do_a, do_b, inner_a, inner_b, rest_a, rest_b = call(
        functools.partial(norm_one_back_kernel, heads=heads, blocks=small), small,
        [
            Held(d_two), *shares(part, small), gain_one, Held(unit_one), Held(scale_one), self_out, so_b,
            Held(att_a, WHOLE), Held(att_b, WHOLE), sums_two, sums_three,
        ],
        [held, head_held, head_held, inner_held, inner_held, rest_shape, rest_shape], scalars,
        scratch=[pltpu.VMEM((length, width), bf16), pltpu.VMEM((8, width), f32), wide_out], micros=6, after=pin,
    )
    rest_got = across(rest_b)
    kept_w = ((3 * each, width), bf16, WHOLE)
    qkv_held = ((length, 3 * each), bf16, HELD_WHOLE)
    self_scratch = [
        pltpu.VMEM((heads, SPAN, WIDE), f32), pltpu.VMEM((heads, length, WIDE), f32), pltpu.VMEM((heads, length, WIDE), f32),
    ]

    def self_back(q, k, v, do, inner, after=()):
        return call(
            functools.partial(self_back_kernel, heads=heads, blocks=small), small,
            [Row(tokens, length), Part(q), k, v, Held(do), Held(inner, WHOLE)], [qkv_held, kept_w], scalars, scratch=self_scratch, micros=14, after=after,
        )

    pin = []
    if short:
        cross = Chain([gc_a], [gc_got], 4 * each, [(n * each, each) for n in range(4)])
        pin, _ = advance([ffn, cross], after=[do_b])
    dqkv_b, gw_b = self_back(q_b, k_b, v_b, do_b, inner_b, pin)
    gw_got = across(gw_b)

    pin = []
    if short:
        pin, (norms,) = advance([ffn, cross], [last(rest_a, rest_got)], [dqkv_b])
        norms = last(norms, along(norms, 0))
    dqkv_a, gw_a = self_back(q_a, k_a, v_a, do_a, inner_a, pin)
    pin = []
    if short:
        own = Chain([gw_a, rest_a], [gw_got, rest_got], 4 * each, [(n * each, each) for n in range(4)])
        pin, (memory_mine, norms) = advance([own, ffn, cross], [memory_plan, norms])
    else:
        ((memory_mine,),) = step([memory_plan], [gw_a])
    tokens_send, tokens_keep = call(
        tokens_grad_kernel, 2, [Held(d_one), Held(dqkv_a), Held(dqkv_b), w_a, w_b],
        [half_low, ((length // 2, width), f32, WHOLE)], scalars, micros=6, after=pin,
    )
    (out_half,) = call(
        pass_kernel, 1, [Row(out_row, length // 2, (PART, CORE_AT))], [half_low], scalars, micros=1, after=[tokens_send]
    )
    out_far = across(out_half)

    def placed(pieces, shift, after=()):
        return call(
            functools.partial(place_kernel, shift=shift), 4, pieces,
            [((2 * length, width), bf16, FAR_ROWS), ((8, WIDE), f32, WHOLE)], scalars, micros=4, after=after,
        )

    def passed(value, rows=length // 2, dtype=bf16):
        return (PASS, [value], rows, dtype, (), 1)

    def pair(mine, far):
        return (STACK, [mine, far], length, None, (), 1)

    if short:
        pin, (memory_mine,) = advance([own, ffn, cross], [passed(memory_mine)], [out_half])
        memory_far = across(memory_mine)
        pin, (tokens_send,) = advance([own, cross], [passed(tokens_send)], [*pin, out_far])
        tokens_plan = plain([tokens_keep, sibling(tokens_send)], length // 2)
        pin, (tokens_mine, memory_pair, out_far) = advance(
            [own, cross], [tokens_plan, pair(memory_mine, memory_far), passed(out_far)], [*pin, ffn.arrays[1]]
        )
        tokens_far, memory_sibling, out_sibling = across(tokens_mine), sibling(memory_pair), sibling(out_far)
        ((gu_wide, gd_wide),) = step([ffn.plan()], pin, 4)
        pin, (norms,) = advance([own], [passed(norms, 16, f32)], [Far(gu_wide), memory_sibling, out_sibling])
        norms = last(norms, along(norms, 2))
        memory_grad, mark = placed([memory_pair, memory_sibling], False, pin)
        pin, (tokens_pair, norms) = advance([own], [pair(tokens_mine, tokens_far), norms], [mark, cross.arrays[1]])
        norms = last(norms, along(norms, 1))
        (cross,) = step([cross.plan()], pin, 3)
        layer_out, mark = placed([out_row, out_far, out_sibling], True, [Far(cross[0])])
        tokens_grad, mark = placed([tokens_pair, sibling(tokens_pair)], False, [mark])
        _, (norms,) = advance([own], [norms], [mark])
        own = own.done
        rest = own[3]
    else:
        memory_far = across(memory_mine)
        tokens_plan = plain([tokens_keep, sibling(tokens_send)], length // 2)
        (tokens_mine,), (memory_pair,) = step([tokens_plan, pair(memory_mine, memory_far)])
        ((tokens_pair,),) = step([pair(tokens_mine, across(tokens_mine))])
        layer_out, _ = placed([out_row, out_far, sibling(out_far)], True)
        memory_grad, _ = placed([memory_pair, sibling(memory_pair)], False)
        tokens_grad, _ = placed([tokens_pair, sibling(tokens_pair)], False)

        def total(mine, got):
            return lax.psum((mine.astype(f32) + got.astype(f32)).astype(bf16), "dp").astype(f32)

        high = scalars[BIT] == 1
        down_a, down_b = (
            jnp.where(high, jnp.concatenate([send, keep]), jnp.concatenate([keep, send]))
            for send, keep in ((send_a, keep_a), (send_b, keep_b))
        )
        gu_wide, gd_wide = total(gu_a, gu_got), total(down_a, across(down_b))
        cross = jnp.split(total(gc_a, gc_got), 4)
        own = jnp.split(total(gw_a, gw_got), 3)
        rest = total(rest_a, rest_got)
        rest, norms = rest[:each], rest[each:]
    return (
        layer_out, tokens_grad, memory_grad,
        own[0].T, own[1].T, own[2].T, rest,
        cross[0].T, cross[1].T, cross[2].T, cross[3],
        gu_wide, gd_wide, *(norms[i] for i in range(6)),
    )


def solution(mesh):
    rows, columns, down = P("dp", None), P(None, "tp"), P("tp", None)
    return jax.shard_map(
        functools.partial(local, mesh.shape["dp"]),
        mesh=mesh,
        in_specs=(rows, rows, rows, P("dp"), P("dp"))
        + (columns, columns, columns, down) * 2
        + (columns, down)
        + (P(),) * 6,
        out_specs=(rows, rows, rows) + (columns, columns, columns, down) * 2 + (columns, down) + (P(),) * 6,
        check_vma=False,
    )
```

```python
import functools

import jax
import jax.numpy as jnp
from jax import lax
from jax.experimental import pallas as pl
from jax.experimental.pallas import tpu as pltpu
from jax.sharding import PartitionSpec as P

HEAD_DIM = 64
WIDE = 2 * HEAD_DIM
EPS = 1e-05
MASKED = -1e30
LOG2E = 1.4426950408889634
LN2 = 0.6931471805599453
f32 = jnp.float32
bf16 = jnp.bfloat16

CORE = [(0, 1), (1, 0), (2, 3), (3, 2)]
ACROSS = [(0, 2), (2, 0), (1, 3), (3, 1)]
MIB = 1 << 20
LIMIT = 16

ROWS, WHOLE, COLUMNS, HALF, PART, SKIP, ARBITRARY = "rows", "whole", "columns", "half", "part", "skip", "arbitrary"
HELD_ROWS, HELD_WHOLE, FAR_ROWS, FAR_WHOLE = "held rows", "held whole", "hbm rows", "hbm whole"
SUM, PACK, WIDEN, STACK, LAST, PASS, TWIN, SPLIT = "sum", "pack", "wide", "stack", "last", "pass", "twin", "split"


def nn(left, right):
    return lax.dot_general(left, right, (((1,), (0,)), ((), ())), preferred_element_type=f32)


def nt(left, right):
    return lax.dot_general(left, right, (((1,), (1,)), ((), ())), preferred_element_type=f32)


def tn(left, right):
    return lax.dot_general(left, right, (((0,), (0,)), ((), ())), preferred_element_type=f32)


def lanes(rows):
    return lax.broadcasted_iota(jnp.int32, (rows, HEAD_DIM), 1)


def three_parts(value):
    high = value.astype(bf16).astype(f32)
    rest = value - high
    middle = rest.astype(bf16).astype(f32)
    return high, middle, rest - middle


def fill_queries(q_ref, rows, count, acc, heads):
    tail = jnp.where(lanes(count) == 0, 1.0, 0.0)
    for h in range(heads):
        part = acc[:, h * HEAD_DIM : (h + 1) * HEAD_DIM]
        q_ref[h, rows, :] = jnp.concatenate([part, tail], 1).astype(bf16)


def fill_keys(k_ref, v_ref, rows, start, count, acc, heads, limit):
    lane = lanes(count)
    index = start + lax.broadcasted_iota(jnp.int32, (count, HEAD_DIM), 0)
    tail = jnp.where(lane == 0, jnp.where(index < limit, 0.0, MASKED), jnp.where(lane < 4, 1.0, 0.0))
    ones = jnp.ones((count, HEAD_DIM), f32)
    for h in range(heads):
        k = acc[:, h * HEAD_DIM : (h + 1) * HEAD_DIM]
        v = acc[:, (heads + h) * HEAD_DIM : (heads + h + 1) * HEAD_DIM]
        k_ref[h, rows, :] = jnp.concatenate([k, tail], 1).astype(bf16)
        v_ref[h, rows, :] = jnp.concatenate([v, ones], 1).astype(bf16)


def attend_block(q_ref, k_ref, v_ref, att_ref, h, rows, count, key_end, causal):
    s = nt(q_ref[h, rows, :], k_ref[h, :key_end, :])
    if causal:
        r = lax.broadcasted_iota(jnp.int32, (count, count), 0)
        c = lax.broadcasted_iota(jnp.int32, (count, count), 1)
        diagonal = jnp.where(c <= r, s[:, key_end - count :], MASKED)
        s = diagonal if key_end == count else jnp.concatenate([s[:, : key_end - count], diagonal], 1)
    peak = jnp.max(s, 1, keepdims=True)
    p = jnp.exp2(s - peak).astype(bf16)
    o = nn(p, v_ref[h, :key_end, :])
    total = jnp.broadcast_to(o[:, HEAD_DIM : HEAD_DIM + 1], o.shape)
    att_ref[rows, h * WIDE : (h + 1) * WIDE] = (o / total).astype(bf16)
    high, middle, low = three_parts(-(peak + jnp.log2(total)))
    lane = lax.broadcasted_iota(jnp.int32, o.shape, 1)
    tail = jnp.where(lane == 65, high, jnp.where(lane == 66, middle, jnp.where(lane == 67, low, q_ref[h, rows, :].astype(f32))))
    q_ref[h, rows, :] = tail.astype(bf16)


def widen_out(wide_ref, out_ref, heads):
    wide_ref[...] = jnp.zeros_like(wide_ref)
    for h in range(heads):
        wide_ref[h * WIDE : h * WIDE + HEAD_DIM, :] = out_ref[h * HEAD_DIM : (h + 1) * HEAD_DIM, :]


def narrow_out(out_ref, wide, first, heads):
    for h in range(heads):
        out_ref[first + h * HEAD_DIM : first + (h + 1) * HEAD_DIM, :] = wide[h * WIDE : h * WIDE + HEAD_DIM, :]


def fill_grads(do_ref, inner_ref, rows, places, e, wide_ref, att, heads):
    grad = nt(e, wide_ref[...]).astype(bf16)
    ones = jnp.ones((8, WIDE), bf16)
    for h in range(heads):
        part = grad[:, h * WIDE : (h + 1) * WIDE]
        do_ref[h, rows, :] = part
        product = part.astype(f32) * att[:, h * WIDE : (h + 1) * WIDE].astype(f32)
        high = product.astype(bf16)
        inner_ref[h, :, places] = nt(ones, high) + nt(ones, (product - high.astype(f32)).astype(bf16))


def back_block(q_ref, k_ref, v_ref, do_ref, inner_ref, dq_ref, dk_ref, dv_ref, h, rows, places, count, key_end, causal):
    q = q_ref[h, rows, :]
    d = do_ref[h, rows, :]
    k = k_ref[h, :key_end, :]
    v = v_ref[h, :key_end, :]
    p = jnp.exp2(nt(k, q))
    if causal:
        r = lax.broadcasted_iota(jnp.int32, (count, count), 0)
        c = lax.broadcasted_iota(jnp.int32, (count, count), 1)
        diagonal = jnp.where(r <= c, p[key_end - count :], 0.0)
        p = diagonal if key_end == count else jnp.concatenate([p[: key_end - count], diagonal], 0)
    ds = (p * (nt(v, d) - inner_ref[h, 0:1, places])).astype(bf16)
    dv = nn(p.astype(bf16), d)
    dk = nn(ds, q)
    dv_ref[h, :key_end, :] += dv
    dk_ref[h, :key_end, :] += dk
    dq_ref[h, rows, :] = tn(k, ds).T


def pack_heads(source, rows, heads, factor):
    return jnp.concatenate([source[h, rows, :HEAD_DIM] * factor for h in range(heads)], 1).astype(bf16)


def norm(resid):
    center = resid - jnp.mean(resid, -1, keepdims=True)
    scale = lax.rsqrt(jnp.mean(center * center, -1, keepdims=True) + EPS)
    return center * scale, scale


def norm_back(grad, gain, unit, scale):
    lifted = grad * gain
    first = jnp.mean(lifted, -1, keepdims=True)
    second = jnp.mean(lifted * unit, -1, keepdims=True)
    return scale * (lifted - first - unit * second)


def gelu_pair(value):
    scaled = value * 0.7071067811865476
    density = jnp.exp(-scaled * scaled) * 0.3989422804014327
    below = 0.5 * (1.0 + lax.erf(scaled))
    return value * below, below + value * density


BLOCK = 512
SPAN = 256
ROW, TGT, SRC, CORE_AT, BIT = 0, 1, 3, 5, 6
FACTOR = HEAD_DIM ** (-0.5) * LOG2E


def vector(ref):
    return ref[...].reshape(1, ref.shape[0])


def branch_of(shares, blocks):
    own0, own1, got0, got1 = shares
    first = pl.program_id(0) < blocks // 2
    own = jnp.where(first, own0[...], own1[...]).astype(f32)
    return own + jnp.where(first, got0[...], got1[...]).astype(f32)


def put_part(first_ref, second_ref, value, blocks):
    at = pl.program_id(0)

    @pl.when(at < blocks // 2)
    def _():
        first_ref[...] = value

    @pl.when(at >= blocks // 2)
    def _():
        second_ref[...] = value


def rows_at(size):
    return pl.ds(pl.multiple_of(pl.program_id(0) * size, size), size)


def project_own_kernel(
    s_ref, x_ref, m_ref, sq_ref, sk_ref, sv_ref, cq_ref, ck_ref, cv_ref, so_ref, co_ref,
    q_ref, k_ref, v_ref, k_out_ref, v_out_ref, mk_ref, mv_ref, wa_ref, cwa_ref, half_out_ref, half_cw_ref, *, heads,
):
    each = heads * HEAD_DIM
    at = pl.program_id(0)

    @pl.when(at == 0)
    def _():
        for n, ref in enumerate((sq_ref, sk_ref, sv_ref)):
            wa_ref[n * each : (n + 1) * each, :] = ref[...]
        for n, ref in enumerate((cq_ref, ck_ref, cv_ref)):
            cwa_ref[n * each : (n + 1) * each, :] = ref[...]
        half_out_ref[...] = jnp.where(s_ref[BIT] == 0, so_ref[...], co_ref[...])
        half = half_cw_ref.shape[0]
        half_cw_ref[...] = cwa_ref[pl.ds(pl.multiple_of(s_ref[BIT + 1] * half, 16), half), :]

    limit = s_ref[TGT + s_ref[ROW]]
    memory_limit = s_ref[SRC + s_ref[ROW]]
    rows = pl.ds(0, BLOCK)
    acc = nt(x_ref[...], wa_ref[...])
    fill_queries(q_ref, rows, BLOCK, acc[:, :each] * FACTOR, heads)
    fill_keys(k_ref, v_ref, rows, at * BLOCK, BLOCK, acc[:, each:], heads, limit)
    k_out_ref[...] = k_ref[...]
    v_out_ref[...] = v_ref[...]
    acc = nt(m_ref[...], cwa_ref[each:, :])
    fill_keys(mk_ref, mv_ref, rows, at * BLOCK, BLOCK, acc, heads, memory_limit)


def causal_blocks(q_ref, k_ref, v_ref, att_ref, heads):
    at = pl.program_id(0)
    for block in range(k_ref.shape[1] // BLOCK):

        @pl.when(at == block)
        def _():
            for h in range(heads):
                attend_block(q_ref, k_ref, v_ref, att_ref, h, pl.ds(0, BLOCK), BLOCK, (block + 1) * BLOCK, True)


def self_own_kernel(s_ref, q_in_ref, k_ref, v_ref, up_ref, down_ref, q_ref, att_ref, halves_ref, mark_ref, *, heads):
    half = up_ref.shape[0]
    halves_ref[:half, :] = up_ref[...]
    halves_ref[half:, :] = down_ref[...]
    mark_ref[...] = jnp.zeros_like(mark_ref)
    q_ref[...] = q_in_ref[...]
    causal_blocks(q_ref, k_ref, v_ref, att_ref, heads)


def self_other_kernel(s_ref, x_ref, near_ref, far_ref, w_ref, q_ref, k_out_ref, v_out_ref, att_ref, k_ref, v_ref, *, heads):
    each = heads * HEAD_DIM
    at = pl.program_id(0)

    @pl.when(at == 0)
    def _():
        put_halves(w_ref, near_ref, far_ref, s_ref[BIT])

    acc = nt(x_ref[...], w_ref[...])
    fill_queries(q_ref, pl.ds(0, BLOCK), BLOCK, acc[:, :each] * FACTOR, heads)
    fill_keys(k_ref, v_ref, rows_at(BLOCK), at * BLOCK, BLOCK, acc[:, each:], heads, s_ref[TGT + s_ref[ROW]])
    k_out_ref[...] = k_ref[:, rows_at(BLOCK), :]
    v_out_ref[...] = v_ref[:, rows_at(BLOCK), :]
    causal_blocks(q_ref, k_ref, v_ref, att_ref, heads)


def self_out_kernel(
    s_ref, atta_ref, attb_ref, soa_ref, near_ref, far_ref, part0_ref, part1_ref, sob_ref, cob_ref, wide_ref, *, heads, blocks
):
    @pl.when(pl.program_id(0) == 0)
    def _():
        low = s_ref[BIT] == 0
        sob_ref[...] = jnp.where(low, near_ref[...], far_ref[...])
        cob_ref[...] = jnp.where(low, far_ref[...], near_ref[...])
        widen_out(wide_ref.at[0], soa_ref, heads)
        widen_out(wide_ref.at[1], sob_ref, heads)

    part = nn(atta_ref[...], wide_ref[0]) + nn(attb_ref[...], wide_ref[1])
    put_part(part0_ref, part1_ref, part.astype(bf16), blocks)


def cross_blocks(q_ref, k_ref, v_ref, att_ref, heads, limit):
    step = 256
    live = (limit + step - 1) // step
    for count in range(1, k_ref.shape[1] // step + 1):

        @pl.when(live == count)
        def _():
            for h in range(heads):
                attend_block(q_ref, k_ref, v_ref, att_ref, h, pl.ds(0, BLOCK), BLOCK, count * step, False)


def cross_own_kernel(
    s_ref, x_ref, own0, own1, got0, got1, gain_ref, shift_ref, cq_ref, k_ref, v_ref,
    h_ref, hl_ref, unit_ref, scale_ref, q_ref, att_ref, *, heads, blocks,
):
    unit, scale = norm(x_ref[...].astype(f32) + branch_of((own0, own1, got0, got1), blocks))
    h = unit * vector(gain_ref) + vector(shift_ref)
    h_ref[...] = h
    unit_ref[...] = unit.astype(bf16)
    scale_ref[...] = scale
    low = h.astype(bf16)
    hl_ref[...] = low
    fill_queries(q_ref, pl.ds(0, BLOCK), BLOCK, nt(low, cq_ref[...]) * FACTOR, heads)
    cross_blocks(q_ref, k_ref, v_ref, att_ref, heads, s_ref[SRC + s_ref[ROW]])


def put_halves(target_ref, near_ref, far_ref, high):
    half = near_ref.shape[0]
    target_ref[pl.ds(pl.multiple_of(high * half, 16), half), :] = near_ref[...]
    target_ref[pl.ds(pl.multiple_of((1 - high) * half, 16), half), :] = far_ref[...]


def cross_other_kernel(s_ref, m_ref, hl_ref, near_ref, far_ref, cwb_ref, k_ref, v_ref, q_ref, att_ref, *, heads):
    each = heads * HEAD_DIM
    limit = s_ref[SRC + s_ref[ROW]]

    @pl.when(pl.program_id(0) == 0)
    def _():
        put_halves(cwb_ref, near_ref, far_ref, s_ref[BIT + 1])

        @pl.loop(0, m_ref.shape[0], step=BLOCK)
        def _(start):
            rows = pl.ds(pl.multiple_of(start, BLOCK), BLOCK)
            fill_keys(k_ref, v_ref, rows, start, BLOCK, nt(m_ref[rows, :], cwb_ref[each:, :]), heads, limit)

    fill_queries(q_ref, pl.ds(0, BLOCK), BLOCK, nt(hl_ref[...], cwb_ref[:each, :]) * FACTOR, heads)
    cross_blocks(q_ref, k_ref, v_ref, att_ref, heads, limit)


def cross_out_kernel(atta_ref, attb_ref, coa_ref, cob_ref, part0_ref, part1_ref, wide_ref, *, heads, blocks):
    @pl.when(pl.program_id(0) == 0)
    def _():
        widen_out(wide_ref.at[0], coa_ref, heads)
        widen_out(wide_ref.at[1], cob_ref, heads)

    part = nn(atta_ref[...], wide_ref[0]) + nn(attb_ref[...], wide_ref[1])
    put_part(part0_ref, part1_ref, part.astype(bf16), blocks)


def ffn_own_kernel(
    h_in_ref, own0, own1, got0, got1, gain_ref, shift_ref, up_ref, down_ref,
    h_ref, hl_ref, unit_ref, scale_ref, act_ref, slope_ref, term_ref, *, blocks,
):
    unit, scale = norm(h_in_ref[...] + branch_of((own0, own1, got0, got1), blocks))
    h = unit * vector(gain_ref) + vector(shift_ref)
    h_ref[...] = h
    unit_ref[...] = unit.astype(bf16)
    scale_ref[...] = scale
    low = h.astype(bf16)
    hl_ref[...] = low
    act, slope = gelu_pair(nn(low, up_ref[...]))
    act = act.astype(bf16)
    act_ref[...] = act
    slope_ref[...] = slope.astype(bf16)
    term_ref[...] = nn(act, down_ref[...])


def ffn_other_kernel(
    s_ref, hl_ref, term_ref, up_near_ref, up_far_ref, down_near_ref, down_far_ref,
    part0_ref, part1_ref, act_ref, slope_ref, up_ref, down_ref, *, blocks,
):
    @pl.when(pl.program_id(0) == 0)
    def _():
        put_halves(up_ref, up_near_ref, up_far_ref, s_ref[BIT])
        put_halves(down_ref, down_near_ref, down_far_ref, s_ref[BIT + 1])

    act, slope = gelu_pair(nn(hl_ref[...], up_ref[...]))
    act = act.astype(bf16)
    act_ref[...] = act
    slope_ref[...] = slope.astype(bf16)
    put_part(part0_ref, part1_ref, (term_ref[...] + nn(act, down_ref[...])).astype(bf16), blocks)


def ffn_back_kernel(
    s_ref, h_ref, own0, own1, got0, got1, cot_ref, gain_ref, shift_ref, upa_ref, upb_ref, downa_ref, downb_ref, slopea_ref, slopeb_ref,
    part0_ref, part1_ref, out_ref, d_ref, e_ref, prea_ref, preb_ref, sums_ref, *, blocks,
):
    limit = s_ref[TGT + s_ref[ROW]]
    at = pl.program_id(0)

    @pl.when(at == 0)
    def _():
        sums_ref[...] = jnp.zeros_like(sums_ref)

    gain = vector(gain_ref)
    unit, scale = norm(h_ref[...] + branch_of((own0, own1, got0, got1), blocks))
    out_ref[...] = (unit * gain + vector(shift_ref)).astype(bf16)
    index = at * SPAN + lax.broadcasted_iota(jnp.int32, (SPAN, 1), 0)
    grad = jnp.where(index < limit, cot_ref[...].astype(f32), 0.0)
    sums_ref[0:1, :] += jnp.sum(grad * unit, 0, keepdims=True)
    sums_ref[1:2, :] += jnp.sum(grad, 0, keepdims=True)
    d = norm_back(grad, gain, unit, scale)
    d_ref[...] = d
    e = d.astype(bf16)
    e_ref[...] = e
    part = None
    for up_ref, down_ref, slope_ref, pre_ref in (
        (upa_ref, downa_ref, slopea_ref, prea_ref),
        (upb_ref, downb_ref, slopeb_ref, preb_ref),
    ):
        pre = (nt(e, down_ref[...]) * slope_ref[...].astype(f32)).astype(bf16)
        pre_ref[...] = pre
        term = nt(pre, up_ref[...])
        part = term if part is None else part + term
    put_part(part0_ref, part1_ref, part.astype(bf16), blocks)


def ffn_grad_kernel(s_ref, h_ref, act_ref, e_ref, pre_ref, up_ref, send_ref, keep_ref):
    up_ref[...] = tn(h_ref[...], pre_ref[...]).astype(bf16)
    down = tn(act_ref[...], e_ref[...]).astype(bf16)
    mine = pl.program_id(0) == s_ref[BIT]

    @pl.when(mine)
    def _():
        keep_ref[...] = down

    @pl.when(jnp.logical_not(mine))
    def _():
        send_ref[...] = down


def norm_step(d_in_ref, shares, gain, unit_ref, scale_ref, d_ref, e_ref, sums_ref, blocks):
    @pl.when(pl.program_id(0) == 0)
    def _():
        sums_ref[...] = jnp.zeros_like(sums_ref)

    grad = d_in_ref[...] + branch_of(shares, blocks)
    unit = unit_ref[...].astype(f32)
    sums_ref[0:1, :] += jnp.sum(grad * unit, 0, keepdims=True)
    sums_ref[1:2, :] += jnp.sum(grad, 0, keepdims=True)
    d = norm_back(grad, gain, unit, scale_ref[...])
    d_ref[...] = d
    e = d.astype(bf16)
    e_ref[...] = e
    return e


def cross_back_heads(s_ref, q_ref, k_ref, v_ref, do_ref, inner_ref, dqo_ref, dkv_ref, dq_ref, dk_ref, dv_ref, heads, blocks):
    at = pl.program_id(0)
    source = k_ref.shape[1]

    @pl.when(at == 0)
    def _():
        dk_ref[...] = jnp.zeros_like(dk_ref)
        dv_ref[...] = jnp.zeros_like(dv_ref)

    step = 256
    live = (s_ref[SRC + s_ref[ROW]] + step - 1) // step
    rows = pl.ds(0, BLOCK)
    for count in range(1, source // step + 1):

        @pl.when(live == count)
        def _():
            @pl.loop(0, heads)
            def _(h):
                back_block(
                    q_ref, k_ref, v_ref, do_ref, inner_ref, dq_ref, dk_ref, dv_ref, h, rows, rows_at(BLOCK), BLOCK, count * step, False
                )

    dqo_ref[...] = pack_heads(dq_ref, rows, heads, HEAD_DIM ** (-0.5))

    @pl.when(at == blocks - 1)
    def _():
        @pl.loop(0, source, step=BLOCK)
        def _(start):
            some = pl.ds(pl.multiple_of(start, BLOCK), BLOCK)
            dkv_ref[some, :] = jnp.concatenate(
                [pack_heads(dk_ref, some, heads, LN2), pack_heads(dv_ref, some, heads, 1.0)], 1
            )


def cross_back_other_kernel(
    s_ref, d_in_ref, own0, own1, got0, got1, gain_ref, unit_ref, scale_ref, coa_ref, cob_ref, atta_ref, attb_ref,
    q_ref, k_ref, v_ref,
    d_ref, e_ref, sums_ref, doa_ref, innera_ref, dqo_ref, dkv_ref, wide_ref, do_ref, inner_ref, dq_ref, dk_ref, dv_ref, *, heads, blocks,
):
    @pl.when(pl.program_id(0) == 0)
    def _():
        widen_out(wide_ref.at[0], coa_ref, heads)
        widen_out(wide_ref.at[1], cob_ref, heads)

    e = norm_step(
        d_in_ref, (own0, own1, got0, got1), vector(gain_ref), unit_ref, scale_ref, d_ref, e_ref, sums_ref, blocks
    )
    rows, places = pl.ds(0, BLOCK), rows_at(BLOCK)
    fill_grads(doa_ref, innera_ref, rows, places, e, wide_ref.at[0], atta_ref[...], heads)
    fill_grads(do_ref, inner_ref, rows, places, e, wide_ref.at[1], attb_ref[...], heads)
    cross_back_heads(s_ref, q_ref, k_ref, v_ref, do_ref, inner_ref, dqo_ref, dkv_ref, dq_ref, dk_ref, dv_ref, heads, blocks)


def cross_back_own_kernel(
    s_ref, q_ref, k_ref, v_ref, do_ref, inner_ref, dqb_ref, cqa_ref, cwb_ref,
    part0_ref, part1_ref, dqo_ref, dkv_ref, dq_ref, dk_ref, dv_ref, *, heads, blocks,
):
    cross_back_heads(s_ref, q_ref, k_ref, v_ref, do_ref, inner_ref, dqo_ref, dkv_ref, dq_ref, dk_ref, dv_ref, heads, blocks)
    part = nn(dqo_ref[...], cqa_ref[...]) + nn(dqb_ref[...], cwb_ref[: heads * HEAD_DIM, :])
    put_part(part0_ref, part1_ref, part.astype(bf16), blocks)


def cross_grad_kernel(s_ref, h_ref, m_ref, att_ref, e_ref, dq_ref, dkv_ref, g_ref):
    each = dq_ref.shape[1]
    g_ref[:each, :] = tn(dq_ref[...], h_ref[...]).astype(bf16)
    g_ref[each : 3 * each, :] = tn(dkv_ref[...], m_ref[...]).astype(bf16)
    narrow_out(g_ref, tn(att_ref[...], e_ref[...]).astype(bf16), 3 * each, each // HEAD_DIM)


def pass_kernel(s_ref, in_ref, out_ref):
    out_ref[...] = in_ref[...]


def relay_kernel(s_ref, in_ref, first_ref, second_ref):
    half = first_ref.shape[0]
    first_ref[...] = in_ref[:half, :]
    second_ref[...] = in_ref[half:, :]


def memory_grad_kernel(s_ref, a_ref, b_ref, wa_ref, wb_ref, send_ref, keep_ref):
    each = a_ref.shape[1] // 2
    part = (nn(a_ref[...], wa_ref[each:, :]) + nn(b_ref[...], wb_ref[each:, :])).astype(bf16)
    mine = pl.program_id(0) == s_ref[CORE_AT]

    @pl.when(mine)
    def _():
        keep_ref[...] = part

    @pl.when(jnp.logical_not(mine))
    def _():
        send_ref[...] = part


def norm_one_back_kernel(
    s_ref, d_in_ref, own0, own1, got0, got1, gain_ref, unit_ref, scale_ref, soa_ref, sob_ref, atta_ref, attb_ref,
    sums_two_ref, sums_three_ref, d_ref, doa_ref, dob_ref, innera_ref, innerb_ref, ra_ref, rb_ref, e_ref, sums_ref, wide_ref, *, heads, blocks,
):
    @pl.when(pl.program_id(0) == 0)
    def _():
        widen_out(wide_ref.at[0], soa_ref, heads)
        widen_out(wide_ref.at[1], sob_ref, heads)

    each = heads * HEAD_DIM
    rows = rows_at(SPAN)
    e = norm_step(
        d_in_ref, (own0, own1, got0, got1), vector(gain_ref), unit_ref, scale_ref, d_ref, e_ref.at[rows, :], sums_ref, blocks
    )
    fill_grads(doa_ref, innera_ref, pl.ds(0, SPAN), rows, e, wide_ref.at[0], atta_ref[rows, :], heads)
    fill_grads(dob_ref, innerb_ref, pl.ds(0, SPAN), rows, e, wide_ref.at[1], attb_ref[rows, :], heads)

    @pl.when(pl.program_id(0) == blocks - 1)
    def _():
        norms = jnp.concatenate(
            [sums_ref[:2, :], sums_two_ref[:2, :], sums_three_ref[:2, :], jnp.zeros((10, d_in_ref.shape[1]), f32)], 0
        ).astype(bf16)
        for att_ref, r_ref in ((atta_ref, ra_ref), (attb_ref, rb_ref)):
            narrow_out(r_ref, tn(att_ref[...], e_ref[...]).astype(bf16), 0, heads)
            r_ref[each:, :] = norms


def self_back_kernel(s_ref, x_ref, q_ref, k_ref, v_ref, do_ref, inner_ref, dqkv_ref, gw_ref, dq_ref, dk_ref, dv_ref, *, heads, blocks):
    at = pl.program_id(0)
    each = heads * HEAD_DIM
    length = k_ref.shape[1]

    @pl.when(at == 0)
    def _():
        dk_ref[...] = jnp.zeros_like(dk_ref)
        dv_ref[...] = jnp.zeros_like(dv_ref)

    rows = pl.ds(0, SPAN)
    for block in range(blocks):

        @pl.when(at == block)
        def _():
            @pl.loop(0, heads)
            def _(h):
                back_block(
                    q_ref, k_ref, v_ref, do_ref, inner_ref, dq_ref, dk_ref, dv_ref, h, rows, pl.ds(block * SPAN, SPAN), SPAN,
                    (block + 1) * SPAN, True,
                )

    dqkv_ref[rows_at(SPAN), :each] = pack_heads(dq_ref, rows, heads, HEAD_DIM ** (-0.5))

    @pl.when(at == blocks - 1)
    def _():
        @pl.loop(0, length, step=BLOCK)
        def _(start):
            some = pl.ds(pl.multiple_of(start, BLOCK), BLOCK)
            dqkv_ref[some, each:] = jnp.concatenate(
                [pack_heads(dk_ref, some, heads, LN2), pack_heads(dv_ref, some, heads, 1.0)], 1
            )
        gw_ref[...] = tn(dqkv_ref[...], x_ref[...]).astype(bf16)


def tokens_grad_kernel(s_ref, d_ref, a_ref, b_ref, wa_ref, wb_ref, send_ref, keep_ref):
    part = nn(a_ref[...], wa_ref[...]) + nn(b_ref[...], wb_ref[...])
    mine = pl.program_id(0) == s_ref[CORE_AT]

    @pl.when(mine)
    def _():
        keep_ref[...] = d_ref[...] + part

    @pl.when(jnp.logical_not(mine))
    def _():
        send_ref[...] = part.astype(bf16)


def place_kernel(s_ref, *refs, shift):
    pieces, out_ref, mark_ref = refs[:-2], refs[-2], refs[-1]
    half = out_ref.shape[0]
    row, core, at = s_ref[ROW], s_ref[CORE_AT], pl.program_id(0)
    mark_ref[...] = jnp.zeros_like(mark_ref)
    if shift:
        sources = [
            (pieces[0].at[:half, :], 2 * row), (pieces[0].at[half:, :], 2 * row + 1),
            (pieces[1], 2 * (1 - row) + core), (pieces[2], 2 * (1 - row) + 1 - core),
        ]
    else:
        sources = [
            (pieces[0].at[:half, :], 2 * row + core), (pieces[1].at[:half, :], 2 * row + 1 - core),
            (pieces[0].at[half:, :], 2 * (1 - row) + core), (pieces[1].at[half:, :], 2 * (1 - row) + 1 - core),
        ]
    for ref, place in sources:

        @pl.when(at == place)
        def _():
            out_ref[...] = ref[...]


def step_kernel(s_ref, *refs, plans):
    scratch = refs[-1]
    inputs = sum(plan[1] for plan in plans)
    ins, outs = list(refs[:inputs]), list(refs[inputs:-1])
    for kind, count, rows, bit, cuts, parts in plans:
        mine, ins = ins[:count], ins[count:]
        if kind == SUM:
            at = 0
            for a_ref, b_ref in zip(mine[: count // 2], mine[count // 2 :]):
                size = min(a_ref.shape[0], rows - at)
                scratch[at : at + size, :] = (a_ref[:size, :].astype(f32) + b_ref[:size, :].astype(f32)).astype(bf16)
                at += size
            if at < rows:
                scratch[at:rows, :] = jnp.zeros((rows - at, scratch.shape[1]), bf16)
            if bit is None:
                outs.pop(0)[...] = scratch[:rows, :]
            else:
                half, high = rows // 2, s_ref[BIT + bit]
                outs.pop(0)[...] = scratch[pl.ds(pl.multiple_of((1 - high) * half, 16), half), :]
                outs.pop(0)[...] = scratch[pl.ds(pl.multiple_of(high * half, 16), half), :]
        elif kind == TWIN:
            for part in range(2):
                total = (mine[part][...].astype(f32) + mine[part + 2][...].astype(f32)).astype(bf16)
                scratch[part * rows : (part + 1) * rows, :] = total
            half, high = rows // 2, s_ref[BIT + bit]
            send_ref, keep_ref = outs.pop(0), outs.pop(0)
            for part in range(2):
                place = slice(part * half, (part + 1) * half)
                send_ref[place, :] = scratch[pl.ds(pl.multiple_of(part * rows + (1 - high) * half, 16), half), :]
                keep_ref[place, :] = scratch[pl.ds(pl.multiple_of(part * rows + high * half, 16), half), :]
        elif kind == SPLIT:
            total = (mine[0][...].astype(f32) + mine[1][...].astype(f32)).astype(bf16)
            outs.pop(0)[...] = total[: rows // 2, :]
            outs.pop(0)[...] = total[rows // 2 :, :]
        elif kind == LAST:
            outs.pop(0)[...] = mine[0][-rows:, :].astype(f32) + mine[1][-rows:, :].astype(f32)
        elif kind == PASS:
            outs.pop(0)[...] = mine[0][...]
        elif kind == STACK:
            size, target = mine[0].shape[0], outs.pop(0)
            target[:size, :] = mine[0][...]
            target[size:, :] = mine[1][...]
        else:
            high, size = s_ref[BIT + bit], mine[0].shape[0] // parts
            target = outs.pop(0) if kind == PACK else scratch
            for part in range(parts):
                some, first = slice(part * size, (part + 1) * size), 2 * part * size
                target[pl.ds(pl.multiple_of(first + high * size, 16), size), :] = mine[0][some, :]
                target[pl.ds(pl.multiple_of(first + (1 - high) * size, 16), size), :] = mine[1][some, :]
            for first, size in cuts:
                outs.pop(0)[...] = scratch[first : first + size, :].astype(f32)


class Row:
    def __init__(self, array, length, how=WHOLE):
        self.array, self.length, self.how = array, length, how


class Part:
    def __init__(self, array, how=ROWS, pick=None):
        self.array, self.how, self.pick = array, how, pick


class Pick:
    def __init__(self, array, scalar, parts):
        self.array, self.scalar, self.parts = array, scalar, parts


class Far:
    def __init__(self, array):
        self.array = array


def block_of(shape, how, blocks, pick=None, once=False):
    rank = len(shape)
    if rank == 1:
        return pl.BlockSpec(shape, lambda *a: (0,))
    if isinstance(how, tuple):
        how, pick = how
    if how == WHOLE:
        return pl.BlockSpec(shape, lambda *a: (0,) * rank, pipeline_mode=pl.Buffered(1) if once else None)
    pick = pick or (lambda i: i)
    dim = rank - 1 if how == COLUMNS else rank - 2
    parts = blocks // 2 if how == HALF else blocks
    block = tuple(n // parts if d == dim else n for d, n in enumerate(shape))
    return pl.BlockSpec(block, lambda i, *a: tuple(pick(i) if d == dim else 0 for d in range(rank)))


def row_of(item, blocks):
    width = item.array.shape[1]
    if item.how == WHOLE:
        return pl.BlockSpec((item.length, width), lambda i, s: (s[0], 0))
    if item.how == ROWS:
        return pl.BlockSpec((item.length // blocks, width), lambda i, s: (s[0] * blocks + i, 0))
    if item.how[0] == PART:
        return pl.BlockSpec((item.length // blocks, width), lambda i, s: (s[item.how[1]] * blocks + i, 0))
    return pl.BlockSpec((item.length, width // blocks), lambda i, s: (s[0], i))


class Held:
    def __init__(self, array, how=ROWS):
        self.array, self.how = array, how


def view_of(shape, how, blocks):
    rank = len(shape)
    if how == WHOLE:
        return None
    if how == ROWS:
        size = shape[-2] // blocks

        def rows(ref):
            place = pl.ds(pl.multiple_of(pl.program_id(0) * size, size), size)
            return ref.at[place, :] if rank == 2 else ref.at[:, place, :]

        return rows
    size = shape[-1] // blocks
    return lambda ref: ref.at[:, pl.ds(pl.multiple_of(pl.program_id(0) * size, size), size)]


def call(kernel, blocks, inputs, outputs, scalars=None, scratch=(), micros=5.0, limit=LIMIT, after=(), scale=0.7):
    specs, arrays, views = [], [], []
    here = pl.BlockSpec(memory_space=pltpu.VMEM)
    for item in inputs:
        view = None
        if isinstance(item, Row):
            specs.append(row_of(item, blocks))
            arrays.append(pltpu.with_memory_space_constraint(item.array, pltpu.HBM))
        elif isinstance(item, Part):
            specs.append(block_of(item.array.shape, item.how, blocks, item.pick))
            arrays.append(item.array)
        elif isinstance(item, Pick):
            rows, width = item.array.shape
            specs.append(pl.BlockSpec((rows // item.parts, width), functools.partial(lambda at, i, s: (s[at], 0), item.scalar)))
            arrays.append(pltpu.with_memory_space_constraint(item.array, pltpu.HBM))
        elif isinstance(item, Far):
            specs.append(block_of(item.array.shape, WHOLE, blocks, once=True))
            arrays.append(pltpu.with_memory_space_constraint(item.array, pltpu.HBM))
        elif isinstance(item, Held):
            specs.append(here)
            arrays.append(pltpu.with_memory_space_constraint(item.array, pltpu.VMEM))
            view = view_of(item.array.shape, item.how, blocks)
        else:
            specs.append(block_of(item.shape, WHOLE, blocks, once=True))
            arrays.append(item)
        views.append(view)
    for item in after:
        specs.append(pl.BlockSpec(memory_space=pl.ANY))
        arrays.append(pltpu.with_memory_space_constraint(item.array, pltpu.HBM) if isinstance(item, Far) else item)
        views.append(SKIP)
    shapes, out_specs = [], []
    for shape, dtype, how in outputs:
        if how[:4] == "held":
            shapes.append(pltpu.VMEM(shape, dtype))
            out_specs.append(here)
            views.append(view_of(shape, how[5:], blocks))
        else:
            far = how[:3] == "hbm"
            shapes.append(pltpu.HBM(shape, dtype) if far else jax.ShapeDtypeStruct(shape, dtype))
            out_specs.append(block_of(shape, how[4:] if far else how, blocks))
            views.append(None)
    lead = 0 if scalars is None else 1

    def viewed(*refs):
        passed = list(refs[:lead])
        for ref, view in zip(refs[lead : lead + len(views)], views):
            if view == SKIP:
                continue
            passed.append(ref if view is None else view(ref))
        return kernel(*passed, *refs[lead + len(views) :])

    settings = dict(
        out_shape=shapes,
        compiler_params=pltpu.CompilerParams(vmem_limit_bytes=limit * MIB, dimension_semantics=(ARBITRARY,)),
        cost_estimate=pl.CostEstimate(flops=int(micros * scale * 1.0e9), bytes_accessed=0, transcendentals=0),
        name=getattr(kernel, "func", kernel).__name__,
    )
    if scalars is None:
        return pl.pallas_call(
            viewed, grid=(blocks,), in_specs=specs, out_specs=out_specs, scratch_shapes=list(scratch), **settings
        )(*arrays)
    grid_spec = pltpu.PrefetchScalarGridSpec(
        num_scalar_prefetch=1, grid=(blocks,), in_specs=specs, out_specs=out_specs, scratch_shapes=list(scratch)
    )
    return pl.pallas_call(viewed, grid_spec=grid_spec, **settings)(scalars, *arrays)


def local(
    size, tokens, memory, cotangent, tgt_len, src_len, self_query, self_key, self_value, self_out,
    cross_query, cross_key, cross_value, cross_out, ffn_up, ffn_down,
    gain_one, shift_one, gain_two, shift_two, gain_three, shift_three,
):
    width = tokens.shape[1]
    length = tokens.shape[0] // 2
    source = memory.shape[0] // 2
    each = self_query.shape[1]
    heads = each // HEAD_DIM
    hidden = ffn_up.shape[1]
    place = lax.axis_index("tp").astype(jnp.int32)
    group = lax.axis_index("dp").astype(jnp.int32)
    scalars = jnp.concatenate(
        [jnp.stack([place // 2]), tgt_len, src_len, jnp.stack([place % 2] + [(group >> b) & 1 for b in range(3)])]
    )
    big, small, third = length // BLOCK, length // SPAN, width // SPAN
    short = size == 8

    def across(value):
        return lax.ppermute(value, "tp", ACROSS)

    def sibling(value):
        return lax.ppermute(value, "tp", CORE)

    def along(value, bit):
        return lax.ppermute(value, "dp", [(i, i ^ (1 << bit)) for i in range(size)])

    def shares(part, blocks):
        per = blocks // 2
        first, second = (lambda i: jnp.minimum(i, per - 1)), (lambda i: jnp.maximum(i - per, 0))
        got = [sibling(p) for p in part]
        return [Part(v, HALF, pick) for v, pick in zip((*part, *got), (first, second) * 2)]

    def part_shapes(blocks):
        per = blocks // 2
        first, second = (lambda i: jnp.minimum(i, per - 1)), (lambda i: jnp.maximum(i - per, 0))
        return [((length // 2, width), bf16, (HALF, pick)) for pick in (first, second)]

    head_rows = ((heads, length, WIDE), bf16, FAR_ROWS)
    head_held = ((heads, length, WIDE), bf16, HELD_ROWS)
    key_held = ((heads, source, WIDE), bf16, HELD_ROWS)
    held = ((length, width), f32, HELD_ROWS)
    held_low = ((length, width), bf16, HELD_ROWS)
    column = ((length, 1), f32, HELD_ROWS)
    att_held = ((length, heads * WIDE), bf16, HELD_ROWS)
    dq_held = ((length, each), bf16, HELD_ROWS)
    hid = ((length, hidden), bf16, HELD_ROWS)
    sums = ((8, width), f32, WHOLE)
    low = ((length, width), bf16, ROWS)
    square = ((width, hidden), bf16, ROWS)
    half_low = ((length // 2, width), bf16, WHOLE)
    out_shape = ((each, width), bf16, WHOLE)
    qkv = functools.partial(pltpu.VMEM, (heads, length, WIDE))
    wide_out = pltpu.VMEM((2, heads * WIDE, width), bf16)
    inner_held = ((heads, 8, length), f32, HELD_WHOLE)

    w_parts = (self_query.T, self_key.T, self_value.T)
    c_parts = (cross_query.T, cross_key.T, cross_value.T)
    bit = scalars[BIT]
    w_half = lax.dynamic_slice_in_dim(jnp.concatenate(w_parts, 0), bit * (3 * each // 2), 3 * each // 2, 0)
    w_near = across(w_half)
    q_new, k_new, v_new, k_a, v_a, ck_a, cv_a, w_a, cw_a, o_half, cw_half = call(
        functools.partial(project_own_kernel, heads=heads), big,
        [
            Row(tokens, length, ROWS), Row(memory, source, ROWS), *(Far(v) for v in (*w_parts, *c_parts, self_out, cross_out)),
        ],
        [
            head_held, head_held, head_held, head_rows, head_rows, key_held, key_held, ((3 * each, width), bf16, WHOLE),
            ((3 * each, width), bf16, WHOLE), out_shape, ((3 * each // 2, width), bf16, WHOLE),
        ],
        scalars, micros=7, scale=0.4,
    )
    o_near = across(o_half)
    cw_near = across(cw_half)
    (w_near,) = call(
        pass_kernel, 1, [w_near], [((3 * each // 2, width), bf16, WHOLE)], scalars, micros=1, scale=0.4, after=[o_half]
    )
    w_far = along(w_near, 0)
    quarter = ((hidden // 2, width), bf16, WHOLE)
    q_a, att_a, ffn_half, mark = call(
        functools.partial(self_own_kernel, heads=heads), big,
        [Held(q_new), Held(k_new, WHOLE), Held(v_new, WHOLE), Pick(ffn_up, BIT, 2), Pick(ffn_down, BIT + 1, 2)],
        [head_rows, att_held, ((width, width), bf16, WHOLE), ((8, WIDE), f32, WHOLE)], scalars, micros=6, scale=0.4, after=[w_near],
    )
    ffn_near = across(ffn_half)
    cw_far = along(cw_near, 1)
    (o_near,) = call(pass_kernel, 1, [o_near], [out_shape], scalars, micros=1, scale=0.4, after=[mark])
    o_far = along(o_near, 0)
    w_b, q_b, k_b, v_b, att_b = call(
        functools.partial(self_other_kernel, heads=heads), big, [Row(tokens, length, ROWS), w_near, w_far],
        [((3 * each, width), bf16, WHOLE), head_rows, head_rows, head_rows, att_held], scalars, scratch=[qkv(bf16), qkv(bf16)],
        micros=9, scale=0.4,
    )
    part0, part1, so_b, co_b = call(
        functools.partial(self_out_kernel, heads=heads, blocks=big), big, [Held(att_a), Held(att_b), self_out, o_near, o_far],
        [*part_shapes(big), out_shape, out_shape], scalars, scratch=[wide_out], micros=3, scale=0.4, after=[cw_near],
    )
    h_one, h_one_low, unit_one, scale_one, cq_a, catt_a = call(
        functools.partial(cross_own_kernel, heads=heads, blocks=big), big,
        [Row(tokens, length, ROWS), *shares((part0, part1), big), gain_one, shift_one, c_parts[0], Held(ck_a, WHOLE), Held(cv_a, WHOLE)],
        [held, held_low, held_low, column, head_held, att_held], scalars, micros=10, scale=0.4,
    )
    up_near, down_near = call(
        relay_kernel, 1, [ffn_near], [quarter, quarter], scalars, micros=1, after=[scale_one]
    )
    up_far, down_far = along(up_near, 0), along(down_near, 1)
    cw_b, ck_b, cv_b, cq_b, catt_b = call(
        functools.partial(cross_other_kernel, heads=heads), big,
        [Row(memory, source), Held(h_one_low), cw_near, cw_far],
        [((3 * each, width), bf16, WHOLE), ((heads, source, WIDE), bf16, HELD_WHOLE), ((heads, source, WIDE), bf16, HELD_WHOLE), head_held, att_held],
        scalars, micros=100, scale=1.0, after=[up_near, down_near],
    )
    part0, part1 = call(
        functools.partial(cross_out_kernel, heads=heads, blocks=big), big, [Held(catt_a), Held(catt_b), cross_out, co_b],
        part_shapes(big), scratch=[wide_out], micros=2, scale=0.4, after=[up_far, down_far],
    )
    h_two, h_two_low, unit_two, scale_two, act_a, slope_a, term = call(
        functools.partial(ffn_own_kernel, blocks=big), big,
        [Held(h_one), *shares((part0, part1), big), gain_two, shift_two, Held(ffn_up, WHOLE), Held(ffn_down, WHOLE)],
        [held, held_low, held_low, column, hid, hid, held], micros=7, scale=0.4, limit=24,
    )
    part0, part1, act_b, slope_b, up_b, down_b = call(
        functools.partial(ffn_other_kernel, blocks=big), big,
        [Held(h_two_low), Held(term), up_near, up_far, down_near, down_far],
        [*part_shapes(big), hid, hid, ((width, hidden), bf16, HELD_WHOLE), ((hidden, width), bf16, HELD_WHOLE)], scalars, micros=5, scale=0.4, limit=24,
    )

    part0, part1, out_row, d_three, e_three, pre_a, pre_b, sums_three = call(
        functools.partial(ffn_back_kernel, blocks=small), small,
        [
            Held(h_two), *shares((part0, part1), small), Row(cotangent, length, ROWS), gain_three, shift_three,
            Held(ffn_up, WHOLE), Held(up_b, WHOLE), Held(ffn_down, WHOLE), Held(down_b, WHOLE), Held(slope_a), Held(slope_b),
        ],
        [*part_shapes(small), ((length, width), bf16, FAR_ROWS), held, held_low, hid, hid, sums], scalars, micros=11,
    )
    part = (part0, part1)
    quarter = ((width // 2, hidden), bf16, WHOLE)

    def ffn_grads(act, pre, after=()):
        return call(
            ffn_grad_kernel, 2,
            [Held(h_two_low, COLUMNS), Held(act, COLUMNS), Held(e_three, WHOLE), Held(pre, WHOLE)],
            [square, quarter, quarter], scalars, micros=4, after=after,
        )

    gu_b, send_b, keep_b = ffn_grads(act_b, pre_b)
    gu_got, got_b = across(gu_b), along(send_b, 0)
    gu_a, send_a, keep_a = ffn_grads(act_a, pre_a, [send_b])
    got_a = along(send_a, 0)
    back_scratch = [
        pltpu.VMEM((heads, BLOCK, WIDE), f32), pltpu.VMEM((heads, source, WIDE), f32), pltpu.VMEM((heads, source, WIDE), f32),
    ]
    dkv_held = ((source, 2 * each), bf16, HELD_WHOLE)
    d_two, e_two, sums_two, do_a, inner_a, dcq_b, dckv_b = call(
        functools.partial(cross_back_other_kernel, heads=heads, blocks=big), big,
        [
            Held(d_three), *shares(part, big), gain_two, Held(unit_two), Held(scale_two), cross_out, co_b, Held(catt_a), Held(catt_b), Held(cq_b), Held(ck_b, WHOLE), Held(cv_b, WHOLE),
        ],
        [held, held_low, sums, head_held, inner_held, dq_held, dkv_held], scalars,
        scratch=[wide_out, pltpu.VMEM((heads, BLOCK, WIDE), bf16), pltpu.VMEM((heads, 8, length), f32)] + back_scratch, micros=6,
    )

    def cross_grads(att, dq, dkv, after=()):
        return call(
            cross_grad_kernel, third,
            [
                Held(h_one_low, COLUMNS), Row(memory, source, COLUMNS), Held(att, WHOLE), Held(e_two, COLUMNS),
                Held(dq, WHOLE), Held(dkv, WHOLE),
            ],
            [((4 * each, width), bf16, COLUMNS)], scalars, micros=5, after=after,
        )[0]

    def step(plans, after=(), micros=2):
        inputs, outputs, kernel_plans, counts, most = [], [], [], [], 16
        for kind, arrays, rows, bit, cuts, parts in plans:
            inputs += arrays
            if kind == SUM:
                made = [((rows, width), bf16, WHOLE)] if bit is None else [((rows // 2, width), bf16, WHOLE)] * 2
            elif kind == TWIN:
                made = [((rows, width), bf16, WHOLE)] * 2
                most = max(most, 2 * rows)
            elif kind == SPLIT:
                made = [((rows // 2, width), bf16, WHOLE)] * 2
            elif kind == LAST:
                made = [((rows, width), f32, WHOLE)]
            elif kind in (PACK, STACK, PASS):
                made = [((rows, width), bit if kind == PASS else bf16, WHOLE)]
            else:
                made = [((size, width), f32, FAR_WHOLE) for _, size in cuts]
            if kind in (SUM, WIDEN):
                most = max(most, rows)
            outputs += made
            counts.append(len(made))
            kernel_plans.append((kind, len(arrays), rows, bit, cuts, parts))
        made = list(
            call(
                functools.partial(step_kernel, plans=kernel_plans), 1, inputs, outputs, scalars,
                scratch=[pltpu.VMEM((most, width), bf16)], micros=micros, after=after,
            )
        )
        return [made[sum(counts[:n]) : sum(counts[: n + 1])] for n in range(len(counts))]

    class Chain:
        def __init__(self, mine, got, rows, cuts, bits=(0, 1, 2), back=(2, 1, 0), parts=1):
            self.arrays, self.rows, self.cuts, self.stage = [*mine, *got], rows, cuts, 0
            self.bits, self.back, self.parts = bits, back, parts

        def plan(self):
            count = len(self.bits)
            if self.stage <= count:
                bit = self.bits[self.stage] if self.stage < count else None
                return (SUM, self.arrays, self.rows >> self.stage, bit, (), 1)
            at = self.stage - count
            rows, last = self.rows >> count << at, at == len(self.back)
            bit = self.back[at - 1]
            return (WIDEN if last else PACK, self.arrays, rows, bit, self.cuts if last else (), self.parts if bit < 2 else 1)

        def take(self, made):
            stage, count, self.stage = self.stage, len(self.bits), self.stage + 1
            if stage < count:
                self.arrays = [made[1], along(made[0], self.bits[stage])]
            elif stage < count + len(self.back):
                self.arrays = [made[0], along(made[0], self.back[stage - count])]
            else:
                self.done = made

    def advance(chains, plans=(), after=(), micros=2):
        made = step([c.plan() for c in chains] + list(plans), after, micros)
        for chain, one in zip(chains, made):
            chain.take(one)
        return [made[0][-1]], [m[0] for m in made[len(chains) :]]

    def plain(arrays, rows):
        return (SUM, arrays, rows, None, (), 1)

    def last(mine, got):
        return (LAST, [mine, got], 16, None, (), 1)

    gc_b = cross_grads(catt_b, dcq_b, dckv_b)
    if short:
        (send_u, keep_u), (send_d, keep_d), (gc_b,) = step(
            [
                (SUM, [gu_a, gu_got], width, 0, (), 1), (TWIN, [keep_a, keep_b, got_a, got_b], width // 2, 1, (), 1),
                (PASS, [gc_b], 4 * each, bf16, (), 1),
            ],
            [gc_b],
        )
        got_u, got_d = along(send_u, 0), along(send_d, 1)
    part0, part1, dcq_a, dckv_a = call(
        functools.partial(cross_back_own_kernel, heads=heads, blocks=big), big,
        [Held(cq_a), Held(ck_a, WHOLE), Held(cv_a, WHOLE), Held(do_a), Held(inner_a, WHOLE), Held(dcq_b), c_parts[0], cw_b],
        [*part_shapes(big), dq_held, dkv_held], scalars, scratch=back_scratch, micros=16, after=[gc_b],
    )
    part = (part0, part1)

    gc_got = across(gc_b)
    pin = []
    if short:
        (send_u, keep_u), (down_a, down_b) = step(
            [(SUM, [keep_u, got_u], width // 2, 1, (), 1), (SPLIT, [keep_d, got_d], width // 2, None, (), 1)], [dcq_a]
        )
        ffn = Chain(
            [keep_u, down_a], [along(send_u, 1), across(down_b)], width // 2, [(0, width), (width, width)], (2,), (2, 1, 0), 2
        )
        pin = [keep_u]
    memory_send, memory_keep = call(
        memory_grad_kernel, 2, [Held(dckv_a), Held(dckv_b), cw_a, cw_b], [half_low, half_low], scalars, micros=5, after=pin,
    )
    memory_got = sibling(memory_send)
    gc_a = cross_grads(catt_a, dcq_a, dckv_a, [memory_send])
    memory_plan = plain([memory_keep, memory_got], length // 2)
    pin = [gc_a]
    rest_shape = ((each + 16, width), bf16, WHOLE)
    d_one, do_a, do_b, inner_a, inner_b, rest_a, rest_b = call(
        functools.partial(norm_one_back_kernel, heads=heads, blocks=small), small,
        [
            Held(d_two), *shares(part, small), gain_one, Held(unit_one), Held(scale_one), self_out, so_b,
            Held(att_a, WHOLE), Held(att_b, WHOLE), sums_two, sums_three,
        ],
        [held, head_held, head_held, inner_held, inner_held, rest_shape, rest_shape], scalars,
        scratch=[pltpu.VMEM((length, width), bf16), pltpu.VMEM((8, width), f32), wide_out], micros=6, after=pin,
    )
    rest_got = across(rest_b)
    kept_w = ((3 * each, width), bf16, WHOLE)
    qkv_held = ((length, 3 * each), bf16, HELD_WHOLE)
    self_scratch = [
        pltpu.VMEM((heads, SPAN, WIDE), f32), pltpu.VMEM((heads, length, WIDE), f32), pltpu.VMEM((heads, length, WIDE), f32),
    ]

    def self_back(q, k, v, do, inner, after=()):
        return call(
            functools.partial(self_back_kernel, heads=heads, blocks=small), small,
            [Row(tokens, length), Part(q), k, v, Held(do), Held(inner, WHOLE)], [qkv_held, kept_w], scalars, scratch=self_scratch, micros=14, after=after,
        )

    pin = []
    if short:
        cross = Chain([gc_a], [gc_got], 4 * each, [(n * each, each) for n in range(4)])
        pin, _ = advance([ffn, cross], after=[do_b])
    dqkv_b, gw_b = self_back(q_b, k_b, v_b, do_b, inner_b, pin)
    gw_got = across(gw_b)

    pin = []
    if short:
        pin, (norms,) = advance([ffn, cross], [last(rest_a, rest_got)], [dqkv_b])
        norms = last(norms, along(norms, 0))
    dqkv_a, gw_a = self_back(q_a, k_a, v_a, do_a, inner_a, pin)
    pin = []
    if short:
        own = Chain([gw_a, rest_a], [gw_got, rest_got], 4 * each, [(n * each, each) for n in range(4)])
        pin, (memory_mine, norms) = advance([own, ffn, cross], [memory_plan, norms])
    else:
        ((memory_mine,),) = step([memory_plan], [gw_a])
    tokens_send, tokens_keep = call(
        tokens_grad_kernel, 2, [Held(d_one), Held(dqkv_a), Held(dqkv_b), w_a, w_b],
        [half_low, ((length // 2, width), f32, WHOLE)], scalars, micros=6, after=pin,
    )
    (out_half,) = call(
        pass_kernel, 1, [Row(out_row, length // 2, (PART, CORE_AT))], [half_low], scalars, micros=1, after=[tokens_send]
    )
    out_far = across(out_half)

    def placed(pieces, shift, after=()):
        return call(
            functools.partial(place_kernel, shift=shift), 4, pieces,
            [((2 * length, width), bf16, FAR_ROWS), ((8, WIDE), f32, WHOLE)], scalars, micros=4, after=after,
        )

    def passed(value, rows=length // 2, dtype=bf16):
        return (PASS, [value], rows, dtype, (), 1)

    def pair(mine, far):
        return (STACK, [mine, far], length, None, (), 1)

    if short:
        pin, (memory_mine,) = advance([own, ffn, cross], [passed(memory_mine)], [out_half])
        memory_far = across(memory_mine)
        pin, (tokens_send,) = advance([own, cross], [passed(tokens_send)], [*pin, out_far])
        tokens_plan = plain([tokens_keep, sibling(tokens_send)], length // 2)
        pin, (tokens_mine, memory_pair, out_far) = advance(
            [own, cross], [tokens_plan, pair(memory_mine, memory_far), passed(out_far)], [*pin, ffn.arrays[1]]
        )
        tokens_far, memory_sibling, out_sibling = across(tokens_mine), sibling(memory_pair), sibling(out_far)
        ((gu_wide, gd_wide),) = step([ffn.plan()], pin, 4)
        pin, (norms,) = advance([own], [passed(norms, 16, f32)], [Far(gu_wide), memory_sibling, out_sibling])
        norms = last(norms, along(norms, 2))
        memory_grad, mark = placed([memory_pair, memory_sibling], False, pin)
        pin, (tokens_pair, norms) = advance([own], [pair(tokens_mine, tokens_far), norms], [mark, cross.arrays[1]])
        norms = last(norms, along(norms, 1))
        (cross,) = step([cross.plan()], pin, 3)
        layer_out, mark = placed([out_row, out_far, out_sibling], True, [Far(cross[0])])
        tokens_grad, mark = placed([tokens_pair, sibling(tokens_pair)], False, [mark])
        _, (norms,) = advance([own], [norms], [mark])
        own = own.done
        rest = own[3]
    else:
        memory_far = across(memory_mine)
        tokens_plan = plain([tokens_keep, sibling(tokens_send)], length // 2)
        (tokens_mine,), (memory_pair,) = step([tokens_plan, pair(memory_mine, memory_far)])
        ((tokens_pair,),) = step([pair(tokens_mine, across(tokens_mine))])
        layer_out, _ = placed([out_row, out_far, sibling(out_far)], True)
        memory_grad, _ = placed([memory_pair, sibling(memory_pair)], False)
        tokens_grad, _ = placed([tokens_pair, sibling(tokens_pair)], False)

        def total(mine, got):
            return lax.psum((mine.astype(f32) + got.astype(f32)).astype(bf16), "dp").astype(f32)

        high = scalars[BIT] == 1
        down_a, down_b = (
            jnp.where(high, jnp.concatenate([send, keep]), jnp.concatenate([keep, send]))
            for send, keep in ((send_a, keep_a), (send_b, keep_b))
        )
        gu_wide, gd_wide = total(gu_a, gu_got), total(down_a, across(down_b))
        cross = jnp.split(total(gc_a, gc_got), 4)
        own = jnp.split(total(gw_a, gw_got), 3)
        rest = total(rest_a, rest_got)
        rest, norms = rest[:each], rest[each:]
    return (
        layer_out, tokens_grad, memory_grad,
        own[0].T, own[1].T, own[2].T, rest,
        cross[0].T, cross[1].T, cross[2].T, cross[3],
        gu_wide, gd_wide, *(norms[i] for i in range(6)),
    )


def solution(mesh):
    rows, columns, down = P("dp", None), P(None, "tp"), P("tp", None)
    return jax.shard_map(
        functools.partial(local, mesh.shape["dp"]),
        mesh=mesh,
        in_specs=(rows, rows, rows, P("dp"), P("dp"))
        + (columns, columns, columns, down) * 2
        + (columns, down)
        + (P(),) * 6,
        out_specs=(rows, rows, rows) + (columns, columns, columns, down) * 2 + (columns, down) + (P(),) * 6,
        check_vma=False,
    )
```
